32 devices in a mesh: dp: 8 (over z, x), head: 4 (over y, core).
Axes of the slice: x: 2, y: 2, z: 4, core: 2. Of those that a mesh axis runs over, the one named last changes fastest.
Arguments:
- token_ids: int32 [2, 4096], P(None, ('dp', 'head')), may hold values from 0 to 31999
- lengths: int32 [2, 8, 3], P(None, 'dp'), may hold values from 1 to 409, 512 in all within a row
- valid: int32 [2, 4096], P(None, ('dp', 'head')), may hold values 0 or 1
- vocab_ids: int32 [4096], replicated, may hold values from 0 to 31999, as said below
- teacher: bfloat16 [2, 4096, 4096], P(None, ('dp', 'head')), may hold values from -12 to 12
- block: float32 [768, 12288], P(None, ('dp', 'head'))
- block_m: float32 [768, 12288], P(None, ('dp', 'head')), may hold values from -2.3841858e-07 to 2.3841858e-07
- block_v: float32 [768, 12288], P(None, ('dp', 'head')), may hold values from 1.1876942e-15 to 4.750777e-15
- bases: float32 [4, 768, 768], replicated
- table: float32 [32000, 768], P('dp'), may hold values from -0.4375 to 0.4375
- table_m: float32 [32000, 768], P('dp'), may hold values from -2.3841858e-07 to 2.3841858e-07
- table_v: float32 [32000, 768], P('dp'), may hold values from 1.1876942e-15 to 4.750777e-15
- gains: float32 [3, 768], replicated, may hold values from 0.5 to 1.5
- gains_m: float32 [3, 768], replicated, may hold values from -9.536743e-07 to 9.536743e-07
- gains_v: float32 [3, 768], replicated, may hold values from 1.899135e-14 to 7.6141784e-14
Outputs:
- loss: float32 [], replicated
- grad_norm: float32 [], replicated
- block_new: float32 [768, 12288], P(None, ('dp', 'head'))
- block_m_new: float32 [768, 12288], P(None, ('dp', 'head'))
- block_v_new: float32 [768, 12288], P(None, ('dp', 'head'))
- table_new: float32 [32000, 768], P('dp')
- table_m_new: float32 [32000, 768], P('dp')
- table_v_new: float32 [32000, 768], P('dp')
- gains_new: float32 [3, 768], replicated
- gains_m_new: float32 [3, 768], replicated
- gains_v_new: float32 [3, 768], replicated
- block_low: bfloat16 [768, 12288], P(None, ('dp', 'head'))
- table_low: bfloat16 [32000, 768], P('dp')
The draws below stay inside these ranges and needn't reach their ends.
Inputs may be any that keep to these rules, and one draw needn't show every extreme that they name: `vocab_ids`: distinct ids. Each row holds the lengths of 3 sequences packed in order into one bucket; they sum to 512 and the largest is exactly 409.
All inputs are finite; a program needn't handle non-finite values. No bound on the sum of `valid` on one device may be relied on, other than what follows from the above.
Results may differ from the reference program's by a relative error of at most 0.02.
Values may be sent and summed in bfloat16 or wider, within the bound.
A program may use at most 248 MiB of HBM per device.

```python
import math
import jax
import jax.numpy as jnp
import numpy as np
from jax import lax

D = 768
H = 12
HD = 64
FF = 3072
V = 32000
TOPV = 4096
MB = 2
NSEQ = 3
STEP = 5
TOK_MB = 128
BUCKET = 512
LONGEST = 409
TOK_ALL = 4096
NCOL = 12288
CSH = 384
NPARAM = 34015488
N_DP = 8
N_HEAD = 4


def draw_block(key, part):
    key = jax.random.fold_in(key, 1)
    noise = jax.random.normal(key, (D, NCOL), jnp.float32)
    local = jnp.arange(NCOL, dtype=jnp.int32) % CSH
    device_total = NCOL // CSH
    first = 3 * D // device_total
    second = first + D // device_total
    third = second + 2 * FF // device_total
    scale = jnp.where(local < first, D ** (-0.5), jnp.where(local < second, (D // 32) ** (-0.5), jnp.where(local < third, D ** (-0.5), FF ** (-0.5))))
    return noise * scale[None, :].astype(jnp.float32)


def draw_bases(key, part):
    key = jax.random.fold_in(key, 2)
    noise = jax.random.normal(key, (4, D, D), jnp.float32)
    return jnp.eye(D, dtype=jnp.float32)[None] + 0.3 * D ** (-0.5) * noise


def draw_vocab_ids(key, part):
    key = jax.random.fold_in(key, 3)
    return jax.random.permutation(key, V)[:TOPV].astype(jnp.int32)


def plant(array, stream_key, low, largest):
    dims = array.shape
    place = [jax.random.randint(jax.random.fold_in(stream_key, axis), (), 0, dims[axis]) for axis in range(len(dims))]
    array = array.at[tuple(place)].set(low)
    longest = dims.index(max(dims))
    place[longest] = (place[longest] + 1) % dims[longest]
    return array.at[tuple(place)].set(largest)


def block_levels(stream_key, dims, split, least, largest):
    level = 1.0
    for axis_at, blocks in split:
        heights = jax.random.uniform(jax.random.fold_in(jax.random.fold_in(stream_key, 6), axis_at), (blocks,), jnp.float32, least / len(split), largest / len(split))
        level = level * jnp.repeat(jnp.exp(heights), dims[axis_at] // blocks).reshape((-1,) + (1,) * (len(dims) - 1 - axis_at))
    return level


def rank_bounds(amount, lean):
    portions = [(1 << 20) // math.isqrt(rank ** lean) + 1 for rank in range(1, amount + 1)]
    spread = 1 + sum(portions) // (1 << 30)
    return np.cumsum(np.array([max(1, weight // spread) for weight in portions]))


def ranked(own_key, shape, amount, skew):
    grid = rank_bounds(amount, skew)
    lot = jax.random.randint(jax.random.fold_in(own_key, 1), shape, 0, int(grid[amount - 1]))
    grade = jnp.searchsorted(jnp.asarray(grid, jnp.int32), lot, side="right")
    return jax.random.permutation(jax.random.fold_in(own_key, 2), amount)[grade].astype(jnp.int32)


def length_profile(amount, total, reach, lean):
    weights = [(1 << 20) // math.isqrt(rank ** lean) + 1 for rank in range(2, amount + 1)]
    surplus, counts = total - reach - (amount - 1), [1] * (amount - 1)
    while surplus > 0:
        free = [i for i in range(amount - 1) if counts[i] < reach]
        whole, left = sum([weights[i] for i in free]), surplus
        for i in free:
            extra = min(reach - counts[i], max(1, left * weights[i] // whole), surplus)
            counts[i] = counts[i] + extra
            surplus = surplus - extra
    return np.array([reach] + counts)


def uneven_parts(own_key, number_of, total, bound, skew):
    if number_of == 2:
        one = jax.random.randint(own_key, (), max(1, total - bound), min(bound, total - 1) + 1)
        return jnp.stack([one, total - one])
    sizes = jnp.asarray(length_profile(number_of, total, bound, skew), jnp.int32)
    pairs = (number_of - 1) // 2
    giver, sink = sizes[1:1 + 2 * pairs:2], sizes[2:2 + 2 * pairs:2]
    room = jnp.minimum(giver - 1, bound - sink)
    shifted = jax.random.randint(jax.random.fold_in(own_key, 1), (pairs,), 0, 1 << 20) % (room + 1)
    sizes = sizes.at[1:1 + 2 * pairs:2].set(giver - shifted).at[2:2 + 2 * pairs:2].set(sink + shifted)
    return sizes[jax.random.permutation(jax.random.fold_in(own_key, 2), number_of)]


def centred(own_key, dims, deviation, bound, cuts=(), kind=jnp.bfloat16):
    array = deviation * jax.random.normal(own_key, dims, jnp.float32)
    if cuts:
        array = array * block_levels(own_key, dims, cuts, -0.22, 0.18)
    return jnp.clip(array, -bound, bound).astype(kind)


def setup_inputs(seed: int = 0) -> dict:
    key_list = jax.random.split(jax.random.key(seed), 16)
    token_ids = plant(ranked(key_list[0], (MB, TOK_ALL), V, 2), jax.random.fold_in(key_list[0], 3), 0, V - 1).astype(jnp.int32)
    lengths = jax.vmap(lambda own: uneven_parts(own, NSEQ, BUCKET, LONGEST, 2))(jax.random.split(key_list[1], MB * N_DP)).reshape((MB, N_DP, NSEQ)).astype(jnp.int32)
    valid = plant((jax.random.randint(key_list[2], (MB, TOK_ALL), 0, 4) < 3).astype(jnp.int32), jax.random.fold_in(key_list[2], 1), 0, 1)
    vocab_ids = draw_vocab_ids(jax.random.fold_in(key_list[15], 71), 0)
    teacher = centred(key_list[4], (MB, TOK_ALL, TOPV), 2.0, 12.0, ((1, 32),))
    block = draw_block(jax.random.fold_in(key_list[15], 71), 0)
    block_m = centred(key_list[6], (D, NCOL), (0.00022 * NPARAM ** -0.5), 2.384185791015625e-07, ((1, 32),), jnp.float32)
    block_v = jnp.clip(jnp.exp(math.log(4.750776984671244e-15) - 1.3862944 * jax.random.uniform(key_list[7], (D, NCOL), jnp.float32) ** block_levels(key_list[7], (D, NCOL), ((1, 32),), -0.2, 0.2)), 1.187694246167811e-15, 4.750776984671244e-15)
    bases = draw_bases(jax.random.fold_in(key_list[15], 71), 0)
    table = centred(key_list[9], (V, D), 0.07, 0.4375, ((0, 8),), jnp.float32)
    table_m = centred(key_list[10], (V, D), (0.00022 * NPARAM ** -0.5), 2.384185791015625e-07, ((0, 8),), jnp.float32)
    table_v = jnp.clip(jnp.exp(math.log(4.750776984671244e-15) - 1.3862944 * jax.random.uniform(key_list[11], (V, D), jnp.float32) ** block_levels(key_list[11], (V, D), ((0, 8),), -0.2, 0.2)), 1.187694246167811e-15, 4.750776984671244e-15)
    gains = jnp.clip(1.0 + 0.1 * jax.random.normal(key_list[12], (3, D), jnp.float32), 0.5, 1.5)
    gains_m = centred(key_list[13], (3, D), (0.00088 * NPARAM ** -0.5), 9.5367431640625e-07, (), jnp.float32)
    gains_v = jnp.clip(jnp.exp(jax.random.uniform(key_list[14], (3, D), jnp.float32, math.log(1.899134942731119e-14), math.log(7.6141783850181e-14))), 1.899134942731119e-14, 7.6141783850181e-14)
    return {"token_ids": token_ids, "lengths": lengths, "valid": valid, "vocab_ids": vocab_ids, "teacher": teacher, "block": block, "block_m": block_m, "block_v": block_v, "bases": bases, "table": table, "table_m": table_m, "table_v": table_v, "gains": gains, "gains_m": gains_m, "gains_v": gains_v}


@jax.custom_vjp
def low(v):
    return lax.optimization_barrier(v.astype(jnp.bfloat16)).astype(jnp.float32)

@jax.custom_vjp
def low_back(v):
    return v

def low_keep(v):
    return (low(v), None)

def low_pass(kept, grad):
    return (grad,)

def back_keep(v):
    return (v, None)

def back_low(kept, grad):
    return (low(grad),)
low.defvjp(low_keep, low_pass)
low_back.defvjp(back_keep, back_low)
highest = lax.Precision.HIGHEST
eps_norm = 1e-05
clip_norm = 0.002
beta_one = 0.9
beta_two = 0.99
adam_eps = 1e-08
decay_rate = 0.1
rate_block = 0.03
rate_table = 0.05
rate_gain = 0.4

def low_both(value):
    return low(low_back(value))

def rms_norm(value, gain):
    return value * lax.rsqrt(lax.optimization_barrier(jnp.mean(value * value, axis=-1, keepdims=True)) + eps_norm) * gain

def rotary(value, cosine, sine):
    half = value.shape[-1] // 2
    turned = jnp.concatenate([-value[..., half:], value[..., :half]], axis=-1)
    return value * cosine[:, None, :] + turned * sine[:, None, :]

def tables(seq_lengths, size):
    ends = jnp.cumsum(seq_lengths).astype(jnp.int32)
    starts = (ends - seq_lengths).astype(jnp.int32)
    places = jnp.arange(size, dtype=jnp.int32)
    segment = lax.optimization_barrier(jnp.sum((places[:, None] >= ends[None, :]).astype(jnp.int32), axis=1)).astype(jnp.int32)
    member = segment[:, None] == jnp.arange(seq_lengths.shape[0], dtype=jnp.int32)[None, :]
    begin = lax.optimization_barrier(jnp.sum(jnp.where(member, starts[None, :], 0), axis=1)).astype(jnp.int32)
    position = (places - begin).astype(jnp.float32)
    freqs = jnp.exp(jnp.arange(0, HD, 2, dtype=jnp.float32) * (-math.log(10000.0) / HD))
    angle = position[:, None] * freqs[None, :]
    angle = jnp.concatenate([angle, angle], axis=1)
    allow = (segment[:, None] == segment[None, :]) & (places[:, None] >= places[None, :])
    return (allow, jnp.cos(angle), jnp.sin(angle))

def split_block(full, device_total):
    rows = full.shape[0]
    grouped = full.reshape(rows, device_total, -1)
    widths = [3 * D // device_total, D // device_total, 2 * FF // device_total, FF // device_total]
    pieces = []
    first = 0
    for width in widths:
        pieces.append(grouped[:, :, first:first + width].reshape(rows, device_total * width))
        first = first + width
    return pieces

def join_block(pieces, device_total):
    rows = pieces[0].shape[0]
    return jnp.concatenate([piece.reshape(rows, device_total, -1) for piece in pieces], axis=2).reshape(rows, -1)

def attend(query, key_rot, value, allow):
    score = low_back(jnp.einsum('qhd,khd->hqk', query, key_rot, precision=highest) * HD ** (-0.5))
    score = jnp.where(allow[None], score, -1e+30)
    weight = jax.nn.softmax(score, axis=-1)
    return low_both(jnp.einsum('hqk,khd->qhd', low(weight), value, precision=highest))

def layer(hidden, weights, gains, cosine, sine, allow):
    w_qkv, w_out, w_gu, w_down = weights
    rows = hidden.shape[0]
    normed = low(rms_norm(hidden, gains[0]))
    qkv = low_back(jnp.dot(normed, w_qkv, precision=highest)).reshape(rows, 3, H, HD)
    query = low_both(rotary(qkv[:, 0], cosine, sine))
    key_rot = low_both(rotary(qkv[:, 1], cosine, sine))
    value = low_both(qkv[:, 2])
    mixed = attend(query, key_rot, value, allow).reshape(rows, D)
    middle = hidden + low_back(jnp.dot(mixed, w_out, precision=highest))
    normed_two = low(rms_norm(middle, gains[1]))
    gate_up = low_back(jnp.dot(normed_two, w_gu, precision=highest))
    action = low(jax.nn.silu(gate_up[:, :FF]) * gate_up[:, FF:])
    return middle + low_back(jnp.dot(action, w_down.T, precision=highest))

def objective(block, table, gains, token_ids, lengths, valid, vocab_ids, teacher):
    device_total = N_DP * N_HEAD
    table_round = low(table)
    weights = [low(piece) for piece in split_block(block, device_total)]
    chosen = table_round[vocab_ids]
    bucket = N_HEAD * TOK_MB
    items = (token_ids.reshape(-1, bucket), lengths.reshape(-1, NSEQ), valid.reshape(-1, bucket), teacher.reshape(-1, bucket, TOPV))

    def one_bucket(total, item):
        ids_row, len_row, valid_row, teacher_row = item
        allow, cosine, sine = tables(len_row, bucket)
        hidden = low_back(table_round[ids_row])
        for repeat in range(2):
            hidden = layer(hidden, weights, gains, cosine, sine, allow)
        normed = low(rms_norm(hidden, gains[2]))
        logits = low_back(jnp.dot(normed, chosen.T, precision=highest))
        log_prob = jax.nn.log_softmax(logits, axis=-1)
        teach = jax.nn.log_softmax(teacher_row.astype(jnp.float32), axis=-1)
        diverge = lax.optimization_barrier(jnp.sum(jnp.exp(teach) * (teach - log_prob), axis=-1))
        return (total + jnp.sum(valid_row.astype(jnp.float32) * diverge), None)
    total, unused = lax.scan(jax.checkpoint(one_bucket), jnp.zeros((), jnp.float32), items)
    return total

def adam_step(weight, gradient, first, second, rate, decay):
    first_new = beta_one * first + (1.0 - beta_one) * gradient
    second_new = beta_two * second + (1.0 - beta_two) * gradient * gradient
    direction = first_new / (1.0 - beta_one ** STEP) / (jnp.sqrt(second_new / (1.0 - beta_two ** STEP)) + adam_eps)
    return (weight - rate * (direction + decay * weight), first_new, second_new)

def reference(token_ids, lengths, valid, vocab_ids, teacher, block, block_m, block_v, bases, table, table_m, table_v, gains, gains_m, gains_v):
    device_total = N_DP * N_HEAD

    def wrapped(block_in, table_in, gains_in):
        return objective(block_in, table_in, gains_in, token_ids, lengths, valid, vocab_ids, teacher)
    total, pullback = jax.vjp(wrapped, block, table, gains)
    g_block, g_table, g_gains = pullback(jnp.ones_like(total))
    count = jnp.sum(valid.astype(jnp.float32))
    g_block = g_block / count
    g_table = g_table / count
    g_gains = g_gains / count
    grad_norm = jnp.sqrt(jnp.sum(g_block * g_block) + jnp.sum(g_table * g_table) + jnp.sum(g_gains * g_gains))
    clip = jnp.minimum(1.0, clip_norm / grad_norm)
    g_block = g_block * clip
    g_table = g_table * clip
    g_gains = g_gains * clip
    rotated = join_block([jnp.dot(bases[index].T, piece, precision=highest) for index, piece in enumerate(split_block(g_block, device_total))], device_total)
    block_m_new = beta_one * block_m + (1.0 - beta_one) * rotated
    block_v_new = beta_two * block_v + (1.0 - beta_two) * rotated * rotated
    direction = block_m_new / (1.0 - beta_one ** STEP) / (jnp.sqrt(block_v_new / (1.0 - beta_two ** STEP)) + adam_eps)
    update = join_block([jnp.dot(bases[index], piece, precision=highest) for index, piece in enumerate(split_block(direction, device_total))], device_total)
    block_new = block - rate_block * (update + decay_rate * block)
    table_new, table_m_new, table_v_new = adam_step(table, g_table, table_m, table_v, rate_table, decay_rate)
    gains_new, gains_m_new, gains_v_new = adam_step(gains, g_gains, gains_m, gains_v, rate_gain, 0.0)
    return (total / count, grad_norm, block_new, block_m_new, block_v_new, table_new, table_m_new, table_v_new, gains_new, gains_m_new, gains_v_new, block_new.astype(jnp.bfloat16), table_new.astype(jnp.bfloat16))
```

```python
import math

import jax
import jax.numpy as jnp
from jax import lax
from jax.sharding import PartitionSpec as P

D = 768
H = 12
HD = 64
FF = 3072
TOPV = 4096
STEP = 5

low = jnp.bfloat16
scale = HD**-0.5
eps_norm = 1e-05
clip_norm = 0.002
beta_one = 0.9
beta_two = 0.99
adam_eps = 1e-08
decay_rate = 0.1
rate_block = 0.03
rate_table = 0.05
rate_gain = 0.4


def product(left, right):
    return jnp.dot(left, right, preferred_element_type=jnp.float32)


def contract_rows(left, right):
    return lax.dot_general(
        left, right, (((0,), (0,)), ((), ())), preferred_element_type=jnp.float32
    )


def contract_cols(left, right):
    return lax.dot_general(
        left, right, (((1,), (1,)), ((), ())), preferred_element_type=jnp.float32
    )


def rms_norm(value, gain):
    return value * lax.rsqrt(jnp.mean(value * value, axis=-1, keepdims=True) + eps_norm) * gain


def rms_back(value, gain, grad):
    r = lax.rsqrt(jnp.mean(value * value, axis=-1, keepdims=True) + eps_norm)
    scaled = grad * gain
    d_value = r * scaled - value * (r * r * r) * jnp.mean(value * scaled, axis=-1, keepdims=True)
    return d_value, jnp.sum(grad * value * r, axis=0)


def rotary(value, cosine, sine):
    half = HD // 2
    turned = jnp.concatenate([-value[..., half:], value[..., :half]], axis=-1)
    return value * cosine[:, None, :] + turned * sine[:, None, :]


def rotary_back(grad, cosine, sine):
    half = HD // 2
    part = grad * sine[:, None, :]
    turned = jnp.concatenate([part[..., half:], -part[..., :half]], axis=-1)
    return grad * cosine[:, None, :] + turned


def segments(lengths, places):
    segment = jnp.zeros_like(places)
    begin = jnp.zeros_like(places)
    end = jnp.zeros((), jnp.int32)
    for index in range(lengths.shape[0] - 1):
        end = end + lengths[index]
        past = places >= end
        segment = segment + past.astype(jnp.int32)
        begin = jnp.where(past, end, begin)
    return segment, places - begin


def scores_of(query, keys, allow):
    score = jnp.einsum("qhd,khd->hqk", query, keys, preferred_element_type=jnp.float32) * scale
    return jnp.where(allow[None], score, -1e30)


def attend(query, keys, values, allow):
    score = scores_of(query, keys, allow)
    summit = jnp.max(score, axis=-1, keepdims=True)
    log_total = summit + jnp.log(jnp.sum(jnp.exp(score - summit), axis=-1, keepdims=True))
    weight = jnp.exp(score - log_total)
    mixed = jnp.einsum(
        "hqk,khd->qhd", weight.astype(low), values, preferred_element_type=jnp.float32
    )
    return mixed.astype(low), log_total


def attend_back(query, keys, values, log_total, upstream, allow):
    weight = jnp.exp(scores_of(query, keys, allow) - log_total)
    d_value = jnp.einsum(
        "hqk,qhd->khd", weight.astype(low), upstream, preferred_element_type=jnp.float32
    )
    d_weight = jnp.einsum("qhd,khd->hqk", upstream, values, preferred_element_type=jnp.float32)
    d_score = (weight * (d_weight - jnp.sum(d_weight * weight, axis=-1, keepdims=True))).astype(low)
    d_query = jnp.einsum("hqk,khd->qhd", d_score, keys, preferred_element_type=jnp.float32) * scale
    d_key = jnp.einsum("hqk,qhd->khd", d_score, query, preferred_element_type=jnp.float32) * scale
    return d_query, d_key, d_value


def swap(value, head_count, offset):
    return lax.ppermute(value, "head", [(h, h ^ offset) for h in range(head_count)])


def layer_forward(hidden, weights, gains, cosine, sine, allow, head_count):
    w_qkv, w_out, w_gu, w_down = weights
    rows = hidden.shape[0]
    normed = rms_norm(hidden, gains[0]).astype(low)
    qkv = contract_cols(normed, w_qkv).reshape(rows, 3, H, HD)
    query = rotary(qkv[:, 0], cosine, sine).astype(low)
    key = rotary(qkv[:, 1], cosine, sine).astype(low)
    own = jnp.concatenate([key, qkv[:, 2].astype(low)], axis=1)
    both = jnp.concatenate([own, swap(own, head_count, 1)], axis=0)
    keys, values = both[:, :H], both[:, H:]
    mixed, log_total = attend(query, keys, values, allow)
    merged = mixed.reshape(rows, D)
    middle = hidden + contract_cols(merged, w_out)
    normed_two = rms_norm(middle, gains[1]).astype(low)
    gate_up = contract_cols(normed_two, w_gu)
    action = (jax.nn.silu(gate_up[:, :FF]) * gate_up[:, FF:]).astype(low)
    output = middle + product(action, w_down)
    saved = (hidden, normed, query, keys, values, log_total, merged, middle, normed_two, gate_up, action)
    return output, saved


def layer_backward(gradient, weights, gains, saved, cosine, sine, allow, head_count):
    w_qkv, w_out, w_gu, w_down = weights
    hidden, normed, query, keys, values, log_total, merged, middle, normed_two, gate_up, action = saved
    rows = hidden.shape[0]
    grad_low = gradient.astype(low)
    d_down = contract_rows(action, grad_low)
    d_action = contract_cols(grad_low, w_down)
    gate, up = gate_up[:, :FF], gate_up[:, FF:]
    chance = jax.nn.sigmoid(gate)
    d_gate = d_action * up * (chance + gate * chance * (1.0 - chance))
    d_up = d_action * gate * chance
    d_gate_up = jnp.concatenate([d_gate, d_up], axis=1).astype(low)
    d_gu = contract_rows(d_gate_up, normed_two)
    d_middle, d_gain_two = rms_back(middle, gains[1], product(d_gate_up, w_gu))
    d_middle = gradient + d_middle
    middle_low = d_middle.astype(low)
    d_out = contract_rows(middle_low, merged)
    upstream = product(middle_low, w_out).astype(low).reshape(rows, H, HD)
    d_query, d_key, d_value = attend_back(query, keys, values, log_total, upstream, allow)
    d_own = jnp.concatenate([d_key[:rows], d_value[:rows]], axis=1)
    d_far = jnp.concatenate([d_key[rows:], d_value[rows:]], axis=1).astype(low)
    d_own = (d_own + swap(d_far, head_count, 1).astype(jnp.float32)).astype(low).astype(jnp.float32)
    d_query = rotary_back(d_query.astype(low).astype(jnp.float32), cosine, sine)
    d_key = rotary_back(d_own[:, :H], cosine, sine)
    d_qkv = jnp.concatenate([d_query, d_key, d_own[:, H:]], axis=1).reshape(rows, 3 * D).astype(low)
    d_qkv_w = contract_rows(d_qkv, normed)
    d_hidden, d_gain_one = rms_back(hidden, gains[0], product(d_qkv, w_qkv))
    return d_middle + d_hidden, [d_qkv_w, d_out, d_gu, d_down], d_gain_one, d_gain_two


def adam_step(weight, gradient, first, second, rate, decay):
    first_new = beta_one * first + (1.0 - beta_one) * gradient
    second_new = beta_two * second + (1.0 - beta_two) * gradient * gradient
    direction = (
        first_new
        / (1.0 - beta_one**STEP)
        / (jnp.sqrt(second_new / (1.0 - beta_two**STEP)) + adam_eps)
    )
    return (weight - rate * (direction + decay * weight), first_new, second_new)


def on_device(
    token_ids,
    lengths,
    valid,
    vocab_ids,
    teacher,
    block,
    block_m,
    block_v,
    bases,
    table,
    table_m,
    table_v,
    gains,
    gains_m,
    gains_v,
):
    dp_count, head_count = lax.axis_size("dp"), lax.axis_size("head")
    device_total = dp_count * head_count
    head, dp = lax.axis_index("head"), lax.axis_index("dp")
    batch = head // 2
    tokens = token_ids.shape[1]
    shard_rows = table.shape[0]
    offset = dp * shard_rows
    part = TOPV // device_total

    codes = lax.all_gather(token_ids * 2 + valid, ("dp", "head"), axis=1, tiled=True)
    count = jnp.sum(codes & 1).astype(jnp.float32)
    codes = lax.dynamic_index_in_dim(codes, batch, 0, keepdims=False).reshape(
        dp_count, head_count, tokens
    )
    first = lax.dynamic_index_in_dim(codes, head, 1, keepdims=False)
    second = lax.dynamic_index_in_dim(codes, head ^ 2, 1, keepdims=False)
    codes = jnp.concatenate([first, second], axis=1)
    weighting = (lax.dynamic_index_in_dim(codes, dp, 0, keepdims=False) & 1).astype(jnp.float32)
    vocab = lax.dynamic_index_in_dim(
        vocab_ids.reshape(dp_count, head_count, part), head, 1, keepdims=False
    )
    local = jnp.concatenate([vocab, codes >> 1], axis=1) - offset
    owned = (local >= 0) & (local < shard_rows)
    rows_out = jnp.where(
        owned[..., None], table[jnp.clip(local, 0, shard_rows - 1)], 0.0
    ).astype(low)
    rows_in = lax.psum_scatter(rows_out, "dp", scatter_dimension=0, tiled=True)
    rows_in = rows_in.reshape(part + 2 * tokens, D)
    chosen = lax.all_gather(rows_in[:part], ("dp", "head"), axis=0, tiled=True)
    hidden = rows_in[part:].astype(jnp.float32)

    widths = [3 * D // device_total, D // device_total, 2 * FF // device_total, FF // device_total]
    cuts = [sum(widths[:index]) for index in range(5)]
    gathered = lax.all_gather(block.T.astype(low), ("dp", "head"), axis=0)
    weights = [
        gathered[:, cuts[index] : cuts[index + 1]].reshape(-1, D) for index in range(4)
    ]

    teacher_own = lax.dynamic_index_in_dim(teacher, batch, 0, keepdims=False)
    teacher_far = swap(
        lax.dynamic_index_in_dim(teacher, 1 - batch, 0, keepdims=False), head_count, 2
    )
    teacher_rows = jnp.concatenate([teacher_own, teacher_far], axis=0)

    run = jnp.arange(tokens, dtype=jnp.int32)
    places = jnp.concatenate([head * tokens + run, (head ^ 2) * tokens + run])
    places_far = jnp.concatenate([(head ^ 1) * tokens + run, (head ^ 3) * tokens + run])
    own_lengths = lax.dynamic_index_in_dim(lengths, batch, 0, keepdims=False)[0]
    segment, position = segments(own_lengths, places)
    segment_far, unused = segments(own_lengths, places_far)
    places_all = jnp.concatenate([places, places_far])
    segment_all = jnp.concatenate([segment, segment_far])
    allow = (segment[:, None] == segment_all[None, :]) & (places[:, None] >= places_all[None, :])
    freqs = jnp.exp(jnp.arange(0, HD, 2, dtype=jnp.float32) * (-math.log(10000.0) / HD))
    angle = position.astype(jnp.float32)[:, None] * freqs[None, :]
    angle = jnp.concatenate([angle, angle], axis=1)
    cosine, sine = jnp.cos(angle), jnp.sin(angle)

    saves = []
    for repeat in range(2):
        hidden, saved = layer_forward(hidden, weights, gains, cosine, sine, allow, head_count)
        saves.append(saved)

    normed = rms_norm(hidden, gains[2]).astype(low)
    log_prob = jax.nn.log_softmax(contract_cols(normed, chosen), axis=-1)
    teach = jax.nn.log_softmax(teacher_rows.astype(jnp.float32), axis=-1)
    loss_sum = jnp.sum(weighting * jnp.sum(jnp.exp(teach) * (teach - log_prob), axis=-1))
    logit_grads = ((jnp.exp(log_prob) - jnp.exp(teach)) * weighting[:, None]).astype(low)
    chosen_grads = contract_rows(logit_grads, normed).astype(low)
    gradient, d_gain_final = rms_back(hidden, gains[2], product(logit_grads, chosen))
    chosen_grads = lax.psum_scatter(chosen_grads, ("dp", "head"), scatter_dimension=0, tiled=True)

    block_grads = None
    d_gains = [0.0, 0.0]
    for repeat in range(2):
        gradient, layer_grads, d_gain_one, d_gain_two = layer_backward(
            gradient, weights, gains, saves[1 - repeat], cosine, sine, allow, head_count
        )
        d_gains = [d_gains[0] + d_gain_one, d_gains[1] + d_gain_two]
        if block_grads is None:
            block_grads = layer_grads
        else:
            block_grads = [total + extra for total, extra in zip(block_grads, layer_grads)]

    joined = jnp.concatenate(
        [piece.astype(low).reshape(device_total, -1, D) for piece in block_grads], axis=1
    )
    block_grads = lax.psum_scatter(joined, ("dp", "head"), scatter_dimension=0, tiled=True)
    block_grads = block_grads.reshape(-1, D).astype(jnp.float32).T

    rows_back = jnp.concatenate([chosen_grads, gradient.astype(low)], axis=0)
    rows_back = lax.all_gather(rows_back, "dp", axis=0, tiled=True)
    dump_index = jnp.where(owned, local, shard_rows).reshape(-1)
    table_grads = jax.ops.segment_sum(
        rows_back.astype(jnp.float32), dump_index, num_segments=shard_rows + 1
    )[:shard_rows]
    table_grads = lax.psum(table_grads.astype(low), "head").astype(jnp.float32)

    small = jnp.concatenate([d_gains[0], d_gains[1], d_gain_final, loss_sum[None]])
    small = lax.psum(small, ("dp", "head"))
    gain_grads = small[: 3 * D].reshape(3, D) / count
    loss = small[3 * D] / count

    squares = lax.psum(
        jnp.sum(block_grads * block_grads)
        + jnp.where(head == 0, jnp.sum(table_grads * table_grads), 0.0),
        ("dp", "head"),
    )
    grad_norm = jnp.sqrt(squares / (count * count) + jnp.sum(gain_grads * gain_grads))
    clip = jnp.minimum(1.0, clip_norm / grad_norm)
    factor = clip / count
    block_grads = block_grads * factor
    table_grads = table_grads * factor
    gain_grads = gain_grads * clip

    rotated = jnp.concatenate(
        [
            contract_rows(bases[index], block_grads[:, cuts[index] : cuts[index + 1]])
            for index in range(4)
        ],
        axis=1,
    )
    block_m_new = beta_one * block_m + (1.0 - beta_one) * rotated
    block_v_new = beta_two * block_v + (1.0 - beta_two) * rotated * rotated
    direction = (
        block_m_new
        / (1.0 - beta_one**STEP)
        / (jnp.sqrt(block_v_new / (1.0 - beta_two**STEP)) + adam_eps)
    )
    update = jnp.concatenate(
        [product(bases[index], direction[:, cuts[index] : cuts[index + 1]]) for index in range(4)],
        axis=1,
    )
    block_new = block - rate_block * (update + decay_rate * block)
    table_new, table_m_new, table_v_new = adam_step(
        table, table_grads, table_m, table_v, rate_table, decay_rate
    )
    gains_new, gains_m_new, gains_v_new = adam_step(
        gains, gain_grads, gains_m, gains_v, rate_gain, 0.0
    )
    return (
        loss,
        grad_norm,
        block_new,
        block_m_new,
        block_v_new,
        table_new,
        table_m_new,
        table_v_new,
        gains_new,
        gains_m_new,
        gains_v_new,
        block_new.astype(low),
        table_new.astype(low),
    )


def solution(mesh):
    tokens = P(None, ("dp", "head"))
    columns = P(None, ("dp", "head"))
    table = P("dp", None)
    return jax.shard_map(
        on_device,
        mesh=mesh,
        in_specs=(
            tokens,
            P(None, "dp", None),
            tokens,
            P(),
            P(None, ("dp", "head"), None),
            columns,
            columns,
            columns,
            P(),
            table,
            table,
            table,
            P(),
            P(),
            P(),
        ),
        out_specs=(
            P(),
            P(),
            columns,
            columns,
            columns,
            table,
            table,
            table,
            P(),
            P(),
            P(),
            columns,
            table,
        ),
        check_vma=False,
    )
```

```python
import functools
import math

import jax
import jax.numpy as jnp
from jax import lax
from jax.experimental import pallas as pl
from jax.experimental.pallas import tpu as pltpu
from jax.sharding import PartitionSpec as P

D = 768
H = 12
HD = 64
FF = 3072
TOPV = 4096
STEP = 5

low = jnp.bfloat16
scale = HD**-0.5
eps_norm = 1e-05
clip_norm = 0.002
beta_one = 0.9
beta_two = 0.99
adam_eps = 1e-08
decay_rate = 0.1
rate_block = 0.03
rate_table = 0.05
rate_gain = 0.4


def product(left, right):
    return jnp.dot(left, right, preferred_element_type=jnp.float32)


def contract_rows(left, right):
    return lax.dot_general(
        left, right, (((0,), (0,)), ((), ())), preferred_element_type=jnp.float32
    )


def contract_cols(left, right):
    return lax.dot_general(
        left, right, (((1,), (1,)), ((), ())), preferred_element_type=jnp.float32
    )


def rms_norm(value, gain):
    return value * lax.rsqrt(jnp.mean(value * value, axis=-1, keepdims=True) + eps_norm) * gain


def rms_back(value, gain, grad):
    r = lax.rsqrt(jnp.mean(value * value, axis=-1, keepdims=True) + eps_norm)
    scaled = grad * gain
    d_value = r * scaled - value * (r * r * r) * jnp.mean(value * scaled, axis=-1, keepdims=True)
    return d_value, jnp.sum(grad * value * r, axis=0)


def rotary(value, cosine, sine):
    half = HD // 2
    turned = jnp.concatenate([-value[..., half:], value[..., :half]], axis=-1)
    return value * cosine[:, None, :] + turned * sine[:, None, :]


def rotary_back(grad, cosine, sine):
    half = HD // 2
    part = grad * sine[:, None, :]
    turned = jnp.concatenate([part[..., half:], -part[..., :half]], axis=-1)
    return grad * cosine[:, None, :] + turned


def segments(lengths, places):
    segment = jnp.zeros_like(places)
    begin = jnp.zeros_like(places)
    end = jnp.zeros((), jnp.int32)
    for index in range(lengths.shape[0] - 1):
        end = end + lengths[index]
        past = places >= end
        segment = segment + past.astype(jnp.int32)
        begin = jnp.where(past, end, begin)
    return segment, places - begin


def scores_of(query, keys, allow):
    score = jnp.einsum("qhd,khd->hqk", query, keys, preferred_element_type=jnp.float32) * scale
    return jnp.where(allow[None], score, -1e30)


def attend(query, keys, values, allow):
    score = scores_of(query, keys, allow)
    summit = jnp.max(score, axis=-1, keepdims=True)
    log_total = summit + jnp.log(jnp.sum(jnp.exp(score - summit), axis=-1, keepdims=True))
    weight = jnp.exp(score - log_total)
    mixed = jnp.einsum(
        "hqk,khd->qhd", weight.astype(low), values, preferred_element_type=jnp.float32
    )
    return mixed.astype(low), log_total


def attend_back(query, keys, values, log_total, upstream, allow):
    weight = jnp.exp(scores_of(query, keys, allow) - log_total)
    d_value = jnp.einsum(
        "hqk,qhd->khd", weight.astype(low), upstream, preferred_element_type=jnp.float32
    )
    d_weight = jnp.einsum("qhd,khd->hqk", upstream, values, preferred_element_type=jnp.float32)
    d_score = (weight * (d_weight - jnp.sum(d_weight * weight, axis=-1, keepdims=True))).astype(low)
    d_query = jnp.einsum("hqk,khd->qhd", d_score, keys, preferred_element_type=jnp.float32) * scale
    d_key = jnp.einsum("hqk,qhd->khd", d_score, query, preferred_element_type=jnp.float32) * scale
    return d_query, d_key, d_value


def swap(value, head_count, offset):
    return lax.ppermute(value, "head", [(h, h ^ offset) for h in range(head_count)])


def layer_forward(hidden, weights, gains, cosine, sine, allow, head_count):
    w_qkv, w_out, w_gu, w_down = weights
    rows = hidden.shape[0]
    normed = rms_norm(hidden, gains[0]).astype(low)
    qkv = contract_cols(normed, w_qkv).reshape(rows, 3, H, HD)
    query = rotary(qkv[:, 0], cosine, sine).astype(low)
    key = rotary(qkv[:, 1], cosine, sine).astype(low)
    own = jnp.concatenate([key, qkv[:, 2].astype(low)], axis=1)
    both = jnp.concatenate([own, swap(own, head_count, 1)], axis=0)
    keys, values = both[:, :H], both[:, H:]
    mixed, log_total = attend(query, keys, values, allow)
    merged = mixed.reshape(rows, D)
    middle = hidden + contract_cols(merged, w_out)
    normed_two = rms_norm(middle, gains[1]).astype(low)
    gate_up = contract_cols(normed_two, w_gu)
    action = (jax.nn.silu(gate_up[:, :FF]) * gate_up[:, FF:]).astype(low)
    output = middle + product(action, w_down)
    saved = (hidden, normed, query, keys, values, log_total, merged, middle, normed_two, gate_up, action)
    return output, saved


def layer_backward(gradient, weights, gains, saved, cosine, sine, allow, head_count):
    w_qkv, w_out, w_gu, w_down = weights
    hidden, normed, query, keys, values, log_total, merged, middle, normed_two, gate_up, action = saved
    rows = hidden.shape[0]
    grad_low = gradient.astype(low)
    d_down = contract_rows(action, grad_low)
    d_action = contract_cols(grad_low, w_down)
    gate, up = gate_up[:, :FF], gate_up[:, FF:]
    chance = jax.nn.sigmoid(gate)
    d_gate = d_action * up * (chance + gate * chance * (1.0 - chance))
    d_up = d_action * gate * chance
    d_gate_up = jnp.concatenate([d_gate, d_up], axis=1).astype(low)
    d_gu = contract_rows(d_gate_up, normed_two)
    d_middle, d_gain_two = rms_back(middle, gains[1], product(d_gate_up, w_gu))
    d_middle = gradient + d_middle
    middle_low = d_middle.astype(low)
    d_out = contract_rows(middle_low, merged)
    upstream = product(middle_low, w_out).astype(low).reshape(rows, H, HD)
    d_query, d_key, d_value = attend_back(query, keys, values, log_total, upstream, allow)
    d_own = jnp.concatenate([d_key[:rows], d_value[:rows]], axis=1)
    d_far = jnp.concatenate([d_key[rows:], d_value[rows:]], axis=1).astype(low)
    d_own = (d_own + swap(d_far, head_count, 1).astype(jnp.float32)).astype(low).astype(jnp.float32)
    d_query = rotary_back(d_query.astype(low).astype(jnp.float32), cosine, sine)
    d_key = rotary_back(d_own[:, :H], cosine, sine)
    d_qkv = jnp.concatenate([d_query, d_key, d_own[:, H:]], axis=1).reshape(rows, 3 * D).astype(low)
    d_qkv_w = contract_rows(d_qkv, normed)
    d_hidden, d_gain_one = rms_back(hidden, gains[0], product(d_qkv, w_qkv))
    return d_middle + d_hidden, [d_qkv_w, d_out, d_gu, d_down], d_gain_one, d_gain_two


MESH = pl.DeviceIdType.MESH
ANY = pl.BlockSpec(memory_space=pl.ANY)


def coordinates(depth):
    dp, head = lax.axis_index("dp"), lax.axis_index("head")
    return dp // 2, dp % 2, head // 2, head % 2


def device(z, x, y, c):
    return (z * 2 + x, y * 2 + c)


def slot(z, x, y, c):
    return ((z * 2 + x) * 2 + y) * 2 + c


def greet(depth, z, x, y, c):
    barrier = pltpu.get_barrier_semaphore()
    for target in (device(z, 1 - x, y, c), device(z, x, 1 - y, c), device(z, x, y, 1 - c)):
        pl.semaphore_signal(barrier, 1, device_id=target, device_id_type=MESH)

    @pl.when(z > 0)
    def below():
        pl.semaphore_signal(barrier, 1, device_id=device(z - 1, x, y, c), device_id_type=MESH)

    @pl.when(z < depth - 1)
    def above():
        pl.semaphore_signal(barrier, 1, device_id=device(z + 1, x, y, c), device_id_type=MESH)

    pl.semaphore_wait(barrier, 3 + jnp.where(z > 0, 1, 0) + jnp.where(z < depth - 1, 1, 0))


def start_kernel(depth, *refs):
    pieces = refs[0:3]
    rows_ref = refs[3]
    wholes = refs[4:7]
    sum_ref = refs[7]
    far_x, from_low, from_high, total = refs[8:12]
    local_sem, up_sem, down_sem, x_sem, y_sem, c_sem, block_sem = refs[12:19]
    rx_send, rx_recv, ru_send, ru_recv, rd_send, rd_recv = refs[19:25]
    z, x, y, c = coordinates(depth)
    mine = slot(z, x, y, c)
    greet(depth, z, x, y, c)

    def own(block, piece, target, sem):
        return pltpu.make_async_remote_copy(
            pieces[piece],
            wholes[piece].at[block],
            sem.at[piece],
            block_sem.at[block, piece],
            device_id=target,
            device_id_type=MESH,
        )

    def onward(block, piece, target, sem):
        return pltpu.make_async_remote_copy(
            wholes[piece].at[block],
            wholes[piece].at[block],
            sem.at[piece],
            block_sem.at[block, piece],
            device_id=target,
            device_id_type=MESH,
        )

    def send(make, block, target, sem):
        for piece in range(3):
            make(block, piece, target, sem).start()

    def arrive(block):
        for piece in range(3):
            onward(block, piece, device(z, x, y, 1 - c), c_sem.at[0]).wait_recv()

    across_x, across_y, across_c = (
        device(z, 1 - x, y, c),
        device(z, x, 1 - y, c),
        device(z, x, y, 1 - c),
    )
    rows_x = [
        pltpu.make_async_remote_copy(
            rows_ref.at[goal * 2 + 1 - x],
            far_x.at[goal],
            rx_send.at[goal],
            rx_recv.at[goal],
            device_id=across_x,
            device_id_type=MESH,
        )
        for goal in range(depth)
    ]

    def rows_up(goal):
        return pltpu.make_async_remote_copy(
            total.at[goal],
            from_low.at[goal],
            ru_send.at[goal],
            ru_recv.at[goal],
            device_id=device(z + 1, x, y, c),
            device_id_type=MESH,
        )

    def rows_down(goal):
        return pltpu.make_async_remote_copy(
            total.at[goal],
            from_high.at[goal],
            rd_send.at[goal],
            rd_recv.at[goal],
            device_id=device(z - 1, x, y, c),
            device_id_type=MESH,
        )

    goals = [
        goal for pair in zip(range(depth // 2), range(depth - 1, 0, -1)) for goal in pair
    ]
    local = [
        pltpu.make_async_copy(pieces[piece], wholes[piece].at[mine], local_sem.at[piece])
        for piece in range(3)
    ]
    send(own, mine, across_y, y_sem.at[mine // 4])
    for goal in goals:
        rows_x[goal].start()

    @pl.when(z < depth - 1)
    def first_up():
        send(own, mine, device(z + 1, x, y, c), up_sem.at[0])

    @pl.when(z > 0)
    def first_down():
        send(own, mine, device(z - 1, x, y, c), down_sem.at[0])

    send(own, mine, across_x, x_sem.at[z])
    send(own, mine, across_c, c_sem.at[mine // 2])
    for copy in local:
        copy.start()

    def spread(block, over_x):
        send(onward, block, across_y, y_sem.at[block // 4])
        if over_x:
            send(onward, block, across_x, x_sem.at[block // 8])
        send(onward, block, across_c, c_sem.at[block // 2])

    for step in range(1, depth):

        @pl.when(z - step >= 0)
        def risen():
            block = slot(z - step, x, y, c)
            arrive(block)

            @pl.when(z < depth - 1)
            def further():
                send(onward, block, device(z + 1, x, y, c), up_sem.at[step])

            spread(block, True)

        @pl.when(z + step < depth)
        def fallen():
            block = slot(z + step, x, y, c)
            arrive(block)

            @pl.when(z > 0)
            def further():
                send(onward, block, device(z - 1, x, y, c), down_sem.at[step])

            spread(block, True)

    for goal in goals:
        rows_x[goal].wait_recv()
        part = rows_ref[goal * 2 + x] + far_x[goal]

        @pl.when(goal > z)
        def rising():
            @pl.when(z > 0)
            def more():
                rows_up(goal).wait_recv()
                total[goal] = part + from_low[goal]

            @pl.when(z == 0)
            def alone():
                total[goal] = part

            rows_up(goal).start()

        @pl.when(goal < z)
        def falling():
            @pl.when(z < depth - 1)
            def more():
                rows_down(goal).wait_recv()
                total[goal] = part + from_high[goal]

            @pl.when(z == depth - 1)
            def alone():
                total[goal] = part

            rows_down(goal).start()

        @pl.when(goal == z)
        def here():
            total[goal] = part

    for step in range(depth):
        for sign in (1, -1) if step else (1,):

            @pl.when((z + sign * step >= 0) & (z + sign * step < depth))
            def crossed():
                block = slot(z + sign * step, 1 - x, y, c)
                arrive(block)
                spread(block, False)

    for goal in range(depth):

        @pl.when(goal == z)
        def landed():
            @pl.when(z > 0)
            def low_part():
                rows_up(goal).wait_recv()
                total[goal] = total[goal] + from_low[goal]

            @pl.when(z < depth - 1)
            def high_part():
                rows_down(goal).wait_recv()
                total[goal] = total[goal] + from_high[goal]

            sum_ref[...] = total[goal]

    for step in range(depth):
        for sign in (1, -1) if step else (1,):

            @pl.when((z + sign * step >= 0) & (z + sign * step < depth))
            def crossed():
                for side in (x, 1 - x):
                    block = slot(z + sign * step, side, 1 - y, c)
                    arrive(block)
                    send(onward, block, across_c, c_sem.at[block // 2])

    for block in range(depth * 8):

        @pl.when(block % 2 != c)
        def from_core():
            arrive(block)

    for copy in local:
        copy.wait()
    for goal in range(depth):
        rows_x[goal].wait_send()

        @pl.when(goal > z)
        def rose():
            rows_up(goal).wait_send()

        @pl.when(goal < z)
        def fell():
            rows_down(goal).wait_send()

    def sent(block, target, sem):
        for piece in range(3):
            onward(block, piece, target, sem).wait_send()

    for step in range(depth):

        @pl.when((z - step >= 0) & (z < depth - 1))
        def rose():
            sent(mine, device(z + 1, x, y, c), up_sem.at[step])

        @pl.when((z + step < depth) & (z > 0))
        def fell():
            sent(mine, device(z - 1, x, y, c), down_sem.at[step])

        sent(mine, across_x, x_sem.at[step])
    for index in range(depth * 2):
        sent(mine, across_y, y_sem.at[index])
    for index in range(depth * 4):
        sent(mine, across_c, c_sem.at[index])


def start(pieces, rows):
    groups, height, width = rows.shape
    depth = groups // 2
    blocks = depth * 8
    dma = pltpu.SemaphoreType.DMA
    buffer = pltpu.VMEM((depth, height, width), low)
    return pl.pallas_call(
        functools.partial(start_kernel, depth),
        out_shape=[jax.ShapeDtypeStruct((blocks,) + piece.shape, low) for piece in pieces]
        + [jax.ShapeDtypeStruct((height, width), low)],
        in_specs=[ANY] * 3 + [pl.BlockSpec(memory_space=pltpu.VMEM)],
        out_specs=[ANY] * 3 + [pl.BlockSpec(memory_space=pltpu.VMEM)],
        scratch_shapes=[buffer] * 4
        + [dma((3,))]
        + [dma((depth, 3))] * 3
        + [dma((depth * 2, 3)), dma((depth * 4, 3)), dma((blocks, 3))]
        + [dma((depth,))] * 6,
        compiler_params=pltpu.CompilerParams(
            collective_id=0, has_side_effects=True, vmem_limit_bytes=58 * 2**20
        ),
        name="start",
    )(*pieces, rows)


def adam_step(weight, gradient, first, second, rate, decay):
    first_new = beta_one * first + (1.0 - beta_one) * gradient
    second_new = beta_two * second + (1.0 - beta_two) * gradient * gradient
    direction = (
        first_new
        / (1.0 - beta_one**STEP)
        / (jnp.sqrt(second_new / (1.0 - beta_two**STEP)) + adam_eps)
    )
    return (weight - rate * (direction + decay * weight), first_new, second_new)


def on_device(
    token_ids,
    lengths,
    valid,
    vocab_ids,
    teacher,
    block,
    block_m,
    block_v,
    bases,
    table,
    table_m,
    table_v,
    gains,
    gains_m,
    gains_v,
):
    dp_count, head_count = lax.axis_size("dp"), lax.axis_size("head")
    device_total = dp_count * head_count
    head, dp = lax.axis_index("head"), lax.axis_index("dp")
    batch = head // 2
    tokens = token_ids.shape[1]
    shard_rows = table.shape[0]
    offset = dp * shard_rows
    part = TOPV // device_total

    codes = lax.all_gather(token_ids * 2 + valid, ("dp", "head"), axis=1, tiled=True)
    count = jnp.sum(codes & 1).astype(jnp.float32)
    codes = lax.dynamic_index_in_dim(codes, batch, 0, keepdims=False).reshape(
        dp_count, head_count, tokens
    )
    first = lax.dynamic_index_in_dim(codes, head, 1, keepdims=False)
    second = lax.dynamic_index_in_dim(codes, head ^ 2, 1, keepdims=False)
    codes = jnp.concatenate([first, second], axis=1)
    weighting = (lax.dynamic_index_in_dim(codes, dp, 0, keepdims=False) & 1).astype(jnp.float32)
    vocab = lax.dynamic_index_in_dim(
        vocab_ids.reshape(dp_count, head_count, part), head, 1, keepdims=False
    )
    local = jnp.concatenate([vocab, codes >> 1], axis=1) - offset
    owned = (local >= 0) & (local < shard_rows)
    rows_out = jnp.where(
        owned[..., None], table[jnp.clip(local, 0, shard_rows - 1)], 0.0
    ).astype(low)
    widths = [3 * D // device_total, D // device_total, 2 * FF // device_total, FF // device_total]
    cuts = [sum(widths[:index]) for index in range(5)]
    block_low = block.T.astype(low)
    attention, gate_up, down, rows_in = start(
        [block_low[: cuts[2]], block_low[cuts[2] : cuts[3]], block_low[cuts[3] :]], rows_out
    )
    weights = [
        attention[:, : cuts[1]].reshape(-1, D),
        attention[:, cuts[1] :].reshape(-1, D),
        gate_up.reshape(-1, D),
        down.reshape(-1, D),
    ]
    chosen = lax.all_gather(rows_in[:part], ("dp", "head"), axis=0, tiled=True)
    hidden = rows_in[part:].astype(jnp.float32)

    teacher_own = lax.dynamic_index_in_dim(teacher, batch, 0, keepdims=False)
    teacher_far = swap(
        lax.dynamic_index_in_dim(teacher, 1 - batch, 0, keepdims=False), head_count, 2
    )
    teacher_rows = jnp.concatenate([teacher_own, teacher_far], axis=0)

    run = jnp.arange(tokens, dtype=jnp.int32)
    places = jnp.concatenate([head * tokens + run, (head ^ 2) * tokens + run])
    places_far = jnp.concatenate([(head ^ 1) * tokens + run, (head ^ 3) * tokens + run])
    own_lengths = lax.dynamic_index_in_dim(lengths, batch, 0, keepdims=False)[0]
    segment, position = segments(own_lengths, places)
    segment_far, unused = segments(own_lengths, places_far)
    places_all = jnp.concatenate([places, places_far])
    segment_all = jnp.concatenate([segment, segment_far])
    allow = (segment[:, None] == segment_all[None, :]) & (places[:, None] >= places_all[None, :])
    freqs = jnp.exp(jnp.arange(0, HD, 2, dtype=jnp.float32) * (-math.log(10000.0) / HD))
    angle = position.astype(jnp.float32)[:, None] * freqs[None, :]
    angle = jnp.concatenate([angle, angle], axis=1)
    cosine, sine = jnp.cos(angle), jnp.sin(angle)

    saves = []
    for repeat in range(2):
        hidden, saved = layer_forward(hidden, weights, gains, cosine, sine, allow, head_count)
        saves.append(saved)

    normed = rms_norm(hidden, gains[2]).astype(low)
    log_prob = jax.nn.log_softmax(contract_cols(normed, chosen), axis=-1)
    teach = jax.nn.log_softmax(teacher_rows.astype(jnp.float32), axis=-1)
    loss_sum = jnp.sum(weighting * jnp.sum(jnp.exp(teach) * (teach - log_prob), axis=-1))
    logit_grads = ((jnp.exp(log_prob) - jnp.exp(teach)) * weighting[:, None]).astype(low)
    chosen_grads = contract_rows(logit_grads, normed).astype(low)
    gradient, d_gain_final = rms_back(hidden, gains[2], product(logit_grads, chosen))
    chosen_grads = lax.psum_scatter(chosen_grads, ("dp", "head"), scatter_dimension=0, tiled=True)

    block_grads = None
    d_gains = [0.0, 0.0]
    for repeat in range(2):
        gradient, layer_grads, d_gain_one, d_gain_two = layer_backward(
            gradient, weights, gains, saves[1 - repeat], cosine, sine, allow, head_count
        )
        d_gains = [d_gains[0] + d_gain_one, d_gains[1] + d_gain_two]
        if block_grads is None:
            block_grads = layer_grads
        else:
            block_grads = [total + extra for total, extra in zip(block_grads, layer_grads)]

    joined = jnp.concatenate(
        [piece.astype(low).reshape(device_total, -1, D) for piece in block_grads], axis=1
    )
    block_grads = lax.psum_scatter(joined, ("dp", "head"), scatter_dimension=0, tiled=True)
    block_grads = block_grads.reshape(-1, D).astype(jnp.float32).T

    rows_back = jnp.concatenate([chosen_grads, gradient.astype(low)], axis=0)
    rows_back = lax.all_gather(rows_back, "dp", axis=0, tiled=True)
    dump_index = jnp.where(owned, local, shard_rows).reshape(-1)
    table_grads = jax.ops.segment_sum(
        rows_back.astype(jnp.float32), dump_index, num_segments=shard_rows + 1
    )[:shard_rows]
    table_grads = lax.psum(table_grads.astype(low), "head").astype(jnp.float32)

    small = jnp.concatenate([d_gains[0], d_gains[1], d_gain_final, loss_sum[None]])
    small = lax.psum(small, ("dp", "head"))
    gain_grads = small[: 3 * D].reshape(3, D) / count
    loss = small[3 * D] / count

    squares = lax.psum(
        jnp.sum(block_grads * block_grads)
        + jnp.where(head == 0, jnp.sum(table_grads * table_grads), 0.0),
        ("dp", "head"),
    )
    grad_norm = jnp.sqrt(squares / (count * count) + jnp.sum(gain_grads * gain_grads))
    clip = jnp.minimum(1.0, clip_norm / grad_norm)
    factor = clip / count
    block_grads = block_grads * factor
    table_grads = table_grads * factor
    gain_grads = gain_grads * clip

    rotated = jnp.concatenate(
        [
            contract_rows(bases[index], block_grads[:, cuts[index] : cuts[index + 1]])
            for index in range(4)
        ],
        axis=1,
    )
    block_m_new = beta_one * block_m + (1.0 - beta_one) * rotated
    block_v_new = beta_two * block_v + (1.0 - beta_two) * rotated * rotated
    direction = (
        block_m_new
        / (1.0 - beta_one**STEP)
        / (jnp.sqrt(block_v_new / (1.0 - beta_two**STEP)) + adam_eps)
    )
    update = jnp.concatenate(
        [product(bases[index], direction[:, cuts[index] : cuts[index + 1]]) for index in range(4)],
        axis=1,
    )
    block_new = block - rate_block * (update + decay_rate * block)
    table_new, table_m_new, table_v_new = adam_step(
        table, table_grads, table_m, table_v, rate_table, decay_rate
    )
    gains_new, gains_m_new, gains_v_new = adam_step(
        gains, gain_grads, gains_m, gains_v, rate_gain, 0.0
    )
    return (
        loss,
        grad_norm,
        block_new,
        block_m_new,
        block_v_new,
        table_new,
        table_m_new,
        table_v_new,
        gains_new,
        gains_m_new,
        gains_v_new,
        block_new.astype(low),
        table_new.astype(low),
    )


def solution(mesh):
    tokens = P(None, ("dp", "head"))
    columns = P(None, ("dp", "head"))
    table = P("dp", None)
    return jax.shard_map(
        on_device,
        mesh=mesh,
        in_specs=(
            tokens,
            P(None, "dp", None),
            tokens,
            P(),
            P(None, ("dp", "head"), None),
            columns,
            columns,
            columns,
            P(),
            table,
            table,
            table,
            P(),
            P(),
            P(),
        ),
        out_specs=(
            P(),
            P(),
            columns,
            columns,
            columns,
            table,
            table,
            table,
            P(),
            P(),
            P(),
            columns,
            table,
        ),
        check_vma=False,
    )
```

```python
import functools
import math

import jax
import jax.numpy as jnp
from jax import lax
from jax.experimental import pallas as pl
from jax.experimental.pallas import tpu as pltpu
from jax.sharding import PartitionSpec as P

D = 768
H = 12
HD = 64
FF = 3072
TOPV = 4096
STEP = 5

low = jnp.bfloat16
scale = HD**-0.5
eps_norm = 1e-05
clip_norm = 0.002
beta_one = 0.9
beta_two = 0.99
adam_eps = 1e-08
decay_rate = 0.1
rate_block = 0.03
rate_table = 0.05
rate_gain = 0.4


def product(left, right):
    return jnp.dot(left, right, preferred_element_type=jnp.float32)


def contract_rows(left, right):
    return lax.dot_general(
        left, right, (((0,), (0,)), ((), ())), preferred_element_type=jnp.float32
    )


def contract_cols(left, right):
    return lax.dot_general(
        left, right, (((1,), (1,)), ((), ())), preferred_element_type=jnp.float32
    )


def rms_norm(value, gain):
    return value * lax.rsqrt(jnp.mean(value * value, axis=-1, keepdims=True) + eps_norm) * gain


def rms_back(value, gain, grad):
    r = lax.rsqrt(jnp.mean(value * value, axis=-1, keepdims=True) + eps_norm)
    scaled = grad * gain
    d_value = r * scaled - value * (r * r * r) * jnp.mean(value * scaled, axis=-1, keepdims=True)
    return d_value, jnp.sum(grad * value * r, axis=0)


def rotary(value, cosine, sine):
    half = HD // 2
    turned = jnp.concatenate([-value[..., half:], value[..., :half]], axis=-1)
    return value * cosine[:, None, :] + turned * sine[:, None, :]


def rotary_back(grad, cosine, sine):
    half = HD // 2
    part = grad * sine[:, None, :]
    turned = jnp.concatenate([part[..., half:], -part[..., :half]], axis=-1)
    return grad * cosine[:, None, :] + turned


def segments(lengths, places):
    segment = jnp.zeros_like(places)
    begin = jnp.zeros_like(places)
    end = jnp.zeros((), jnp.int32)
    for index in range(lengths.shape[0] - 1):
        end = end + lengths[index]
        past = places >= end
        segment = segment + past.astype(jnp.int32)
        begin = jnp.where(past, end, begin)
    return segment, places - begin


def scores_of(query, keys, allow):
    score = jnp.einsum("qhd,khd->hqk", query, keys, preferred_element_type=jnp.float32) * scale
    return jnp.where(allow[None], score, -1e30)


def attend(query, keys, values, allow):
    score = scores_of(query, keys, allow)
    summit = jnp.max(score, axis=-1, keepdims=True)
    log_total = summit + jnp.log(jnp.sum(jnp.exp(score - summit), axis=-1, keepdims=True))
    weight = jnp.exp(score - log_total)
    mixed = jnp.einsum(
        "hqk,khd->qhd", weight.astype(low), values, preferred_element_type=jnp.float32
    )
    return mixed.astype(low), log_total


def attend_back(query, keys, values, log_total, upstream, allow):
    weight = jnp.exp(scores_of(query, keys, allow) - log_total)
    d_value = jnp.einsum(
        "hqk,qhd->khd", weight.astype(low), upstream, preferred_element_type=jnp.float32
    )
    d_weight = jnp.einsum("qhd,khd->hqk", upstream, values, preferred_element_type=jnp.float32)
    d_score = (weight * (d_weight - jnp.sum(d_weight * weight, axis=-1, keepdims=True))).astype(low)
    d_query = jnp.einsum("hqk,khd->qhd", d_score, keys, preferred_element_type=jnp.float32) * scale
    d_key = jnp.einsum("hqk,qhd->khd", d_score, query, preferred_element_type=jnp.float32) * scale
    return d_query, d_key, d_value


def swap(value, head_count, offset):
    return lax.ppermute(value, "head", [(h, h ^ offset) for h in range(head_count)])


def layer_forward(hidden, weights, gains, cosine, sine, allow, head_count):
    w_qkv, w_out, w_gu, w_down = weights
    rows = hidden.shape[0]
    normed = rms_norm(hidden, gains[0]).astype(low)
    qkv = contract_cols(normed, w_qkv).reshape(rows, 3, H, HD)
    query = rotary(qkv[:, 0], cosine, sine).astype(low)
    key = rotary(qkv[:, 1], cosine, sine).astype(low)
    own = jnp.concatenate([key, qkv[:, 2].astype(low)], axis=1)
    both = jnp.concatenate([own, swap(own, head_count, 1)], axis=0)
    keys, values = both[:, :H], both[:, H:]
    mixed, log_total = attend(query, keys, values, allow)
    merged = mixed.reshape(rows, D)
    middle = hidden + contract_cols(merged, w_out)
    normed_two = rms_norm(middle, gains[1]).astype(low)
    gate_up = contract_cols(normed_two, w_gu)
    action = (jax.nn.silu(gate_up[:, :FF]) * gate_up[:, FF:]).astype(low)
    output = middle + product(action, w_down)
    saved = (hidden, normed, query, keys, values, log_total, merged, middle, normed_two, gate_up, action)
    return output, saved


def layer_backward(gradient, weights, gains, saved, cosine, sine, allow, head_count):
    w_qkv, w_out, w_gu, w_down = weights
    hidden, normed, query, keys, values, log_total, merged, middle, normed_two, gate_up, action = saved
    rows = hidden.shape[0]
    grad_low = gradient.astype(low)
    d_down = contract_rows(action, grad_low)
    d_action = contract_cols(grad_low, w_down)
    gate, up = gate_up[:, :FF], gate_up[:, FF:]
    chance = jax.nn.sigmoid(gate)
    d_gate = d_action * up * (chance + gate * chance * (1.0 - chance))
    d_up = d_action * gate * chance
    d_gate_up = jnp.concatenate([d_gate, d_up], axis=1).astype(low)
    d_gu = contract_rows(d_gate_up, normed_two)
    d_middle, d_gain_two = rms_back(middle, gains[1], product(d_gate_up, w_gu))
    d_middle = gradient + d_middle
    middle_low = d_middle.astype(low)
    d_out = contract_rows(middle_low, merged)
    upstream = product(middle_low, w_out).astype(low).reshape(rows, H, HD)
    d_query, d_key, d_value = attend_back(query, keys, values, log_total, upstream, allow)
    d_own = jnp.concatenate([d_key[:rows], d_value[:rows]], axis=1)
    d_far = jnp.concatenate([d_key[rows:], d_value[rows:]], axis=1).astype(low)
    d_own = (d_own + swap(d_far, head_count, 1).astype(jnp.float32)).astype(low).astype(jnp.float32)
    d_query = rotary_back(d_query.astype(low).astype(jnp.float32), cosine, sine)
    d_key = rotary_back(d_own[:, :H], cosine, sine)
    d_qkv = jnp.concatenate([d_query, d_key, d_own[:, H:]], axis=1).reshape(rows, 3 * D).astype(low)
    d_qkv_w = contract_rows(d_qkv, normed)
    d_hidden, d_gain_one = rms_back(hidden, gains[0], product(d_qkv, w_qkv))
    return d_middle + d_hidden, [d_qkv_w, d_out, d_gu, d_down], d_gain_one, d_gain_two


MESH = pl.DeviceIdType.MESH
ANY = pl.BlockSpec(memory_space=pl.ANY)


def coordinates(depth):
    dp, head = lax.axis_index("dp"), lax.axis_index("head")
    return dp // 2, dp % 2, head // 2, head % 2


def device(z, x, y, c):
    return (z * 2 + x, y * 2 + c)


def slot(z, x, y, c):
    return ((z * 2 + x) * 2 + y) * 2 + c


def greet(depth, z, x, y, c):
    barrier = pltpu.get_barrier_semaphore()
    for target in (device(z, 1 - x, y, c), device(z, x, 1 - y, c), device(z, x, y, 1 - c)):
        pl.semaphore_signal(barrier, 1, device_id=target, device_id_type=MESH)

    @pl.when(z > 0)
    def below():
        pl.semaphore_signal(barrier, 1, device_id=device(z - 1, x, y, c), device_id_type=MESH)

    @pl.when(z < depth - 1)
    def above():
        pl.semaphore_signal(barrier, 1, device_id=device(z + 1, x, y, c), device_id_type=MESH)

    pl.semaphore_wait(barrier, 3 + jnp.where(z > 0, 1, 0) + jnp.where(z < depth - 1, 1, 0))


def start_kernel(depth, *refs):
    pieces = refs[0:3]
    rows_ref = refs[3]
    wholes = refs[4:7]
    sum_ref = refs[7]
    far_x, from_low, from_high, total = refs[8:12]
    local_sem, up_sem, down_sem, x_sem, y_sem, c_sem, block_sem = refs[12:19]
    rx_send, rx_recv, ru_send, ru_recv, rd_send, rd_recv = refs[19:25]
    z, x, y, c = coordinates(depth)
    mine = slot(z, x, y, c)
    greet(depth, z, x, y, c)

    def own(block, piece, target, sem):
        return pltpu.make_async_remote_copy(
            pieces[piece],
            wholes[piece].at[block],
            sem.at[piece],
            block_sem.at[block, piece],
            device_id=target,
            device_id_type=MESH,
        )

    def onward(block, piece, target, sem):
        return pltpu.make_async_remote_copy(
            wholes[piece].at[block],
            wholes[piece].at[block],
            sem.at[piece],
            block_sem.at[block, piece],
            device_id=target,
            device_id_type=MESH,
        )

    def send(make, block, target, sem):
        for piece in range(3):
            make(block, piece, target, sem).start()

    def arrive(block):
        for piece in range(3):
            onward(block, piece, device(z, x, y, 1 - c), c_sem.at[0]).wait_recv()

    across_x, across_y, across_c = (
        device(z, 1 - x, y, c),
        device(z, x, 1 - y, c),
        device(z, x, y, 1 - c),
    )
    rows_x = [
        pltpu.make_async_remote_copy(
            rows_ref.at[goal * 2 + 1 - x],
            far_x.at[goal],
            rx_send.at[goal],
            rx_recv.at[goal],
            device_id=across_x,
            device_id_type=MESH,
        )
        for goal in range(depth)
    ]

    def rows_up(goal):
        return pltpu.make_async_remote_copy(
            total.at[goal],
            from_low.at[goal],
            ru_send.at[goal],
            ru_recv.at[goal],
            device_id=device(z + 1, x, y, c),
            device_id_type=MESH,
        )

    def rows_down(goal):
        return pltpu.make_async_remote_copy(
            total.at[goal],
            from_high.at[goal],
            rd_send.at[goal],
            rd_recv.at[goal],
            device_id=device(z - 1, x, y, c),
            device_id_type=MESH,
        )

    goals = [
        goal for pair in zip(range(depth // 2), range(depth - 1, 0, -1)) for goal in pair
    ]
    local = [
        pltpu.make_async_copy(pieces[piece], wholes[piece].at[mine], local_sem.at[piece])
        for piece in range(3)
    ]
    send(own, mine, across_y, y_sem.at[mine // 4])
    for goal in goals:
        rows_x[goal].start()

    @pl.when(z < depth - 1)
    def first_up():
        send(own, mine, device(z + 1, x, y, c), up_sem.at[0])

    @pl.when(z > 0)
    def first_down():
        send(own, mine, device(z - 1, x, y, c), down_sem.at[0])

    send(own, mine, across_x, x_sem.at[z])
    send(own, mine, across_c, c_sem.at[mine // 2])
    for copy in local:
        copy.start()

    def spread(block, over_x):
        send(onward, block, across_y, y_sem.at[block // 4])
        if over_x:
            send(onward, block, across_x, x_sem.at[block // 8])
        send(onward, block, across_c, c_sem.at[block // 2])

    for step in range(1, depth):

        @pl.when(z - step >= 0)
        def risen():
            block = slot(z - step, x, y, c)
            arrive(block)

            @pl.when(z < depth - 1)
            def further():
                send(onward, block, device(z + 1, x, y, c), up_sem.at[step])

            spread(block, True)

        @pl.when(z + step < depth)
        def fallen():
            block = slot(z + step, x, y, c)
            arrive(block)

            @pl.when(z > 0)
            def further():
                send(onward, block, device(z - 1, x, y, c), down_sem.at[step])

            spread(block, True)

    for goal in goals:
        rows_x[goal].wait_recv()
        part = rows_ref[goal * 2 + x] + far_x[goal]

        @pl.when(goal > z)
        def rising():
            @pl.when(z > 0)
            def more():
                rows_up(goal).wait_recv()
                total[goal] = part + from_low[goal]

            @pl.when(z == 0)
            def alone():
                total[goal] = part

            rows_up(goal).start()

        @pl.when(goal < z)
        def falling():
            @pl.when(z < depth - 1)
            def more():
                rows_down(goal).wait_recv()
                total[goal] = part + from_high[goal]

            @pl.when(z == depth - 1)
            def alone():
                total[goal] = part

            rows_down(goal).start()

        @pl.when(goal == z)
        def here():
            total[goal] = part

    for step in range(depth):
        for sign in (1, -1) if step else (1,):

            @pl.when((z + sign * step >= 0) & (z + sign * step < depth))
            def crossed():
                block = slot(z + sign * step, 1 - x, y, c)
                arrive(block)
                spread(block, False)

    for goal in range(depth):

        @pl.when(goal == z)
        def landed():
            @pl.when(z > 0)
            def low_part():
                rows_up(goal).wait_recv()
                total[goal] = total[goal] + from_low[goal]

            @pl.when(z < depth - 1)
            def high_part():
                rows_down(goal).wait_recv()
                total[goal] = total[goal] + from_high[goal]

            sum_ref[...] = total[goal]

    for step in range(depth):
        for sign in (1, -1) if step else (1,):

            @pl.when((z + sign * step >= 0) & (z + sign * step < depth))
            def crossed():
                for side in (x, 1 - x):
                    block = slot(z + sign * step, side, 1 - y, c)
                    arrive(block)
                    send(onward, block, across_c, c_sem.at[block // 2])

    for block in range(depth * 8):

        @pl.when(block % 2 != c)
        def from_core():
            arrive(block)

    for copy in local:
        copy.wait()
    for goal in range(depth):
        rows_x[goal].wait_send()

        @pl.when(goal > z)
        def rose():
            rows_up(goal).wait_send()

        @pl.when(goal < z)
        def fell():
            rows_down(goal).wait_send()

    def sent(block, target, sem):
        for piece in range(3):
            onward(block, piece, target, sem).wait_send()

    for step in range(depth):

        @pl.when((z - step >= 0) & (z < depth - 1))
        def rose():
            sent(mine, device(z + 1, x, y, c), up_sem.at[step])

        @pl.when((z + step < depth) & (z > 0))
        def fell():
            sent(mine, device(z - 1, x, y, c), down_sem.at[step])

        sent(mine, across_x, x_sem.at[step])
    for index in range(depth * 2):
        sent(mine, across_y, y_sem.at[index])
    for index in range(depth * 4):
        sent(mine, across_c, c_sem.at[index])


def start(pieces, rows):
    groups, height, width = rows.shape
    depth = groups // 2
    blocks = depth * 8
    dma = pltpu.SemaphoreType.DMA
    buffer = pltpu.VMEM((depth, height, width), low)
    return pl.pallas_call(
        functools.partial(start_kernel, depth),
        out_shape=[jax.ShapeDtypeStruct((blocks,) + piece.shape, low) for piece in pieces]
        + [jax.ShapeDtypeStruct((height, width), low)],
        in_specs=[ANY] * 3 + [pl.BlockSpec(memory_space=pltpu.VMEM)],
        out_specs=[ANY] * 3 + [pl.BlockSpec(memory_space=pltpu.VMEM)],
        scratch_shapes=[buffer] * 4
        + [dma((3,))]
        + [dma((depth, 3))] * 3
        + [dma((depth * 2, 3)), dma((depth * 4, 3)), dma((blocks, 3))]
        + [dma((depth,))] * 6,
        compiler_params=pltpu.CompilerParams(
            collective_id=0, has_side_effects=True, vmem_limit_bytes=58 * 2**20
        ),
        name="start",
    )(*pieces, rows)


def by_distance(depth, z, act):
    for step in range(depth - 1, -1, -1):
        for sign in (1, -1) if step else (1,):

            @pl.when((z + sign * step >= 0) & (z + sign * step < depth))
            def reached():
                act(z + sign * step)


def add_into(total, block, *terms):
    height = total.shape[1]
    chunk = 96 if height % 96 == 0 else height

    @pl.loop(0, height // chunk)
    def chunks(index):
        part = pl.ds(pl.multiple_of(index * chunk, chunk), chunk)
        value = total[block, part].astype(jnp.float32)
        for buffer, place in terms:
            value = value + buffer[place, part].astype(jnp.float32)
        total[block, part] = value.astype(low)


def end_kernel(depth, heights, *refs):
    pieces, rows_ref, grad_ref, rows_out = refs[0:3], refs[3], refs[4], refs[5]
    total, far_c, far_y, far_x, from_low, from_high = refs[6:12]
    local_sem, c_send, c_recv, y_send, y_recv, x_send, x_recv = refs[12:19]
    u_send, u_recv, d_send, d_recv = refs[19:23]
    own_sem, ru_send, rd_send, rx_send, r_recv = refs[23:28]
    z, x, y, c = coordinates(depth)
    greet(depth, z, x, y, c)
    firsts = [sum(heights[:index]) for index in range(3)]
    up, down = device(z + 1, x, y, c), device(z - 1, x, y, c)
    across_x, across_y, across_c = (
        device(z, 1 - x, y, c),
        device(z, x, 1 - y, c),
        device(z, x, y, 1 - c),
    )

    def remote(source, goal, send_sem, recv_sem, target):
        return pltpu.make_async_remote_copy(
            source, goal, send_sem, recv_sem, device_id=target, device_id_type=MESH
        )

    def local(block, piece):
        return pltpu.make_async_copy(
            pieces[piece].at[block * 2 + c],
            total.at[block, pl.ds(firsts[piece], heights[piece])],
            local_sem.at[block, piece],
        )

    def over_c(block, piece):
        return remote(
            pieces[piece].at[block * 2 + 1 - c],
            far_c.at[block, pl.ds(firsts[piece], heights[piece])],
            c_send.at[block, piece],
            c_recv.at[block, piece],
            across_c,
        )

    def over_y(place, side):
        pair = place * 2 + side
        return remote(
            total.at[pair * 2 + 1 - y], far_y.at[pair], y_send.at[pair], y_recv.at[pair], across_y
        )

    def over_x(place):
        return remote(
            total.at[(place * 2 + 1 - x) * 2 + y],
            far_x.at[place],
            x_send.at[place],
            x_recv.at[place],
            across_x,
        )

    def rise(place):
        block = (place * 2 + x) * 2 + y
        return remote(
            total.at[block], from_low.at[place], u_send.at[place], u_recv.at[place], up
        )

    def fall(place):
        block = (place * 2 + x) * 2 + y
        return remote(
            total.at[block], from_high.at[place], d_send.at[place], d_recv.at[place], down
        )

    def own_rows(send_sem, target):
        mine = z * 2 + x
        return remote(rows_ref, rows_out.at[mine], send_sem, r_recv.at[mine], target)

    def rows_on(place, send_sem, target):
        there = place * 2 + x
        return remote(rows_out.at[there], rows_out.at[there], send_sem, r_recv.at[there], target)

    own = pltpu.make_async_copy(rows_ref, rows_out.at[z * 2 + x], own_sem)
    own.start()

    @pl.when(z < depth - 1)
    def first_up():
        own_rows(ru_send.at[0], up).start()

    @pl.when(z > 0)
    def first_down():
        own_rows(rd_send.at[0], down).start()

    own_rows(rx_send.at[z], across_x).start()
    for turn in range(2):
        for side in (1 - x, x):

            def launch(place):
                block = (place * 2 + side) * 2 + (1 - y if turn == 0 else y)
                for piece in range(3):
                    over_c(block, piece).start()
                    local(block, piece).start()

            by_distance(depth, z, launch)

    def ready(block):
        for piece in range(3):
            local(block, piece).wait()
            over_c(block, piece).wait_recv()

    for side in (1 - x, x):

        def give_y(place):
            block = (place * 2 + side) * 2 + 1 - y
            ready(block)
            add_into(total, block, (far_c, block))
            over_y(place, side).start()

        by_distance(depth, z, give_y)

    def rows_step(step):
        @pl.when(z - step >= 0)
        def risen():
            rows_on(z - step, ru_send.at[step], up).wait_recv()

            @pl.when(z < depth - 1)
            def further():
                rows_on(z - step, ru_send.at[step], up).start()

            rows_on(z - step, rx_send.at[z - step], across_x).start()

        @pl.when(z + step < depth)
        def fallen():
            rows_on(z + step, rd_send.at[step], down).wait_recv()

            @pl.when(z > 0)
            def further():
                rows_on(z + step, rd_send.at[step], down).start()

            rows_on(z + step, rx_send.at[z + step], across_x).start()

    def give_x(place):
        block = (place * 2 + 1 - x) * 2 + y
        ready(block)
        over_y(place, 1 - x).wait_recv()
        add_into(total, block, (far_c, block), (far_y, place * 2 + 1 - x))
        over_x(place).start()

    for step in range(depth - 1, -1, -1):
        if step:
            rows_step(depth - step)
        for sign in (1, -1) if step else (1,):

            @pl.when((z + sign * step >= 0) & (z + sign * step < depth))
            def reached():
                give_x(z + sign * step)

    def give_z(place):
        block = (place * 2 + x) * 2 + y
        pair = place * 2 + x
        ready(block)
        over_y(place, x).wait_recv()
        over_x(place).wait_recv()
        add_into(total, block, (far_c, block), (far_y, pair), (far_x, place))

        @pl.when(place > z)
        def rising():
            @pl.when(z > 0)
            def more():
                rise(place).wait_recv()
                add_into(total, block, (from_low, place))

            rise(place).start()

        @pl.when(place < z)
        def falling():
            @pl.when(z < depth - 1)
            def more():
                fall(place).wait_recv()
                add_into(total, block, (from_high, place))

            fall(place).start()

    by_distance(depth, z, give_z)
    mine = (z * 2 + x) * 2 + y
    grad_ref[...] = total[mine].astype(jnp.float32)

    @pl.when(z > 0)
    def low_part():
        rise(z).wait_recv()
        grad_ref[...] = grad_ref[...] + from_low[z].astype(jnp.float32)

    @pl.when(z < depth - 1)
    def high_part():
        fall(z).wait_recv()
        grad_ref[...] = grad_ref[...] + from_high[z].astype(jnp.float32)

    own.wait()
    for place in range(depth):
        there = place * 2 + 1 - x
        remote(
            rows_out.at[there], rows_out.at[there], rx_send.at[place], r_recv.at[there], across_x
        ).wait_recv()
        rows_on(place, rx_send.at[place], across_x).wait_send()
        over_x(place).wait_send()
        for side in range(2):
            over_y(place, side).wait_send()
            for rank in range(2):
                for piece in range(3):
                    over_c((place * 2 + side) * 2 + rank, piece).wait_send()

        @pl.when(place > z)
        def rose():
            rise(place).wait_send()

        @pl.when(place < z)
        def fell():
            fall(place).wait_send()

        @pl.when((z - place >= 0) & (z < depth - 1))
        def rows_rose():
            rows_on(z, ru_send.at[place], up).wait_send()

        @pl.when((z + place < depth) & (z > 0))
        def rows_fell():
            rows_on(z, rd_send.at[place], down).wait_send()


def end(pieces, rows):
    blocks = pieces[0].shape[0]
    heights = [piece.shape[1] for piece in pieces]
    height, width = sum(heights), pieces[0].shape[2]
    depth = blocks // 8
    dma = pltpu.SemaphoreType.DMA

    def buffer(count):
        return pltpu.VMEM((count, height, width), low)

    return pl.pallas_call(
        functools.partial(end_kernel, depth, heights),
        out_shape=[
            jax.ShapeDtypeStruct((height, width), jnp.float32),
            jax.ShapeDtypeStruct((depth * 2,) + rows.shape, low),
        ],
        in_specs=[ANY] * 4,
        out_specs=[pl.BlockSpec(memory_space=pltpu.VMEM), ANY],
        scratch_shapes=[buffer(depth * 4), buffer(depth * 4), buffer(depth * 2)]
        + [buffer(depth)] * 3
        + [dma((depth * 4, 3))] * 3
        + [dma((depth * 2,))] * 2
        + [dma((depth,))] * 6
        + [dma(())]
        + [dma((depth,))] * 3
        + [dma((depth * 2,))],
        compiler_params=pltpu.CompilerParams(
            collective_id=1, has_side_effects=True, vmem_limit_bytes=58 * 2**20
        ),
        name="end",
    )(*pieces, rows)


def collect_kernel(step, places_ref, rows_ref, table_ref):
    base = pl.program_id(0) * step
    at = base + lax.broadcasted_iota(jnp.int32, (step, places_ref.shape[1]), 0)
    picked = jnp.where(at == places_ref[...], 1.0, 0.0).astype(low)
    table_ref[...] = product(picked, rows_ref[...]).astype(low)


def collect(places, rows, height, step):
    count, width = rows.shape
    return pl.pallas_call(
        functools.partial(collect_kernel, step),
        grid=(height // step,),
        out_shape=jax.ShapeDtypeStruct((height, width), low),
        in_specs=[
            pl.BlockSpec((1, count), lambda i: (0, 0)),
            pl.BlockSpec((count, width), lambda i: (0, 0)),
        ],
        out_specs=pl.BlockSpec((step, width), lambda i: (i, 0)),
        compiler_params=pltpu.CompilerParams(vmem_limit_bytes=58 * 2**20),
        cost_estimate=pl.CostEstimate(
            flops=2 * count * width * height,
            bytes_accessed=2 * width * (count + height),
            transcendentals=0,
        ),
        name="collect",
    )(places, rows)


def share_kernel(depth, table_ref, small_ref, table_out, small_out, *refs):
    far_c, part, far_y, small, far_small = refs[0:5]
    c_send, c_recv, y_send, y_recv, o_send, o_recv, s_send, s_recv = refs[5:13]
    z, x, y, c = coordinates(depth)
    partners = [device(z, x, y, 1 - c), device(z, x, 1 - y, c), device(z, 1 - x, y, c)]
    reach = 1
    while reach < depth:
        partners.append(device(z ^ reach, x, y, c))
        reach = reach * 2
    barrier = pltpu.get_barrier_semaphore()
    for target in partners:
        pl.semaphore_signal(barrier, 1, device_id=target, device_id_type=MESH)
    pl.semaphore_wait(barrier, len(partners))
    across_c, across_y = partners[:2]

    def remote(source, goal, send_sem, recv_sem, target):
        return pltpu.make_async_remote_copy(
            source, goal, send_sem, recv_sem, device_id=target, device_id_type=MESH
        )

    def over_c(rank):
        return remote(
            table_ref.at[rank * 2 + 1 - c],
            far_c.at[rank],
            c_send.at[rank],
            c_recv.at[rank],
            across_c,
        )

    def out(rank, core, index, target):
        where = table_out.at[rank * 2 + core]
        return remote(where, where, o_send.at[index], o_recv.at[rank * 2 + core], target)

    height = part.shape[0]
    chunk = 80 if height % 80 == 0 else height
    over_c(1 - y).start()
    over_c(y).start()
    over_c(1 - y).wait_recv()

    @pl.loop(0, height // chunk)
    def first_sum(index):
        rows = pl.ds(pl.multiple_of(index * chunk, chunk), chunk)
        part[rows] = (
            table_ref[(1 - y) * 2 + c, rows].astype(jnp.float32)
            + far_c[1 - y, rows].astype(jnp.float32)
        ).astype(low)

    over_y = remote(part, far_y, y_send, y_recv, across_y)
    over_y.start()
    over_c(y).wait_recv()
    over_y.wait_recv()
    mine = y * 2 + c

    def second_sum(index, squares):
        rows = pl.ds(pl.multiple_of(index * chunk, chunk), chunk)
        value = (
            table_ref[mine, rows].astype(jnp.float32)
            + far_c[y, rows].astype(jnp.float32)
            + far_y[rows].astype(jnp.float32)
        ).astype(low)
        table_out[mine, rows] = value
        value = value.astype(jnp.float32)
        return squares + jnp.sum((value * value).reshape(-1, 8, 768), axis=0)

    squares = lax.fori_loop(0, height // chunk, second_sum, jnp.zeros((8, 768), jnp.float32))
    out(y, c, 0, across_y).start()
    out(y, c, 1, across_c).start()
    lines = lax.broadcasted_iota(jnp.int32, small.shape[1:], 0)
    lanes = lax.broadcasted_iota(jnp.int32, small.shape[1:], 1)
    last = (lines == small.shape[1] - 1) & (lanes == 0)
    small[0] = small_ref[...] + jnp.where(last, jnp.sum(squares), 0.0)
    for turn, target in enumerate(partners):
        copy = remote(
            small.at[turn], far_small.at[turn], s_send.at[turn], s_recv.at[turn], target
        )
        copy.start()
        copy.wait_recv()
        small[turn + 1] = small[turn] + far_small[turn]
    small_out[...] = small[len(partners)]
    out(1 - y, c, 0, across_y).wait_recv()
    out(1 - y, c, 2, across_c).start()
    out(y, 1 - c, 1, across_c).wait_recv()
    out(1 - y, 1 - c, 2, across_c).wait_recv()
    for turn, target in enumerate(partners):
        remote(
            small.at[turn], far_small.at[turn], s_send.at[turn], s_recv.at[turn], target
        ).wait_send()
    over_y.wait_send()
    for rank in range(2):
        over_c(rank).wait_send()
    out(y, c, 0, across_y).wait_send()
    out(y, c, 1, across_c).wait_send()
    out(1 - y, c, 2, across_c).wait_send()


def share(depth, table, small):
    quarters, height, width = table.shape
    turns = 3 + (depth - 1).bit_length()
    dma = pltpu.SemaphoreType.DMA
    vmem = pl.BlockSpec(memory_space=pltpu.VMEM)
    return pl.pallas_call(
        functools.partial(share_kernel, depth),
        out_shape=[
            jax.ShapeDtypeStruct(table.shape, low),
            jax.ShapeDtypeStruct(small.shape, jnp.float32),
        ],
        in_specs=[vmem, vmem],
        out_specs=[vmem, vmem],
        scratch_shapes=[
            pltpu.VMEM((2, height, width), low),
            pltpu.VMEM((height, width), low),
            pltpu.VMEM((height, width), low),
            pltpu.VMEM((turns + 1,) + small.shape, jnp.float32),
            pltpu.VMEM((turns,) + small.shape, jnp.float32),
            dma((2,)),
            dma((2,)),
            dma(()),
            dma(()),
            dma((3,)),
            dma((4,)),
            dma((turns,)),
            dma((turns,)),
        ],
        compiler_params=pltpu.CompilerParams(
            collective_id=2, has_side_effects=True, vmem_limit_bytes=58 * 2**20
        ),
        name="share",
    )(table, small)


def adam_step(weight, gradient, first, second, rate, decay):
    first_new = beta_one * first + (1.0 - beta_one) * gradient
    second_new = beta_two * second + (1.0 - beta_two) * gradient * gradient
    direction = (
        first_new
        / (1.0 - beta_one**STEP)
        / (jnp.sqrt(second_new / (1.0 - beta_two**STEP)) + adam_eps)
    )
    return (weight - rate * (direction + decay * weight), first_new, second_new)


def on_device(
    token_ids,
    lengths,
    valid,
    vocab_ids,
    teacher,
    block,
    block_m,
    block_v,
    bases,
    table,
    table_m,
    table_v,
    gains,
    gains_m,
    gains_v,
):
    dp_count, head_count = lax.axis_size("dp"), lax.axis_size("head")
    device_total = dp_count * head_count
    head, dp = lax.axis_index("head"), lax.axis_index("dp")
    batch = head // 2
    tokens = token_ids.shape[1]
    shard_rows = table.shape[0]
    offset = dp * shard_rows
    part = TOPV // device_total

    codes = lax.all_gather(token_ids * 2 + valid, ("dp", "head"), axis=1, tiled=True)
    count = jnp.sum(codes & 1).astype(jnp.float32)
    codes = lax.dynamic_index_in_dim(codes, batch, 0, keepdims=False).reshape(
        dp_count, head_count, tokens
    )
    first = lax.dynamic_index_in_dim(codes, head, 1, keepdims=False)
    second = lax.dynamic_index_in_dim(codes, head ^ 2, 1, keepdims=False)
    codes = jnp.concatenate([first, second], axis=1)
    weighting = (lax.dynamic_index_in_dim(codes, dp, 0, keepdims=False) & 1).astype(jnp.float32)
    vocab = lax.dynamic_index_in_dim(
        vocab_ids.reshape(dp_count, head_count, part), head, 1, keepdims=False
    )
    local = jnp.concatenate([vocab, codes >> 1], axis=1) - offset
    owned = (local >= 0) & (local < shard_rows)
    rows_out = jnp.where(
        owned[..., None], table[jnp.clip(local, 0, shard_rows - 1)], 0.0
    ).astype(low)
    widths = [3 * D // device_total, D // device_total, 2 * FF // device_total, FF // device_total]
    cuts = [sum(widths[:index]) for index in range(5)]
    block_low = block.T.astype(low)
    attention, gate_up, down, rows_in = start(
        [block_low[: cuts[2]], block_low[cuts[2] : cuts[3]], block_low[cuts[3] :]], rows_out
    )
    weights = [
        attention[:, : cuts[1]].reshape(-1, D),
        attention[:, cuts[1] :].reshape(-1, D),
        gate_up.reshape(-1, D),
        down.reshape(-1, D),
    ]
    chosen = lax.all_gather(rows_in[:part], ("dp", "head"), axis=0, tiled=True)
    hidden = rows_in[part:].astype(jnp.float32)

    teacher_own = lax.dynamic_index_in_dim(teacher, batch, 0, keepdims=False)
    teacher_far = swap(
        lax.dynamic_index_in_dim(teacher, 1 - batch, 0, keepdims=False), head_count, 2
    )
    teacher_rows = jnp.concatenate([teacher_own, teacher_far], axis=0)

    run = jnp.arange(tokens, dtype=jnp.int32)
    places = jnp.concatenate([head * tokens + run, (head ^ 2) * tokens + run])
    places_far = jnp.concatenate([(head ^ 1) * tokens + run, (head ^ 3) * tokens + run])
    own_lengths = lax.dynamic_index_in_dim(lengths, batch, 0, keepdims=False)[0]
    segment, position = segments(own_lengths, places)
    segment_far, unused = segments(own_lengths, places_far)
    places_all = jnp.concatenate([places, places_far])
    segment_all = jnp.concatenate([segment, segment_far])
    allow = (segment[:, None] == segment_all[None, :]) & (places[:, None] >= places_all[None, :])
    freqs = jnp.exp(jnp.arange(0, HD, 2, dtype=jnp.float32) * (-math.log(10000.0) / HD))
    angle = position.astype(jnp.float32)[:, None] * freqs[None, :]
    angle = jnp.concatenate([angle, angle], axis=1)
    cosine, sine = jnp.cos(angle), jnp.sin(angle)

    saves = []
    for repeat in range(2):
        hidden, saved = layer_forward(hidden, weights, gains, cosine, sine, allow, head_count)
        saves.append(saved)

    normed = rms_norm(hidden, gains[2]).astype(low)
    log_prob = jax.nn.log_softmax(contract_cols(normed, chosen), axis=-1)
    teach = jax.nn.log_softmax(teacher_rows.astype(jnp.float32), axis=-1)
    loss_sum = jnp.sum(weighting * jnp.sum(jnp.exp(teach) * (teach - log_prob), axis=-1))
    logit_grads = ((jnp.exp(log_prob) - jnp.exp(teach)) * weighting[:, None]).astype(low)
    chosen_grads = contract_rows(logit_grads, normed).astype(low)
    gradient, d_gain_final = rms_back(hidden, gains[2], product(logit_grads, chosen))
    chosen_grads = lax.psum_scatter(chosen_grads, ("dp", "head"), scatter_dimension=0, tiled=True)

    block_grads = None
    d_gains = [0.0, 0.0]
    for repeat in range(2):
        gradient, layer_grads, d_gain_one, d_gain_two = layer_backward(
            gradient, weights, gains, saves[1 - repeat], cosine, sine, allow, head_count
        )
        d_gains = [d_gains[0] + d_gain_one, d_gains[1] + d_gain_two]
        if block_grads is None:
            block_grads = layer_grads
        else:
            block_grads = [total + extra for total, extra in zip(block_grads, layer_grads)]

    d_qkv, d_out, d_gu, d_down = [
        piece.astype(low).reshape(device_total, -1, D) for piece in block_grads
    ]
    rows_back = jnp.concatenate([chosen_grads, gradient.astype(low)], axis=0)
    block_grads, rows_back = end(
        [jnp.concatenate([d_qkv, d_out], axis=1), d_gu, d_down], rows_back
    )
    block_grads = block_grads.T

    step = 80 if shard_rows % 80 == 0 else 40
    quarter = -(-shard_rows // (step * head_count)) * step
    tile = quarter // 5 if quarter % 80 == 0 and quarter // 5 % 16 == 0 else step
    table_grads = collect(
        jnp.where(owned, local, -1).reshape(1, -1),
        rows_back.reshape(-1, D),
        quarter * head_count,
        tile,
    )
    squares = jnp.sum(block_grads * block_grads)
    small = jnp.concatenate([d_gains[0], d_gains[1], d_gain_final, loss_sum[None]])
    small = jnp.pad(small, (0, 6 * 128 - 1)).reshape(-1, 128)
    small = small.at[-1, 0].set(squares)
    table_grads, small = share(
        dp_count // 2, table_grads.reshape(head_count, quarter, D), small
    )
    table_grads = table_grads.reshape(-1, D)[:shard_rows].astype(jnp.float32)
    squares = small[-1, 0]
    small = small.reshape(-1)
    gain_grads = small[: 3 * D].reshape(3, D) / count
    loss = small[3 * D] / count
    grad_norm = jnp.sqrt(squares / (count * count) + jnp.sum(gain_grads * gain_grads))
    clip = jnp.minimum(1.0, clip_norm / grad_norm)
    factor = clip / count
    block_grads = block_grads * factor
    table_grads = table_grads * factor
    gain_grads = gain_grads * clip

    rotated = jnp.concatenate(
        [
            contract_rows(bases[index], block_grads[:, cuts[index] : cuts[index + 1]])
            for index in range(4)
        ],
        axis=1,
    )
    block_m_new = beta_one * block_m + (1.0 - beta_one) * rotated
    block_v_new = beta_two * block_v + (1.0 - beta_two) * rotated * rotated
    direction = (
        block_m_new
        / (1.0 - beta_one**STEP)
        / (jnp.sqrt(block_v_new / (1.0 - beta_two**STEP)) + adam_eps)
    )
    update = jnp.concatenate(
        [product(bases[index], direction[:, cuts[index] : cuts[index + 1]]) for index in range(4)],
        axis=1,
    )
    block_new = block - rate_block * (update + decay_rate * block)
    table_new, table_m_new, table_v_new = adam_step(
        table, table_grads, table_m, table_v, rate_table, decay_rate
    )
    gains_new, gains_m_new, gains_v_new = adam_step(
        gains, gain_grads, gains_m, gains_v, rate_gain, 0.0
    )
    return (
        loss,
        grad_norm,
        block_new,
        block_m_new,
        block_v_new,
        table_new,
        table_m_new,
        table_v_new,
        gains_new,
        gains_m_new,
        gains_v_new,
        block_new.astype(low),
        table_new.astype(low),
    )


def solution(mesh):
    tokens = P(None, ("dp", "head"))
    columns = P(None, ("dp", "head"))
    table = P("dp", None)
    return jax.shard_map(
        on_device,
        mesh=mesh,
        in_specs=(
            tokens,
            P(None, "dp", None),
            tokens,
            P(),
            P(None, ("dp", "head"), None),
            columns,
            columns,
            columns,
            P(),
            table,
            table,
            table,
            P(),
            P(),
            P(),
        ),
        out_specs=(
            P(),
            P(),
            columns,
            columns,
            columns,
            table,
            table,
            table,
            P(),
            P(),
            P(),
            columns,
            table,
        ),
        check_vma=False,
    )
```

```python
import functools
import math

import jax
import jax.numpy as jnp
from jax import lax
from jax.experimental import pallas as pl
from jax.experimental.pallas import tpu as pltpu
from jax.sharding import PartitionSpec as P

D = 768
H = 12
HD = 64
FF = 3072
TOPV = 4096
STEP = 5

low = jnp.bfloat16
scale = HD**-0.5
eps_norm = 1e-05
clip_norm = 0.002
beta_one = 0.9
beta_two = 0.99
adam_eps = 1e-08
decay_rate = 0.1
rate_block = 0.03
rate_table = 0.05
rate_gain = 0.4


def product(left, right):
    return jnp.dot(left, right, preferred_element_type=jnp.float32)


def contract_rows(left, right):
    return lax.dot_general(
        left, right, (((0,), (0,)), ((), ())), preferred_element_type=jnp.float32
    )


def contract_cols(left, right):
    return lax.dot_general(
        left, right, (((1,), (1,)), ((), ())), preferred_element_type=jnp.float32
    )


def rms_norm(value, gain):
    return value * lax.rsqrt(jnp.mean(value * value, axis=-1, keepdims=True) + eps_norm) * gain


def rms_back(value, gain, grad):
    r = lax.rsqrt(jnp.mean(value * value, axis=-1, keepdims=True) + eps_norm)
    scaled = grad * gain
    d_value = r * scaled - value * (r * r * r) * jnp.mean(value * scaled, axis=-1, keepdims=True)
    return d_value, jnp.sum(grad * value * r, axis=0)


def rotary(value, cosine, sine):
    half = HD // 2
    turned = jnp.concatenate([-value[..., half:], value[..., :half]], axis=-1)
    return value * cosine[:, None, :] + turned * sine[:, None, :]


def rotary_back(grad, cosine, sine):
    half = HD // 2
    part = grad * sine[:, None, :]
    turned = jnp.concatenate([part[..., half:], -part[..., :half]], axis=-1)
    return grad * cosine[:, None, :] + turned


def segments(lengths, places):
    segment = jnp.zeros_like(places)
    begin = jnp.zeros_like(places)
    end = jnp.zeros((), jnp.int32)
    for index in range(lengths.shape[0] - 1):
        end = end + lengths[index]
        past = places >= end
        segment = segment + past.astype(jnp.int32)
        begin = jnp.where(past, end, begin)
    return segment, places - begin


def scores_of(query, keys, allow):
    score = jnp.einsum("qhd,khd->hqk", query, keys, preferred_element_type=jnp.float32) * scale
    return jnp.where(allow[None], score, -1e30)


def attend(query, keys, values, allow):
    score = scores_of(query, keys, allow)
    summit = jnp.max(score, axis=-1, keepdims=True)
    log_total = summit + jnp.log(jnp.sum(jnp.exp(score - summit), axis=-1, keepdims=True))
    weight = jnp.exp(score - log_total)
    mixed = jnp.einsum(
        "hqk,khd->qhd", weight.astype(low), values, preferred_element_type=jnp.float32
    )
    return mixed.astype(low), log_total


def attend_back(query, keys, values, log_total, upstream, allow):
    weight = jnp.exp(scores_of(query, keys, allow) - log_total)
    d_value = jnp.einsum(
        "hqk,qhd->khd", weight.astype(low), upstream, preferred_element_type=jnp.float32
    )
    d_weight = jnp.einsum("qhd,khd->hqk", upstream, values, preferred_element_type=jnp.float32)
    d_score = (weight * (d_weight - jnp.sum(d_weight * weight, axis=-1, keepdims=True))).astype(low)
    d_query = jnp.einsum("hqk,khd->qhd", d_score, keys, preferred_element_type=jnp.float32) * scale
    d_key = jnp.einsum("hqk,qhd->khd", d_score, query, preferred_element_type=jnp.float32) * scale
    return d_query, d_key, d_value


def swap(value, head_count, offset):
    return lax.ppermute(value, "head", [(h, h ^ offset) for h in range(head_count)])


def layer_forward(hidden, weights, gains, cosine, sine, allow, head_count):
    w_qkv, w_out, w_gu, w_down = weights
    rows = hidden.shape[0]
    normed = rms_norm(hidden, gains[0]).astype(low)
    qkv = contract_cols(normed, w_qkv).reshape(rows, 3, H, HD)
    query = rotary(qkv[:, 0], cosine, sine).astype(low)
    key = rotary(qkv[:, 1], cosine, sine).astype(low)
    own = jnp.concatenate([key, qkv[:, 2].astype(low)], axis=1)
    both = jnp.concatenate([own, swap(own, head_count, 1)], axis=0)
    keys, values = both[:, :H], both[:, H:]
    mixed, log_total = attend(query, keys, values, allow)
    merged = mixed.reshape(rows, D)
    middle = hidden + contract_cols(merged, w_out)
    normed_two = rms_norm(middle, gains[1]).astype(low)
    gate_up = contract_cols(normed_two, w_gu)
    action = (jax.nn.silu(gate_up[:, :FF]) * gate_up[:, FF:]).astype(low)
    output = middle + product(action, w_down)
    saved = (hidden, normed, query, keys, values, log_total, merged, middle, normed_two, gate_up, action)
    return output, saved


def layer_backward(gradient, weights, gains, saved, cosine, sine, allow, head_count):
    w_qkv, w_out, w_gu, w_down = weights
    hidden, normed, query, keys, values, log_total, merged, middle, normed_two, gate_up, action = saved
    rows = hidden.shape[0]
    grad_low = gradient.astype(low)
    d_down = contract_rows(action, grad_low)
    d_action = contract_cols(grad_low, w_down)
    gate, up = gate_up[:, :FF], gate_up[:, FF:]
    chance = jax.nn.sigmoid(gate)
    d_gate = d_action * up * (chance + gate * chance * (1.0 - chance))
    d_up = d_action * gate * chance
    d_gate_up = jnp.concatenate([d_gate, d_up], axis=1).astype(low)
    d_gu = contract_rows(d_gate_up, normed_two)
    d_middle, d_gain_two = rms_back(middle, gains[1], product(d_gate_up, w_gu))
    d_middle = gradient + d_middle
    middle_low = d_middle.astype(low)
    d_out = contract_rows(middle_low, merged)
    upstream = product(middle_low, w_out).astype(low).reshape(rows, H, HD)
    d_query, d_key, d_value = attend_back(query, keys, values, log_total, upstream, allow)
    d_own = jnp.concatenate([d_key[:rows], d_value[:rows]], axis=1)
    d_far = jnp.concatenate([d_key[rows:], d_value[rows:]], axis=1).astype(low)
    d_own = (d_own + swap(d_far, head_count, 1).astype(jnp.float32)).astype(low).astype(jnp.float32)
    d_query = rotary_back(d_query.astype(low).astype(jnp.float32), cosine, sine)
    d_key = rotary_back(d_own[:, :H], cosine, sine)
    d_qkv = jnp.concatenate([d_query, d_key, d_own[:, H:]], axis=1).reshape(rows, 3 * D).astype(low)
    d_qkv_w = contract_rows(d_qkv, normed)
    d_hidden, d_gain_one = rms_back(hidden, gains[0], product(d_qkv, w_qkv))
    return d_middle + d_hidden, [d_qkv_w, d_out, d_gu, d_down], d_gain_one, d_gain_two


MESH = pl.DeviceIdType.MESH
ANY = pl.BlockSpec(memory_space=pl.ANY)


def coordinates(depth):
    dp, head = lax.axis_index("dp"), lax.axis_index("head")
    return dp // 2, dp % 2, head // 2, head % 2


def device(z, x, y, c):
    return (z * 2 + x, y * 2 + c)


def slot(z, x, y, c):
    return ((z * 2 + x) * 2 + y) * 2 + c


def greet(depth, z, x, y, c):
    barrier = pltpu.get_barrier_semaphore()
    for target in (device(z, 1 - x, y, c), device(z, x, 1 - y, c), device(z, x, y, 1 - c)):
        pl.semaphore_signal(barrier, 1, device_id=target, device_id_type=MESH)

    @pl.when(z > 0)
    def below():
        pl.semaphore_signal(barrier, 1, device_id=device(z - 1, x, y, c), device_id_type=MESH)

    @pl.when(z < depth - 1)
    def above():
        pl.semaphore_signal(barrier, 1, device_id=device(z + 1, x, y, c), device_id_type=MESH)

    pl.semaphore_wait(barrier, 3 + jnp.where(z > 0, 1, 0) + jnp.where(z < depth - 1, 1, 0))


def start_kernel(depth, *refs):
    pieces = refs[0:3]
    table_ref, codes_ref, vocab_ref = refs[3:6]
    wholes = refs[6:9]
    sum_ref, ids_ref = refs[9:11]
    far_x, from_low, from_high, total, rows_ref, shard, ids = refs[11:18]
    local_sem, up_sem, down_sem, x_sem, y_sem, c_sem, block_sem = refs[18:25]
    rx_send, rx_recv, ru_send, ru_recv, rd_send, rd_recv = refs[25:31]
    id_send, id_recv, table_sem, copy_sem = refs[31:35]
    z, x, y, c = coordinates(depth)
    mine = slot(z, x, y, c)
    dp, head = z * 2 + x, y * 2 + c
    groups, height = rows_ref.shape[:2]
    shard_rows, tokens = table_ref.shape[0], codes_ref.shape[2]
    part = height - 2 * tokens
    offset = dp * shard_rows
    barrier = pltpu.get_barrier_semaphore()
    pl.semaphore_signal(barrier, 1, device_id=device(z, x, y, 1 - c), device_id_type=MESH)
    for group in range(groups):
        for rank in range(2):

            @pl.when((group != dp) | (rank != y))
            def hello():
                pl.semaphore_signal(
                    barrier, 1, device_id=(group, rank * 2 + c), device_id_type=MESH
                )

    pl.semaphore_wait(barrier, groups * 2)

    def tell(group, rank):
        second = jnp.where(rank == y, 0, 1)
        return pltpu.make_async_remote_copy(
            codes_ref.at[rank],
            ids_ref.at[dp, second],
            id_send.at[group, rank],
            id_recv.at[dp, second],
            device_id=(group, rank * 2 + c),
            device_id_type=MESH,
        )

    def told(group, second):
        return pltpu.make_async_remote_copy(
            codes_ref.at[0],
            ids_ref.at[group, second],
            id_send.at[group, second],
            id_recv.at[group, second],
            device_id=device(z, x, y, 1 - c),
            device_id_type=MESH,
        )

    keep = pltpu.make_async_copy(codes_ref.at[y], ids_ref.at[dp, 0], copy_sem)
    fetch = pltpu.make_async_copy(table_ref, shard.at[pl.ds(0, shard_rows)], table_sem)
    fetch.start()
    keep.start()
    for group in range(groups):
        for rank in range(2):

            @pl.when((group != dp) | (rank != y))
            def telling():
                tell(group, rank).start()

    def gather(group):
        def load(first, read):
            @pl.loop(0, (tokens if first else part) // 16)
            def some(index):
                base = index * 16
                lines = []
                for line in range(16):
                    place = read(base + line) - offset
                    held = (place >= 0) & (place < shard_rows)
                    lines.append(shard[pl.ds(jnp.where(held, place, shard_rows), 1)])
                rows_ref[group, pl.ds(pl.multiple_of(first + base, 16), 16)] = jnp.concatenate(
                    lines, axis=0
                ).astype(low)

        load(0, lambda index: vocab_ref[(group * 4 + head) * part + index])
        for second in range(2):
            load(part + second * tokens, lambda index: ids[group, second, 0, index] >> 1)

    def own(block, piece, target, sem):
        return pltpu.make_async_remote_copy(
            pieces[piece],
            wholes[piece].at[block],
            sem.at[piece],
            block_sem.at[block, piece],
            device_id=target,
            device_id_type=MESH,
        )

    def onward(block, piece, target, sem):
        return pltpu.make_async_remote_copy(
            wholes[piece].at[block],
            wholes[piece].at[block],
            sem.at[piece],
            block_sem.at[block, piece],
            device_id=target,
            device_id_type=MESH,
        )

    def send(make, block, target, sem):
        for piece in range(3):
            make(block, piece, target, sem).start()

    def arrive(block):
        for piece in range(3):
            onward(block, piece, device(z, x, y, 1 - c), c_sem.at[0]).wait_recv()

    across_x, across_y, across_c = (
        device(z, 1 - x, y, c),
        device(z, x, 1 - y, c),
        device(z, x, y, 1 - c),
    )
    rows_x = [
        pltpu.make_async_remote_copy(
            rows_ref.at[goal * 2 + 1 - x],
            far_x.at[goal],
            rx_send.at[goal],
            rx_recv.at[goal],
            device_id=across_x,
            device_id_type=MESH,
        )
        for goal in range(depth)
    ]

    def rows_up(goal):
        return pltpu.make_async_remote_copy(
            total.at[goal],
            from_low.at[goal],
            ru_send.at[goal],
            ru_recv.at[goal],
            device_id=device(z + 1, x, y, c),
            device_id_type=MESH,
        )

    def rows_down(goal):
        return pltpu.make_async_remote_copy(
            total.at[goal],
            from_high.at[goal],
            rd_send.at[goal],
            rd_recv.at[goal],
            device_id=device(z - 1, x, y, c),
            device_id_type=MESH,
        )

    goals = [
        goal for pair in zip(range(depth // 2), range(depth - 1, 0, -1)) for goal in pair
    ]
    local = [
        pltpu.make_async_copy(pieces[piece], wholes[piece].at[mine], local_sem.at[piece])
        for piece in range(3)
    ]
    send(own, mine, across_y, y_sem.at[mine // 4])

    @pl.when(z < depth - 1)
    def first_up():
        send(own, mine, device(z + 1, x, y, c), up_sem.at[0])

    @pl.when(z > 0)
    def first_down():
        send(own, mine, device(z - 1, x, y, c), down_sem.at[0])

    send(own, mine, across_x, x_sem.at[z])
    send(own, mine, across_c, c_sem.at[mine // 2])
    for copy in local:
        copy.start()
    shard[pl.ds(shard_rows, 8)] = jnp.zeros((8, shard.shape[1]), jnp.float32)
    keep.wait()
    for group in range(groups):
        for second in range(2):

            @pl.when((group != dp) | (second != 0))
            def heard():
                told(group, second).wait_recv()

    to_scalars = pltpu.make_async_copy(ids_ref, ids, copy_sem)
    to_scalars.start()
    fetch.wait()
    to_scalars.wait()
    for goal in goals:
        gather(goal * 2 + 1 - x)
        rows_x[goal].start()
    nearer = list(goals)

    def spread(block, over_x):
        send(onward, block, across_y, y_sem.at[block // 4])
        if over_x:
            send(onward, block, across_x, x_sem.at[block // 8])
        send(onward, block, across_c, c_sem.at[block // 2])

    for step in range(1, depth):

        @pl.when(z - step >= 0)
        def risen():
            block = slot(z - step, x, y, c)
            arrive(block)

            @pl.when(z < depth - 1)
            def further():
                send(onward, block, device(z + 1, x, y, c), up_sem.at[step])

            spread(block, True)

        @pl.when(z + step < depth)
        def fallen():
            block = slot(z + step, x, y, c)
            arrive(block)

            @pl.when(z > 0)
            def further():
                send(onward, block, device(z - 1, x, y, c), down_sem.at[step])

            spread(block, True)

        for goal in nearer[:2]:
            gather(goal * 2 + x)
        nearer = nearer[2:]

    for goal in goals:
        rows_x[goal].wait_recv()
        part = rows_ref[goal * 2 + x] + far_x[goal]

        @pl.when(goal > z)
        def rising():
            @pl.when(z > 0)
            def more():
                rows_up(goal).wait_recv()
                total[goal] = part + from_low[goal]

            @pl.when(z == 0)
            def alone():
                total[goal] = part

            rows_up(goal).start()

        @pl.when(goal < z)
        def falling():
            @pl.when(z < depth - 1)
            def more():
                rows_down(goal).wait_recv()
                total[goal] = part + from_high[goal]

            @pl.when(z == depth - 1)
            def alone():
                total[goal] = part

            rows_down(goal).start()

        @pl.when(goal == z)
        def here():
            total[goal] = part

    for step in range(depth):
        for sign in (1, -1) if step else (1,):

            @pl.when((z + sign * step >= 0) & (z + sign * step < depth))
            def crossed():
                block = slot(z + sign * step, 1 - x, y, c)
                arrive(block)
                spread(block, False)

    for goal in range(depth):

        @pl.when(goal == z)
        def landed():
            @pl.when(z > 0)
            def low_part():
                rows_up(goal).wait_recv()
                total[goal] = total[goal] + from_low[goal]

            @pl.when(z < depth - 1)
            def high_part():
                rows_down(goal).wait_recv()
                total[goal] = total[goal] + from_high[goal]

            sum_ref[...] = total[goal]

    for step in range(depth):
        for sign in (1, -1) if step else (1,):

            @pl.when((z + sign * step >= 0) & (z + sign * step < depth))
            def crossed():
                for side in (x, 1 - x):
                    block = slot(z + sign * step, side, 1 - y, c)
                    arrive(block)
                    send(onward, block, across_c, c_sem.at[block // 2])

    for block in range(depth * 8):

        @pl.when(block % 2 != c)
        def from_core():
            arrive(block)

    for copy in local:
        copy.wait()
    for group in range(groups):
        for rank in range(2):

            @pl.when((group != dp) | (rank != y))
            def spoken():
                tell(group, rank).wait_send()

    for goal in range(depth):
        rows_x[goal].wait_send()

        @pl.when(goal > z)
        def rose():
            rows_up(goal).wait_send()

        @pl.when(goal < z)
        def fell():
            rows_down(goal).wait_send()

    def sent(block, target, sem):
        for piece in range(3):
            onward(block, piece, target, sem).wait_send()

    for step in range(depth):

        @pl.when((z - step >= 0) & (z < depth - 1))
        def rose():
            sent(mine, device(z + 1, x, y, c), up_sem.at[step])

        @pl.when((z + step < depth) & (z > 0))
        def fell():
            sent(mine, device(z - 1, x, y, c), down_sem.at[step])

        sent(mine, across_x, x_sem.at[step])
    for index in range(depth * 2):
        sent(mine, across_y, y_sem.at[index])
    for index in range(depth * 4):
        sent(mine, across_c, c_sem.at[index])


def start(pieces, table, codes, vocab_ids, groups):
    width = table.shape[1]
    height = vocab_ids.shape[0] // (groups * 4) + 2 * codes.shape[2]
    depth = groups // 2
    blocks = depth * 8
    told = (groups, 2, 1, codes.shape[2])
    dma = pltpu.SemaphoreType.DMA
    buffer = pltpu.VMEM((depth, height, width), low)
    return pl.pallas_call(
        functools.partial(start_kernel, depth),
        out_shape=[jax.ShapeDtypeStruct((blocks,) + piece.shape, low) for piece in pieces]
        + [jax.ShapeDtypeStruct((height, width), low), jax.ShapeDtypeStruct(told, jnp.int32)],
        in_specs=[ANY] * 4
        + [pl.BlockSpec(memory_space=pltpu.VMEM), pl.BlockSpec(memory_space=pltpu.SMEM)],
        out_specs=[ANY] * 3 + [pl.BlockSpec(memory_space=pltpu.VMEM)] * 2,
        scratch_shapes=[buffer] * 4
        + [
            pltpu.VMEM((groups, height, width), low),
            pltpu.VMEM((table.shape[0] + 8, width), jnp.float32),
            pltpu.SMEM(told, jnp.int32),
        ]
        + [dma((3,))]
        + [dma((depth, 3))] * 3
        + [dma((depth * 2, 3)), dma((depth * 4, 3)), dma((blocks, 3))]
        + [dma((depth,))] * 6
        + [dma((groups, 2))] * 2
        + [dma(())] * 2,
        compiler_params=pltpu.CompilerParams(
            collective_id=0, has_side_effects=True, vmem_limit_bytes=58 * 2**20
        ),
        name="start",
    )(*pieces, table, codes, vocab_ids)


def by_distance(depth, z, act):
    for step in range(depth - 1, -1, -1):
        for sign in (1, -1) if step else (1,):

            @pl.when((z + sign * step >= 0) & (z + sign * step < depth))
            def reached():
                act(z + sign * step)


def add_into(total, block, *terms):
    height = total.shape[1]
    chunk = 96 if height % 96 == 0 else height

    @pl.loop(0, height // chunk)
    def chunks(index):
        part = pl.ds(pl.multiple_of(index * chunk, chunk), chunk)
        value = total[block, part].astype(jnp.float32)
        for buffer, place in terms:
            value = value + buffer[place, part].astype(jnp.float32)
        total[block, part] = value.astype(low)


def end_kernel(depth, heights, *refs):
    pieces, rows_ref, grad_ref, rows_out = refs[0:3], refs[3], refs[4], refs[5]
    total, far_c, far_y, far_x, from_low, from_high = refs[6:12]
    local_sem, c_send, c_recv, y_send, y_recv, x_send, x_recv = refs[12:19]
    u_send, u_recv, d_send, d_recv = refs[19:23]
    own_sem, ru_send, rd_send, rx_send, r_recv = refs[23:28]
    z, x, y, c = coordinates(depth)
    greet(depth, z, x, y, c)
    firsts = [sum(heights[:index]) for index in range(3)]
    up, down = device(z + 1, x, y, c), device(z - 1, x, y, c)
    across_x, across_y, across_c = (
        device(z, 1 - x, y, c),
        device(z, x, 1 - y, c),
        device(z, x, y, 1 - c),
    )

    def remote(source, goal, send_sem, recv_sem, target):
        return pltpu.make_async_remote_copy(
            source, goal, send_sem, recv_sem, device_id=target, device_id_type=MESH
        )

    def local(block, piece):
        return pltpu.make_async_copy(
            pieces[piece].at[block * 2 + c],
            total.at[block, pl.ds(firsts[piece], heights[piece])],
            local_sem.at[block, piece],
        )

    def over_c(block, piece):
        return remote(
            pieces[piece].at[block * 2 + 1 - c],
            far_c.at[block, pl.ds(firsts[piece], heights[piece])],
            c_send.at[block, piece],
            c_recv.at[block, piece],
            across_c,
        )

    def over_y(place, side):
        pair = place * 2 + side
        return remote(
            total.at[pair * 2 + 1 - y], far_y.at[pair], y_send.at[pair], y_recv.at[pair], across_y
        )

    def over_x(place):
        return remote(
            total.at[(place * 2 + 1 - x) * 2 + y],
            far_x.at[place],
            x_send.at[place],
            x_recv.at[place],
            across_x,
        )

    def rise(place):
        block = (place * 2 + x) * 2 + y
        return remote(
            total.at[block], from_low.at[place], u_send.at[place], u_recv.at[place], up
        )

    def fall(place):
        block = (place * 2 + x) * 2 + y
        return remote(
            total.at[block], from_high.at[place], d_send.at[place], d_recv.at[place], down
        )

    def own_rows(send_sem, target):
        mine = z * 2 + x
        return remote(rows_ref, rows_out.at[mine], send_sem, r_recv.at[mine], target)

    def rows_on(place, send_sem, target):
        there = place * 2 + x
        return remote(rows_out.at[there], rows_out.at[there], send_sem, r_recv.at[there], target)

    own = pltpu.make_async_copy(rows_ref, rows_out.at[z * 2 + x], own_sem)
    own.start()

    @pl.when(z < depth - 1)
    def first_up():
        own_rows(ru_send.at[0], up).start()

    @pl.when(z > 0)
    def first_down():
        own_rows(rd_send.at[0], down).start()

    own_rows(rx_send.at[z], across_x).start()
    for turn in range(2):
        for side in (1 - x, x):

            def launch(place):
                block = (place * 2 + side) * 2 + (1 - y if turn == 0 else y)
                for piece in range(3):
                    over_c(block, piece).start()
                    local(block, piece).start()

            by_distance(depth, z, launch)

    def ready(block):
        for piece in range(3):
            local(block, piece).wait()
            over_c(block, piece).wait_recv()

    for side in (1 - x, x):

        def give_y(place):
            block = (place * 2 + side) * 2 + 1 - y
            ready(block)
            add_into(total, block, (far_c, block))
            over_y(place, side).start()

        by_distance(depth, z, give_y)

    def rows_step(step):
        @pl.when(z - step >= 0)
        def risen():
            rows_on(z - step, ru_send.at[step], up).wait_recv()

            @pl.when(z < depth - 1)
            def further():
                rows_on(z - step, ru_send.at[step], up).start()

            rows_on(z - step, rx_send.at[z - step], across_x).start()

        @pl.when(z + step < depth)
        def fallen():
            rows_on(z + step, rd_send.at[step], down).wait_recv()

            @pl.when(z > 0)
            def further():
                rows_on(z + step, rd_send.at[step], down).start()

            rows_on(z + step, rx_send.at[z + step], across_x).start()

    def give_x(place):
        block = (place * 2 + 1 - x) * 2 + y
        ready(block)
        over_y(place, 1 - x).wait_recv()
        add_into(total, block, (far_c, block), (far_y, place * 2 + 1 - x))
        over_x(place).start()

    for step in range(depth - 1, -1, -1):
        if step:
            rows_step(depth - step)
        for sign in (1, -1) if step else (1,):

            @pl.when((z + sign * step >= 0) & (z + sign * step < depth))
            def reached():
                give_x(z + sign * step)

    def give_z(place):
        block = (place * 2 + x) * 2 + y
        pair = place * 2 + x
        ready(block)
        over_y(place, x).wait_recv()
        over_x(place).wait_recv()
        add_into(total, block, (far_c, block), (far_y, pair), (far_x, place))

        @pl.when(place > z)
        def rising():
            @pl.when(z > 0)
            def more():
                rise(place).wait_recv()
                add_into(total, block, (from_low, place))

            rise(place).start()

        @pl.when(place < z)
        def falling():
            @pl.when(z < depth - 1)
            def more():
                fall(place).wait_recv()
                add_into(total, block, (from_high, place))

            fall(place).start()

    by_distance(depth, z, give_z)
    mine = (z * 2 + x) * 2 + y
    grad_ref[...] = total[mine].astype(jnp.float32)

    @pl.when(z > 0)
    def low_part():
        rise(z).wait_recv()
        grad_ref[...] = grad_ref[...] + from_low[z].astype(jnp.float32)

    @pl.when(z < depth - 1)
    def high_part():
        fall(z).wait_recv()
        grad_ref[...] = grad_ref[...] + from_high[z].astype(jnp.float32)

    own.wait()
    for place in range(depth):
        there = place * 2 + 1 - x
        remote(
            rows_out.at[there], rows_out.at[there], rx_send.at[place], r_recv.at[there], across_x
        ).wait_recv()
        rows_on(place, rx_send.at[place], across_x).wait_send()
        over_x(place).wait_send()
        for side in range(2):
            over_y(place, side).wait_send()
            for rank in range(2):
                for piece in range(3):
                    over_c((place * 2 + side) * 2 + rank, piece).wait_send()

        @pl.when(place > z)
        def rose():
            rise(place).wait_send()

        @pl.when(place < z)
        def fell():
            fall(place).wait_send()

        @pl.when((z - place >= 0) & (z < depth - 1))
        def rows_rose():
            rows_on(z, ru_send.at[place], up).wait_send()

        @pl.when((z + place < depth) & (z > 0))
        def rows_fell():
            rows_on(z, rd_send.at[place], down).wait_send()


def end(pieces, rows):
    blocks = pieces[0].shape[0]
    heights = [piece.shape[1] for piece in pieces]
    height, width = sum(heights), pieces[0].shape[2]
    depth = blocks // 8
    dma = pltpu.SemaphoreType.DMA

    def buffer(count):
        return pltpu.VMEM((count, height, width), low)

    return pl.pallas_call(
        functools.partial(end_kernel, depth, heights),
        out_shape=[
            jax.ShapeDtypeStruct((height, width), jnp.float32),
            jax.ShapeDtypeStruct((depth * 2,) + rows.shape, low),
        ],
        in_specs=[ANY] * 4,
        out_specs=[pl.BlockSpec(memory_space=pltpu.VMEM), ANY],
        scratch_shapes=[buffer(depth * 4), buffer(depth * 4), buffer(depth * 2)]
        + [buffer(depth)] * 3
        + [dma((depth * 4, 3))] * 3
        + [dma((depth * 2,))] * 2
        + [dma((depth,))] * 6
        + [dma(())]
        + [dma((depth,))] * 3
        + [dma((depth * 2,))],
        compiler_params=pltpu.CompilerParams(
            collective_id=1, has_side_effects=True, vmem_limit_bytes=58 * 2**20
        ),
        name="end",
    )(*pieces, rows)


def collect_kernel(step, places_ref, rows_ref, table_ref):
    base = pl.program_id(0) * step
    at = base + lax.broadcasted_iota(jnp.int32, (step, places_ref.shape[1]), 0)
    picked = jnp.where(at == places_ref[...], 1.0, 0.0).astype(low)
    table_ref[...] = product(picked, rows_ref[...]).astype(low)


def collect(places, rows, height, step):
    count, width = rows.shape
    return pl.pallas_call(
        functools.partial(collect_kernel, step),
        grid=(height // step,),
        out_shape=jax.ShapeDtypeStruct((height, width), low),
        in_specs=[
            pl.BlockSpec((1, count), lambda i: (0, 0)),
            pl.BlockSpec((count, width), lambda i: (0, 0)),
        ],
        out_specs=pl.BlockSpec((step, width), lambda i: (i, 0)),
        compiler_params=pltpu.CompilerParams(vmem_limit_bytes=58 * 2**20),
        cost_estimate=pl.CostEstimate(
            flops=2 * count * width * height,
            bytes_accessed=2 * width * (count + height),
            transcendentals=0,
        ),
        name="collect",
    )(places, rows)


def share_kernel(depth, table_ref, small_ref, table_out, small_out, *refs):
    far_c, part, far_y, small, far_small = refs[0:5]
    c_send, c_recv, y_send, y_recv, o_send, o_recv, s_send, s_recv = refs[5:13]
    z, x, y, c = coordinates(depth)
    partners = [device(z, x, y, 1 - c), device(z, x, 1 - y, c), device(z, 1 - x, y, c)]
    reach = 1
    while reach < depth:
        partners.append(device(z ^ reach, x, y, c))
        reach = reach * 2
    barrier = pltpu.get_barrier_semaphore()
    for target in partners:
        pl.semaphore_signal(barrier, 1, device_id=target, device_id_type=MESH)
    pl.semaphore_wait(barrier, len(partners))
    across_c, across_y = partners[:2]

    def remote(source, goal, send_sem, recv_sem, target):
        return pltpu.make_async_remote_copy(
            source, goal, send_sem, recv_sem, device_id=target, device_id_type=MESH
        )

    def over_c(rank):
        return remote(
            table_ref.at[rank * 2 + 1 - c],
            far_c.at[rank],
            c_send.at[rank],
            c_recv.at[rank],
            across_c,
        )

    def out(rank, core, index, target):
        where = table_out.at[rank * 2 + core]
        return remote(where, where, o_send.at[index], o_recv.at[rank * 2 + core], target)

    height = part.shape[0]
    chunk = 80 if height % 80 == 0 else height
    over_c(1 - y).start()
    over_c(y).start()
    over_c(1 - y).wait_recv()

    @pl.loop(0, height // chunk)
    def first_sum(index):
        rows = pl.ds(pl.multiple_of(index * chunk, chunk), chunk)
        part[rows] = (
            table_ref[(1 - y) * 2 + c, rows].astype(jnp.float32)
            + far_c[1 - y, rows].astype(jnp.float32)
        ).astype(low)

    over_y = remote(part, far_y, y_send, y_recv, across_y)
    over_y.start()
    over_c(y).wait_recv()
    over_y.wait_recv()
    mine = y * 2 + c

    def second_sum(index, squares):
        rows = pl.ds(pl.multiple_of(index * chunk, chunk), chunk)
        value = (
            table_ref[mine, rows].astype(jnp.float32)
            + far_c[y, rows].astype(jnp.float32)
            + far_y[rows].astype(jnp.float32)
        ).astype(low)
        table_out[mine, rows] = value
        value = value.astype(jnp.float32)
        return squares + jnp.sum((value * value).reshape(-1, 8, 768), axis=0)

    squares = lax.fori_loop(0, height // chunk, second_sum, jnp.zeros((8, 768), jnp.float32))
    out(y, c, 0, across_y).start()
    out(y, c, 1, across_c).start()
    lines = lax.broadcasted_iota(jnp.int32, small.shape[1:], 0)
    lanes = lax.broadcasted_iota(jnp.int32, small.shape[1:], 1)
    last = (lines == small.shape[1] - 1) & (lanes == 0)
    small[0] = small_ref[...] + jnp.where(last, jnp.sum(squares), 0.0)
    for turn, target in enumerate(partners):
        copy = remote(
            small.at[turn], far_small.at[turn], s_send.at[turn], s_recv.at[turn], target
        )
        copy.start()
        copy.wait_recv()
        small[turn + 1] = small[turn] + far_small[turn]
    small_out[...] = small[len(partners)]
    out(1 - y, c, 0, across_y).wait_recv()
    out(1 - y, c, 2, across_c).start()
    out(y, 1 - c, 1, across_c).wait_recv()
    out(1 - y, 1 - c, 2, across_c).wait_recv()
    for turn, target in enumerate(partners):
        remote(
            small.at[turn], far_small.at[turn], s_send.at[turn], s_recv.at[turn], target
        ).wait_send()
    over_y.wait_send()
    for rank in range(2):
        over_c(rank).wait_send()
    out(y, c, 0, across_y).wait_send()
    out(y, c, 1, across_c).wait_send()
    out(1 - y, c, 2, across_c).wait_send()


def share(depth, table, small):
    quarters, height, width = table.shape
    turns = 3 + (depth - 1).bit_length()
    dma = pltpu.SemaphoreType.DMA
    vmem = pl.BlockSpec(memory_space=pltpu.VMEM)
    return pl.pallas_call(
        functools.partial(share_kernel, depth),
        out_shape=[
            jax.ShapeDtypeStruct(table.shape, low),
            jax.ShapeDtypeStruct(small.shape, jnp.float32),
        ],
        in_specs=[vmem, vmem],
        out_specs=[vmem, vmem],
        scratch_shapes=[
            pltpu.VMEM((2, height, width), low),
            pltpu.VMEM((height, width), low),
            pltpu.VMEM((height, width), low),
            pltpu.VMEM((turns + 1,) + small.shape, jnp.float32),
            pltpu.VMEM((turns,) + small.shape, jnp.float32),
            dma((2,)),
            dma((2,)),
            dma(()),
            dma(()),
            dma((3,)),
            dma((4,)),
            dma((turns,)),
            dma((turns,)),
        ],
        compiler_params=pltpu.CompilerParams(
            collective_id=2, has_side_effects=True, vmem_limit_bytes=58 * 2**20
        ),
        name="share",
    )(table, small)


def adam_step(weight, gradient, first, second, rate, decay):
    first_new = beta_one * first + (1.0 - beta_one) * gradient
    second_new = beta_two * second + (1.0 - beta_two) * gradient * gradient
    direction = (
        first_new
        / (1.0 - beta_one**STEP)
        / (jnp.sqrt(second_new / (1.0 - beta_two**STEP)) + adam_eps)
    )
    return (weight - rate * (direction + decay * weight), first_new, second_new)


def on_device(
    token_ids,
    lengths,
    valid,
    vocab_ids,
    teacher,
    block,
    block_m,
    block_v,
    bases,
    table,
    table_m,
    table_v,
    gains,
    gains_m,
    gains_v,
):
    dp_count, head_count = lax.axis_size("dp"), lax.axis_size("head")
    device_total = dp_count * head_count
    head, dp = lax.axis_index("head"), lax.axis_index("dp")
    batch = head // 2
    tokens = token_ids.shape[1]
    shard_rows = table.shape[0]
    offset = dp * shard_rows
    part = TOPV // device_total

    widths = [3 * D // device_total, D // device_total, 2 * FF // device_total, FF // device_total]
    cuts = [sum(widths[:index]) for index in range(5)]
    block_low = block.T.astype(low)
    attention, gate_up, down, rows_in, codes = start(
        [block_low[: cuts[2]], block_low[cuts[2] : cuts[3]], block_low[cuts[3] :]],
        table,
        (token_ids * 2 + valid).reshape(-1, 1, tokens),
        vocab_ids,
        dp_count,
    )
    codes = codes.reshape(dp_count, 2 * tokens)
    weighting = (lax.dynamic_index_in_dim(codes, dp, 0, keepdims=False) & 1).astype(jnp.float32)
    vocab = lax.dynamic_index_in_dim(
        vocab_ids.reshape(dp_count, head_count, part), head, 1, keepdims=False
    )
    local = jnp.concatenate([vocab, codes >> 1], axis=1) - offset
    owned = (local >= 0) & (local < shard_rows)
    weights = [
        attention[:, : cuts[1]].reshape(-1, D),
        attention[:, cuts[1] :].reshape(-1, D),
        gate_up.reshape(-1, D),
        down.reshape(-1, D),
    ]
    chosen = lax.all_gather(rows_in[:part], ("dp", "head"), axis=0, tiled=True)
    hidden = rows_in[part:].astype(jnp.float32)

    teacher_own = lax.dynamic_index_in_dim(teacher, batch, 0, keepdims=False)
    teacher_far = swap(
        lax.dynamic_index_in_dim(teacher, 1 - batch, 0, keepdims=False), head_count, 2
    )
    teacher_rows = jnp.concatenate([teacher_own, teacher_far], axis=0)

    run = jnp.arange(tokens, dtype=jnp.int32)
    places = jnp.concatenate([head * tokens + run, (head ^ 2) * tokens + run])
    places_far = jnp.concatenate([(head ^ 1) * tokens + run, (head ^ 3) * tokens + run])
    own_lengths = lax.dynamic_index_in_dim(lengths, batch, 0, keepdims=False)[0]
    segment, position = segments(own_lengths, places)
    segment_far, unused = segments(own_lengths, places_far)
    places_all = jnp.concatenate([places, places_far])
    segment_all = jnp.concatenate([segment, segment_far])
    allow = (segment[:, None] == segment_all[None, :]) & (places[:, None] >= places_all[None, :])
    freqs = jnp.exp(jnp.arange(0, HD, 2, dtype=jnp.float32) * (-math.log(10000.0) / HD))
    angle = position.astype(jnp.float32)[:, None] * freqs[None, :]
    angle = jnp.concatenate([angle, angle], axis=1)
    cosine, sine = jnp.cos(angle), jnp.sin(angle)

    saves = []
    for repeat in range(2):
        hidden, saved = layer_forward(hidden, weights, gains, cosine, sine, allow, head_count)
        saves.append(saved)

    normed = rms_norm(hidden, gains[2]).astype(low)
    log_prob = jax.nn.log_softmax(contract_cols(normed, chosen), axis=-1)
    teach = jax.nn.log_softmax(teacher_rows.astype(jnp.float32), axis=-1)
    loss_sum = jnp.sum(weighting * jnp.sum(jnp.exp(teach) * (teach - log_prob), axis=-1))
    logit_grads = ((jnp.exp(log_prob) - jnp.exp(teach)) * weighting[:, None]).astype(low)
    chosen_grads = contract_rows(logit_grads, normed).astype(low)
    gradient, d_gain_final = rms_back(hidden, gains[2], product(logit_grads, chosen))
    chosen_grads = lax.psum_scatter(chosen_grads, ("dp", "head"), scatter_dimension=0, tiled=True)

    block_grads = None
    d_gains = [0.0, 0.0]
    for repeat in range(2):
        gradient, layer_grads, d_gain_one, d_gain_two = layer_backward(
            gradient, weights, gains, saves[1 - repeat], cosine, sine, allow, head_count
        )
        d_gains = [d_gains[0] + d_gain_one, d_gains[1] + d_gain_two]
        if block_grads is None:
            block_grads = layer_grads
        else:
            block_grads = [total + extra for total, extra in zip(block_grads, layer_grads)]

    d_qkv, d_out, d_gu, d_down = [
        piece.astype(low).reshape(device_total, -1, D) for piece in block_grads
    ]
    rows_back = jnp.concatenate([chosen_grads, gradient.astype(low)], axis=0)
    block_grads, rows_back = end(
        [jnp.concatenate([d_qkv, d_out], axis=1), d_gu, d_down], rows_back
    )
    block_grads = block_grads.T

    step = 80 if shard_rows % 80 == 0 else 40
    quarter = -(-shard_rows // (step * head_count)) * step
    tile = quarter // 5 if quarter % 80 == 0 and quarter // 5 % 16 == 0 else step
    table_grads = collect(
        jnp.where(owned, local, -1).reshape(1, -1),
        rows_back.reshape(-1, D),
        quarter * head_count,
        tile,
    )
    squares = jnp.sum(block_grads * block_grads)
    small = jnp.concatenate([d_gains[0], d_gains[1], d_gain_final, loss_sum[None], jnp.sum(weighting)[None]])
    small = jnp.pad(small, (0, 6 * 128 - 2)).reshape(-1, 128)
    small = small.at[-1, 0].set(squares)
    table_grads, small = share(
        dp_count // 2, table_grads.reshape(head_count, quarter, D), small
    )
    table_grads = table_grads.reshape(-1, D)[:shard_rows].astype(jnp.float32)
    squares = small[-1, 0]
    small = small.reshape(-1)
    count = small[3 * D + 1]
    gain_grads = small[: 3 * D].reshape(3, D) / count
    loss = small[3 * D] / count
    grad_norm = jnp.sqrt(squares / (count * count) + jnp.sum(gain_grads * gain_grads))
    clip = jnp.minimum(1.0, clip_norm / grad_norm)
    factor = clip / count
    block_grads = block_grads * factor
    table_grads = table_grads * factor
    gain_grads = gain_grads * clip

    rotated = jnp.concatenate(
        [
            contract_rows(bases[index], block_grads[:, cuts[index] : cuts[index + 1]])
            for index in range(4)
        ],
        axis=1,
    )
    block_m_new = beta_one * block_m + (1.0 - beta_one) * rotated
    block_v_new = beta_two * block_v + (1.0 - beta_two) * rotated * rotated
    direction = (
        block_m_new
        / (1.0 - beta_one**STEP)
        / (jnp.sqrt(block_v_new / (1.0 - beta_two**STEP)) + adam_eps)
    )
    update = jnp.concatenate(
        [product(bases[index], direction[:, cuts[index] : cuts[index + 1]]) for index in range(4)],
        axis=1,
    )
    block_new = block - rate_block * (update + decay_rate * block)
    table_new, table_m_new, table_v_new = adam_step(
        table, table_grads, table_m, table_v, rate_table, decay_rate
    )
    gains_new, gains_m_new, gains_v_new = adam_step(
        gains, gain_grads, gains_m, gains_v, rate_gain, 0.0
    )
    return (
        loss,
        grad_norm,
        block_new,
        block_m_new,
        block_v_new,
        table_new,
        table_m_new,
        table_v_new,
        gains_new,
        gains_m_new,
        gains_v_new,
        block_new.astype(low),
        table_new.astype(low),
    )


def solution(mesh):
    tokens = P(None, ("dp", "head"))
    columns = P(None, ("dp", "head"))
    table = P("dp", None)
    return jax.shard_map(
        on_device,
        mesh=mesh,
        in_specs=(
            tokens,
            P(None, "dp", None),
            tokens,
            P(),
            P(None, ("dp", "head"), None),
            columns,
            columns,
            columns,
            P(),
            table,
            table,
            table,
            P(),
            P(),
            P(),
        ),
        out_specs=(
            P(),
            P(),
            columns,
            columns,
            columns,
            table,
            table,
            table,
            P(),
            P(),
            P(),
            columns,
            table,
        ),
        check_vma=False,
    )
```

```python
import functools
import math

import jax
import jax.numpy as jnp
from jax import lax
from jax.experimental import pallas as pl
from jax.experimental.pallas import tpu as pltpu
from jax.sharding import PartitionSpec as P

D = 768
H = 12
HD = 64
FF = 3072
TOPV = 4096
STEP = 5

low = jnp.bfloat16
scale = HD**-0.5
eps_norm = 1e-05
clip_norm = 0.002
beta_one = 0.9
beta_two = 0.99
adam_eps = 1e-08
decay_rate = 0.1
rate_block = 0.03
rate_table = 0.05
rate_gain = 0.4


def product(left, right):
    return jnp.dot(left, right, preferred_element_type=jnp.float32)


def contract_rows(left, right):
    return lax.dot_general(
        left, right, (((0,), (0,)), ((), ())), preferred_element_type=jnp.float32
    )


def contract_cols(left, right):
    return lax.dot_general(
        left, right, (((1,), (1,)), ((), ())), preferred_element_type=jnp.float32
    )


def rms_norm(value, gain):
    return value * lax.rsqrt(jnp.mean(value * value, axis=-1, keepdims=True) + eps_norm) * gain


def rms_back(value, gain, grad):
    r = lax.rsqrt(jnp.mean(value * value, axis=-1, keepdims=True) + eps_norm)
    scaled = grad * gain
    d_value = r * scaled - value * (r * r * r) * jnp.mean(value * scaled, axis=-1, keepdims=True)
    return d_value, jnp.sum(grad * value * r, axis=0)


def rotary(value, cosine, sine):
    half = HD // 2
    turned = jnp.concatenate([-value[..., half:], value[..., :half]], axis=-1)
    return value * cosine[:, None, :] + turned * sine[:, None, :]


def rotary_back(grad, cosine, sine):
    half = HD // 2
    part = grad * sine[:, None, :]
    turned = jnp.concatenate([part[..., half:], -part[..., :half]], axis=-1)
    return grad * cosine[:, None, :] + turned


def segments(lengths, places):
    segment = jnp.zeros_like(places)
    begin = jnp.zeros_like(places)
    end = jnp.zeros((), jnp.int32)
    for index in range(lengths.shape[0] - 1):
        end = end + lengths[index]
        past = places >= end
        segment = segment + past.astype(jnp.int32)
        begin = jnp.where(past, end, begin)
    return segment, places - begin


def scores_of(query, keys, allow):
    score = jnp.einsum("qhd,khd->hqk", query, keys, preferred_element_type=jnp.float32) * scale
    return jnp.where(allow[None], score, -1e30)


def attend(query, keys, values, allow):
    score = scores_of(query, keys, allow)
    summit = jnp.max(score, axis=-1, keepdims=True)
    log_total = summit + jnp.log(jnp.sum(jnp.exp(score - summit), axis=-1, keepdims=True))
    weight = jnp.exp(score - log_total)
    mixed = jnp.einsum(
        "hqk,khd->qhd", weight.astype(low), values, preferred_element_type=jnp.float32
    )
    return mixed.astype(low), log_total


def attend_back(query, keys, values, log_total, upstream, allow):
    weight = jnp.exp(scores_of(query, keys, allow) - log_total)
    d_value = jnp.einsum(
        "hqk,qhd->khd", weight.astype(low), upstream, preferred_element_type=jnp.float32
    )
    d_weight = jnp.einsum("qhd,khd->hqk", upstream, values, preferred_element_type=jnp.float32)
    d_score = (weight * (d_weight - jnp.sum(d_weight * weight, axis=-1, keepdims=True))).astype(low)
    d_query = jnp.einsum("hqk,khd->qhd", d_score, keys, preferred_element_type=jnp.float32) * scale
    d_key = jnp.einsum("hqk,qhd->khd", d_score, query, preferred_element_type=jnp.float32) * scale
    return d_query, d_key, d_value


def swap(value, head_count, offset):
    return lax.ppermute(value, "head", [(h, h ^ offset) for h in range(head_count)])


def layer_forward(hidden, weights, gains, cosine, sine, allow, head_count):
    w_qkv, w_out, w_gu, w_down = weights
    rows = hidden.shape[0]
    normed = rms_norm(hidden, gains[0]).astype(low)
    qkv = contract_cols(normed, w_qkv).reshape(rows, 3, H, HD)
    query = rotary(qkv[:, 0], cosine, sine).astype(low)
    key = rotary(qkv[:, 1], cosine, sine).astype(low)
    own = jnp.concatenate([key, qkv[:, 2].astype(low)], axis=1)
    both = jnp.concatenate([own, swap(own, head_count, 1)], axis=0)
    keys, values = both[:, :H], both[:, H:]
    mixed, log_total = attend(query, keys, values, allow)
    merged = mixed.reshape(rows, D)
    middle = hidden + contract_cols(merged, w_out)
    normed_two = rms_norm(middle, gains[1]).astype(low)
    gate_up = contract_cols(normed_two, w_gu)
    action = (jax.nn.silu(gate_up[:, :FF]) * gate_up[:, FF:]).astype(low)
    output = middle + product(action, w_down)
    saved = (hidden, normed, query, keys, values, log_total, merged, middle, normed_two, gate_up, action)
    return output, saved


def layer_backward(gradient, weights, gains, saved, cosine, sine, allow, head_count):
    w_qkv, w_out, w_gu, w_down = weights
    hidden, normed, query, keys, values, log_total, merged, middle, normed_two, gate_up, action = saved
    rows = hidden.shape[0]
    grad_low = gradient.astype(low)
    d_down = contract_rows(action, grad_low)
    d_action = contract_cols(grad_low, w_down)
    gate, up = gate_up[:, :FF], gate_up[:, FF:]
    chance = jax.nn.sigmoid(gate)
    d_gate = d_action * up * (chance + gate * chance * (1.0 - chance))
    d_up = d_action * gate * chance
    d_gate_up = jnp.concatenate([d_gate, d_up], axis=1).astype(low)
    d_gu = contract_rows(d_gate_up, normed_two)
    d_middle, d_gain_two = rms_back(middle, gains[1], product(d_gate_up, w_gu))
    d_middle = gradient + d_middle
    middle_low = d_middle.astype(low)
    d_out = contract_rows(middle_low, merged)
    upstream = product(middle_low, w_out).astype(low).reshape(rows, H, HD)
    d_query, d_key, d_value = attend_back(query, keys, values, log_total, upstream, allow)
    d_own = jnp.concatenate([d_key[:rows], d_value[:rows]], axis=1)
    d_far = jnp.concatenate([d_key[rows:], d_value[rows:]], axis=1).astype(low)
    d_own = (d_own + swap(d_far, head_count, 1).astype(jnp.float32)).astype(low).astype(jnp.float32)
    d_query = rotary_back(d_query.astype(low).astype(jnp.float32), cosine, sine)
    d_key = rotary_back(d_own[:, :H], cosine, sine)
    d_qkv = jnp.concatenate([d_query, d_key, d_own[:, H:]], axis=1).reshape(rows, 3 * D).astype(low)
    d_qkv_w = contract_rows(d_qkv, normed)
    d_hidden, d_gain_one = rms_back(hidden, gains[0], product(d_qkv, w_qkv))
    return d_middle + d_hidden, [d_qkv_w, d_out, d_gu, d_down], d_gain_one, d_gain_two


MESH = pl.DeviceIdType.MESH
ANY = pl.BlockSpec(memory_space=pl.ANY)


def coordinates(depth):
    dp, head = lax.axis_index("dp"), lax.axis_index("head")
    return dp // 2, dp % 2, head // 2, head % 2


def device(z, x, y, c):
    return (z * 2 + x, y * 2 + c)


def slot(z, x, y, c):
    return ((z * 2 + x) * 2 + y) * 2 + c


def greet(depth, z, x, y, c):
    barrier = pltpu.get_barrier_semaphore()
    for target in (device(z, 1 - x, y, c), device(z, x, 1 - y, c), device(z, x, y, 1 - c)):
        pl.semaphore_signal(barrier, 1, device_id=target, device_id_type=MESH)

    @pl.when(z > 0)
    def below():
        pl.semaphore_signal(barrier, 1, device_id=device(z - 1, x, y, c), device_id_type=MESH)

    @pl.when(z < depth - 1)
    def above():
        pl.semaphore_signal(barrier, 1, device_id=device(z + 1, x, y, c), device_id_type=MESH)

    pl.semaphore_wait(barrier, 3 + jnp.where(z > 0, 1, 0) + jnp.where(z < depth - 1, 1, 0))


def start_kernel(depth, *refs):
    pieces = refs[0:3]
    table_ref, codes_ref, vocab_ref = refs[3:6]
    wholes = refs[6:9]
    sum_ref, ids_ref = refs[9:11]
    far_x, from_low, from_high, total, rows_ref, shard, ids = refs[11:18]
    local_sem, up_sem, down_sem, x_sem, y_sem, c_sem, block_sem = refs[18:25]
    rx_send, rx_recv, ru_send, ru_recv, rd_send, rd_recv = refs[25:31]
    id_send, id_recv, table_sem, copy_sem = refs[31:35]
    z, x, y, c = coordinates(depth)
    mine = slot(z, x, y, c)
    dp, head = z * 2 + x, y * 2 + c
    groups, height = rows_ref.shape[:2]
    shard_rows, tokens = table_ref.shape[0], codes_ref.shape[2]
    part = height - 2 * tokens
    offset = dp * shard_rows
    barrier = pltpu.get_barrier_semaphore()
    pl.semaphore_signal(barrier, 1, device_id=device(z, x, y, 1 - c), device_id_type=MESH)
    for group in range(groups):
        for rank in range(2):

            @pl.when((group != dp) | (rank != y))
            def hello():
                pl.semaphore_signal(
                    barrier, 1, device_id=(group, rank * 2 + c), device_id_type=MESH
                )

    pl.semaphore_wait(barrier, groups * 2)

    def tell(group, rank):
        second = jnp.where(rank == y, 0, 1)
        return pltpu.make_async_remote_copy(
            codes_ref.at[rank],
            ids_ref.at[dp, second],
            id_send.at[group, rank],
            id_recv.at[dp, second],
            device_id=(group, rank * 2 + c),
            device_id_type=MESH,
        )

    def told(group, second):
        return pltpu.make_async_remote_copy(
            codes_ref.at[0],
            ids_ref.at[group, second],
            id_send.at[group, second],
            id_recv.at[group, second],
            device_id=device(z, x, y, 1 - c),
            device_id_type=MESH,
        )

    keep = pltpu.make_async_copy(codes_ref.at[y], ids_ref.at[dp, 0], copy_sem)
    fetch = pltpu.make_async_copy(table_ref, shard.at[pl.ds(0, shard_rows)], table_sem)
    fetch.start()
    keep.start()
    for group in range(groups):
        for rank in range(2):

            @pl.when((group != dp) | (rank != y))
            def telling():
                tell(group, rank).start()

    def gather(group):
        def load(first, read):
            @pl.loop(0, (tokens if first else part) // 16)
            def some(index):
                base = index * 16
                lines = []
                for line in range(16):
                    place = read(base + line) - offset
                    held = (place >= 0) & (place < shard_rows)
                    lines.append(shard[pl.ds(jnp.where(held, place, shard_rows), 1)])
                rows_ref[group, pl.ds(pl.multiple_of(first + base, 16), 16)] = jnp.concatenate(
                    lines, axis=0
                ).astype(low)

        load(0, lambda index: vocab_ref[(group * 4 + head) * part + index])
        for second in range(2):
            load(part + second * tokens, lambda index: ids[group, second, 0, index] >> 1)

    def own(block, piece, target, sem):
        return pltpu.make_async_remote_copy(
            pieces[piece],
            wholes[piece].at[block],
            sem.at[piece],
            block_sem.at[block, piece],
            device_id=target,
            device_id_type=MESH,
        )

    def onward(block, piece, target, sem):
        return pltpu.make_async_remote_copy(
            wholes[piece].at[block],
            wholes[piece].at[block],
            sem.at[piece],
            block_sem.at[block, piece],
            device_id=target,
            device_id_type=MESH,
        )

    def send(make, block, target, sem):
        for piece in range(3):
            make(block, piece, target, sem).start()

    def arrive(block):
        for piece in range(3):
            onward(block, piece, device(z, x, y, 1 - c), c_sem.at[0]).wait_recv()

    across_x, across_y, across_c = (
        device(z, 1 - x, y, c),
        device(z, x, 1 - y, c),
        device(z, x, y, 1 - c),
    )
    rows_x = [
        pltpu.make_async_remote_copy(
            rows_ref.at[goal * 2 + 1 - x],
            far_x.at[goal],
            rx_send.at[goal],
            rx_recv.at[goal],
            device_id=across_x,
            device_id_type=MESH,
        )
        for goal in range(depth)
    ]

    def rows_up(goal):
        return pltpu.make_async_remote_copy(
            total.at[goal],
            from_low.at[goal],
            ru_send.at[goal],
            ru_recv.at[goal],
            device_id=device(z + 1, x, y, c),
            device_id_type=MESH,
        )

    def rows_down(goal):
        return pltpu.make_async_remote_copy(
            total.at[goal],
            from_high.at[goal],
            rd_send.at[goal],
            rd_recv.at[goal],
            device_id=device(z - 1, x, y, c),
            device_id_type=MESH,
        )

    goals = [
        goal for pair in zip(range(depth // 2), range(depth - 1, 0, -1)) for goal in pair
    ]
    local = [
        pltpu.make_async_copy(pieces[piece], wholes[piece].at[mine], local_sem.at[piece])
        for piece in range(3)
    ]
    send(own, mine, across_y, y_sem.at[mine // 4])

    @pl.when(z < depth - 1)
    def first_up():
        send(own, mine, device(z + 1, x, y, c), up_sem.at[0])

    @pl.when(z > 0)
    def first_down():
        send(own, mine, device(z - 1, x, y, c), down_sem.at[0])

    send(own, mine, across_x, x_sem.at[z])
    send(own, mine, across_c, c_sem.at[mine // 2])
    for copy in local:
        copy.start()
    shard[pl.ds(shard_rows, 8)] = jnp.zeros((8, shard.shape[1]), jnp.float32)
    keep.wait()
    for group in range(groups):
        for second in range(2):

            @pl.when((group != dp) | (second != 0))
            def heard():
                told(group, second).wait_recv()

    to_scalars = pltpu.make_async_copy(ids_ref, ids, copy_sem)
    to_scalars.start()
    fetch.wait()
    to_scalars.wait()
    for goal in goals:
        gather(goal * 2 + 1 - x)
        rows_x[goal].start()
    nearer = list(goals)

    def spread(block, over_x):
        send(onward, block, across_y, y_sem.at[block // 4])
        if over_x:
            send(onward, block, across_x, x_sem.at[block // 8])
        send(onward, block, across_c, c_sem.at[block // 2])

    for step in range(1, depth):

        @pl.when(z - step >= 0)
        def risen():
            block = slot(z - step, x, y, c)
            arrive(block)

            @pl.when(z < depth - 1)
            def further():
                send(onward, block, device(z + 1, x, y, c), up_sem.at[step])

            spread(block, True)

        @pl.when(z + step < depth)
        def fallen():
            block = slot(z + step, x, y, c)
            arrive(block)

            @pl.when(z > 0)
            def further():
                send(onward, block, device(z - 1, x, y, c), down_sem.at[step])

            spread(block, True)

        for goal in nearer[:2]:
            gather(goal * 2 + x)
        nearer = nearer[2:]

    for goal in goals:
        rows_x[goal].wait_recv()
        part = rows_ref[goal * 2 + x] + far_x[goal]

        @pl.when(goal > z)
        def rising():
            @pl.when(z > 0)
            def more():
                rows_up(goal).wait_recv()
                total[goal] = part + from_low[goal]

            @pl.when(z == 0)
            def alone():
                total[goal] = part

            rows_up(goal).start()

        @pl.when(goal < z)
        def falling():
            @pl.when(z < depth - 1)
            def more():
                rows_down(goal).wait_recv()
                total[goal] = part + from_high[goal]

            @pl.when(z == depth - 1)
            def alone():
                total[goal] = part

            rows_down(goal).start()

        @pl.when(goal == z)
        def here():
            total[goal] = part

    for step in range(depth):
        for sign in (1, -1) if step else (1,):

            @pl.when((z + sign * step >= 0) & (z + sign * step < depth))
            def crossed():
                block = slot(z + sign * step, 1 - x, y, c)
                arrive(block)
                spread(block, False)

    for goal in range(depth):

        @pl.when(goal == z)
        def landed():
            @pl.when(z > 0)
            def low_part():
                rows_up(goal).wait_recv()
                total[goal] = total[goal] + from_low[goal]

            @pl.when(z < depth - 1)
            def high_part():
                rows_down(goal).wait_recv()
                total[goal] = total[goal] + from_high[goal]

            sum_ref[...] = total[goal]

    for step in range(depth):
        for sign in (1, -1) if step else (1,):

            @pl.when((z + sign * step >= 0) & (z + sign * step < depth))
            def crossed():
                for side in (x, 1 - x):
                    block = slot(z + sign * step, side, 1 - y, c)
                    arrive(block)
                    send(onward, block, across_c, c_sem.at[block // 2])

    for block in range(depth * 8):

        @pl.when(block % 2 != c)
        def from_core():
            arrive(block)

    for copy in local:
        copy.wait()
    for group in range(groups):
        for rank in range(2):

            @pl.when((group != dp) | (rank != y))
            def spoken():
                tell(group, rank).wait_send()

    for goal in range(depth):
        rows_x[goal].wait_send()

        @pl.when(goal > z)
        def rose():
            rows_up(goal).wait_send()

        @pl.when(goal < z)
        def fell():
            rows_down(goal).wait_send()

    def sent(block, target, sem):
        for piece in range(3):
            onward(block, piece, target, sem).wait_send()

    for step in range(depth):

        @pl.when((z - step >= 0) & (z < depth - 1))
        def rose():
            sent(mine, device(z + 1, x, y, c), up_sem.at[step])

        @pl.when((z + step < depth) & (z > 0))
        def fell():
            sent(mine, device(z - 1, x, y, c), down_sem.at[step])

        sent(mine, across_x, x_sem.at[step])
    for index in range(depth * 2):
        sent(mine, across_y, y_sem.at[index])
    for index in range(depth * 4):
        sent(mine, across_c, c_sem.at[index])


def start(pieces, table, codes, vocab_ids, groups):
    width = table.shape[1]
    height = vocab_ids.shape[0] // (groups * 4) + 2 * codes.shape[2]
    depth = groups // 2
    blocks = depth * 8
    told = (groups, 2, 1, codes.shape[2])
    dma = pltpu.SemaphoreType.DMA
    buffer = pltpu.VMEM((depth, height, width), low)
    return pl.pallas_call(
        functools.partial(start_kernel, depth),
        out_shape=[jax.ShapeDtypeStruct((blocks,) + piece.shape, low) for piece in pieces]
        + [jax.ShapeDtypeStruct((height, width), low), jax.ShapeDtypeStruct(told, jnp.int32)],
        in_specs=[ANY] * 4
        + [pl.BlockSpec(memory_space=pltpu.VMEM), pl.BlockSpec(memory_space=pltpu.SMEM)],
        out_specs=[ANY] * 3 + [pl.BlockSpec(memory_space=pltpu.VMEM)] * 2,
        scratch_shapes=[buffer] * 4
        + [
            pltpu.VMEM((groups, height, width), low),
            pltpu.VMEM((table.shape[0] + 8, width), jnp.float32),
            pltpu.SMEM(told, jnp.int32),
        ]
        + [dma((3,))]
        + [dma((depth, 3))] * 3
        + [dma((depth * 2, 3)), dma((depth * 4, 3)), dma((blocks, 3))]
        + [dma((depth,))] * 6
        + [dma((groups, 2))] * 2
        + [dma(())] * 2,
        compiler_params=pltpu.CompilerParams(
            collective_id=0, has_side_effects=True, vmem_limit_bytes=58 * 2**20
        ),
        name="start",
    )(*pieces, table, codes, vocab_ids)


def by_distance(depth, z, act):
    for step in range(depth - 1, -1, -1):
        for sign in (1, -1) if step else (1,):

            @pl.when((z + sign * step >= 0) & (z + sign * step < depth))
            def reached():
                act(z + sign * step)


def add_into(total, block, *terms):
    height = total.shape[1]
    chunk = 96 if height % 96 == 0 else height

    @pl.loop(0, height // chunk)
    def chunks(index):
        part = pl.ds(pl.multiple_of(index * chunk, chunk), chunk)
        value = total[block, part].astype(jnp.float32)
        for buffer, place in terms:
            value = value + buffer[place, part].astype(jnp.float32)
        total[block, part] = value.astype(low)


def finish_kernel(depth, heights, tile, *refs):
    pieces = refs[0:3]
    rows_ref, places_ref, small_ref = refs[3:6]
    grad_ref, table_out, small_out = refs[6:9]
    total, far_c, far_p, far_s, from_low, from_high = refs[9:15]
    rows, given, far_t, part, mine, far_part, small, far_small = refs[15:23]
    local_sem, c_send, c_recv, p_send, p_recv, s_send, s_recv = refs[23:30]
    u_send, u_recv, d_send, d_recv = refs[30:34]
    own_sem, ru_send, rd_send, rx_send, r_recv = refs[34:39]
    t_send, t_recv, ty_send, ty_recv, o_send, o_recv, e_send, e_recv = refs[39:47]
    z, x, y, c = coordinates(depth)
    dp = z * 2 + x
    firsts = [sum(heights[:index]) for index in range(3)]
    up, down = device(z + 1, x, y, c), device(z - 1, x, y, c)
    across_x, across_y, across_c = (
        device(z, 1 - x, y, c),
        device(z, x, 1 - y, c),
        device(z, x, y, 1 - c),
    )
    even = c == 0
    across_p = tuple(jnp.where(even, a, b) for a, b in zip(across_y, across_x))
    across_s = tuple(jnp.where(even, b, a) for a, b in zip(across_y, across_x))
    own_p, own_s = jnp.where(even, y, x), jnp.where(even, x, y)
    partners = [across_c, across_y, across_x]
    reach = 1
    while reach < depth:
        partners.append(device(z ^ reach, x, y, c))
        reach = reach * 2

    barrier = pltpu.get_barrier_semaphore()
    for target in partners[:3] + partners[4:]:
        pl.semaphore_signal(barrier, 1, device_id=target, device_id_type=MESH)

    @pl.when(z > 0)
    def below():
        pl.semaphore_signal(barrier, 1, device_id=down, device_id_type=MESH)

    @pl.when(z < depth - 1)
    def above():
        pl.semaphore_signal(barrier, 1, device_id=up, device_id_type=MESH)

    pl.semaphore_wait(
        barrier, len(partners) - 1 + jnp.where(z > 0, 1, 0) + jnp.where(z < depth - 1, 1, 0)
    )

    def remote(source, goal, send_sem, recv_sem, target):
        return pltpu.make_async_remote_copy(
            source, goal, send_sem, recv_sem, device_id=target, device_id_type=MESH
        )

    def block_of(place, s, p):
        return place * 4 + jnp.where(even, s * 2 + p, p * 2 + s)

    def local(block, piece):
        return pltpu.make_async_copy(
            pieces[piece].at[block * 2 + c],
            total.at[block, pl.ds(firsts[piece], heights[piece])],
            local_sem.at[block, piece],
        )

    def over_c(block, piece):
        return remote(
            pieces[piece].at[block * 2 + 1 - c],
            far_c.at[block, pl.ds(firsts[piece], heights[piece])],
            c_send.at[block, piece],
            c_recv.at[block, piece],
            across_c,
        )

    def over_p(place, s):
        pair = place * 2 + s
        return remote(
            total.at[block_of(place, s, 1 - own_p)],
            far_p.at[pair],
            p_send.at[pair],
            p_recv.at[pair],
            across_p,
        )

    def over_s(place):
        return remote(
            total.at[block_of(place, 1 - own_s, own_p)],
            far_s.at[place],
            s_send.at[place],
            s_recv.at[place],
            across_s,
        )

    def rise(place):
        block = block_of(place, own_s, own_p)
        return remote(
            total.at[block], from_low.at[place], u_send.at[place], u_recv.at[place], up
        )

    def fall(place):
        block = block_of(place, own_s, own_p)
        return remote(
            total.at[block], from_high.at[place], d_send.at[place], d_recv.at[place], down
        )

    def own_rows(send_sem, target):
        return remote(rows_ref, rows.at[dp], send_sem, r_recv.at[dp], target)

    def rows_on(place, send_sem, target):
        there = place * 2 + x
        return remote(rows.at[there], rows.at[there], send_sem, r_recv.at[there], target)

    own = pltpu.make_async_copy(rows_ref, rows.at[dp], own_sem)
    own.start()

    @pl.when(z < depth - 1)
    def first_up():
        own_rows(ru_send.at[0], up).start()

    @pl.when(z > 0)
    def first_down():
        own_rows(rd_send.at[0], down).start()

    own_rows(rx_send.at[z], across_x).start()

    for turn in range(2):
        for s, s_there in ((1 - own_s, 1 - own_p), (own_s, own_p)):
            p, p_there = (1 - own_p, 1 - own_s) if turn == 0 else (own_p, own_s)

            def launch(place):
                for piece in range(3):
                    over_c(
                        place * 4 + jnp.where(even, p_there * 2 + s_there, s_there * 2 + p_there),
                        piece,
                    ).start()
                    local(block_of(place, s, p), piece).start()

            by_distance(depth, z, launch)

    def ready(block):
        for piece in range(3):
            local(block, piece).wait()
            over_c(block, piece).wait_recv()

    def give_p():
        for s in (1 - own_s, own_s):

            def give(place):
                block = block_of(place, s, 1 - own_p)
                ready(block)
                add_into(total, block, (far_c, block))
                over_p(place, s).start()

            by_distance(depth, z, give)

    @pl.when(even)
    def early():
        give_p()

    for step in range(1, depth):

        @pl.when(z - step >= 0)
        def risen():
            rows_on(z - step, ru_send.at[step], up).wait_recv()

            @pl.when(z < depth - 1)
            def further():
                rows_on(z - step, ru_send.at[step], up).start()

            rows_on(z - step, rx_send.at[z - step], across_x).start()

        @pl.when(z + step < depth)
        def fallen():
            rows_on(z + step, rd_send.at[step], down).wait_recv()

            @pl.when(z > 0)
            def further():
                rows_on(z + step, rd_send.at[step], down).start()

            rows_on(z + step, rx_send.at[z + step], across_x).start()

    @pl.when(c == 1)
    def late():
        give_p()

    own.wait()
    for place in range(depth):
        there = place * 2 + 1 - x
        remote(
            rows.at[there], rows.at[there], rx_send.at[place], r_recv.at[there], across_x
        ).wait_recv()

    height = part.shape[0]
    count = places_ref.shape[1]

    def collect(rank, core, goal):
        @pl.loop(0, height // tile)
        def tiles(index):
            first = index * tile
            at = (
                (rank * 2 + core) * height
                + first
                + lax.broadcasted_iota(jnp.int32, (tile, count), 0)
            )
            picked = jnp.where(at == places_ref[...], 1.0, 0.0).astype(low)
            goal[pl.ds(pl.multiple_of(first, tile), tile)] = product(
                picked, rows[...].reshape(count, rows.shape[2])
            ).astype(low)

    def over_t(rank):
        index = jnp.where(rank == y, 1, 0)
        return remote(
            given.at[index], far_t.at[index], t_send.at[index], t_recv.at[index], across_c
        )

    chunk = 80 if height % 80 == 0 else height

    def pieces_of(act):
        @pl.loop(0, height // chunk)
        def step(index):
            act(pl.ds(pl.multiple_of(index * chunk, chunk), chunk))

    collect(1 - y, 1 - c, given.at[0])
    over_t(1 - y).start()
    collect(y, 1 - c, given.at[1])
    over_t(y).start()
    collect(1 - y, c, part)
    over_t(1 - y).wait_recv()

    def first_sum(lines):
        part[lines] = (part[lines].astype(jnp.float32) + far_t[0, lines].astype(jnp.float32)).astype(
            low
        )

    pieces_of(first_sum)
    over_part = remote(part, far_part, ty_send, ty_recv, across_y)
    over_part.start()
    collect(y, c, mine)

    def give_s(place):
        block = block_of(place, 1 - own_s, own_p)
        ready(block)
        over_p(place, 1 - own_s).wait_recv()
        add_into(total, block, (far_c, block), (far_p, place * 2 + 1 - own_s))
        over_s(place).start()

    by_distance(depth, z, give_s)

    over_t(y).wait_recv()
    over_part.wait_recv()

    def second_sum(index, squares):
        lines = pl.ds(pl.multiple_of(index * chunk, chunk), chunk)
        value = (
            mine[lines].astype(jnp.float32)
            + far_t[1, lines].astype(jnp.float32)
            + far_part[lines].astype(jnp.float32)
        ).astype(low)
        mine[lines] = value
        value = value.astype(jnp.float32)
        return squares + jnp.sum((value * value).reshape(-1, 8, value.shape[1]), axis=0)

    squares = lax.fori_loop(
        0, height // chunk, second_sum, jnp.zeros((8, part.shape[1]), jnp.float32)
    )

    def out_mine(index, target):
        where = table_out.at[y * 2 + c]
        return remote(mine, where, o_send.at[index], o_recv.at[y * 2 + c], target)

    def out(rank, core):
        where = table_out.at[rank * 2 + core]
        return remote(where, where, o_send.at[2], o_recv.at[rank * 2 + core], across_c)

    keep = pltpu.make_async_copy(mine, table_out.at[y * 2 + c], own_sem)
    out_mine(0, across_y).start()
    out_mine(1, across_c).start()
    keep.start()

    def give_z(place):
        block = block_of(place, own_s, own_p)
        ready(block)
        over_p(place, own_s).wait_recv()
        over_s(place).wait_recv()
        add_into(total, block, (far_c, block), (far_p, place * 2 + own_s), (far_s, place))

        @pl.when(place > z)
        def rising():
            @pl.when(z > 0)
            def more():
                rise(place).wait_recv()
                add_into(total, block, (from_low, place))

            rise(place).start()

        @pl.when(place < z)
        def falling():
            @pl.when(z < depth - 1)
            def more():
                fall(place).wait_recv()
                add_into(total, block, (from_high, place))

            fall(place).start()

    by_distance(depth, z, give_z)
    grad_ref[...] = total[block_of(z, own_s, own_p)].astype(jnp.float32)

    @pl.when(z > 0)
    def low_part():
        rise(z).wait_recv()
        grad_ref[...] = grad_ref[...] + from_low[z].astype(jnp.float32)

    @pl.when(z < depth - 1)
    def high_part():
        fall(z).wait_recv()
        grad_ref[...] = grad_ref[...] + from_high[z].astype(jnp.float32)

    lines = lax.broadcasted_iota(jnp.int32, small.shape[1:], 0)
    lanes = lax.broadcasted_iota(jnp.int32, small.shape[1:], 1)
    last = (lines == small.shape[1] - 1) & (lanes == 0)
    grad_squares = jnp.sum(grad_ref[...] * grad_ref[...])
    small[0] = small_ref[...] + jnp.where(last, jnp.sum(squares) + grad_squares, 0.0)

    def exchange(turn):
        return remote(
            small.at[turn], far_small.at[turn], e_send.at[turn], e_recv.at[turn], partners[turn]
        )

    for turn in range(len(partners)):
        exchange(turn).start()
        exchange(turn).wait_recv()
        small[turn + 1] = small[turn] + far_small[turn]
    small_out[...] = small[len(partners)]
    out(1 - y, c).wait_recv()
    out(1 - y, c).start()
    out(y, 1 - c).wait_recv()
    out(1 - y, 1 - c).wait_recv()

    keep.wait()
    out_mine(0, across_y).wait_send()
    out_mine(1, across_c).wait_send()
    out(1 - y, c).wait_send()
    over_part.wait_send()
    for turn in range(len(partners)):
        exchange(turn).wait_send()
    for rank in range(2):
        over_t(rank).wait_send()
    for place in range(depth):
        rows_on(place, rx_send.at[place], across_x).wait_send()
        over_s(place).wait_send()
        for side in range(2):
            over_p(place, side).wait_send()
            for rank in range(2):
                for piece in range(3):
                    over_c((place * 2 + side) * 2 + rank, piece).wait_send()

        @pl.when(place > z)
        def rose():
            rise(place).wait_send()

        @pl.when(place < z)
        def fell():
            fall(place).wait_send()

        @pl.when((z - place >= 0) & (z < depth - 1))
        def rows_rose():
            rows_on(z, ru_send.at[place], up).wait_send()

        @pl.when((z + place < depth) & (z > 0))
        def rows_fell():
            rows_on(z, rd_send.at[place], down).wait_send()


def finish(pieces, rows, places, small, quarter, tile):
    blocks = pieces[0].shape[0]
    heights = [piece.shape[1] for piece in pieces]
    height, width = sum(heights), pieces[0].shape[2]
    depth = blocks // 8
    turns = 3 + (depth - 1).bit_length()
    dma = pltpu.SemaphoreType.DMA
    vmem = pl.BlockSpec(memory_space=pltpu.VMEM)

    def buffer(count):
        return pltpu.VMEM((count, height, width), low)

    return pl.pallas_call(
        functools.partial(finish_kernel, depth, heights, tile),
        out_shape=[
            jax.ShapeDtypeStruct((height, width), jnp.float32),
            jax.ShapeDtypeStruct((4, quarter, width), low),
            jax.ShapeDtypeStruct(small.shape, jnp.float32),
        ],
        in_specs=[ANY] * 4 + [vmem] * 2,
        out_specs=[vmem, ANY, vmem],
        scratch_shapes=[buffer(depth * 4), buffer(depth * 4), buffer(depth * 2)]
        + [buffer(depth)] * 3
        + [
            pltpu.VMEM((depth * 2,) + rows.shape, low),
            pltpu.VMEM((2, quarter, width), low),
            pltpu.VMEM((2, quarter, width), low),
            pltpu.VMEM((quarter, width), low),
            pltpu.VMEM((quarter, width), low),
            pltpu.VMEM((quarter, width), low),
            pltpu.VMEM((turns + 1,) + small.shape, jnp.float32),
            pltpu.VMEM((turns,) + small.shape, jnp.float32),
        ]
        + [dma((depth * 4, 3))] * 3
        + [dma((depth * 2,))] * 2
        + [dma((depth,))] * 6
        + [dma(())]
        + [dma((depth,))] * 3
        + [dma((depth * 2,))]
        + [dma((2,))] * 2
        + [dma(())] * 2
        + [dma((3,)), dma((4,))]
        + [dma((turns,))] * 2,
        compiler_params=pltpu.CompilerParams(
            collective_id=1, has_side_effects=True, vmem_limit_bytes=62 * 2**20
        ),
        name="finish",
    )(*pieces, rows, places, small)


def adam_step(weight, gradient, first, second, rate, decay):
    first_new = beta_one * first + (1.0 - beta_one) * gradient
    second_new = beta_two * second + (1.0 - beta_two) * gradient * gradient
    direction = (
        first_new
        / (1.0 - beta_one**STEP)
        / (jnp.sqrt(second_new / (1.0 - beta_two**STEP)) + adam_eps)
    )
    return (weight - rate * (direction + decay * weight), first_new, second_new)


def on_device(
    token_ids,
    lengths,
    valid,
    vocab_ids,
    teacher,
    block,
    block_m,
    block_v,
    bases,
    table,
    table_m,
    table_v,
    gains,
    gains_m,
    gains_v,
):
    dp_count, head_count = lax.axis_size("dp"), lax.axis_size("head")
    device_total = dp_count * head_count
    head, dp = lax.axis_index("head"), lax.axis_index("dp")
    batch = head // 2
    tokens = token_ids.shape[1]
    shard_rows = table.shape[0]
    offset = dp * shard_rows
    part = TOPV // device_total

    widths = [3 * D // device_total, D // device_total, 2 * FF // device_total, FF // device_total]
    cuts = [sum(widths[:index]) for index in range(5)]
    block_low = block.T.astype(low)
    attention, gate_up, down, rows_in, codes = start(
        [block_low[: cuts[2]], block_low[cuts[2] : cuts[3]], block_low[cuts[3] :]],
        table,
        (token_ids * 2 + valid).reshape(-1, 1, tokens),
        vocab_ids,
        dp_count,
    )
    codes = codes.reshape(dp_count, 2 * tokens)
    weighting = (lax.dynamic_index_in_dim(codes, dp, 0, keepdims=False) & 1).astype(jnp.float32)
    vocab = lax.dynamic_index_in_dim(
        vocab_ids.reshape(dp_count, head_count, part), head, 1, keepdims=False
    )
    local = jnp.concatenate([vocab, codes >> 1], axis=1) - offset
    owned = (local >= 0) & (local < shard_rows)
    weights = [
        attention[:, : cuts[1]].reshape(-1, D),
        attention[:, cuts[1] :].reshape(-1, D),
        gate_up.reshape(-1, D),
        down.reshape(-1, D),
    ]
    chosen = lax.all_gather(rows_in[:part], ("dp", "head"), axis=0, tiled=True)
    hidden = rows_in[part:].astype(jnp.float32)

    teacher_own = lax.dynamic_index_in_dim(teacher, batch, 0, keepdims=False)
    teacher_far = swap(
        lax.dynamic_index_in_dim(teacher, 1 - batch, 0, keepdims=False), head_count, 2
    )
    teacher_rows = jnp.concatenate([teacher_own, teacher_far], axis=0)

    run = jnp.arange(tokens, dtype=jnp.int32)
    places = jnp.concatenate([head * tokens + run, (head ^ 2) * tokens + run])
    places_far = jnp.concatenate([(head ^ 1) * tokens + run, (head ^ 3) * tokens + run])
    own_lengths = lax.dynamic_index_in_dim(lengths, batch, 0, keepdims=False)[0]
    segment, position = segments(own_lengths, places)
    segment_far, unused = segments(own_lengths, places_far)
    places_all = jnp.concatenate([places, places_far])
    segment_all = jnp.concatenate([segment, segment_far])
    allow = (segment[:, None] == segment_all[None, :]) & (places[:, None] >= places_all[None, :])
    freqs = jnp.exp(jnp.arange(0, HD, 2, dtype=jnp.float32) * (-math.log(10000.0) / HD))
    angle = position.astype(jnp.float32)[:, None] * freqs[None, :]
    angle = jnp.concatenate([angle, angle], axis=1)
    cosine, sine = jnp.cos(angle), jnp.sin(angle)

    saves = []
    for repeat in range(2):
        hidden, saved = layer_forward(hidden, weights, gains, cosine, sine, allow, head_count)
        saves.append(saved)

    normed = rms_norm(hidden, gains[2]).astype(low)
    log_prob = jax.nn.log_softmax(contract_cols(normed, chosen), axis=-1)
    teach = jax.nn.log_softmax(teacher_rows.astype(jnp.float32), axis=-1)
    loss_sum = jnp.sum(weighting * jnp.sum(jnp.exp(teach) * (teach - log_prob), axis=-1))
    logit_grads = ((jnp.exp(log_prob) - jnp.exp(teach)) * weighting[:, None]).astype(low)
    chosen_grads = contract_rows(logit_grads, normed).astype(low)
    gradient, d_gain_final = rms_back(hidden, gains[2], product(logit_grads, chosen))
    chosen_grads = lax.psum_scatter(chosen_grads, ("dp", "head"), scatter_dimension=0, tiled=True)

    block_grads = None
    d_gains = [0.0, 0.0]
    for repeat in range(2):
        gradient, layer_grads, d_gain_one, d_gain_two = layer_backward(
            gradient, weights, gains, saves[1 - repeat], cosine, sine, allow, head_count
        )
        d_gains = [d_gains[0] + d_gain_one, d_gains[1] + d_gain_two]
        if block_grads is None:
            block_grads = layer_grads
        else:
            block_grads = [total + extra for total, extra in zip(block_grads, layer_grads)]

    d_qkv, d_out, d_gu, d_down = [
        piece.astype(low).reshape(device_total, -1, D) for piece in block_grads
    ]
    rows_back = jnp.concatenate([chosen_grads, gradient.astype(low)], axis=0)
    step = 80 if shard_rows % 80 == 0 else 40
    quarter = -(-shard_rows // (step * head_count)) * step
    tile = quarter // 5 if quarter % 80 == 0 and quarter // 5 % 16 == 0 else step
    small = [d_gains[0], d_gains[1], d_gain_final, loss_sum[None], jnp.sum(weighting)[None]]
    small = jnp.pad(jnp.concatenate(small), (0, 6 * 128 - 2)).reshape(-1, 128)
    block_grads, table_grads, small = finish(
        [jnp.concatenate([d_qkv, d_out], axis=1), d_gu, d_down],
        rows_back,
        jnp.where(owned, local, -1).reshape(1, -1),
        small,
        quarter,
        tile,
    )
    block_grads = block_grads.T
    table_grads = table_grads.reshape(-1, D)[:shard_rows].astype(jnp.float32)
    squares = small[-1, 0]
    small = small.reshape(-1)
    count = small[3 * D + 1]
    gain_grads = small[: 3 * D].reshape(3, D) / count
    loss = small[3 * D] / count
    grad_norm = jnp.sqrt(squares / (count * count) + jnp.sum(gain_grads * gain_grads))
    clip = jnp.minimum(1.0, clip_norm / grad_norm)
    factor = clip / count
    block_grads = block_grads * factor
    table_grads = table_grads * factor
    gain_grads = gain_grads * clip

    rotated = jnp.concatenate(
        [
            contract_rows(bases[index], block_grads[:, cuts[index] : cuts[index + 1]])
            for index in range(4)
        ],
        axis=1,
    )
    block_m_new = beta_one * block_m + (1.0 - beta_one) * rotated
    block_v_new = beta_two * block_v + (1.0 - beta_two) * rotated * rotated
    direction = (
        block_m_new
        / (1.0 - beta_one**STEP)
        / (jnp.sqrt(block_v_new / (1.0 - beta_two**STEP)) + adam_eps)
    )
    update = jnp.concatenate(
        [product(bases[index], direction[:, cuts[index] : cuts[index + 1]]) for index in range(4)],
        axis=1,
    )
    block_new = block - rate_block * (update + decay_rate * block)
    table_new, table_m_new, table_v_new = adam_step(
        table, table_grads, table_m, table_v, rate_table, decay_rate
    )
    gains_new, gains_m_new, gains_v_new = adam_step(
        gains, gain_grads, gains_m, gains_v, rate_gain, 0.0
    )
    return (
        loss,
        grad_norm,
        block_new,
        block_m_new,
        block_v_new,
        table_new,
        table_m_new,
        table_v_new,
        gains_new,
        gains_m_new,
        gains_v_new,
        block_new.astype(low),
        table_new.astype(low),
    )


def solution(mesh):
    tokens = P(None, ("dp", "head"))
    columns = P(None, ("dp", "head"))
    table = P("dp", None)
    return jax.shard_map(
        on_device,
        mesh=mesh,
        in_specs=(
            tokens,
            P(None, "dp", None),
            tokens,
            P(),
            P(None, ("dp", "head"), None),
            columns,
            columns,
            columns,
            P(),
            table,
            table,
            table,
            P(),
            P(),
            P(),
        ),
        out_specs=(
            P(),
            P(),
            columns,
            columns,
            columns,
            table,
            table,
            table,
            P(),
            P(),
            P(),
            columns,
            table,
        ),
        check_vma=False,
    )
```

```python
import functools
import math

import jax
import jax.numpy as jnp
from jax import lax
from jax.experimental import pallas as pl
from jax.experimental.pallas import tpu as pltpu
from jax.sharding import PartitionSpec as P

D = 768
H = 12
HD = 64
FF = 3072
TOPV = 4096
STEP = 5

low = jnp.bfloat16
scale = HD**-0.5
eps_norm = 1e-05
clip_norm = 0.002
beta_one = 0.9
beta_two = 0.99
adam_eps = 1e-08
decay_rate = 0.1
rate_block = 0.03
rate_table = 0.05
rate_gain = 0.4


def product(left, right):
    return jnp.dot(left, right, preferred_element_type=jnp.float32)


def contract_rows(left, right):
    return lax.dot_general(
        left, right, (((0,), (0,)), ((), ())), preferred_element_type=jnp.float32
    )


def contract_cols(left, right):
    return lax.dot_general(
        left, right, (((1,), (1,)), ((), ())), preferred_element_type=jnp.float32
    )


def rms_norm(value, gain):
    return value * lax.rsqrt(jnp.mean(value * value, axis=-1, keepdims=True) + eps_norm) * gain


def rms_back(value, gain, grad):
    r = lax.rsqrt(jnp.mean(value * value, axis=-1, keepdims=True) + eps_norm)
    scaled = grad * gain
    d_value = r * scaled - value * (r * r * r) * jnp.mean(value * scaled, axis=-1, keepdims=True)
    return d_value, jnp.sum(grad * value * r, axis=0)


def rotary(value, cosine, sine):
    half = HD // 2
    turned = jnp.concatenate([-value[..., half:], value[..., :half]], axis=-1)
    return value * cosine[:, None, :] + turned * sine[:, None, :]


def rotary_back(grad, cosine, sine):
    half = HD // 2
    part = grad * sine[:, None, :]
    turned = jnp.concatenate([part[..., half:], -part[..., :half]], axis=-1)
    return grad * cosine[:, None, :] + turned


def segments(lengths, places):
    segment = jnp.zeros_like(places)
    begin = jnp.zeros_like(places)
    end = jnp.zeros((), jnp.int32)
    for index in range(lengths.shape[0] - 1):
        end = end + lengths[index]
        past = places >= end
        segment = segment + past.astype(jnp.int32)
        begin = jnp.where(past, end, begin)
    return segment, places - begin


def scores_of(query, keys, allow):
    score = jnp.einsum("qhd,khd->hqk", query, keys, preferred_element_type=jnp.float32) * scale
    return jnp.where(allow[None], score, -1e30)


def attend(query, keys, values, allow):
    score = scores_of(query, keys, allow)
    summit = jnp.max(score, axis=-1, keepdims=True)
    log_total = summit + jnp.log(jnp.sum(jnp.exp(score - summit), axis=-1, keepdims=True))
    weight = jnp.exp(score - log_total)
    mixed = jnp.einsum(
        "hqk,khd->qhd", weight.astype(low), values, preferred_element_type=jnp.float32
    )
    return mixed.astype(low), log_total


def attend_back(query, keys, values, log_total, upstream, allow):
    weight = jnp.exp(scores_of(query, keys, allow) - log_total)
    d_value = jnp.einsum(
        "hqk,qhd->khd", weight.astype(low), upstream, preferred_element_type=jnp.float32
    )
    d_weight = jnp.einsum("qhd,khd->hqk", upstream, values, preferred_element_type=jnp.float32)
    d_score = (weight * (d_weight - jnp.sum(d_weight * weight, axis=-1, keepdims=True))).astype(low)
    d_query = jnp.einsum("hqk,khd->qhd", d_score, keys, preferred_element_type=jnp.float32) * scale
    d_key = jnp.einsum("hqk,qhd->khd", d_score, query, preferred_element_type=jnp.float32) * scale
    return d_query, d_key, d_value


def swap(value, head_count, offset):
    return lax.ppermute(value, "head", [(h, h ^ offset) for h in range(head_count)])


def layer_forward(hidden, weights, gains, cosine, sine, allow, head_count):
    w_qkv, w_out, w_gu, w_down = weights
    rows = hidden.shape[0]
    normed = rms_norm(hidden, gains[0]).astype(low)
    qkv = contract_cols(normed, w_qkv).reshape(rows, 3, H, HD)
    query = rotary(qkv[:, 0], cosine, sine).astype(low)
    key = rotary(qkv[:, 1], cosine, sine).astype(low)
    own = jnp.concatenate([key, qkv[:, 2].astype(low)], axis=1)
    both = jnp.concatenate([own, swap(own, head_count, 1)], axis=0)
    keys, values = both[:, :H], both[:, H:]
    mixed, log_total = attend(query, keys, values, allow)
    merged = mixed.reshape(rows, D)
    middle = hidden + contract_cols(merged, w_out)
    normed_two = rms_norm(middle, gains[1]).astype(low)
    gate_up = contract_cols(normed_two, w_gu)
    action = (jax.nn.silu(gate_up[:, :FF]) * gate_up[:, FF:]).astype(low)
    output = middle + product(action, w_down)
    saved = (hidden, normed, query, keys, values, log_total, merged, middle, normed_two, gate_up, action)
    return output, saved


def layer_backward(gradient, weights, gains, saved, cosine, sine, allow, head_count):
    w_qkv, w_out, w_gu, w_down = weights
    hidden, normed, query, keys, values, log_total, merged, middle, normed_two, gate_up, action = saved
    rows = hidden.shape[0]
    grad_low = gradient.astype(low)
    d_down = contract_rows(action, grad_low)
    d_action = contract_cols(grad_low, w_down)
    gate, up = gate_up[:, :FF], gate_up[:, FF:]
    chance = jax.nn.sigmoid(gate)
    d_gate = d_action * up * (chance + gate * chance * (1.0 - chance))
    d_up = d_action * gate * chance
    d_gate_up = jnp.concatenate([d_gate, d_up], axis=1).astype(low)
    d_gu = contract_rows(d_gate_up, normed_two)
    d_middle, d_gain_two = rms_back(middle, gains[1], product(d_gate_up, w_gu))
    d_middle = gradient + d_middle
    middle_low = d_middle.astype(low)
    d_out = contract_rows(middle_low, merged)
    upstream = product(middle_low, w_out).astype(low).reshape(rows, H, HD)
    d_query, d_key, d_value = attend_back(query, keys, values, log_total, upstream, allow)
    d_own = jnp.concatenate([d_key[:rows], d_value[:rows]], axis=1)
    d_far = jnp.concatenate([d_key[rows:], d_value[rows:]], axis=1).astype(low)
    d_own = (d_own + swap(d_far, head_count, 1).astype(jnp.float32)).astype(low).astype(jnp.float32)
    d_query = rotary_back(d_query.astype(low).astype(jnp.float32), cosine, sine)
    d_key = rotary_back(d_own[:, :H], cosine, sine)
    d_qkv = jnp.concatenate([d_query, d_key, d_own[:, H:]], axis=1).reshape(rows, 3 * D).astype(low)
    d_qkv_w = contract_rows(d_qkv, normed)
    d_hidden, d_gain_one = rms_back(hidden, gains[0], product(d_qkv, w_qkv))
    return d_middle + d_hidden, [d_qkv_w, d_out, d_gu, d_down], d_gain_one, d_gain_two


MESH = pl.DeviceIdType.MESH
ANY = pl.BlockSpec(memory_space=pl.ANY)


def coordinates(depth):
    dp, head = lax.axis_index("dp"), lax.axis_index("head")
    return dp // 2, dp % 2, head // 2, head % 2


def device(z, x, y, c):
    return (z * 2 + x, y * 2 + c)


def slot(z, x, y, c):
    return ((z * 2 + x) * 2 + y) * 2 + c


def greet(depth, z, x, y, c):
    barrier = pltpu.get_barrier_semaphore()
    for target in (device(z, 1 - x, y, c), device(z, x, 1 - y, c), device(z, x, y, 1 - c)):
        pl.semaphore_signal(barrier, 1, device_id=target, device_id_type=MESH)

    @pl.when(z > 0)
    def below():
        pl.semaphore_signal(barrier, 1, device_id=device(z - 1, x, y, c), device_id_type=MESH)

    @pl.when(z < depth - 1)
    def above():
        pl.semaphore_signal(barrier, 1, device_id=device(z + 1, x, y, c), device_id_type=MESH)

    pl.semaphore_wait(barrier, 3 + jnp.where(z > 0, 1, 0) + jnp.where(z < depth - 1, 1, 0))


def start_kernel(depth, *refs):
    pieces = refs[0:3]
    table_ref, codes_ref, vocab_ref = refs[3:6]
    wholes = refs[6:9]
    sum_ref, ids_ref = refs[9:11]
    far_x, from_low, from_high, total, rows_ref, shard, ids = refs[11:18]
    local_sem, up_sem, down_sem, x_sem, y_sem, c_sem, block_sem = refs[18:25]
    rx_send, rx_recv, ru_send, ru_recv, rd_send, rd_recv = refs[25:31]
    id_send, id_recv, table_sem, copy_sem = refs[31:35]
    z, x, y, c = coordinates(depth)
    mine = slot(z, x, y, c)
    dp, head = z * 2 + x, y * 2 + c
    groups, height = rows_ref.shape[:2]
    shard_rows, tokens = table_ref.shape[0], codes_ref.shape[2]
    part = height - 2 * tokens
    offset = dp * shard_rows
    barrier = pltpu.get_barrier_semaphore()
    pl.semaphore_signal(barrier, 1, device_id=device(z, x, y, 1 - c), device_id_type=MESH)
    for group in range(groups):
        for rank in range(2):

            @pl.when((group != dp) | (rank != y))
            def hello():
                pl.semaphore_signal(
                    barrier, 1, device_id=(group, rank * 2 + c), device_id_type=MESH
                )

    pl.semaphore_wait(barrier, groups * 2)

    def tell(group, rank):
        second = jnp.where(rank == y, 0, 1)
        return pltpu.make_async_remote_copy(
            codes_ref.at[rank],
            ids_ref.at[dp, second],
            id_send.at[group, rank],
            id_recv.at[dp, second],
            device_id=(group, rank * 2 + c),
            device_id_type=MESH,
        )

    def told(group, second):
        return pltpu.make_async_remote_copy(
            codes_ref.at[0],
            ids_ref.at[group, second],
            id_send.at[group, second],
            id_recv.at[group, second],
            device_id=device(z, x, y, 1 - c),
            device_id_type=MESH,
        )

    keep = pltpu.make_async_copy(codes_ref.at[y], ids_ref.at[dp, 0], copy_sem)
    fetch = pltpu.make_async_copy(table_ref, shard.at[pl.ds(0, shard_rows)], table_sem)
    fetch.start()
    keep.start()
    for group in range(groups):
        for rank in range(2):

            @pl.when((group != dp) | (rank != y))
            def telling():
                tell(group, rank).start()

    def gather(group):
        def load(first, read):
            @pl.loop(0, (tokens if first else part) // 16)
            def some(index):
                base = index * 16
                lines = []
                for line in range(16):
                    place = read(base + line) - offset
                    held = (place >= 0) & (place < shard_rows)
                    lines.append(shard[pl.ds(jnp.where(held, place, shard_rows), 1)])
                rows_ref[group, pl.ds(pl.multiple_of(first + base, 16), 16)] = jnp.concatenate(
                    lines, axis=0
                ).astype(low)

        load(0, lambda index: vocab_ref[(head * groups + group) * part + index])
        for second in range(2):
            load(part + second * tokens, lambda index: ids[group, second, 0, index] >> 1)

    def own(block, piece, target, sem):
        return pltpu.make_async_remote_copy(
            pieces[piece],
            wholes[piece].at[block],
            sem.at[piece],
            block_sem.at[block, piece],
            device_id=target,
            device_id_type=MESH,
        )

    def onward(block, piece, target, sem):
        return pltpu.make_async_remote_copy(
            wholes[piece].at[block],
            wholes[piece].at[block],
            sem.at[piece],
            block_sem.at[block, piece],
            device_id=target,
            device_id_type=MESH,
        )

    def send(make, block, target, sem):
        for piece in range(3):
            make(block, piece, target, sem).start()

    def arrive(block):
        for piece in range(3):
            onward(block, piece, device(z, x, y, 1 - c), c_sem.at[0]).wait_recv()

    across_x, across_y, across_c = (
        device(z, 1 - x, y, c),
        device(z, x, 1 - y, c),
        device(z, x, y, 1 - c),
    )
    rows_x = [
        pltpu.make_async_remote_copy(
            rows_ref.at[goal * 2 + 1 - x],
            far_x.at[goal],
            rx_send.at[goal],
            rx_recv.at[goal],
            device_id=across_x,
            device_id_type=MESH,
        )
        for goal in range(depth)
    ]

    def rows_up(goal):
        return pltpu.make_async_remote_copy(
            total.at[goal],
            from_low.at[goal],
            ru_send.at[goal],
            ru_recv.at[goal],
            device_id=device(z + 1, x, y, c),
            device_id_type=MESH,
        )

    def rows_down(goal):
        return pltpu.make_async_remote_copy(
            total.at[goal],
            from_high.at[goal],
            rd_send.at[goal],
            rd_recv.at[goal],
            device_id=device(z - 1, x, y, c),
            device_id_type=MESH,
        )

    goals = [
        goal for pair in zip(range(depth // 2), range(depth - 1, 0, -1)) for goal in pair
    ]
    local = [
        pltpu.make_async_copy(pieces[piece], wholes[piece].at[mine], local_sem.at[piece])
        for piece in range(3)
    ]
    send(own, mine, across_y, y_sem.at[mine // 4])

    @pl.when(z < depth - 1)
    def first_up():
        send(own, mine, device(z + 1, x, y, c), up_sem.at[0])

    @pl.when(z > 0)
    def first_down():
        send(own, mine, device(z - 1, x, y, c), down_sem.at[0])

    send(own, mine, across_x, x_sem.at[z])
    send(own, mine, across_c, c_sem.at[mine // 2])
    for copy in local:
        copy.start()
    shard[pl.ds(shard_rows, 8)] = jnp.zeros((8, shard.shape[1]), jnp.float32)
    keep.wait()
    for group in range(groups):
        for second in range(2):

            @pl.when((group != dp) | (second != 0))
            def heard():
                told(group, second).wait_recv()

    to_scalars = pltpu.make_async_copy(ids_ref, ids, copy_sem)
    to_scalars.start()
    fetch.wait()
    to_scalars.wait()
    for goal in goals:
        gather(goal * 2 + 1 - x)
        rows_x[goal].start()
    nearer = list(goals)

    def spread(block, over_x):
        send(onward, block, across_y, y_sem.at[block // 4])
        if over_x:
            send(onward, block, across_x, x_sem.at[block // 8])
        send(onward, block, across_c, c_sem.at[block // 2])

    for step in range(1, depth):

        @pl.when(z - step >= 0)
        def risen():
            block = slot(z - step, x, y, c)
            arrive(block)

            @pl.when(z < depth - 1)
            def further():
                send(onward, block, device(z + 1, x, y, c), up_sem.at[step])

            spread(block, True)

        @pl.when(z + step < depth)
        def fallen():
            block = slot(z + step, x, y, c)
            arrive(block)

            @pl.when(z > 0)
            def further():
                send(onward, block, device(z - 1, x, y, c), down_sem.at[step])

            spread(block, True)

        for goal in nearer[:2]:
            gather(goal * 2 + x)
        nearer = nearer[2:]

    for goal in goals:
        rows_x[goal].wait_recv()
        part = rows_ref[goal * 2 + x] + far_x[goal]

        @pl.when(goal > z)
        def rising():
            @pl.when(z > 0)
            def more():
                rows_up(goal).wait_recv()
                total[goal] = part + from_low[goal]

            @pl.when(z == 0)
            def alone():
                total[goal] = part

            rows_up(goal).start()

        @pl.when(goal < z)
        def falling():
            @pl.when(z < depth - 1)
            def more():
                rows_down(goal).wait_recv()
                total[goal] = part + from_high[goal]

            @pl.when(z == depth - 1)
            def alone():
                total[goal] = part

            rows_down(goal).start()

        @pl.when(goal == z)
        def here():
            total[goal] = part

    for step in range(depth):
        for sign in (1, -1) if step else (1,):

            @pl.when((z + sign * step >= 0) & (z + sign * step < depth))
            def crossed():
                block = slot(z + sign * step, 1 - x, y, c)
                arrive(block)
                spread(block, False)

    for goal in range(depth):

        @pl.when(goal == z)
        def landed():
            @pl.when(z > 0)
            def low_part():
                rows_up(goal).wait_recv()
                total[goal] = total[goal] + from_low[goal]

            @pl.when(z < depth - 1)
            def high_part():
                rows_down(goal).wait_recv()
                total[goal] = total[goal] + from_high[goal]

            sum_ref[...] = total[goal]

    for step in range(depth):
        for sign in (1, -1) if step else (1,):

            @pl.when((z + sign * step >= 0) & (z + sign * step < depth))
            def crossed():
                for side in (x, 1 - x):
                    block = slot(z + sign * step, side, 1 - y, c)
                    arrive(block)
                    send(onward, block, across_c, c_sem.at[block // 2])

    for block in range(depth * 8):

        @pl.when(block % 2 != c)
        def from_core():
            arrive(block)

    for copy in local:
        copy.wait()
    for group in range(groups):
        for rank in range(2):

            @pl.when((group != dp) | (rank != y))
            def spoken():
                tell(group, rank).wait_send()

    for goal in range(depth):
        rows_x[goal].wait_send()

        @pl.when(goal > z)
        def rose():
            rows_up(goal).wait_send()

        @pl.when(goal < z)
        def fell():
            rows_down(goal).wait_send()

    def sent(block, target, sem):
        for piece in range(3):
            onward(block, piece, target, sem).wait_send()

    for step in range(depth):

        @pl.when((z - step >= 0) & (z < depth - 1))
        def rose():
            sent(mine, device(z + 1, x, y, c), up_sem.at[step])

        @pl.when((z + step < depth) & (z > 0))
        def fell():
            sent(mine, device(z - 1, x, y, c), down_sem.at[step])

        sent(mine, across_x, x_sem.at[step])
    for index in range(depth * 2):
        sent(mine, across_y, y_sem.at[index])
    for index in range(depth * 4):
        sent(mine, across_c, c_sem.at[index])


def start(pieces, table, codes, vocab_ids, groups):
    width = table.shape[1]
    height = vocab_ids.shape[0] // (groups * 4) + 2 * codes.shape[2]
    depth = groups // 2
    blocks = depth * 8
    told = (groups, 2, 1, codes.shape[2])
    dma = pltpu.SemaphoreType.DMA
    buffer = pltpu.VMEM((depth, height, width), low)
    return pl.pallas_call(
        functools.partial(start_kernel, depth),
        out_shape=[jax.ShapeDtypeStruct((blocks,) + piece.shape, low) for piece in pieces]
        + [jax.ShapeDtypeStruct((height, width), low), jax.ShapeDtypeStruct(told, jnp.int32)],
        in_specs=[ANY] * 4
        + [pl.BlockSpec(memory_space=pltpu.VMEM), pl.BlockSpec(memory_space=pltpu.SMEM)],
        out_specs=[ANY] * 3 + [pl.BlockSpec(memory_space=pltpu.VMEM)] * 2,
        scratch_shapes=[buffer] * 4
        + [
            pltpu.VMEM((groups, height, width), low),
            pltpu.VMEM((table.shape[0] + 8, width), jnp.float32),
            pltpu.SMEM(told, jnp.int32),
        ]
        + [dma((3,))]
        + [dma((depth, 3))] * 3
        + [dma((depth * 2, 3)), dma((depth * 4, 3)), dma((blocks, 3))]
        + [dma((depth,))] * 6
        + [dma((groups, 2))] * 2
        + [dma(())] * 2,
        compiler_params=pltpu.CompilerParams(
            collective_id=0, has_side_effects=True, vmem_limit_bytes=58 * 2**20
        ),
        name="start",
    )(*pieces, table, codes, vocab_ids)


def by_distance(depth, z, act):
    for step in range(depth - 1, -1, -1):
        for sign in (1, -1) if step else (1,):

            @pl.when((z + sign * step >= 0) & (z + sign * step < depth))
            def reached():
                act(z + sign * step)


def add_into(total, block, *terms):
    height = total.shape[1]
    chunk = 96 if height % 96 == 0 else height

    @pl.loop(0, height // chunk)
    def chunks(index):
        part = pl.ds(pl.multiple_of(index * chunk, chunk), chunk)
        value = total[block, part].astype(jnp.float32)
        for buffer, place in terms:
            value = value + buffer[place, part].astype(jnp.float32)
        total[block, part] = value.astype(low)


def finish_kernel(depth, heights, tile, *refs):
    pieces = refs[0:3]
    rows_ref, places_ref, small_ref = refs[3:6]
    grad_ref, table_out, small_out = refs[6:9]
    total, far_c, far_p, far_s, from_low, from_high = refs[9:15]
    rows, given, far_t, part, mine, far_part, small, far_small = refs[15:23]
    local_sem, c_send, c_recv, p_send, p_recv, s_send, s_recv = refs[23:30]
    u_send, u_recv, d_send, d_recv = refs[30:34]
    own_sem, ru_send, rd_send, rx_send, r_recv = refs[34:39]
    t_send, t_recv, ty_send, ty_recv, o_send, o_recv, e_send, e_recv = refs[39:47]
    z, x, y, c = coordinates(depth)
    dp = z * 2 + x
    firsts = [sum(heights[:index]) for index in range(3)]
    up, down = device(z + 1, x, y, c), device(z - 1, x, y, c)
    across_x, across_y, across_c = (
        device(z, 1 - x, y, c),
        device(z, x, 1 - y, c),
        device(z, x, y, 1 - c),
    )
    even = c == 0
    across_p = tuple(jnp.where(even, a, b) for a, b in zip(across_y, across_x))
    across_s = tuple(jnp.where(even, b, a) for a, b in zip(across_y, across_x))
    own_p, own_s = jnp.where(even, y, x), jnp.where(even, x, y)
    partners = [across_c, across_y, across_x]
    reach = 1
    while reach < depth:
        partners.append(device(z ^ reach, x, y, c))
        reach = reach * 2

    barrier = pltpu.get_barrier_semaphore()
    for target in partners[:3] + partners[4:]:
        pl.semaphore_signal(barrier, 1, device_id=target, device_id_type=MESH)

    @pl.when(z > 0)
    def below():
        pl.semaphore_signal(barrier, 1, device_id=down, device_id_type=MESH)

    @pl.when(z < depth - 1)
    def above():
        pl.semaphore_signal(barrier, 1, device_id=up, device_id_type=MESH)

    pl.semaphore_wait(
        barrier, len(partners) - 1 + jnp.where(z > 0, 1, 0) + jnp.where(z < depth - 1, 1, 0)
    )

    def remote(source, goal, send_sem, recv_sem, target):
        return pltpu.make_async_remote_copy(
            source, goal, send_sem, recv_sem, device_id=target, device_id_type=MESH
        )

    def block_of(place, s, p):
        return place * 4 + jnp.where(even, s * 2 + p, p * 2 + s)

    def local(block, piece):
        return pltpu.make_async_copy(
            pieces[piece].at[block * 2 + c],
            total.at[block, pl.ds(firsts[piece], heights[piece])],
            local_sem.at[block, piece],
        )

    def over_c(block, piece):
        return remote(
            pieces[piece].at[block * 2 + 1 - c],
            far_c.at[block, pl.ds(firsts[piece], heights[piece])],
            c_send.at[block, piece],
            c_recv.at[block, piece],
            across_c,
        )

    def over_p(place, s):
        pair = place * 2 + s
        return remote(
            total.at[block_of(place, s, 1 - own_p)],
            far_p.at[pair],
            p_send.at[pair],
            p_recv.at[pair],
            across_p,
        )

    def over_s(place):
        return remote(
            total.at[block_of(place, 1 - own_s, own_p)],
            far_s.at[place],
            s_send.at[place],
            s_recv.at[place],
            across_s,
        )

    def rise(place):
        block = block_of(place, own_s, own_p)
        return remote(
            total.at[block], from_low.at[place], u_send.at[place], u_recv.at[place], up
        )

    def fall(place):
        block = block_of(place, own_s, own_p)
        return remote(
            total.at[block], from_high.at[place], d_send.at[place], d_recv.at[place], down
        )

    def own_rows(send_sem, target):
        return remote(rows_ref, rows.at[dp], send_sem, r_recv.at[dp], target)

    def rows_on(place, send_sem, target):
        there = place * 2 + x
        return remote(rows.at[there], rows.at[there], send_sem, r_recv.at[there], target)

    own = pltpu.make_async_copy(rows_ref, rows.at[dp], own_sem)
    own.start()

    @pl.when(z < depth - 1)
    def first_up():
        own_rows(ru_send.at[0], up).start()

    @pl.when(z > 0)
    def first_down():
        own_rows(rd_send.at[0], down).start()

    own_rows(rx_send.at[z], across_x).start()

    for turn in range(2):
        for s, s_there in ((1 - own_s, 1 - own_p), (own_s, own_p)):
            p, p_there = (1 - own_p, 1 - own_s) if turn == 0 else (own_p, own_s)

            def launch(place):
                for piece in range(3):
                    over_c(
                        place * 4 + jnp.where(even, p_there * 2 + s_there, s_there * 2 + p_there),
                        piece,
                    ).start()
                    local(block_of(place, s, p), piece).start()

            by_distance(depth, z, launch)

    def ready(block):
        for piece in range(3):
            local(block, piece).wait()
            over_c(block, piece).wait_recv()

    def give_p():
        for s in (1 - own_s, own_s):

            def give(place):
                block = block_of(place, s, 1 - own_p)
                ready(block)
                add_into(total, block, (far_c, block))
                over_p(place, s).start()

            by_distance(depth, z, give)

    @pl.when(even)
    def early():
        give_p()

    for step in range(1, depth):

        @pl.when(z - step >= 0)
        def risen():
            rows_on(z - step, ru_send.at[step], up).wait_recv()

            @pl.when(z < depth - 1)
            def further():
                rows_on(z - step, ru_send.at[step], up).start()

            rows_on(z - step, rx_send.at[z - step], across_x).start()

        @pl.when(z + step < depth)
        def fallen():
            rows_on(z + step, rd_send.at[step], down).wait_recv()

            @pl.when(z > 0)
            def further():
                rows_on(z + step, rd_send.at[step], down).start()

            rows_on(z + step, rx_send.at[z + step], across_x).start()

    @pl.when(c == 1)
    def late():
        give_p()

    own.wait()
    for place in range(depth):
        there = place * 2 + 1 - x
        remote(
            rows.at[there], rows.at[there], rx_send.at[place], r_recv.at[there], across_x
        ).wait_recv()

    height = part.shape[0]
    count = places_ref.shape[1]

    def collect(rank, core, goal):
        @pl.loop(0, height // tile)
        def tiles(index):
            first = index * tile
            at = (
                (rank * 2 + core) * height
                + first
                + lax.broadcasted_iota(jnp.int32, (tile, count), 0)
            )
            picked = jnp.where(at == places_ref[...], 1.0, 0.0).astype(low)
            goal[pl.ds(pl.multiple_of(first, tile), tile)] = product(
                picked, rows[...].reshape(count, rows.shape[2])
            ).astype(low)

    def over_t(rank):
        index = jnp.where(rank == y, 1, 0)
        return remote(
            given.at[index], far_t.at[index], t_send.at[index], t_recv.at[index], across_c
        )

    chunk = 80 if height % 80 == 0 else height

    def pieces_of(act):
        @pl.loop(0, height // chunk)
        def step(index):
            act(pl.ds(pl.multiple_of(index * chunk, chunk), chunk))

    collect(1 - y, 1 - c, given.at[0])
    over_t(1 - y).start()
    collect(y, 1 - c, given.at[1])
    over_t(y).start()
    collect(1 - y, c, part)
    over_t(1 - y).wait_recv()

    def first_sum(lines):
        part[lines] = (part[lines].astype(jnp.float32) + far_t[0, lines].astype(jnp.float32)).astype(
            low
        )

    pieces_of(first_sum)
    over_part = remote(part, far_part, ty_send, ty_recv, across_y)
    over_part.start()
    collect(y, c, mine)

    def give_s(place):
        block = block_of(place, 1 - own_s, own_p)
        ready(block)
        over_p(place, 1 - own_s).wait_recv()
        add_into(total, block, (far_c, block), (far_p, place * 2 + 1 - own_s))
        over_s(place).start()

    by_distance(depth, z, give_s)

    over_t(y).wait_recv()
    over_part.wait_recv()

    def second_sum(index, squares):
        lines = pl.ds(pl.multiple_of(index * chunk, chunk), chunk)
        value = (
            mine[lines].astype(jnp.float32)
            + far_t[1, lines].astype(jnp.float32)
            + far_part[lines].astype(jnp.float32)
        ).astype(low)
        mine[lines] = value
        value = value.astype(jnp.float32)
        return squares + jnp.sum((value * value).reshape(-1, 8, value.shape[1]), axis=0)

    squares = lax.fori_loop(
        0, height // chunk, second_sum, jnp.zeros((8, part.shape[1]), jnp.float32)
    )

    def out_mine(index, target):
        where = table_out.at[y * 2 + c]
        return remote(mine, where, o_send.at[index], o_recv.at[y * 2 + c], target)

    def out(rank, core):
        where = table_out.at[rank * 2 + core]
        return remote(where, where, o_send.at[2], o_recv.at[rank * 2 + core], across_c)

    keep = pltpu.make_async_copy(mine, table_out.at[y * 2 + c], own_sem)
    out_mine(0, across_y).start()
    out_mine(1, across_c).start()
    keep.start()

    def give_z(place):
        block = block_of(place, own_s, own_p)
        ready(block)
        over_p(place, own_s).wait_recv()
        over_s(place).wait_recv()
        add_into(total, block, (far_c, block), (far_p, place * 2 + own_s), (far_s, place))

        @pl.when(place > z)
        def rising():
            @pl.when(z > 0)
            def more():
                rise(place).wait_recv()
                add_into(total, block, (from_low, place))

            rise(place).start()

        @pl.when(place < z)
        def falling():
            @pl.when(z < depth - 1)
            def more():
                fall(place).wait_recv()
                add_into(total, block, (from_high, place))

            fall(place).start()

    by_distance(depth, z, give_z)
    grad_ref[...] = total[block_of(z, own_s, own_p)].astype(jnp.float32)

    @pl.when(z > 0)
    def low_part():
        rise(z).wait_recv()
        grad_ref[...] = grad_ref[...] + from_low[z].astype(jnp.float32)

    @pl.when(z < depth - 1)
    def high_part():
        fall(z).wait_recv()
        grad_ref[...] = grad_ref[...] + from_high[z].astype(jnp.float32)

    lines = lax.broadcasted_iota(jnp.int32, small.shape[1:], 0)
    lanes = lax.broadcasted_iota(jnp.int32, small.shape[1:], 1)
    last = (lines == small.shape[1] - 1) & (lanes == 0)
    grad_squares = jnp.sum(grad_ref[...] * grad_ref[...])
    small[0] = small_ref[...] + jnp.where(last, jnp.sum(squares) + grad_squares, 0.0)

    def exchange(turn):
        return remote(
            small.at[turn], far_small.at[turn], e_send.at[turn], e_recv.at[turn], partners[turn]
        )

    for turn in range(len(partners)):
        exchange(turn).start()
        exchange(turn).wait_recv()
        small[turn + 1] = small[turn] + far_small[turn]
    small_out[...] = small[len(partners)]
    out(1 - y, c).wait_recv()
    out(1 - y, c).start()
    out(y, 1 - c).wait_recv()
    out(1 - y, 1 - c).wait_recv()

    keep.wait()
    out_mine(0, across_y).wait_send()
    out_mine(1, across_c).wait_send()
    out(1 - y, c).wait_send()
    over_part.wait_send()
    for turn in range(len(partners)):
        exchange(turn).wait_send()
    for rank in range(2):
        over_t(rank).wait_send()
    for place in range(depth):
        rows_on(place, rx_send.at[place], across_x).wait_send()
        over_s(place).wait_send()
        for side in range(2):
            over_p(place, side).wait_send()
            for rank in range(2):
                for piece in range(3):
                    over_c((place * 2 + side) * 2 + rank, piece).wait_send()

        @pl.when(place > z)
        def rose():
            rise(place).wait_send()

        @pl.when(place < z)
        def fell():
            fall(place).wait_send()

        @pl.when((z - place >= 0) & (z < depth - 1))
        def rows_rose():
            rows_on(z, ru_send.at[place], up).wait_send()

        @pl.when((z + place < depth) & (z > 0))
        def rows_fell():
            rows_on(z, rd_send.at[place], down).wait_send()


def finish(pieces, rows, places, small, quarter, tile):
    blocks = pieces[0].shape[0]
    heights = [piece.shape[1] for piece in pieces]
    height, width = sum(heights), pieces[0].shape[2]
    depth = blocks // 8
    turns = 3 + (depth - 1).bit_length()
    dma = pltpu.SemaphoreType.DMA
    vmem = pl.BlockSpec(memory_space=pltpu.VMEM)

    def buffer(count):
        return pltpu.VMEM((count, height, width), low)

    return pl.pallas_call(
        functools.partial(finish_kernel, depth, heights, tile),
        out_shape=[
            jax.ShapeDtypeStruct((height, width), jnp.float32),
            jax.ShapeDtypeStruct((4, quarter, width), low),
            jax.ShapeDtypeStruct(small.shape, jnp.float32),
        ],
        in_specs=[ANY] * 4 + [vmem] * 2,
        out_specs=[vmem, ANY, vmem],
        scratch_shapes=[buffer(depth * 4), buffer(depth * 4), buffer(depth * 2)]
        + [buffer(depth)] * 3
        + [
            pltpu.VMEM((depth * 2,) + rows.shape, low),
            pltpu.VMEM((2, quarter, width), low),
            pltpu.VMEM((2, quarter, width), low),
            pltpu.VMEM((quarter, width), low),
            pltpu.VMEM((quarter, width), low),
            pltpu.VMEM((quarter, width), low),
            pltpu.VMEM((turns + 1,) + small.shape, jnp.float32),
            pltpu.VMEM((turns,) + small.shape, jnp.float32),
        ]
        + [dma((depth * 4, 3))] * 3
        + [dma((depth * 2,))] * 2
        + [dma((depth,))] * 6
        + [dma(())]
        + [dma((depth,))] * 3
        + [dma((depth * 2,))]
        + [dma((2,))] * 2
        + [dma(())] * 2
        + [dma((3,)), dma((4,))]
        + [dma((turns,))] * 2,
        compiler_params=pltpu.CompilerParams(
            collective_id=1, has_side_effects=True, vmem_limit_bytes=62 * 2**20
        ),
        name="finish",
    )(*pieces, rows, places, small)


def moments(gradient, first, second):
    first_new = beta_one * first + (1.0 - beta_one) * gradient
    second_new = beta_two * second + (1.0 - beta_two) * gradient * gradient
    direction = (
        first_new
        / (1.0 - beta_one**STEP)
        / (jnp.sqrt(second_new / (1.0 - beta_two**STEP)) + adam_eps)
    )
    return direction, first_new, second_new


def update_kernel(steps, cuts, *refs):
    table_ref, table_m_ref, table_v_ref, table_g_ref = refs[0:4]
    small_ref, sums_ref, gains_ref, gains_m_ref, gains_v_ref = refs[4:9]
    grad_ref, block_ref, block_m_ref, block_v_ref, bases_ref = refs[9:14]
    table_new, table_m_new, table_v_new, table_low = refs[14:18]
    values_ref, gains_new, gains_m_new, gains_v_new = refs[18:22]
    block_new, block_m_new, block_v_new, block_low = refs[22:26]
    bases, turned, factor_ref, bases_sem = refs[26:30]
    now = pl.program_id(0)

    def base(index):
        return pltpu.make_async_copy(bases_ref.at[index], bases.at[index], bases_sem.at[index])

    @pl.when(now == 0)
    def begin():
        for index in range(4):
            base(index).start()
        lines = lax.broadcasted_iota(jnp.int32, small_ref.shape, 0)
        lanes = lax.broadcasted_iota(jnp.int32, small_ref.shape, 1)

        def value_at(place):
            chosen = (lines == place // 128) & (lanes == place % 128)
            return jnp.sum(jnp.where(chosen, small_ref[...], 0.0), axis=(0, 1), keepdims=True)

        count = value_at(3 * D + 1)
        gain_grads = sums_ref[...] / count
        squares = value_at((small_ref.shape[0] - 1) * 128) / (count * count)
        norm = jnp.sqrt(squares + jnp.sum(gain_grads * gain_grads, axis=(0, 1), keepdims=True))
        clip = jnp.minimum(1.0, clip_norm / norm)
        factor_ref[...] = jnp.broadcast_to(clip / count, factor_ref.shape)
        spots = lax.broadcasted_iota(jnp.int32, values_ref.shape, 1)
        values_ref[...] = jnp.where(spots == 0, value_at(3 * D) / count, norm)
        direction, gains_m_new[...], gains_v_new[...] = moments(
            gain_grads * clip, gains_m_ref[...], gains_v_ref[...]
        )
        gains_new[...] = gains_ref[...] - rate_gain * direction

    factor = factor_ref[0:1, 0:1]
    direction, table_m_new[...], table_v_new[...] = moments(
        table_g_ref[...].astype(jnp.float32) * factor, table_m_ref[...], table_v_ref[...]
    )
    table_tile = table_ref[...]
    table_tile = table_tile - rate_table * (direction + decay_rate * table_tile)
    table_new[...] = table_tile
    table_low[...] = table_tile.astype(low)

    spots = lax.broadcasted_iota(jnp.int32, turned.shape, 1)

    def columns(index, value):
        mine = (spots >= cuts[index]) & (spots < cuts[index + 1])
        return jnp.where(mine, value, 0.0).astype(low)

    for index in range(4):

        @pl.when(now == min(2 + index, steps - 1))
        def rotate():
            base(index).wait()
            term = contract_rows(
                bases[index].astype(low), columns(index, grad_ref[...] * factor_ref[0:1, 0:1])
            )
            turned[...] = term if index == 0 else turned[...] + term

    @pl.when(now == min(6, steps - 1))
    def move():
        direction, block_m_new[...], block_v_new[...] = moments(
            turned[...], block_m_ref[...], block_v_ref[...]
        )
        turned[...] = direction
        block_new[...] = jnp.zeros_like(block_new)

    for index in range(4):

        @pl.when(now == min(7 + index, steps - 1))
        def rotate_back():
            block_new[...] += product(bases[index].astype(low), columns(index, turned[...]))

    @pl.when(now == min(11, steps - 1))
    def store():
        block = block_ref[...]
        block = block - rate_block * (block_new[...] + decay_rate * block)
        block_new[...] = block
        block_low[...] = block.astype(low)


def update(cuts, tables, table_grads, small, gain_sums, gains, block_grads, blocks, bases):
    rows, width = tables[0].shape
    tile = max(
        size
        for size in range(8, 201, 8)
        if rows % size == 0 and (size % 16 == 0 or rows % 16)
    )
    steps = rows // tile
    f32 = jnp.float32

    def whole(array):
        return pl.BlockSpec(array.shape, lambda i: (0,) * array.ndim)

    tiles = pl.BlockSpec((tile, width), lambda i: (i, 0))
    table = jax.ShapeDtypeStruct(tables[0].shape, f32)
    gain = jax.ShapeDtypeStruct(gains[0].shape, f32)
    matrix = jax.ShapeDtypeStruct(blocks[0].shape, f32)
    values = jax.ShapeDtypeStruct((8, 128), f32)
    outs = [table] * 3 + [jax.ShapeDtypeStruct(table.shape, low)]
    outs += [values] + [gain] * 3
    outs += [matrix] * 3 + [jax.ShapeDtypeStruct(matrix.shape, low)]
    return pl.pallas_call(
        functools.partial(update_kernel, steps, cuts),
        grid=(steps,),
        out_shape=outs,
        in_specs=[tiles] * 4
        + [whole(small), whole(gain_sums)]
        + [whole(gain)] * 3
        + [whole(matrix)] * 4
        + [ANY],
        out_specs=[tiles] * 4 + [whole(values)] + [whole(gain)] * 3 + [whole(matrix)] * 4,
        scratch_shapes=[
            pltpu.VMEM(bases.shape, f32),
            pltpu.VMEM(matrix.shape, f32),
            pltpu.VMEM((8, 128), f32),
            pltpu.SemaphoreType.DMA((4,)),
        ],
        compiler_params=pltpu.CompilerParams(vmem_limit_bytes=58 * 2**20),
        name="update",
    )(*tables, table_grads, small, gain_sums, *gains, block_grads, *blocks, bases)


def loss_kernel(hidden_ref, gain_ref, near_ref, far_ref, own_ref, other_ref, weight_ref, *refs):
    gradient_ref, gain_out, loss_ref, near_out, far_out, logits, teach = refs
    head = lax.axis_index("head")
    rows = hidden_ref.shape[0]
    half = rows // 2
    size = near_ref.shape[1]
    hidden = hidden_ref[...]
    r = lax.rsqrt(jnp.mean(hidden * hidden, axis=-1, keepdims=True) + eps_norm)
    normed = (hidden * r * gain_ref[...]).astype(low)
    parts = [(near_ref, near_out, 0, 0), (near_ref, near_out, 1, 2)]
    parts += [(far_ref, far_out, 0, 1), (far_ref, far_out, 1, 3)]
    for index, (source, unused, place, offset) in enumerate(parts):
        columns = pl.ds(pl.multiple_of((head ^ offset) * size, size), size)
        logits[index] = contract_cols(normed, source[place])
        teach[index, :half] = own_ref[:, columns].astype(jnp.float32)
        teach[index, half:] = other_ref[:, columns].astype(jnp.float32)

    def log_total(values):
        summit = jnp.max(jnp.max(values[...], axis=0), axis=-1, keepdims=True)
        return summit + jnp.log(
            jnp.sum(jnp.sum(jnp.exp(values[...] - summit[None]), axis=0), axis=-1, keepdims=True)
        )

    log_logits, log_teach = log_total(logits), log_total(teach)
    weighting = weight_ref[...]
    gradient = jnp.zeros((rows, hidden.shape[1]), jnp.float32)
    loss = jnp.zeros((rows, 1), jnp.float32)
    for index, (source, goal, place, offset) in enumerate(parts):
        log_prob = logits[index] - log_logits
        log_true = teach[index] - log_teach
        true = jnp.exp(log_true)
        loss = loss + jnp.sum(true * (log_true - log_prob), axis=-1, keepdims=True)
        d_logits = ((jnp.exp(log_prob) - true) * weighting).astype(low)
        goal[place] = contract_rows(d_logits, normed).astype(low)
        gradient = gradient + product(d_logits, source[place])
    loss_ref[...] = jnp.broadcast_to(
        jnp.sum(loss * weighting, axis=0, keepdims=True), loss_ref.shape
    )
    scaled = gradient * gain_ref[...]
    gradient_ref[...] = r * scaled - hidden * (r * r * r) * jnp.mean(
        hidden * scaled, axis=-1, keepdims=True
    )
    gain_out[...] = jnp.sum(gradient * hidden * r, axis=0, keepdims=True)


def distill(hidden, gain, near, far, own, other, weighting):
    rows, width = hidden.shape
    size = near.shape[1]
    vmem = pl.BlockSpec(memory_space=pltpu.VMEM)
    f32 = jnp.float32
    return pl.pallas_call(
        loss_kernel,
        out_shape=[
            jax.ShapeDtypeStruct(hidden.shape, f32),
            jax.ShapeDtypeStruct(gain.shape, f32),
            jax.ShapeDtypeStruct((8, 128), f32),
            jax.ShapeDtypeStruct(near.shape, low),
            jax.ShapeDtypeStruct(far.shape, low),
        ],
        in_specs=[vmem] * 7,
        out_specs=[vmem] * 5,
        scratch_shapes=[pltpu.VMEM((4, rows, size), f32)] * 2,
        compiler_params=pltpu.CompilerParams(vmem_limit_bytes=58 * 2**20),
        name="distill",
    )(hidden, gain, near, far, own, other, weighting)


def on_device(
    token_ids,
    lengths,
    valid,
    vocab_ids,
    teacher,
    block,
    block_m,
    block_v,
    bases,
    table,
    table_m,
    table_v,
    gains,
    gains_m,
    gains_v,
):
    dp_count, head_count = lax.axis_size("dp"), lax.axis_size("head")
    device_total = dp_count * head_count
    head, dp = lax.axis_index("head"), lax.axis_index("dp")
    batch = head // 2
    tokens = token_ids.shape[1]
    shard_rows = table.shape[0]
    offset = dp * shard_rows
    part = TOPV // device_total

    widths = [3 * D // device_total, D // device_total, 2 * FF // device_total, FF // device_total]
    cuts = [sum(widths[:index]) for index in range(5)]
    block_low = block.T.astype(low)
    attention, gate_up, down, rows_in, codes = start(
        [block_low[: cuts[2]], block_low[cuts[2] : cuts[3]], block_low[cuts[3] :]],
        table,
        (token_ids * 2 + valid).reshape(-1, 1, tokens),
        vocab_ids,
        dp_count,
    )
    codes = codes.reshape(dp_count, 2 * tokens)
    weighting = (lax.dynamic_index_in_dim(codes, dp, 0, keepdims=False) & 1).astype(jnp.float32)
    vocab = lax.dynamic_index_in_dim(
        vocab_ids.reshape(head_count, dp_count, part), head, 0, keepdims=False
    )
    local = jnp.concatenate([vocab, codes >> 1], axis=1) - offset
    owned = (local >= 0) & (local < shard_rows)
    weights = [
        attention[:, : cuts[1]].reshape(-1, D),
        attention[:, cuts[1] :].reshape(-1, D),
        gate_up.reshape(-1, D),
        down.reshape(-1, D),
    ]
    quarter = lax.all_gather(rows_in[:part], "dp", axis=0, tiled=True)
    near = jnp.stack([quarter, swap(quarter, head_count, 2)])
    far = swap(near, head_count, 1)
    hidden = rows_in[part:].astype(jnp.float32)

    teacher_own = lax.dynamic_index_in_dim(teacher, batch, 0, keepdims=False)
    teacher_far = swap(
        lax.dynamic_index_in_dim(teacher, 1 - batch, 0, keepdims=False), head_count, 2
    )

    run = jnp.arange(tokens, dtype=jnp.int32)
    places = jnp.concatenate([head * tokens + run, (head ^ 2) * tokens + run])
    places_far = jnp.concatenate([(head ^ 1) * tokens + run, (head ^ 3) * tokens + run])
    own_lengths = lax.dynamic_index_in_dim(lengths, batch, 0, keepdims=False)[0]
    segment, position = segments(own_lengths, places)
    segment_far, unused = segments(own_lengths, places_far)
    places_all = jnp.concatenate([places, places_far])
    segment_all = jnp.concatenate([segment, segment_far])
    allow = (segment[:, None] == segment_all[None, :]) & (places[:, None] >= places_all[None, :])
    freqs = jnp.exp(jnp.arange(0, HD, 2, dtype=jnp.float32) * (-math.log(10000.0) / HD))
    angle = position.astype(jnp.float32)[:, None] * freqs[None, :]
    angle = jnp.concatenate([angle, angle], axis=1)
    cosine, sine = jnp.cos(angle), jnp.sin(angle)

    saves = []
    for repeat in range(2):
        hidden, saved = layer_forward(hidden, weights, gains, cosine, sine, allow, head_count)
        saves.append(saved)

    gradient, d_gain_final, loss_sum, d_near, d_far = distill(
        hidden, gains[2:3], near, far, teacher_own, teacher_far, weighting[:, None]
    )
    d_gain_final, loss_sum = d_gain_final[0], loss_sum[0, 0]
    f32 = jnp.float32
    d_near = d_near.astype(f32) + swap(d_far, head_count, 1).astype(f32)
    d_near = d_near.astype(low)
    d_quarter = d_near[0].astype(f32) + swap(d_near[1], head_count, 2).astype(f32)
    chosen_grads = lax.psum_scatter(
        d_quarter.astype(low), "dp", scatter_dimension=0, tiled=True
    )

    block_grads = None
    d_gains = [0.0, 0.0]
    for repeat in range(2):
        gradient, layer_grads, d_gain_one, d_gain_two = layer_backward(
            gradient, weights, gains, saves[1 - repeat], cosine, sine, allow, head_count
        )
        d_gains = [d_gains[0] + d_gain_one, d_gains[1] + d_gain_two]
        if block_grads is None:
            block_grads = layer_grads
        else:
            block_grads = [total + extra for total, extra in zip(block_grads, layer_grads)]

    d_qkv, d_out, d_gu, d_down = [
        piece.astype(low).reshape(device_total, -1, D) for piece in block_grads
    ]
    rows_back = jnp.concatenate([chosen_grads, gradient.astype(low)], axis=0)
    step = 80 if shard_rows % 80 == 0 else 40
    quarter = -(-shard_rows // (step * head_count)) * step
    tile = quarter // 5 if quarter % 80 == 0 and quarter // 5 % 16 == 0 else step
    small = [d_gains[0], d_gains[1], d_gain_final, loss_sum[None], jnp.sum(weighting)[None]]
    small = jnp.pad(jnp.concatenate(small), (0, 6 * 128 - 2)).reshape(-1, 128)
    block_grads, table_grads, small = finish(
        [jnp.concatenate([d_qkv, d_out], axis=1), d_gu, d_down],
        rows_back,
        jnp.where(owned, local, -1).reshape(1, -1),
        small,
        quarter,
        tile,
    )
    outs = update(
        cuts,
        [table, table_m, table_v],
        table_grads.reshape(-1, D),
        small,
        small[: 3 * D // 128].reshape(3, D),
        [gains, gains_m, gains_v],
        block_grads.T,
        [block, block_m, block_v],
        bases,
    )
    table_new, table_m_new, table_v_new, table_low = outs[0:4]
    values, gains_new, gains_m_new, gains_v_new = outs[4:8]
    block_new, block_m_new, block_v_new, block_low = outs[8:12]
    return (
        values[0, 0],
        values[0, 1],
        block_new,
        block_m_new,
        block_v_new,
        table_new,
        table_m_new,
        table_v_new,
        gains_new,
        gains_m_new,
        gains_v_new,
        block_low,
        table_low,
    )


def solution(mesh):
    tokens = P(None, ("dp", "head"))
    columns = P(None, ("dp", "head"))
    table = P("dp", None)
    return jax.shard_map(
        on_device,
        mesh=mesh,
        in_specs=(
            tokens,
            P(None, "dp", None),
            tokens,
            P(),
            P(None, ("dp", "head"), None),
            columns,
            columns,
            columns,
            P(),
            table,
            table,
            table,
            P(),
            P(),
            P(),
        ),
        out_specs=(
            P(),
            P(),
            columns,
            columns,
            columns,
            table,
            table,
            table,
            P(),
            P(),
            P(),
            columns,
            table,
        ),
        check_vma=False,
    )
```

```python
import functools
import math

import jax
import jax.numpy as jnp
from jax import lax
from jax.experimental import pallas as pl
from jax.experimental.pallas import tpu as pltpu
from jax.sharding import PartitionSpec as P

D = 768
H = 12
HD = 64
FF = 3072
TOPV = 4096
STEP = 5

low = jnp.bfloat16
scale = HD**-0.5
eps_norm = 1e-05
clip_norm = 0.002
beta_one = 0.9
beta_two = 0.99
adam_eps = 1e-08
decay_rate = 0.1
rate_block = 0.03
rate_table = 0.05
rate_gain = 0.4


def product(left, right):
    return jnp.dot(left, right, preferred_element_type=jnp.float32)


def contract_rows(left, right):
    return lax.dot_general(
        left, right, (((0,), (0,)), ((), ())), preferred_element_type=jnp.float32
    )


def contract_cols(left, right):
    return lax.dot_general(
        left, right, (((1,), (1,)), ((), ())), preferred_element_type=jnp.float32
    )


def segments(lengths, places):
    segment = jnp.zeros_like(places)
    begin = jnp.zeros_like(places)
    end = jnp.zeros((), jnp.int32)
    for index in range(lengths.shape[0] - 1):
        end = end + lengths[index]
        past = places >= end
        segment = segment + past.astype(jnp.int32)
        begin = jnp.where(past, end, begin)
    return segment, places - begin


def swap(value, head_count, offset):
    return lax.ppermute(value, "head", [(h, h ^ offset) for h in range(head_count)])


MESH = pl.DeviceIdType.MESH
ANY = pl.BlockSpec(memory_space=pl.ANY)


def coordinates(depth):
    dp, head = lax.axis_index("dp"), lax.axis_index("head")
    return dp // 2, dp % 2, head // 2, head % 2


def device(z, x, y, c):
    return (z * 2 + x, y * 2 + c)


def slot(z, x, y, c):
    return ((z * 2 + x) * 2 + y) * 2 + c


def greet(depth, z, x, y, c):
    barrier = pltpu.get_barrier_semaphore()
    for target in (device(z, 1 - x, y, c), device(z, x, 1 - y, c), device(z, x, y, 1 - c)):
        pl.semaphore_signal(barrier, 1, device_id=target, device_id_type=MESH)

    @pl.when(z > 0)
    def below():
        pl.semaphore_signal(barrier, 1, device_id=device(z - 1, x, y, c), device_id_type=MESH)

    @pl.when(z < depth - 1)
    def above():
        pl.semaphore_signal(barrier, 1, device_id=device(z + 1, x, y, c), device_id_type=MESH)

    pl.semaphore_wait(barrier, 3 + jnp.where(z > 0, 1, 0) + jnp.where(z < depth - 1, 1, 0))


def start_kernel(depth, *refs):
    pieces = refs[0:3]
    table_ref, codes_ref, vocab_ref = refs[3:6]
    wholes = refs[6:9]
    sum_ref, ids_ref, near_ref, far_ref = refs[9:13]
    far_x, from_low, from_high, total, rows_ref, shard, ids = refs[13:20]
    local_sem, up_sem, down_sem, x_sem, y_sem, c_sem, block_sem = refs[20:27]
    rx_send, rx_recv, ru_send, ru_recv, rd_send, rd_recv = refs[27:33]
    id_send, id_recv, table_sem, copy_sem = refs[33:37]
    su_send, sd_send, sx_send, sy_send, sc_send, s_recv, keep_sem = refs[37:44]
    z, x, y, c = coordinates(depth)
    mine = slot(z, x, y, c)
    dp, head = z * 2 + x, y * 2 + c
    groups, height = rows_ref.shape[:2]
    shard_rows, tokens = table_ref.shape[0], codes_ref.shape[2]
    part = height - 2 * tokens
    offset = dp * shard_rows
    barrier = pltpu.get_barrier_semaphore()
    pl.semaphore_signal(barrier, 1, device_id=device(z, x, y, 1 - c), device_id_type=MESH)
    for group in range(groups):
        for rank in range(2):

            @pl.when((group != dp) | (rank != y))
            def hello():
                pl.semaphore_signal(
                    barrier, 1, device_id=(group, rank * 2 + c), device_id_type=MESH
                )

    pl.semaphore_wait(barrier, groups * 2)

    def tell(group, rank):
        second = jnp.where(rank == y, 0, 1)
        return pltpu.make_async_remote_copy(
            codes_ref.at[rank],
            ids_ref.at[dp, second],
            id_send.at[group, rank],
            id_recv.at[dp, second],
            device_id=(group, rank * 2 + c),
            device_id_type=MESH,
        )

    def told(group, second):
        return pltpu.make_async_remote_copy(
            codes_ref.at[0],
            ids_ref.at[group, second],
            id_send.at[group, second],
            id_recv.at[group, second],
            device_id=device(z, x, y, 1 - c),
            device_id_type=MESH,
        )

    keep = pltpu.make_async_copy(codes_ref.at[y], ids_ref.at[dp, 0], copy_sem)
    fetch = pltpu.make_async_copy(table_ref, shard.at[pl.ds(0, shard_rows)], table_sem)
    fetch.start()
    keep.start()
    for group in range(groups):
        for rank in range(2):

            @pl.when((group != dp) | (rank != y))
            def telling():
                tell(group, rank).start()

    def gather(group):
        def load(first, read):
            @pl.loop(0, (tokens if first else part) // 16)
            def some(index):
                base = index * 16
                lines = []
                for line in range(16):
                    place = read(base + line) - offset
                    held = (place >= 0) & (place < shard_rows)
                    lines.append(shard[pl.ds(jnp.where(held, place, shard_rows), 1)])
                rows_ref[group, pl.ds(pl.multiple_of(first + base, 16), 16)] = jnp.concatenate(
                    lines, axis=0
                ).astype(low)

        load(0, lambda index: vocab_ref[(head * groups + group) * part + index])
        for second in range(2):
            load(part + second * tokens, lambda index: ids[group, second, 0, index] >> 1)

    def own(block, piece, target, sem):
        return pltpu.make_async_remote_copy(
            pieces[piece],
            wholes[piece].at[block],
            sem.at[piece],
            block_sem.at[block, piece],
            device_id=target,
            device_id_type=MESH,
        )

    def onward(block, piece, target, sem):
        return pltpu.make_async_remote_copy(
            wholes[piece].at[block],
            wholes[piece].at[block],
            sem.at[piece],
            block_sem.at[block, piece],
            device_id=target,
            device_id_type=MESH,
        )

    def send(make, block, target, sem):
        for piece in range(3):
            make(block, piece, target, sem).start()

    def arrive(block):
        for piece in range(3):
            onward(block, piece, device(z, x, y, 1 - c), c_sem.at[0]).wait_recv()

    across_x, across_y, across_c = (
        device(z, 1 - x, y, c),
        device(z, x, 1 - y, c),
        device(z, x, y, 1 - c),
    )
    rows_x = [
        pltpu.make_async_remote_copy(
            rows_ref.at[goal * 2 + 1 - x],
            far_x.at[goal],
            rx_send.at[goal],
            rx_recv.at[goal],
            device_id=across_x,
            device_id_type=MESH,
        )
        for goal in range(depth)
    ]

    def rows_up(goal):
        return pltpu.make_async_remote_copy(
            total.at[goal],
            from_low.at[goal],
            ru_send.at[goal],
            ru_recv.at[goal],
            device_id=device(z + 1, x, y, c),
            device_id_type=MESH,
        )

    def rows_down(goal):
        return pltpu.make_async_remote_copy(
            total.at[goal],
            from_high.at[goal],
            rd_send.at[goal],
            rd_recv.at[goal],
            device_id=device(z - 1, x, y, c),
            device_id_type=MESH,
        )

    goals = [
        goal for pair in zip(range(depth // 2), range(depth - 1, 0, -1)) for goal in pair
    ]
    local = [
        pltpu.make_async_copy(pieces[piece], wholes[piece].at[mine], local_sem.at[piece])
        for piece in range(3)
    ]
    send(own, mine, across_y, y_sem.at[mine // 4])

    @pl.when(z < depth - 1)
    def first_up():
        send(own, mine, device(z + 1, x, y, c), up_sem.at[0])

    @pl.when(z > 0)
    def first_down():
        send(own, mine, device(z - 1, x, y, c), down_sem.at[0])

    send(own, mine, across_x, x_sem.at[z])
    send(own, mine, across_c, c_sem.at[mine // 2])
    for copy in local:
        copy.start()
    shard[pl.ds(shard_rows, 8)] = jnp.zeros((8, shard.shape[1]), jnp.float32)
    keep.wait()
    for group in range(groups):
        for second in range(2):

            @pl.when((group != dp) | (second != 0))
            def heard():
                told(group, second).wait_recv()

    to_scalars = pltpu.make_async_copy(ids_ref, ids, copy_sem)
    to_scalars.start()
    fetch.wait()
    to_scalars.wait()
    for goal in goals:
        gather(goal * 2 + 1 - x)
        rows_x[goal].start()
    nearer = list(goals)

    def spread(block, over_x):
        send(onward, block, across_y, y_sem.at[block // 4])
        if over_x:
            send(onward, block, across_x, x_sem.at[block // 8])
        send(onward, block, across_c, c_sem.at[block // 2])

    for step in range(1, depth):

        @pl.when(z - step >= 0)
        def risen():
            block = slot(z - step, x, y, c)
            arrive(block)

            @pl.when(z < depth - 1)
            def further():
                send(onward, block, device(z + 1, x, y, c), up_sem.at[step])

            spread(block, True)

        @pl.when(z + step < depth)
        def fallen():
            block = slot(z + step, x, y, c)
            arrive(block)

            @pl.when(z > 0)
            def further():
                send(onward, block, device(z - 1, x, y, c), down_sem.at[step])

            spread(block, True)

        for goal in nearer[:2]:
            gather(goal * 2 + x)
        nearer = nearer[2:]

    for goal in goals:
        rows_x[goal].wait_recv()
        both = rows_ref[goal * 2 + x] + far_x[goal]

        @pl.when(goal > z)
        def rising():
            @pl.when(z > 0)
            def more():
                rows_up(goal).wait_recv()
                total[goal] = both + from_low[goal]

            @pl.when(z == 0)
            def alone():
                total[goal] = both

            rows_up(goal).start()

        @pl.when(goal < z)
        def falling():
            @pl.when(z < depth - 1)
            def more():
                rows_down(goal).wait_recv()
                total[goal] = both + from_high[goal]

            @pl.when(z == depth - 1)
            def alone():
                total[goal] = both

            rows_down(goal).start()

        @pl.when(goal == z)
        def here():
            total[goal] = both

    for step in range(depth):
        for sign in (1, -1) if step else (1,):

            @pl.when((z + sign * step >= 0) & (z + sign * step < depth))
            def crossed():
                block = slot(z + sign * step, 1 - x, y, c)
                arrive(block)
                spread(block, False)

    for goal in range(depth):

        @pl.when(goal == z)
        def landed():
            @pl.when(z > 0)
            def low_part():
                rows_up(goal).wait_recv()
                total[goal] = total[goal] + from_low[goal]

            @pl.when(z < depth - 1)
            def high_part():
                rows_down(goal).wait_recv()
                total[goal] = total[goal] + from_high[goal]

            sum_ref[...] = total[goal]

    def shared(source, ref, quarter, group, send_sem, target):
        where = ref.at[quarter, group]
        return pltpu.make_async_remote_copy(
            where if source is None else source,
            where,
            send_sem,
            s_recv.at[quarter if ref is near_ref else 2 + quarter, group],
            device_id=target,
            device_id_type=MESH,
        )

    own_shared = sum_ref.at[pl.ds(0, part)]
    keep_shared = pltpu.make_async_copy(own_shared, near_ref.at[0, dp], keep_sem)
    keep_shared.start()

    def plane(group):
        return near_ref.at[0, group]

    def shared_y(source, group):
        return pltpu.make_async_remote_copy(
            source,
            near_ref.at[1, group],
            sy_send.at[group],
            s_recv.at[1, group],
            device_id=across_y,
            device_id_type=MESH,
        )

    def shared_c(source, quarter, group):
        return pltpu.make_async_remote_copy(
            source,
            far_ref.at[quarter, group],
            sc_send.at[quarter, group],
            s_recv.at[2 + quarter, group],
            device_id=across_c,
            device_id_type=MESH,
        )

    @pl.when(z < depth - 1)
    def shared_up():
        shared(own_shared, near_ref, 0, dp, su_send.at[0], device(z + 1, x, y, c)).start()

    @pl.when(z > 0)
    def shared_down():
        shared(own_shared, near_ref, 0, dp, sd_send.at[0], device(z - 1, x, y, c)).start()

    shared(own_shared, near_ref, 0, dp, sx_send.at[z], across_x).start()
    shared_y(own_shared, dp).start()
    shared_c(own_shared, 0, dp).start()
    for step in range(1, depth):

        @pl.when(z - step >= 0)
        def shared_risen():
            group = (z - step) * 2 + x
            copy = shared(
                None, near_ref, 0, group, su_send.at[step], device(z + 1, x, y, c)
            )
            copy.wait_recv()

            @pl.when(z < depth - 1)
            def further():
                copy.start()

            shared(None, near_ref, 0, group, sx_send.at[z - step], across_x).start()
            shared_y(plane(group), group).start()
            shared_c(plane(group), 0, group).start()

        @pl.when(z + step < depth)
        def shared_fallen():
            group = (z + step) * 2 + x
            copy = shared(
                None, near_ref, 0, group, sd_send.at[step], device(z - 1, x, y, c)
            )
            copy.wait_recv()

            @pl.when(z > 0)
            def further():
                copy.start()

            shared(None, near_ref, 0, group, sx_send.at[z + step], across_x).start()
            shared_y(plane(group), group).start()
            shared_c(plane(group), 0, group).start()

    for place in range(depth):
        group = place * 2 + 1 - x
        shared(None, near_ref, 0, group, sx_send.at[place], across_x).wait_recv()
        shared_y(plane(group), group).start()
        shared_c(plane(group), 0, group).start()

    for step in range(depth):
        for sign in (1, -1) if step else (1,):

            @pl.when((z + sign * step >= 0) & (z + sign * step < depth))
            def crossed():
                for side in (x, 1 - x):
                    block = slot(z + sign * step, side, 1 - y, c)
                    arrive(block)
                    send(onward, block, across_c, c_sem.at[block // 2])

    for group in range(groups):
        shared_y(plane(group), group).wait_recv()
        shared_c(near_ref.at[1, group], 1, group).start()

    for block in range(depth * 8):

        @pl.when(block % 2 != c)
        def from_core():
            arrive(block)

    for group in range(groups):
        for quarter in range(2):
            shared_c(near_ref.at[quarter, group], quarter, group).wait_recv()

    keep_shared.wait()
    for group in range(groups):
        shared_y(plane(group), group).wait_send()
        for quarter in range(2):
            shared_c(near_ref.at[quarter, group], quarter, group).wait_send()
    for place in range(depth):
        shared(None, near_ref, 0, dp, sx_send.at[place], across_x).wait_send()

        @pl.when((z - place >= 0) & (z < depth - 1))
        def shared_rose():
            shared(None, near_ref, 0, dp, su_send.at[place], across_x).wait_send()

        @pl.when((z + place < depth) & (z > 0))
        def shared_fell():
            shared(None, near_ref, 0, dp, sd_send.at[place], across_x).wait_send()

    for copy in local:
        copy.wait()
    for group in range(groups):
        for rank in range(2):

            @pl.when((group != dp) | (rank != y))
            def spoken():
                tell(group, rank).wait_send()

    for goal in range(depth):
        rows_x[goal].wait_send()

        @pl.when(goal > z)
        def rose():
            rows_up(goal).wait_send()

        @pl.when(goal < z)
        def fell():
            rows_down(goal).wait_send()

    def sent(block, target, sem):
        for piece in range(3):
            onward(block, piece, target, sem).wait_send()

    for step in range(depth):

        @pl.when((z - step >= 0) & (z < depth - 1))
        def rose():
            sent(mine, device(z + 1, x, y, c), up_sem.at[step])

        @pl.when((z + step < depth) & (z > 0))
        def fell():
            sent(mine, device(z - 1, x, y, c), down_sem.at[step])

        sent(mine, across_x, x_sem.at[step])
    for index in range(depth * 2):
        sent(mine, across_y, y_sem.at[index])
    for index in range(depth * 4):
        sent(mine, across_c, c_sem.at[index])


def start(pieces, table, codes, vocab_ids, groups):
    width = table.shape[1]
    height = vocab_ids.shape[0] // (groups * 4) + 2 * codes.shape[2]
    depth = groups // 2
    blocks = depth * 8
    told = (groups, 2, 1, codes.shape[2])
    dma = pltpu.SemaphoreType.DMA
    buffer = pltpu.VMEM((depth, height, width), low)
    return pl.pallas_call(
        functools.partial(start_kernel, depth),
        out_shape=[jax.ShapeDtypeStruct((blocks,) + piece.shape, low) for piece in pieces]
        + [jax.ShapeDtypeStruct((height, width), low), jax.ShapeDtypeStruct(told, jnp.int32)]
        + [jax.ShapeDtypeStruct((2, groups, vocab_ids.shape[0] // blocks, width), low)] * 2,
        in_specs=[ANY] * 4
        + [pl.BlockSpec(memory_space=pltpu.VMEM), pl.BlockSpec(memory_space=pltpu.SMEM)],
        out_specs=[ANY] * 3 + [pl.BlockSpec(memory_space=pltpu.VMEM)] * 2 + [ANY] * 2,
        scratch_shapes=[buffer] * 4
        + [
            pltpu.VMEM((groups, height, width), low),
            pltpu.VMEM((table.shape[0] + 8, width), jnp.float32),
            pltpu.SMEM(told, jnp.int32),
        ]
        + [dma((3,))]
        + [dma((depth, 3))] * 3
        + [dma((depth * 2, 3)), dma((depth * 4, 3)), dma((blocks, 3))]
        + [dma((depth,))] * 6
        + [dma((groups, 2))] * 2
        + [dma(())] * 2
        + [dma((depth,))] * 3
        + [dma((groups,)), dma((2, groups)), dma((4, groups)), dma(())],
        compiler_params=pltpu.CompilerParams(
            collective_id=0, has_side_effects=True, vmem_limit_bytes=58 * 2**20
        ),
        name="start",
    )(*pieces, table, codes, vocab_ids)


def by_distance(depth, z, act):
    for step in range(depth - 1, -1, -1):
        for sign in (1, -1) if step else (1,):

            @pl.when((z + sign * step >= 0) & (z + sign * step < depth))
            def reached():
                act(z + sign * step)


def add_into(total, block, *terms):
    height = total.shape[1]
    chunk = 96 if height % 96 == 0 else height

    @pl.loop(0, height // chunk)
    def chunks(index):
        part = pl.ds(pl.multiple_of(index * chunk, chunk), chunk)
        value = total[block, part].astype(jnp.float32)
        for buffer, place in terms:
            value = value + buffer[place, part].astype(jnp.float32)
        total[block, part] = value.astype(low)


def finish_kernel(depth, heights, tile, *refs):
    pieces = refs[0:3]
    rows_ref, places_ref, small_ref = refs[3:6]
    grad_ref, table_out, small_out = refs[6:9]
    total, far_c, far_p, far_s, from_low, from_high = refs[9:15]
    rows, given, far_t, part, mine, far_part, small, far_small = refs[15:23]
    local_sem, c_send, c_recv, p_send, p_recv, s_send, s_recv = refs[23:30]
    u_send, u_recv, d_send, d_recv = refs[30:34]
    own_sem, ru_send, rd_send, rx_send, r_recv = refs[34:39]
    t_send, t_recv, ty_send, ty_recv, o_send, o_recv, e_send, e_recv = refs[39:47]
    z, x, y, c = coordinates(depth)
    dp = z * 2 + x
    firsts = [sum(heights[:index]) for index in range(3)]
    up, down = device(z + 1, x, y, c), device(z - 1, x, y, c)
    across_x, across_y, across_c = (
        device(z, 1 - x, y, c),
        device(z, x, 1 - y, c),
        device(z, x, y, 1 - c),
    )
    even = c == 0
    across_p = tuple(jnp.where(even, a, b) for a, b in zip(across_y, across_x))
    across_s = tuple(jnp.where(even, b, a) for a, b in zip(across_y, across_x))
    own_p, own_s = jnp.where(even, y, x), jnp.where(even, x, y)
    partners = [across_c, across_y, across_x]
    reach = 1
    while reach < depth:
        partners.append(device(z ^ reach, x, y, c))
        reach = reach * 2

    barrier = pltpu.get_barrier_semaphore()
    for target in partners[:3] + partners[4:]:
        pl.semaphore_signal(barrier, 1, device_id=target, device_id_type=MESH)

    @pl.when(z > 0)
    def below():
        pl.semaphore_signal(barrier, 1, device_id=down, device_id_type=MESH)

    @pl.when(z < depth - 1)
    def above():
        pl.semaphore_signal(barrier, 1, device_id=up, device_id_type=MESH)

    pl.semaphore_wait(
        barrier, len(partners) - 1 + jnp.where(z > 0, 1, 0) + jnp.where(z < depth - 1, 1, 0)
    )

    def remote(source, goal, send_sem, recv_sem, target):
        return pltpu.make_async_remote_copy(
            source, goal, send_sem, recv_sem, device_id=target, device_id_type=MESH
        )

    def block_of(place, s, p):
        return place * 4 + jnp.where(even, s * 2 + p, p * 2 + s)

    def local(block, piece):
        return pltpu.make_async_copy(
            pieces[piece].at[block * 2 + c],
            total.at[block, pl.ds(firsts[piece], heights[piece])],
            local_sem.at[block, piece],
        )

    def over_c(block, piece):
        return remote(
            pieces[piece].at[block * 2 + 1 - c],
            far_c.at[block, pl.ds(firsts[piece], heights[piece])],
            c_send.at[block, piece],
            c_recv.at[block, piece],
            across_c,
        )

    def over_p(place, s):
        pair = place * 2 + s
        return remote(
            total.at[block_of(place, s, 1 - own_p)],
            far_p.at[pair],
            p_send.at[pair],
            p_recv.at[pair],
            across_p,
        )

    def over_s(place):
        return remote(
            total.at[block_of(place, 1 - own_s, own_p)],
            far_s.at[place],
            s_send.at[place],
            s_recv.at[place],
            across_s,
        )

    def rise(place):
        block = block_of(place, own_s, own_p)
        return remote(
            total.at[block], from_low.at[place], u_send.at[place], u_recv.at[place], up
        )

    def fall(place):
        block = block_of(place, own_s, own_p)
        return remote(
            total.at[block], from_high.at[place], d_send.at[place], d_recv.at[place], down
        )

    def own_rows(send_sem, target):
        return remote(rows_ref, rows.at[dp], send_sem, r_recv.at[dp], target)

    def rows_on(place, send_sem, target):
        there = place * 2 + x
        return remote(rows.at[there], rows.at[there], send_sem, r_recv.at[there], target)

    own = pltpu.make_async_copy(rows_ref, rows.at[dp], own_sem)
    own.start()

    @pl.when(z < depth - 1)
    def first_up():
        own_rows(ru_send.at[0], up).start()

    @pl.when(z > 0)
    def first_down():
        own_rows(rd_send.at[0], down).start()

    own_rows(rx_send.at[z], across_x).start()

    for turn in range(2):
        for s, s_there in ((1 - own_s, 1 - own_p), (own_s, own_p)):
            p, p_there = (1 - own_p, 1 - own_s) if turn == 0 else (own_p, own_s)

            def launch(place):
                for piece in range(3):
                    over_c(
                        place * 4 + jnp.where(even, p_there * 2 + s_there, s_there * 2 + p_there),
                        piece,
                    ).start()
                    local(block_of(place, s, p), piece).start()

            by_distance(depth, z, launch)

    def ready(block):
        for piece in range(3):
            local(block, piece).wait()
            over_c(block, piece).wait_recv()

    def give_p():
        for s in (1 - own_s, own_s):

            def give(place):
                block = block_of(place, s, 1 - own_p)
                ready(block)
                add_into(total, block, (far_c, block))
                over_p(place, s).start()

            by_distance(depth, z, give)

    @pl.when(even)
    def early():
        give_p()

    for step in range(1, depth):

        @pl.when(z - step >= 0)
        def risen():
            rows_on(z - step, ru_send.at[step], up).wait_recv()

            @pl.when(z < depth - 1)
            def further():
                rows_on(z - step, ru_send.at[step], up).start()

            rows_on(z - step, rx_send.at[z - step], across_x).start()

        @pl.when(z + step < depth)
        def fallen():
            rows_on(z + step, rd_send.at[step], down).wait_recv()

            @pl.when(z > 0)
            def further():
                rows_on(z + step, rd_send.at[step], down).start()

            rows_on(z + step, rx_send.at[z + step], across_x).start()

    @pl.when(c == 1)
    def late():
        give_p()

    own.wait()
    for place in range(depth):
        there = place * 2 + 1 - x
        remote(
            rows.at[there], rows.at[there], rx_send.at[place], r_recv.at[there], across_x
        ).wait_recv()

    height = part.shape[0]
    count = places_ref.shape[1]

    def collect(rank, core, goal):
        @pl.loop(0, height // tile)
        def tiles(index):
            first = index * tile
            at = (
                (rank * 2 + core) * height
                + first
                + lax.broadcasted_iota(jnp.int32, (tile, count), 0)
            )
            picked = jnp.where(at == places_ref[...], 1.0, 0.0).astype(low)
            goal[pl.ds(pl.multiple_of(first, tile), tile)] = product(
                picked, rows[...].reshape(count, rows.shape[2])
            ).astype(low)

    def over_t(rank):
        index = jnp.where(rank == y, 1, 0)
        return remote(
            given.at[index], far_t.at[index], t_send.at[index], t_recv.at[index], across_c
        )

    chunk = 80 if height % 80 == 0 else height

    def pieces_of(act):
        @pl.loop(0, height // chunk)
        def step(index):
            act(pl.ds(pl.multiple_of(index * chunk, chunk), chunk))

    collect(1 - y, 1 - c, given.at[0])
    over_t(1 - y).start()
    collect(y, 1 - c, given.at[1])
    over_t(y).start()
    collect(1 - y, c, part)
    over_t(1 - y).wait_recv()

    def first_sum(lines):
        part[lines] = (part[lines].astype(jnp.float32) + far_t[0, lines].astype(jnp.float32)).astype(
            low
        )

    pieces_of(first_sum)
    over_part = remote(part, far_part, ty_send, ty_recv, across_y)
    over_part.start()
    collect(y, c, mine)

    def give_s(place):
        block = block_of(place, 1 - own_s, own_p)
        ready(block)
        over_p(place, 1 - own_s).wait_recv()
        add_into(total, block, (far_c, block), (far_p, place * 2 + 1 - own_s))
        over_s(place).start()

    by_distance(depth, z, give_s)

    over_t(y).wait_recv()
    over_part.wait_recv()

    def second_sum(index, squares):
        lines = pl.ds(pl.multiple_of(index * chunk, chunk), chunk)
        value = (
            mine[lines].astype(jnp.float32)
            + far_t[1, lines].astype(jnp.float32)
            + far_part[lines].astype(jnp.float32)
        ).astype(low)
        mine[lines] = value
        value = value.astype(jnp.float32)
        return squares + jnp.sum((value * value).reshape(-1, 8, value.shape[1]), axis=0)

    squares = lax.fori_loop(
        0, height // chunk, second_sum, jnp.zeros((8, part.shape[1]), jnp.float32)
    )

    def out_mine(index, target):
        where = table_out.at[y * 2 + c]
        return remote(mine, where, o_send.at[index], o_recv.at[y * 2 + c], target)

    def out(rank, core):
        where = table_out.at[rank * 2 + core]
        return remote(where, where, o_send.at[2], o_recv.at[rank * 2 + core], across_c)

    keep = pltpu.make_async_copy(mine, table_out.at[y * 2 + c], own_sem)
    out_mine(0, across_y).start()
    out_mine(1, across_c).start()
    keep.start()

    def give_z(place):
        block = block_of(place, own_s, own_p)
        ready(block)
        over_p(place, own_s).wait_recv()
        over_s(place).wait_recv()
        add_into(total, block, (far_c, block), (far_p, place * 2 + own_s), (far_s, place))

        @pl.when(place > z)
        def rising():
            @pl.when(z > 0)
            def more():
                rise(place).wait_recv()
                add_into(total, block, (from_low, place))

            rise(place).start()

        @pl.when(place < z)
        def falling():
            @pl.when(z < depth - 1)
            def more():
                fall(place).wait_recv()
                add_into(total, block, (from_high, place))

            fall(place).start()

    by_distance(depth, z, give_z)
    grad_ref[...] = total[block_of(z, own_s, own_p)].astype(jnp.float32)

    @pl.when(z > 0)
    def low_part():
        rise(z).wait_recv()
        grad_ref[...] = grad_ref[...] + from_low[z].astype(jnp.float32)

    @pl.when(z < depth - 1)
    def high_part():
        fall(z).wait_recv()
        grad_ref[...] = grad_ref[...] + from_high[z].astype(jnp.float32)

    lines = lax.broadcasted_iota(jnp.int32, small.shape[1:], 0)
    lanes = lax.broadcasted_iota(jnp.int32, small.shape[1:], 1)
    last = (lines == small.shape[1] - 1) & (lanes == 0)
    grad_squares = jnp.sum(grad_ref[...] * grad_ref[...])
    small[0] = small_ref[...] + jnp.where(last, jnp.sum(squares) + grad_squares, 0.0)

    def exchange(turn):
        return remote(
            small.at[turn], far_small.at[turn], e_send.at[turn], e_recv.at[turn], partners[turn]
        )

    for turn in range(len(partners)):
        exchange(turn).start()
        exchange(turn).wait_recv()
        small[turn + 1] = small[turn] + far_small[turn]
    small_out[...] = small[len(partners)]
    out(1 - y, c).wait_recv()
    out(1 - y, c).start()
    out(y, 1 - c).wait_recv()
    out(1 - y, 1 - c).wait_recv()

    keep.wait()
    out_mine(0, across_y).wait_send()
    out_mine(1, across_c).wait_send()
    out(1 - y, c).wait_send()
    over_part.wait_send()
    for turn in range(len(partners)):
        exchange(turn).wait_send()
    for rank in range(2):
        over_t(rank).wait_send()
    for place in range(depth):
        rows_on(place, rx_send.at[place], across_x).wait_send()
        over_s(place).wait_send()
        for side in range(2):
            over_p(place, side).wait_send()
            for rank in range(2):
                for piece in range(3):
                    over_c((place * 2 + side) * 2 + rank, piece).wait_send()

        @pl.when(place > z)
        def rose():
            rise(place).wait_send()

        @pl.when(place < z)
        def fell():
            fall(place).wait_send()

        @pl.when((z - place >= 0) & (z < depth - 1))
        def rows_rose():
            rows_on(z, ru_send.at[place], up).wait_send()

        @pl.when((z + place < depth) & (z > 0))
        def rows_fell():
            rows_on(z, rd_send.at[place], down).wait_send()


def finish(pieces, rows, places, small, quarter, tile):
    blocks = pieces[0].shape[0]
    heights = [piece.shape[1] for piece in pieces]
    height, width = sum(heights), pieces[0].shape[2]
    depth = blocks // 8
    turns = 3 + (depth - 1).bit_length()
    dma = pltpu.SemaphoreType.DMA
    vmem = pl.BlockSpec(memory_space=pltpu.VMEM)

    def buffer(count):
        return pltpu.VMEM((count, height, width), low)

    return pl.pallas_call(
        functools.partial(finish_kernel, depth, heights, tile),
        out_shape=[
            jax.ShapeDtypeStruct((height, width), jnp.float32),
            jax.ShapeDtypeStruct((4, quarter, width), low),
            jax.ShapeDtypeStruct(small.shape, jnp.float32),
        ],
        in_specs=[ANY] * 4 + [vmem] * 2,
        out_specs=[vmem, ANY, vmem],
        scratch_shapes=[buffer(depth * 4), buffer(depth * 4), buffer(depth * 2)]
        + [buffer(depth)] * 3
        + [
            pltpu.VMEM((depth * 2,) + rows.shape, low),
            pltpu.VMEM((2, quarter, width), low),
            pltpu.VMEM((2, quarter, width), low),
            pltpu.VMEM((quarter, width), low),
            pltpu.VMEM((quarter, width), low),
            pltpu.VMEM((quarter, width), low),
            pltpu.VMEM((turns + 1,) + small.shape, jnp.float32),
            pltpu.VMEM((turns,) + small.shape, jnp.float32),
        ]
        + [dma((depth * 4, 3))] * 3
        + [dma((depth * 2,))] * 2
        + [dma((depth,))] * 6
        + [dma(())]
        + [dma((depth,))] * 3
        + [dma((depth * 2,))]
        + [dma((2,))] * 2
        + [dma(())] * 2
        + [dma((3,)), dma((4,))]
        + [dma((turns,))] * 2,
        compiler_params=pltpu.CompilerParams(
            collective_id=1, has_side_effects=True, vmem_limit_bytes=62 * 2**20
        ),
        name="finish",
    )(*pieces, rows, places, small)


def moments(gradient, first, second):
    first_new = beta_one * first + (1.0 - beta_one) * gradient
    second_new = beta_two * second + (1.0 - beta_two) * gradient * gradient
    direction = (
        first_new
        / (1.0 - beta_one**STEP)
        / (jnp.sqrt(second_new / (1.0 - beta_two**STEP)) + adam_eps)
    )
    return direction, first_new, second_new


def update_kernel(steps, cuts, *refs):
    table_ref, table_m_ref, table_v_ref, table_g_ref = refs[0:4]
    small_ref, sums_ref, gains_ref, gains_m_ref, gains_v_ref = refs[4:9]
    grad_ref, block_ref, block_m_ref, block_v_ref, bases_ref = refs[9:14]
    table_new, table_m_new, table_v_new, table_low = refs[14:18]
    values_ref, gains_new, gains_m_new, gains_v_new = refs[18:22]
    block_new, block_m_new, block_v_new, block_low = refs[22:26]
    bases, turned, factor_ref, bases_sem = refs[26:30]
    now = pl.program_id(0)

    def base(index):
        return pltpu.make_async_copy(bases_ref.at[index], bases.at[index], bases_sem.at[index])

    @pl.when(now == 0)
    def begin():
        for index in range(4):
            base(index).start()
        lines = lax.broadcasted_iota(jnp.int32, small_ref.shape, 0)
        lanes = lax.broadcasted_iota(jnp.int32, small_ref.shape, 1)

        def value_at(place):
            chosen = (lines == place // 128) & (lanes == place % 128)
            return jnp.sum(jnp.where(chosen, small_ref[...], 0.0), axis=(0, 1), keepdims=True)

        count = value_at(3 * D + 1)
        gain_grads = sums_ref[...] / count
        squares = value_at((small_ref.shape[0] - 1) * 128) / (count * count)
        norm = jnp.sqrt(squares + jnp.sum(gain_grads * gain_grads, axis=(0, 1), keepdims=True))
        clip = jnp.minimum(1.0, clip_norm / norm)
        factor_ref[...] = jnp.broadcast_to(clip / count, factor_ref.shape)
        spots = lax.broadcasted_iota(jnp.int32, values_ref.shape, 1)
        values_ref[...] = jnp.where(spots == 0, value_at(3 * D) / count, norm)
        direction, gains_m_new[...], gains_v_new[...] = moments(
            gain_grads * clip, gains_m_ref[...], gains_v_ref[...]
        )
        gains_new[...] = gains_ref[...] - rate_gain * direction

    factor = factor_ref[0:1, 0:1]
    direction, table_m_new[...], table_v_new[...] = moments(
        table_g_ref[...].astype(jnp.float32) * factor, table_m_ref[...], table_v_ref[...]
    )
    table_tile = table_ref[...]
    table_tile = table_tile - rate_table * (direction + decay_rate * table_tile)
    table_new[...] = table_tile
    table_low[...] = table_tile.astype(low)

    spots = lax.broadcasted_iota(jnp.int32, turned.shape, 1)

    def columns(index, value):
        mine = (spots >= cuts[index]) & (spots < cuts[index + 1])
        return jnp.where(mine, value, 0.0).astype(low)

    for index in range(4):

        @pl.when(now == min(2 + index, steps - 1))
        def rotate():
            base(index).wait()
            term = contract_rows(
                bases[index].astype(low), columns(index, grad_ref[...] * factor_ref[0:1, 0:1])
            )
            turned[...] = term if index == 0 else turned[...] + term

    @pl.when(now == min(6, steps - 1))
    def move():
        direction, block_m_new[...], block_v_new[...] = moments(
            turned[...], block_m_ref[...], block_v_ref[...]
        )
        turned[...] = direction
        block_new[...] = jnp.zeros_like(block_new)

    for index in range(4):

        @pl.when(now == min(7 + index, steps - 1))
        def rotate_back():
            block_new[...] += product(bases[index].astype(low), columns(index, turned[...]))

    @pl.when(now == min(11, steps - 1))
    def store():
        block = block_ref[...]
        block = block - rate_block * (block_new[...] + decay_rate * block)
        block_new[...] = block
        block_low[...] = block.astype(low)


def update(cuts, tables, table_grads, small, gain_sums, gains, block_grads, blocks, bases):
    rows, width = tables[0].shape
    tile = max(
        size
        for size in range(8, 201, 8)
        if rows % size == 0 and (size % 16 == 0 or rows % 16)
    )
    steps = rows // tile
    f32 = jnp.float32

    def whole(array):
        return pl.BlockSpec(array.shape, lambda i: (0,) * array.ndim)

    tiles = pl.BlockSpec((tile, width), lambda i: (i, 0))
    table = jax.ShapeDtypeStruct(tables[0].shape, f32)
    gain = jax.ShapeDtypeStruct(gains[0].shape, f32)
    matrix = jax.ShapeDtypeStruct(blocks[0].shape, f32)
    values = jax.ShapeDtypeStruct((8, 128), f32)
    outs = [table] * 3 + [jax.ShapeDtypeStruct(table.shape, low)]
    outs += [values] + [gain] * 3
    outs += [matrix] * 3 + [jax.ShapeDtypeStruct(matrix.shape, low)]
    return pl.pallas_call(
        functools.partial(update_kernel, steps, cuts),
        grid=(steps,),
        out_shape=outs,
        in_specs=[tiles] * 4
        + [whole(small), whole(gain_sums)]
        + [whole(gain)] * 3
        + [whole(matrix)] * 4
        + [ANY],
        out_specs=[tiles] * 4 + [whole(values)] + [whole(gain)] * 3 + [whole(matrix)] * 4,
        scratch_shapes=[
            pltpu.VMEM(bases.shape, f32),
            pltpu.VMEM(matrix.shape, f32),
            pltpu.VMEM((8, 128), f32),
            pltpu.SemaphoreType.DMA((4,)),
        ],
        compiler_params=pltpu.CompilerParams(vmem_limit_bytes=58 * 2**20),
        name="update",
    )(*tables, table_grads, small, gain_sums, *gains, block_grads, *blocks, bases)


NONE = pl.CostEstimate(flops=0, bytes_accessed=0, transcendentals=0)
LARGE = 58 * 2**20
CHUNK = 512


def inverse_rms(value):
    return lax.rsqrt(jnp.mean(value * value, axis=-1, keepdims=True) + eps_norm)


def norm_back(value, r, gain, grad):
    scaled = grad * gain
    d_value = r * scaled - value * (r * r * r) * jnp.mean(value * scaled, axis=-1, keepdims=True)
    return d_value, jnp.sum(grad * value * r, axis=0, keepdims=True)


def local_call(kernel, name, outs, args, scratch=(), remain=()):
    vmem = pl.BlockSpec(memory_space=pltpu.VMEM)
    return pl.pallas_call(
        kernel,
        out_shape=[jax.ShapeDtypeStruct(shape, kind) for shape, kind in outs],
        in_specs=[ANY if place in remain else vmem for place in range(len(args))],
        out_specs=[vmem] * len(outs),
        scratch_shapes=list(scratch),
        compiler_params=pltpu.CompilerParams(vmem_limit_bytes=LARGE),
        cost_estimate=NONE,
        name=name,
    )(*args)


def project_kernel(hidden_ref, gain_ref, weight_ref, cosine_ref, sine_ref, *refs):
    normed_ref, query_ref, own_ref = refs
    hidden = hidden_ref[...]
    normed = (hidden * inverse_rms(hidden) * gain_ref[...]).astype(low)
    normed_ref[...] = normed
    cosine, sine = cosine_ref[...], sine_ref[...]
    first = lax.broadcasted_iota(jnp.int32, cosine.shape, 1) % HD < HD // 2
    for index in range(3 * D // 128):
        columns = pl.ds(index * 128, 128)
        value = contract_cols(normed, weight_ref[columns])
        if index < 2 * D // 128:
            turned = jnp.where(
                first, -pltpu.roll(value, 128 - HD // 2, 1), pltpu.roll(value, HD // 2, 1)
            )
            value = value * cosine + turned * sine
        if index < D // 128:
            query_ref[:, columns] = value.astype(low)
        else:
            own_ref[:, pl.ds(index * 128 - D, 128)] = value.astype(low)


def project(hidden, gain, weight, cosine, sine):
    rows = hidden.shape[0]
    outs = [((rows, D), low), ((rows, D), low), ((rows, 2 * D), low)]
    return local_call(project_kernel, "project", outs, [hidden, gain, weight, cosine, sine])


def allowed(rows_ref, columns_ref):
    return (rows_ref[:, 0:1] == columns_ref[0:1]) & (rows_ref[:, 1:2] >= columns_ref[1:2])


def pair_of_heads(index):
    return pl.ds(index * 128, 128)


def attention_weight(query, keys, allow):
    score = jnp.where(allow, contract_cols(query, keys) * scale, -1e30)
    power = jnp.exp(score - jnp.max(score, axis=-1, keepdims=True))
    return power * (1.0 / jnp.sum(power, axis=-1, keepdims=True))


def forward_kernel(hidden_ref, query_ref, own_ref, far_ref, rows_ref, columns_ref, *refs):
    out_weight, gain_ref, gate_hbm, down_hbm, output_ref, merged_ref, middle_ref = refs[:7]
    gates, downs, sems = refs[7:]
    copies = weight_copies(gate_hbm, down_hbm, gates, downs, sems)
    for group in copies:
        for copy in group:
            copy.start()
    allow = allowed(rows_ref, columns_ref)
    rows = hidden_ref.shape[0]
    first = lax.broadcasted_iota(jnp.int32, (rows, 128), 1) < HD

    @pl.loop(0, D // 128)
    def heads(index):
        columns = pl.ds(pl.multiple_of(index * 128, 128), 128)
        values_at = pl.ds(pl.multiple_of(index * 128 + D, 128), 128)
        query = query_ref[:, columns]
        keys = jnp.concatenate([own_ref[:, columns], far_ref[:, columns]], axis=0)
        values = jnp.concatenate([own_ref[:, values_at], far_ref[:, values_at]], axis=0)
        mixed = []
        for side in range(2):
            mine = jnp.where(first == (side == 0), query, jnp.zeros_like(query))
            weight = attention_weight(mine, keys, allow).astype(low)
            mixed.append(product(weight, values))
        merged_ref[:, columns] = jnp.where(first, mixed[0], mixed[1]).astype(low)

    middle = hidden_ref[...] + contract_cols(merged_ref[...], out_weight[...])
    middle_ref[...] = middle
    normed = (middle * inverse_rms(middle) * gain_ref[...]).astype(low)
    output_ref[...] = middle
    for index, group in enumerate(copies):
        for copy in group:
            copy.wait()
        gate = contract_cols(normed, gates[pl.ds(index * CHUNK, CHUNK)])
        up = contract_cols(normed, gates[pl.ds(FF + index * CHUNK, CHUNK)])
        action = (gate * jax.nn.sigmoid(gate) * up).astype(low)
        output_ref[...] += product(action, downs[pl.ds(index * CHUNK, CHUNK)])


def weight_copies(gate_hbm, down_hbm, gates, downs, sems):
    groups = []
    for index in range(FF // CHUNK):
        parts = [
            (gate_hbm, gates, index * CHUNK),
            (gate_hbm, gates, FF + index * CHUNK),
            (down_hbm, downs, index * CHUNK),
        ]
        groups.append(
            [
                pltpu.make_async_copy(
                    source.at[pl.ds(at, CHUNK)], goal.at[pl.ds(at, CHUNK)], sems.at[index, place]
                )
                for place, (source, goal, at) in enumerate(parts)
            ]
        )
    return groups


def weight_buffers():
    return [
        pltpu.VMEM((2 * FF, D), low),
        pltpu.VMEM((FF, D), low),
        pltpu.SemaphoreType.DMA((FF // CHUNK, 3)),
    ]


def forward(hidden, query, own, far, rows, columns, w_out, gain, w_gu, w_down):
    count = hidden.shape[0]
    outs = [((count, D), jnp.float32), ((count, D), low), ((count, D), jnp.float32)]
    args = [hidden, query, own, far, rows, columns, w_out, gain, w_gu, w_down]
    return local_call(forward_kernel, "forward", outs, args, weight_buffers(), (8, 9))


def backward_kernel(gradient_ref, middle_ref, query_ref, own_ref, far_ref, *refs):
    rows_ref, columns_ref, out_weight, gain_ref, gate_hbm, down_hbm = refs[:6]
    d_query_ref, d_own_ref, d_far_ref, d_middle_ref, gain_out = refs[6:11]
    low_ref, normed_ref, action_ref, d_gate_ref, middle_low_ref = refs[11:16]
    gates, downs, sems, total = refs[16:]
    copies = weight_copies(gate_hbm, down_hbm, gates, downs, sems)
    for group in copies:
        for copy in group:
            copy.start()
    gradient = gradient_ref[...]
    grad_low = gradient.astype(low)
    low_ref[...] = grad_low
    middle = middle_ref[...]
    r = inverse_rms(middle)
    normed = (middle * r * gain_ref[...]).astype(low)
    normed_ref[...] = normed
    total[...] = jnp.zeros_like(total)
    for index, group in enumerate(copies):
        for copy in group:
            copy.wait()
        first = pl.ds(index * CHUNK, CHUNK)
        second = pl.ds(FF + index * CHUNK, CHUNK)
        gate = contract_cols(normed, gates[first])
        up = contract_cols(normed, gates[second])
        chance = jax.nn.sigmoid(gate)
        action_ref[:, first] = (gate * chance * up).astype(low)
        d_action = contract_cols(grad_low, downs[first])
        d_gate = (d_action * up * (chance + gate * chance * (1.0 - chance))).astype(low)
        d_up = (d_action * gate * chance).astype(low)
        d_gate_ref[:, first] = d_gate
        d_gate_ref[:, second] = d_up
        total[...] += product(d_gate, gates[first]) + product(d_up, gates[second])
    d_middle, gain_out[...] = norm_back(middle, r, gain_ref[...], total[...])
    d_middle = gradient + d_middle
    d_middle_ref[...] = d_middle
    middle_low = d_middle.astype(low)
    middle_low_ref[...] = middle_low
    total[...] = product(middle_low, out_weight[...])
    allow = allowed(rows_ref, columns_ref)
    rows = gradient.shape[0]
    first = lax.broadcasted_iota(jnp.int32, (rows, 128), 1) < HD
    first_all = lax.broadcasted_iota(jnp.int32, (2 * rows, 128), 1) < HD

    @pl.loop(0, D // 128)
    def heads(index):
        columns = pl.ds(pl.multiple_of(index * 128, 128), 128)
        values_at = pl.ds(pl.multiple_of(index * 128 + D, 128), 128)
        query = query_ref[:, columns]
        upstream = total[:, columns].astype(low)
        keys = jnp.concatenate([own_ref[:, columns], far_ref[:, columns]], axis=0)
        values = jnp.concatenate([own_ref[:, values_at], far_ref[:, values_at]], axis=0)
        d_queries, d_keys, d_values = [], [], []
        for side in range(2):
            mine = jnp.where(first == (side == 0), query, jnp.zeros_like(query))
            grad = jnp.where(first == (side == 0), upstream, jnp.zeros_like(upstream))
            weight = attention_weight(mine, keys, allow)
            d_values.append(contract_rows(weight.astype(low), upstream))
            d_weight = contract_cols(grad, values)
            d_score = weight * (d_weight - jnp.sum(d_weight * weight, axis=-1, keepdims=True))
            d_score = d_score.astype(low)
            d_queries.append(product(d_score, keys) * scale)
            d_keys.append(contract_rows(d_score, query) * scale)
        d_query_ref[:, columns] = jnp.where(first, *d_queries).astype(low)
        d_key = jnp.where(first_all, *d_keys)
        d_value = jnp.where(first_all, *d_values)
        d_own_ref[:, columns] = d_key[:rows]
        d_own_ref[:, values_at] = d_value[:rows]
        d_far_ref[:, columns] = d_key[rows:].astype(low)
        d_far_ref[:, values_at] = d_value[rows:].astype(low)


def backward(gradient, middle, query, own, far, rows, columns, w_out, gain, w_gu, w_down):
    count = gradient.shape[0]
    f32 = jnp.float32
    outs = [
        ((count, D), low),
        ((count, 2 * D), f32),
        ((count, 2 * D), low),
        ((count, D), f32),
        ((1, D), f32),
        ((count, D), low),
        ((count, D), low),
        ((count, FF), low),
        ((count, 2 * FF), low),
        ((count, D), low),
    ]
    args = [gradient, middle, query, own, far, rows, columns, w_out, gain, w_gu, w_down]
    scratch = weight_buffers() + [pltpu.VMEM((count, D), f32)]
    return local_call(backward_kernel, "backward", outs, args, scratch, (9, 10))


def unproject_kernel(d_query_ref, d_own_ref, d_far_ref, d_middle_ref, hidden_ref, *refs):
    gain_ref, weight_ref, cosine_ref, sine_ref, gradient_ref, gain_out, d_qkv_ref = refs
    cosine, sine = cosine_ref[...], sine_ref[...]
    first = lax.broadcasted_iota(jnp.int32, cosine.shape, 1) % HD < HD // 2
    for index in range(3 * D // 128):
        columns = pl.ds(index * 128, 128)
        if index < D // 128:
            value = d_query_ref[:, columns].astype(jnp.float32)
        else:
            there = pl.ds(index * 128 - D, 128)
            value = d_own_ref[:, there] + d_far_ref[:, there].astype(jnp.float32)
            value = value.astype(low).astype(jnp.float32)
        if index < 2 * D // 128:
            part = value * sine
            turned = jnp.where(
                first, pltpu.roll(part, 128 - HD // 2, 1), -pltpu.roll(part, HD // 2, 1)
            )
            value = value * cosine + turned
        d_qkv_ref[:, columns] = value.astype(low)
    hidden = hidden_ref[...]
    d_hidden, gain_out[...] = norm_back(
        hidden, inverse_rms(hidden), gain_ref[...], product(d_qkv_ref[...], weight_ref[...])
    )
    gradient_ref[...] = d_middle_ref[...] + d_hidden


def unproject(d_query, d_own, d_far, d_middle, hidden, gain, weight, cosine, sine):
    rows = hidden.shape[0]
    outs = [((rows, D), jnp.float32), ((1, D), jnp.float32), ((rows, 3 * D), low)]
    args = [d_query, d_own, d_far, d_middle, hidden, gain, weight, cosine, sine]
    return local_call(unproject_kernel, "unproject", outs, args)


def weigh_kernel(*refs):
    pairs = [refs[4 * index : 4 * index + 4] for index in range(4)]
    outs = refs[16:20]
    now = pl.program_id(0)

    def gradient(index):
        left_one, left_two, right_one, right_two = pairs[index]
        total = contract_rows(left_one[...], right_one[...])
        total = total + contract_rows(left_two[...], right_two[...])
        outs[index][...] = total.astype(low).reshape(outs[index].shape)

    gradient(0)
    gradient(1)

    @pl.when(now < 6)
    def qkv():
        gradient(2)

    @pl.when(now >= 6)
    def out():
        gradient(3)


def weigh(d_gates, normed_twos, actions, lows, d_qkvs, normeds, middles, merges, blocks):
    rows = lows[0].shape[0]

    def both(arrays, width, place):
        return [(array, pl.BlockSpec((rows, width), place)) for array in arrays]

    def whole(arrays):
        return [(array, pl.BlockSpec((rows, D), lambda i: (0, 0))) for array in arrays]

    def early(i):
        return (0, jnp.minimum(i, 5))

    def late(i):
        return (0, jnp.maximum(i - 6, 0))

    listed = both(d_gates, 768, lambda i: (0, i)) + whole(normed_twos)
    listed += both(actions, 384, lambda i: (0, i)) + whole(lows)
    listed += both(d_qkvs, 384, early) + whole(normeds)
    listed += both(middles, 384, late) + whole(merges)
    part = blocks // 8
    return pl.pallas_call(
        weigh_kernel,
        grid=(8,),
        out_shape=[
            jax.ShapeDtypeStruct((blocks, 2 * FF // blocks, D), low),
            jax.ShapeDtypeStruct((blocks, FF // blocks, D), low),
            jax.ShapeDtypeStruct((3 * D, D), low),
            jax.ShapeDtypeStruct((D, D), low),
        ],
        in_specs=[spec for unused, spec in listed],
        out_specs=[
            pl.BlockSpec((part, 2 * FF // blocks, D), lambda i: (i, 0, 0)),
            pl.BlockSpec((part, FF // blocks, D), lambda i: (i, 0, 0)),
            pl.BlockSpec((384, D), lambda i: (jnp.minimum(i, 5), 0)),
            pl.BlockSpec((384, D), lambda i: (jnp.maximum(i - 6, 0), 0)),
        ],
        compiler_params=pltpu.CompilerParams(vmem_limit_bytes=LARGE),
        cost_estimate=NONE,
        name="weigh",
    )(*[array for array, unused in listed])


def loss_kernel(hidden_ref, gain_ref, near_ref, far_ref, own_ref, other_ref, weight_ref, *refs):
    gradient_ref, gain_out, loss_ref, near_out, far_out, logits, teach = refs
    head = lax.axis_index("head")
    rows = hidden_ref.shape[0]
    half = rows // 2
    size = near_ref.shape[1]
    hidden = hidden_ref[...]
    r = inverse_rms(hidden)
    normed = (hidden * r * gain_ref[...]).astype(low)
    parts = [(near_ref, near_out, 0, 0), (near_ref, near_out, 1, 2)]
    parts += [(far_ref, far_out, 0, 1), (far_ref, far_out, 1, 3)]
    for index, (source, unused, place, offset) in enumerate(parts):
        columns = pl.ds(pl.multiple_of((head ^ offset) * size, size), size)
        logits[index] = contract_cols(normed, source[place])
        teach[index, :half] = own_ref[:, columns].astype(jnp.float32)
        teach[index, half:] = other_ref[:, columns].astype(jnp.float32)

    def log_total(values):
        summit = jnp.max(jnp.max(values[...], axis=0), axis=-1, keepdims=True)
        return summit + jnp.log(
            jnp.sum(jnp.sum(jnp.exp(values[...] - summit[None]), axis=0), axis=-1, keepdims=True)
        )

    log_logits, log_teach = log_total(logits), log_total(teach)
    weighting = weight_ref[...]
    gradient = jnp.zeros((rows, hidden.shape[1]), jnp.float32)
    loss = jnp.zeros((rows, 1), jnp.float32)
    for index, (source, goal, place, offset) in enumerate(parts):
        log_prob = logits[index] - log_logits
        log_true = teach[index] - log_teach
        true = jnp.exp(log_true)
        loss = loss + jnp.sum(true * (log_true - log_prob), axis=-1, keepdims=True)
        d_logits = ((jnp.exp(log_prob) - true) * weighting).astype(low)
        goal[place] = contract_rows(d_logits, normed).astype(low)
        gradient = gradient + product(d_logits, source[place])
    loss_ref[...] = jnp.broadcast_to(
        jnp.sum(loss * weighting, axis=0, keepdims=True), loss_ref.shape
    )
    gradient_ref[...], gain_out[...] = norm_back(hidden, r, gain_ref[...], gradient)


def distill(hidden, gain, near, far, own, other, weighting):
    rows, width = hidden.shape
    size = near.shape[1]
    vmem = pl.BlockSpec(memory_space=pltpu.VMEM)
    f32 = jnp.float32
    return pl.pallas_call(
        loss_kernel,
        out_shape=[
            jax.ShapeDtypeStruct(hidden.shape, f32),
            jax.ShapeDtypeStruct(gain.shape, f32),
            jax.ShapeDtypeStruct((8, 128), f32),
            jax.ShapeDtypeStruct(near.shape, low),
            jax.ShapeDtypeStruct(far.shape, low),
        ],
        in_specs=[vmem] * 7,
        out_specs=[vmem] * 5,
        scratch_shapes=[pltpu.VMEM((4, rows, size), f32)] * 2,
        compiler_params=pltpu.CompilerParams(vmem_limit_bytes=58 * 2**20),
        name="distill",
    )(hidden, gain, near, far, own, other, weighting)


def on_device(
    token_ids,
    lengths,
    valid,
    vocab_ids,
    teacher,
    block,
    block_m,
    block_v,
    bases,
    table,
    table_m,
    table_v,
    gains,
    gains_m,
    gains_v,
):
    dp_count, head_count = lax.axis_size("dp"), lax.axis_size("head")
    device_total = dp_count * head_count
    head, dp = lax.axis_index("head"), lax.axis_index("dp")
    batch = head // 2
    tokens = token_ids.shape[1]
    shard_rows = table.shape[0]
    offset = dp * shard_rows
    part = TOPV // device_total

    widths = [3 * D // device_total, D // device_total, 2 * FF // device_total, FF // device_total]
    cuts = [sum(widths[:index]) for index in range(5)]
    block_low = block.T.astype(low)
    attention, gate_up, down, rows_in, codes, near, far = start(
        [block_low[: cuts[2]], block_low[cuts[2] : cuts[3]], block_low[cuts[3] :]],
        table,
        (token_ids * 2 + valid).reshape(-1, 1, tokens),
        vocab_ids,
        dp_count,
    )
    codes = codes.reshape(dp_count, 2 * tokens)
    weighting = (lax.dynamic_index_in_dim(codes, dp, 0, keepdims=False) & 1).astype(jnp.float32)
    vocab = lax.dynamic_index_in_dim(
        vocab_ids.reshape(head_count, dp_count, part), head, 0, keepdims=False
    )
    local = jnp.concatenate([vocab, codes >> 1], axis=1) - offset
    owned = (local >= 0) & (local < shard_rows)
    weights = [
        attention[:, : cuts[1]].reshape(-1, D),
        attention[:, cuts[1] :].reshape(-1, D),
        gate_up.reshape(-1, D),
        down.reshape(-1, D),
    ]
    near = near.reshape(2, -1, D)
    far = far.reshape(2, -1, D)
    hidden = rows_in[part:].astype(jnp.float32)

    teacher_own = lax.dynamic_index_in_dim(teacher, batch, 0, keepdims=False)
    teacher_far = swap(
        lax.dynamic_index_in_dim(teacher, 1 - batch, 0, keepdims=False), head_count, 2
    )

    run = jnp.arange(tokens, dtype=jnp.int32)
    places = jnp.concatenate([head * tokens + run, (head ^ 2) * tokens + run])
    places_far = jnp.concatenate([(head ^ 1) * tokens + run, (head ^ 3) * tokens + run])
    own_lengths = lax.dynamic_index_in_dim(lengths, batch, 0, keepdims=False)[0]
    segment, position = segments(own_lengths, places)
    segment_far, unused = segments(own_lengths, places_far)
    queries_at = jnp.stack([segment, places], axis=1)
    keys_at = jnp.stack(
        [jnp.concatenate([segment, segment_far]), jnp.concatenate([places, places_far])]
    )
    freqs = jnp.exp(jnp.arange(0, HD, 2, dtype=jnp.float32) * (-math.log(10000.0) / HD))
    angle = position.astype(jnp.float32)[:, None] * jnp.tile(freqs, 4)[None, :]
    cosine, sine = jnp.cos(angle), jnp.sin(angle)

    w_qkv, w_out, w_gu, w_down = weights
    saves = []
    for repeat in range(2):
        normed, query, own = project(hidden, gains[0:1], w_qkv, cosine, sine)
        other = swap(own, head_count, 1)
        output, merged, middle = forward(
            hidden, query, own, other, queries_at, keys_at, w_out, gains[1:2], w_gu, w_down
        )
        saves.append((hidden, normed, query, own, other, merged, middle))
        hidden = output

    gradient, d_gain_final, loss_sum, d_near, d_far = distill(
        hidden, gains[2:3], near, far, teacher_own, teacher_far, weighting[:, None]
    )
    d_gain_final, loss_sum = d_gain_final[0], loss_sum[0, 0]
    f32 = jnp.float32
    d_near = d_near.astype(f32) + swap(d_far, head_count, 1).astype(f32)
    d_near = d_near.astype(low)
    d_quarter = d_near[0].astype(f32) + swap(d_near[1], head_count, 2).astype(f32)
    chosen_grads = lax.psum_scatter(
        d_quarter.astype(low), "dp", scatter_dimension=0, tiled=True
    )

    d_gains = [0.0, 0.0]
    parts = []
    for repeat in range(2):
        hidden, normed, query, own, other, merged, middle = saves[1 - repeat]
        back = backward(
            gradient, middle, query, own, other, queries_at, keys_at, w_out, gains[1:2], w_gu, w_down
        )
        d_query, d_own, d_other, d_middle, d_gain_two = back[:5]
        grad_low, normed_two, action, d_gate, middle_low = back[5:]
        gradient, d_gain_one, d_qkv = unproject(
            d_query,
            d_own,
            swap(d_other, head_count, 1),
            d_middle,
            hidden,
            gains[0:1],
            w_qkv,
            cosine,
            sine,
        )
        parts.append((d_gate, normed_two, action, grad_low, d_qkv, normed, middle_low, merged))
        d_gains = [d_gains[0] + d_gain_one[0], d_gains[1] + d_gain_two[0]]

    d_gu, d_down, d_qkv, d_out = weigh(*zip(*parts), device_total)
    d_qkv, d_out = [piece.reshape(device_total, -1, D) for piece in (d_qkv, d_out)]
    rows_back = jnp.concatenate([chosen_grads, gradient.astype(low)], axis=0)
    step = 80 if shard_rows % 80 == 0 else 40
    quarter = -(-shard_rows // (step * head_count)) * step
    tile = quarter // 5 if quarter % 80 == 0 and quarter // 5 % 16 == 0 else step
    small = [d_gains[0], d_gains[1], d_gain_final, loss_sum[None], jnp.sum(weighting)[None]]
    small = jnp.pad(jnp.concatenate(small), (0, 6 * 128 - 2)).reshape(-1, 128)
    block_grads, table_grads, small = finish(
        [jnp.concatenate([d_qkv, d_out], axis=1), d_gu, d_down],
        rows_back,
        jnp.where(owned, local, -1).reshape(1, -1),
        small,
        quarter,
        tile,
    )
    outs = update(
        cuts,
        [table, table_m, table_v],
        table_grads.reshape(-1, D),
        small,
        small[: 3 * D // 128].reshape(3, D),
        [gains, gains_m, gains_v],
        block_grads.T,
        [block, block_m, block_v],
        bases,
    )
    table_new, table_m_new, table_v_new, table_low = outs[0:4]
    values, gains_new, gains_m_new, gains_v_new = outs[4:8]
    block_new, block_m_new, block_v_new, block_low = outs[8:12]
    return (
        values[0, 0],
        values[0, 1],
        block_new,
        block_m_new,
        block_v_new,
        table_new,
        table_m_new,
        table_v_new,
        gains_new,
        gains_m_new,
        gains_v_new,
        block_low,
        table_low,
    )


def solution(mesh):
    tokens = P(None, ("dp", "head"))
    columns = P(None, ("dp", "head"))
    table = P("dp", None)
    return jax.shard_map(
        on_device,
        mesh=mesh,
        in_specs=(
            tokens,
            P(None, "dp", None),
            tokens,
            P(),
            P(None, ("dp", "head"), None),
            columns,
            columns,
            columns,
            P(),
            table,
            table,
            table,
            P(),
            P(),
            P(),
        ),
        out_specs=(
            P(),
            P(),
            columns,
            columns,
            columns,
            table,
            table,
            table,
            P(),
            P(),
            P(),
            columns,
            table,
        ),
        check_vma=False,
    )
```

```python
import functools
import math

import jax
import jax.numpy as jnp
from jax import lax
from jax.experimental import pallas as pl
from jax.experimental.pallas import tpu as pltpu
from jax.sharding import PartitionSpec as P

D = 768
H = 12
HD = 64
FF = 3072
TOPV = 4096
STEP = 5

low = jnp.bfloat16
scale = HD**-0.5
eps_norm = 1e-05
clip_norm = 0.002
beta_one = 0.9
beta_two = 0.99
adam_eps = 1e-08
decay_rate = 0.1
rate_block = 0.03
rate_table = 0.05
rate_gain = 0.4


def product(left, right):
    return jnp.dot(left, right, preferred_element_type=jnp.float32)


def contract_rows(left, right):
    return lax.dot_general(
        left, right, (((0,), (0,)), ((), ())), preferred_element_type=jnp.float32
    )


def contract_cols(left, right):
    return lax.dot_general(
        left, right, (((1,), (1,)), ((), ())), preferred_element_type=jnp.float32
    )


def segments(lengths, places):
    segment = jnp.zeros_like(places)
    begin = jnp.zeros_like(places)
    end = jnp.zeros((), jnp.int32)
    for index in range(lengths.shape[0] - 1):
        end = end + lengths[index]
        past = places >= end
        segment = segment + past.astype(jnp.int32)
        begin = jnp.where(past, end, begin)
    return segment, places - begin


def swap(value, head_count, offset):
    return lax.ppermute(value, "head", [(h, h ^ offset) for h in range(head_count)])


MESH = pl.DeviceIdType.MESH
ANY = pl.BlockSpec(memory_space=pl.ANY)


def coordinates(depth):
    dp, head = lax.axis_index("dp"), lax.axis_index("head")
    return dp // 2, dp % 2, head // 2, head % 2


def device(z, x, y, c):
    return (z * 2 + x, y * 2 + c)


def slot(z, x, y, c):
    return ((z * 2 + x) * 2 + y) * 2 + c


def greet(depth, z, x, y, c):
    barrier = pltpu.get_barrier_semaphore()
    for target in (device(z, 1 - x, y, c), device(z, x, 1 - y, c), device(z, x, y, 1 - c)):
        pl.semaphore_signal(barrier, 1, device_id=target, device_id_type=MESH)

    @pl.when(z > 0)
    def below():
        pl.semaphore_signal(barrier, 1, device_id=device(z - 1, x, y, c), device_id_type=MESH)

    @pl.when(z < depth - 1)
    def above():
        pl.semaphore_signal(barrier, 1, device_id=device(z + 1, x, y, c), device_id_type=MESH)

    pl.semaphore_wait(barrier, 3 + jnp.where(z > 0, 1, 0) + jnp.where(z < depth - 1, 1, 0))


def start_kernel(depth, *refs):
    pieces = refs[0:3]
    table_ref, codes_ref, vocab_ref = refs[3:6]
    wholes = refs[6:9]
    sum_ref, ids_ref, near_ref, far_ref = refs[9:13]
    far_x, from_low, from_high, total, rows_ref, shard, ids = refs[13:20]
    local_sem, up_sem, down_sem, x_sem, y_sem, c_sem, block_sem = refs[20:27]
    rx_send, rx_recv, ru_send, ru_recv, rd_send, rd_recv = refs[27:33]
    id_send, id_recv, table_sem, copy_sem = refs[33:37]
    su_send, sd_send, sx_send, sy_send, sc_send, s_recv, keep_sem = refs[37:44]
    z, x, y, c = coordinates(depth)
    mine = slot(z, x, y, c)
    dp, head = z * 2 + x, y * 2 + c
    groups, height = rows_ref.shape[:2]
    shard_rows, tokens = table_ref.shape[0], codes_ref.shape[2]
    part = height - 2 * tokens
    offset = dp * shard_rows
    barrier = pltpu.get_barrier_semaphore()
    pl.semaphore_signal(barrier, 1, device_id=device(z, x, y, 1 - c), device_id_type=MESH)
    for group in range(groups):
        for rank in range(2):

            @pl.when((group != dp) | (rank != y))
            def hello():
                pl.semaphore_signal(
                    barrier, 1, device_id=(group, rank * 2 + c), device_id_type=MESH
                )

    pl.semaphore_wait(barrier, groups * 2)

    def tell(group, rank):
        second = jnp.where(rank == y, 0, 1)
        return pltpu.make_async_remote_copy(
            codes_ref.at[rank],
            ids_ref.at[dp, second],
            id_send.at[group, rank],
            id_recv.at[dp, second],
            device_id=(group, rank * 2 + c),
            device_id_type=MESH,
        )

    def told(group, second):
        return pltpu.make_async_remote_copy(
            codes_ref.at[0],
            ids_ref.at[group, second],
            id_send.at[group, second],
            id_recv.at[group, second],
            device_id=device(z, x, y, 1 - c),
            device_id_type=MESH,
        )

    keep = pltpu.make_async_copy(codes_ref.at[y], ids_ref.at[dp, 0], copy_sem)
    fetch = pltpu.make_async_copy(table_ref, shard.at[pl.ds(0, shard_rows)], table_sem)
    fetch.start()
    keep.start()
    for group in range(groups):
        for rank in range(2):

            @pl.when((group != dp) | (rank != y))
            def telling():
                tell(group, rank).start()

    def gather(stage, group):
        def load(first, read):
            @pl.loop(0, (tokens if first else part) // 16)
            def some(index):
                base = index * 16
                lines = []
                for line in range(16):
                    place = read(base + line) - offset
                    held = (place >= 0) & (place < shard_rows)
                    lines.append(shard[pl.ds(jnp.where(held, place, shard_rows), 1)])
                rows_ref[group, pl.ds(pl.multiple_of(first + base, 16), 16)] = jnp.concatenate(
                    lines, axis=0
                ).astype(low)

        if stage == 0:
            load(0, lambda index: vocab_ref[(head * groups + group) * part + index])
        for second in range(2 if stage else 0):
            load(part + second * tokens, lambda index: ids[group, second, 0, index] >> 1)

    def own(block, piece, target, sem):
        return pltpu.make_async_remote_copy(
            pieces[piece],
            wholes[piece].at[block],
            sem.at[piece],
            block_sem.at[block, piece],
            device_id=target,
            device_id_type=MESH,
        )

    def onward(block, piece, target, sem):
        return pltpu.make_async_remote_copy(
            wholes[piece].at[block],
            wholes[piece].at[block],
            sem.at[piece],
            block_sem.at[block, piece],
            device_id=target,
            device_id_type=MESH,
        )

    def send(make, block, target, sem):
        for piece in range(3):
            make(block, piece, target, sem).start()

    def arrive(block):
        for piece in range(3):
            onward(block, piece, device(z, x, y, 1 - c), c_sem.at[0]).wait_recv()

    across_x, across_y, across_c = (
        device(z, 1 - x, y, c),
        device(z, x, 1 - y, c),
        device(z, x, y, 1 - c),
    )
    spans = (pl.ds(0, part), pl.ds(part, 2 * tokens))

    def rows_x(stage, goal):
        return pltpu.make_async_remote_copy(
            rows_ref.at[goal * 2 + 1 - x, spans[stage]],
            far_x.at[goal, spans[stage]],
            rx_send.at[stage, goal],
            rx_recv.at[stage, goal],
            device_id=across_x,
            device_id_type=MESH,
        )

    def rows_up(stage, goal):
        return pltpu.make_async_remote_copy(
            total.at[goal, spans[stage]],
            from_low.at[goal, spans[stage]],
            ru_send.at[stage, goal],
            ru_recv.at[stage, goal],
            device_id=device(z + 1, x, y, c),
            device_id_type=MESH,
        )

    def rows_down(stage, goal):
        return pltpu.make_async_remote_copy(
            total.at[goal, spans[stage]],
            from_high.at[goal, spans[stage]],
            rd_send.at[stage, goal],
            rd_recv.at[stage, goal],
            device_id=device(z - 1, x, y, c),
            device_id_type=MESH,
        )

    goals = [
        goal for pair in zip(range(depth // 2), range(depth - 1, 0, -1)) for goal in pair
    ]
    goals += [goal for goal in range(depth) if goal not in goals]

    def reduce(stage):
        span = spans[stage]
        for goal in goals:
            rows_x(stage, goal).wait_recv()
            both = rows_ref[goal * 2 + x, span] + far_x[goal, span]

            @pl.when(goal > z)
            def rising():
                @pl.when(z > 0)
                def more():
                    rows_up(stage, goal).wait_recv()
                    total[goal, span] = both + from_low[goal, span]

                @pl.when(z == 0)
                def alone():
                    total[goal, span] = both

                rows_up(stage, goal).start()

            @pl.when(goal < z)
            def falling():
                @pl.when(z < depth - 1)
                def more():
                    rows_down(stage, goal).wait_recv()
                    total[goal, span] = both + from_high[goal, span]

                @pl.when(z == depth - 1)
                def alone():
                    total[goal, span] = both

                rows_down(stage, goal).start()

            @pl.when(goal == z)
            def here():
                total[goal, span] = both

    def land(stage):
        span = spans[stage]
        for goal in range(depth):

            @pl.when(goal == z)
            def landed():
                @pl.when(z > 0)
                def low_part():
                    rows_up(stage, goal).wait_recv()
                    total[goal, span] = total[goal, span] + from_low[goal, span]

                @pl.when(z < depth - 1)
                def high_part():
                    rows_down(stage, goal).wait_recv()
                    total[goal, span] = total[goal, span] + from_high[goal, span]

                sum_ref[span] = total[goal, span]

    local = [
        pltpu.make_async_copy(pieces[piece], wholes[piece].at[mine], local_sem.at[piece])
        for piece in range(3)
    ]
    send(own, mine, across_y, y_sem.at[mine // 4])

    @pl.when(z < depth - 1)
    def first_up():
        send(own, mine, device(z + 1, x, y, c), up_sem.at[0])

    @pl.when(z > 0)
    def first_down():
        send(own, mine, device(z - 1, x, y, c), down_sem.at[0])

    send(own, mine, across_x, x_sem.at[z])
    send(own, mine, across_c, c_sem.at[mine // 2])
    for copy in local:
        copy.start()
    shard[pl.ds(shard_rows, 8)] = jnp.zeros((8, shard.shape[1]), jnp.float32)
    fetch.wait()
    for goal in goals:
        gather(0, goal * 2 + 1 - x)
        rows_x(0, goal).start()
    for goal in goals:
        gather(0, goal * 2 + x)
    keep.wait()
    for group in range(groups):
        for second in range(2):

            @pl.when((group != dp) | (second != 0))
            def heard():
                told(group, second).wait_recv()

    to_scalars = pltpu.make_async_copy(ids_ref, ids, copy_sem)
    to_scalars.start()

    def spread(block, over_x):
        send(onward, block, across_y, y_sem.at[block // 4])
        if over_x:
            send(onward, block, across_x, x_sem.at[block // 8])
        send(onward, block, across_c, c_sem.at[block // 2])

    def pass_on(step):
        @pl.when(z - step >= 0)
        def risen():
            block = slot(z - step, x, y, c)
            arrive(block)

            @pl.when(z < depth - 1)
            def further():
                send(onward, block, device(z + 1, x, y, c), up_sem.at[step])

            spread(block, True)

        @pl.when(z + step < depth)
        def fallen():
            block = slot(z + step, x, y, c)
            arrive(block)

            @pl.when(z > 0)
            def further():
                send(onward, block, device(z - 1, x, y, c), down_sem.at[step])

            spread(block, True)

    def crossed(step):
        for sign in (1, -1) if step else (1,):

            @pl.when((z + sign * step >= 0) & (z + sign * step < depth))
            def there():
                block = slot(z + sign * step, 1 - x, y, c)
                arrive(block)
                spread(block, False)

    pass_on(1)
    to_scalars.wait()
    for goal in goals:
        gather(1, goal * 2 + 1 - x)
        rows_x(1, goal).start()
    for step in range(2, min(depth, 3)):
        pass_on(step)
    reduce(0)
    for goal in goals:
        gather(1, goal * 2 + x)
    for step in range(3, depth):
        pass_on(step)
    land(0)

    def shared(source, ref, quarter, group, send_sem, target):
        where = ref.at[quarter, group]
        return pltpu.make_async_remote_copy(
            where if source is None else source,
            where,
            send_sem,
            s_recv.at[quarter if ref is near_ref else 2 + quarter, group],
            device_id=target,
            device_id_type=MESH,
        )

    own_shared = sum_ref.at[pl.ds(0, part)]
    keep_shared = pltpu.make_async_copy(own_shared, near_ref.at[0, dp], keep_sem)
    keep_shared.start()

    def plane(group):
        return near_ref.at[0, group]

    def shared_y(source, group):
        return pltpu.make_async_remote_copy(
            source,
            near_ref.at[1, group],
            sy_send.at[group],
            s_recv.at[1, group],
            device_id=across_y,
            device_id_type=MESH,
        )

    def shared_c(source, quarter, group):
        return pltpu.make_async_remote_copy(
            source,
            far_ref.at[quarter, group],
            sc_send.at[quarter, group],
            s_recv.at[2 + quarter, group],
            device_id=across_c,
            device_id_type=MESH,
        )

    @pl.when(z < depth - 1)
    def shared_up():
        shared(own_shared, near_ref, 0, dp, su_send.at[0], device(z + 1, x, y, c)).start()

    @pl.when(z > 0)
    def shared_down():
        shared(own_shared, near_ref, 0, dp, sd_send.at[0], device(z - 1, x, y, c)).start()

    shared(own_shared, near_ref, 0, dp, sx_send.at[z], across_x).start()
    shared_y(own_shared, dp).start()
    shared_c(own_shared, 0, dp).start()
    for step in range(1, depth):

        @pl.when(z - step >= 0)
        def shared_risen():
            group = (z - step) * 2 + x
            copy = shared(
                None, near_ref, 0, group, su_send.at[step], device(z + 1, x, y, c)
            )
            copy.wait_recv()

            @pl.when(z < depth - 1)
            def further():
                copy.start()

            shared(None, near_ref, 0, group, sx_send.at[z - step], across_x).start()
            shared_y(plane(group), group).start()
            shared_c(plane(group), 0, group).start()

        @pl.when(z + step < depth)
        def shared_fallen():
            group = (z + step) * 2 + x
            copy = shared(
                None, near_ref, 0, group, sd_send.at[step], device(z - 1, x, y, c)
            )
            copy.wait_recv()

            @pl.when(z > 0)
            def further():
                copy.start()

            shared(None, near_ref, 0, group, sx_send.at[z + step], across_x).start()
            shared_y(plane(group), group).start()
            shared_c(plane(group), 0, group).start()

    crossed(0)
    reduce(1)
    for step in range(1, depth):
        crossed(step)
    for place in range(depth):
        group = place * 2 + 1 - x
        shared(None, near_ref, 0, group, sx_send.at[place], across_x).wait_recv()
        shared_y(plane(group), group).start()
        shared_c(plane(group), 0, group).start()
    land(1)

    for step in range(depth):
        for sign in (1, -1) if step else (1,):

            @pl.when((z + sign * step >= 0) & (z + sign * step < depth))
            def level():
                for side in (x, 1 - x):
                    block = slot(z + sign * step, side, 1 - y, c)
                    arrive(block)
                    send(onward, block, across_c, c_sem.at[block // 2])

    for group in range(groups):
        shared_y(plane(group), group).wait_recv()
        shared_c(near_ref.at[1, group], 1, group).start()

    for block in range(depth * 8):

        @pl.when(block % 2 != c)
        def from_core():
            arrive(block)

    for group in range(groups):
        for quarter in range(2):
            shared_c(near_ref.at[quarter, group], quarter, group).wait_recv()

    keep_shared.wait()
    for group in range(groups):
        shared_y(plane(group), group).wait_send()
        for quarter in range(2):
            shared_c(near_ref.at[quarter, group], quarter, group).wait_send()
    for place in range(depth):
        shared(None, near_ref, 0, dp, sx_send.at[place], across_x).wait_send()

        @pl.when((z - place >= 0) & (z < depth - 1))
        def shared_rose():
            shared(None, near_ref, 0, dp, su_send.at[place], across_x).wait_send()

        @pl.when((z + place < depth) & (z > 0))
        def shared_fell():
            shared(None, near_ref, 0, dp, sd_send.at[place], across_x).wait_send()

    for copy in local:
        copy.wait()
    for group in range(groups):
        for rank in range(2):

            @pl.when((group != dp) | (rank != y))
            def spoken():
                tell(group, rank).wait_send()

    for goal in range(depth):
        for stage in range(2):
            rows_x(stage, goal).wait_send()

            @pl.when(goal > z)
            def rose():
                rows_up(stage, goal).wait_send()

            @pl.when(goal < z)
            def fell():
                rows_down(stage, goal).wait_send()

    def sent(block, target, sem):
        for piece in range(3):
            onward(block, piece, target, sem).wait_send()

    for step in range(depth):

        @pl.when((z - step >= 0) & (z < depth - 1))
        def rose():
            sent(mine, device(z + 1, x, y, c), up_sem.at[step])

        @pl.when((z + step < depth) & (z > 0))
        def fell():
            sent(mine, device(z - 1, x, y, c), down_sem.at[step])

        sent(mine, across_x, x_sem.at[step])
    for index in range(depth * 2):
        sent(mine, across_y, y_sem.at[index])
    for index in range(depth * 4):
        sent(mine, across_c, c_sem.at[index])


def start(pieces, table, codes, vocab_ids, groups):
    width = table.shape[1]
    height = vocab_ids.shape[0] // (groups * 4) + 2 * codes.shape[2]
    depth = groups // 2
    blocks = depth * 8
    told = (groups, 2, 1, codes.shape[2])
    dma = pltpu.SemaphoreType.DMA
    buffer = pltpu.VMEM((depth, height, width), low)
    return pl.pallas_call(
        functools.partial(start_kernel, depth),
        out_shape=[jax.ShapeDtypeStruct((blocks,) + piece.shape, low) for piece in pieces]
        + [jax.ShapeDtypeStruct((height, width), low), jax.ShapeDtypeStruct(told, jnp.int32)]
        + [jax.ShapeDtypeStruct((2, groups, vocab_ids.shape[0] // blocks, width), low)] * 2,
        in_specs=[ANY] * 4
        + [pl.BlockSpec(memory_space=pltpu.VMEM), pl.BlockSpec(memory_space=pltpu.SMEM)],
        out_specs=[ANY] * 3 + [pl.BlockSpec(memory_space=pltpu.VMEM)] * 2 + [ANY] * 2,
        scratch_shapes=[buffer] * 4
        + [
            pltpu.VMEM((groups, height, width), low),
            pltpu.VMEM((table.shape[0] + 8, width), jnp.float32),
            pltpu.SMEM(told, jnp.int32),
        ]
        + [dma((3,))]
        + [dma((depth, 3))] * 3
        + [dma((depth * 2, 3)), dma((depth * 4, 3)), dma((blocks, 3))]
        + [dma((2, depth))] * 6
        + [dma((groups, 2))] * 2
        + [dma(())] * 2
        + [dma((depth,))] * 3
        + [dma((groups,)), dma((2, groups)), dma((4, groups)), dma(())],
        compiler_params=pltpu.CompilerParams(
            collective_id=0, has_side_effects=True, vmem_limit_bytes=58 * 2**20
        ),
        name="start",
    )(*pieces, table, codes, vocab_ids)


def by_distance(depth, z, act):
    for step in range(depth - 1, -1, -1):
        for sign in (1, -1) if step else (1,):

            @pl.when((z + sign * step >= 0) & (z + sign * step < depth))
            def reached():
                act(z + sign * step)


def add_into(total, block, *terms):
    height = total.shape[1]
    chunk = 96 if height % 96 == 0 else height

    @pl.loop(0, height // chunk)
    def chunks(index):
        part = pl.ds(pl.multiple_of(index * chunk, chunk), chunk)
        value = total[block, part].astype(jnp.float32)
        for buffer, place in terms:
            value = value + buffer[place, part].astype(jnp.float32)
        total[block, part] = value.astype(low)


def finish_kernel(depth, heights, tile, *refs):
    pieces = refs[0:3]
    rows_ref, places_ref, small_ref = refs[3:6]
    grad_ref, table_out, small_out = refs[6:9]
    total, far_c, far_p, far_s, from_low, from_high = refs[9:15]
    rows, given, far_t, part, mine, far_part, small, far_small = refs[15:23]
    local_sem, c_send, c_recv, p_send, p_recv, s_send, s_recv = refs[23:30]
    u_send, u_recv, d_send, d_recv = refs[30:34]
    own_sem, ru_send, rd_send, rx_send, r_recv = refs[34:39]
    t_send, t_recv, ty_send, ty_recv, o_send, o_recv, e_send, e_recv = refs[39:47]
    z, x, y, c = coordinates(depth)
    dp = z * 2 + x
    firsts = [sum(heights[:index]) for index in range(3)]
    up, down = device(z + 1, x, y, c), device(z - 1, x, y, c)
    across_x, across_y, across_c = (
        device(z, 1 - x, y, c),
        device(z, x, 1 - y, c),
        device(z, x, y, 1 - c),
    )
    even = c == 0
    across_p = tuple(jnp.where(even, a, b) for a, b in zip(across_y, across_x))
    across_s = tuple(jnp.where(even, b, a) for a, b in zip(across_y, across_x))
    own_p, own_s = jnp.where(even, y, x), jnp.where(even, x, y)
    partners = [across_c, across_y, across_x]
    reach = 1
    while reach < depth:
        partners.append(device(z ^ reach, x, y, c))
        reach = reach * 2

    barrier = pltpu.get_barrier_semaphore()
    for target in partners[:3] + partners[4:]:
        pl.semaphore_signal(barrier, 1, device_id=target, device_id_type=MESH)

    @pl.when(z > 0)
    def below():
        pl.semaphore_signal(barrier, 1, device_id=down, device_id_type=MESH)

    @pl.when(z < depth - 1)
    def above():
        pl.semaphore_signal(barrier, 1, device_id=up, device_id_type=MESH)

    pl.semaphore_wait(
        barrier, len(partners) - 1 + jnp.where(z > 0, 1, 0) + jnp.where(z < depth - 1, 1, 0)
    )

    def remote(source, goal, send_sem, recv_sem, target):
        return pltpu.make_async_remote_copy(
            source, goal, send_sem, recv_sem, device_id=target, device_id_type=MESH
        )

    def block_of(place, s, p):
        return place * 4 + jnp.where(even, s * 2 + p, p * 2 + s)

    def local(block, piece):
        return pltpu.make_async_copy(
            pieces[piece].at[block * 2 + c],
            total.at[block, pl.ds(firsts[piece], heights[piece])],
            local_sem.at[block, piece],
        )

    def over_c(block, piece):
        return remote(
            pieces[piece].at[block * 2 + 1 - c],
            far_c.at[block, pl.ds(firsts[piece], heights[piece])],
            c_send.at[block, piece],
            c_recv.at[block, piece],
            across_c,
        )

    def over_p(place, s):
        pair = place * 2 + s
        return remote(
            total.at[block_of(place, s, 1 - own_p)],
            far_p.at[pair],
            p_send.at[pair],
            p_recv.at[pair],
            across_p,
        )

    def over_s(place):
        return remote(
            total.at[block_of(place, 1 - own_s, own_p)],
            far_s.at[place],
            s_send.at[place],
            s_recv.at[place],
            across_s,
        )

    def rise(place):
        block = block_of(place, own_s, own_p)
        return remote(
            total.at[block], from_low.at[place], u_send.at[place], u_recv.at[place], up
        )

    def fall(place):
        block = block_of(place, own_s, own_p)
        return remote(
            total.at[block], from_high.at[place], d_send.at[place], d_recv.at[place], down
        )

    def own_rows(send_sem, target):
        return remote(rows_ref, rows.at[dp], send_sem, r_recv.at[dp], target)

    def rows_on(place, send_sem, target):
        there = place * 2 + x
        return remote(rows.at[there], rows.at[there], send_sem, r_recv.at[there], target)

    own = pltpu.make_async_copy(rows_ref, rows.at[dp], own_sem)
    own.start()

    @pl.when(z < depth - 1)
    def first_up():
        own_rows(ru_send.at[0], up).start()

    @pl.when(z > 0)
    def first_down():
        own_rows(rd_send.at[0], down).start()

    own_rows(rx_send.at[z], across_x).start()

    for turn in range(2):
        for s, s_there in ((1 - own_s, 1 - own_p), (own_s, own_p)):
            p, p_there = (1 - own_p, 1 - own_s) if turn == 0 else (own_p, own_s)

            def launch(place):
                for piece in range(3):
                    over_c(
                        place * 4 + jnp.where(even, p_there * 2 + s_there, s_there * 2 + p_there),
                        piece,
                    ).start()
                    local(block_of(place, s, p), piece).start()

            by_distance(depth, z, launch)

    def ready(block):
        for piece in range(3):
            local(block, piece).wait()
            over_c(block, piece).wait_recv()

    def give_p():
        for s in (1 - own_s, own_s):

            def give(place):
                block = block_of(place, s, 1 - own_p)
                ready(block)
                add_into(total, block, (far_c, block))
                over_p(place, s).start()

            by_distance(depth, z, give)

    @pl.when(even)
    def early():
        give_p()

    for step in range(1, depth):

        @pl.when(z - step >= 0)
        def risen():
            rows_on(z - step, ru_send.at[step], up).wait_recv()

            @pl.when(z < depth - 1)
            def further():
                rows_on(z - step, ru_send.at[step], up).start()

            rows_on(z - step, rx_send.at[z - step], across_x).start()

        @pl.when(z + step < depth)
        def fallen():
            rows_on(z + step, rd_send.at[step], down).wait_recv()

            @pl.when(z > 0)
            def further():
                rows_on(z + step, rd_send.at[step], down).start()

            rows_on(z + step, rx_send.at[z + step], across_x).start()

    @pl.when(c == 1)
    def late():
        give_p()

    own.wait()
    for place in range(depth):
        there = place * 2 + 1 - x
        remote(
            rows.at[there], rows.at[there], rx_send.at[place], r_recv.at[there], across_x
        ).wait_recv()

    height = part.shape[0]
    count = places_ref.shape[1]

    def collect(rank, core, goal):
        @pl.loop(0, height // tile)
        def tiles(index):
            first = index * tile
            at = (
                (rank * 2 + core) * height
                + first
                + lax.broadcasted_iota(jnp.int32, (tile, count), 0)
            )
            picked = jnp.where(at == places_ref[...], 1.0, 0.0).astype(low)
            goal[pl.ds(pl.multiple_of(first, tile), tile)] = product(
                picked, rows[...].reshape(count, rows.shape[2])
            ).astype(low)

    def over_t(rank):
        index = jnp.where(rank == y, 1, 0)
        return remote(
            given.at[index], far_t.at[index], t_send.at[index], t_recv.at[index], across_c
        )

    chunk = 80 if height % 80 == 0 else height

    def pieces_of(act):
        @pl.loop(0, height // chunk)
        def step(index):
            act(pl.ds(pl.multiple_of(index * chunk, chunk), chunk))

    collect(1 - y, 1 - c, given.at[0])
    over_t(1 - y).start()
    collect(y, 1 - c, given.at[1])
    over_t(y).start()
    collect(1 - y, c, part)
    over_t(1 - y).wait_recv()

    def first_sum(lines):
        part[lines] = (part[lines].astype(jnp.float32) + far_t[0, lines].astype(jnp.float32)).astype(
            low
        )

    pieces_of(first_sum)
    over_part = remote(part, far_part, ty_send, ty_recv, across_y)
    over_part.start()
    collect(y, c, mine)

    def give_s(place):
        block = block_of(place, 1 - own_s, own_p)
        ready(block)
        over_p(place, 1 - own_s).wait_recv()
        add_into(total, block, (far_c, block), (far_p, place * 2 + 1 - own_s))
        over_s(place).start()

    by_distance(depth, z, give_s)

    over_t(y).wait_recv()
    over_part.wait_recv()

    def second_sum(index, squares):
        lines = pl.ds(pl.multiple_of(index * chunk, chunk), chunk)
        value = (
            mine[lines].astype(jnp.float32)
            + far_t[1, lines].astype(jnp.float32)
            + far_part[lines].astype(jnp.float32)
        ).astype(low)
        mine[lines] = value
        value = value.astype(jnp.float32)
        return squares + jnp.sum((value * value).reshape(-1, 8, value.shape[1]), axis=0)

    squares = lax.fori_loop(
        0, height // chunk, second_sum, jnp.zeros((8, part.shape[1]), jnp.float32)
    )

    def out_mine(index, target):
        where = table_out.at[y * 2 + c]
        return remote(mine, where, o_send.at[index], o_recv.at[y * 2 + c], target)

    def out(rank, core):
        where = table_out.at[rank * 2 + core]
        return remote(where, where, o_send.at[2], o_recv.at[rank * 2 + core], across_c)

    keep = pltpu.make_async_copy(mine, table_out.at[y * 2 + c], own_sem)
    out_mine(0, across_y).start()
    out_mine(1, across_c).start()
    keep.start()

    def give_z(place):
        block = block_of(place, own_s, own_p)
        ready(block)
        over_p(place, own_s).wait_recv()
        over_s(place).wait_recv()
        add_into(total, block, (far_c, block), (far_p, place * 2 + own_s), (far_s, place))

        @pl.when(place > z)
        def rising():
            @pl.when(z > 0)
            def more():
                rise(place).wait_recv()
                add_into(total, block, (from_low, place))

            rise(place).start()

        @pl.when(place < z)
        def falling():
            @pl.when(z < depth - 1)
            def more():
                fall(place).wait_recv()
                add_into(total, block, (from_high, place))

            fall(place).start()

    by_distance(depth, z, give_z)
    grad_ref[...] = total[block_of(z, own_s, own_p)].astype(jnp.float32)

    @pl.when(z > 0)
    def low_part():
        rise(z).wait_recv()
        grad_ref[...] = grad_ref[...] + from_low[z].astype(jnp.float32)

    @pl.when(z < depth - 1)
    def high_part():
        fall(z).wait_recv()
        grad_ref[...] = grad_ref[...] + from_high[z].astype(jnp.float32)

    lines = lax.broadcasted_iota(jnp.int32, small.shape[1:], 0)
    lanes = lax.broadcasted_iota(jnp.int32, small.shape[1:], 1)
    last = (lines == small.shape[1] - 1) & (lanes == 0)
    grad_squares = jnp.sum(grad_ref[...] * grad_ref[...])
    small[0] = small_ref[...] + jnp.where(last, jnp.sum(squares) + grad_squares, 0.0)

    def exchange(turn):
        return remote(
            small.at[turn], far_small.at[turn], e_send.at[turn], e_recv.at[turn], partners[turn]
        )

    for turn in range(len(partners)):
        exchange(turn).start()
        exchange(turn).wait_recv()
        small[turn + 1] = small[turn] + far_small[turn]
    small_out[...] = small[len(partners)]
    out(1 - y, c).wait_recv()
    out(1 - y, c).start()
    out(y, 1 - c).wait_recv()
    out(1 - y, 1 - c).wait_recv()

    keep.wait()
    out_mine(0, across_y).wait_send()
    out_mine(1, across_c).wait_send()
    out(1 - y, c).wait_send()
    over_part.wait_send()
    for turn in range(len(partners)):
        exchange(turn).wait_send()
    for rank in range(2):
        over_t(rank).wait_send()
    for place in range(depth):
        rows_on(place, rx_send.at[place], across_x).wait_send()
        over_s(place).wait_send()
        for side in range(2):
            over_p(place, side).wait_send()
            for rank in range(2):
                for piece in range(3):
                    over_c((place * 2 + side) * 2 + rank, piece).wait_send()

        @pl.when(place > z)
        def rose():
            rise(place).wait_send()

        @pl.when(place < z)
        def fell():
            fall(place).wait_send()

        @pl.when((z - place >= 0) & (z < depth - 1))
        def rows_rose():
            rows_on(z, ru_send.at[place], up).wait_send()

        @pl.when((z + place < depth) & (z > 0))
        def rows_fell():
            rows_on(z, rd_send.at[place], down).wait_send()


def finish(pieces, rows, places, small, quarter, tile):
    blocks = pieces[0].shape[0]
    heights = [piece.shape[1] for piece in pieces]
    height, width = sum(heights), pieces[0].shape[2]
    depth = blocks // 8
    turns = 3 + (depth - 1).bit_length()
    dma = pltpu.SemaphoreType.DMA
    vmem = pl.BlockSpec(memory_space=pltpu.VMEM)

    def buffer(count):
        return pltpu.VMEM((count, height, width), low)

    return pl.pallas_call(
        functools.partial(finish_kernel, depth, heights, tile),
        out_shape=[
            jax.ShapeDtypeStruct((height, width), jnp.float32),
            jax.ShapeDtypeStruct((4, quarter, width), low),
            jax.ShapeDtypeStruct(small.shape, jnp.float32),
        ],
        in_specs=[ANY] * 4 + [vmem] * 2,
        out_specs=[vmem, ANY, vmem],
        scratch_shapes=[buffer(depth * 4), buffer(depth * 4), buffer(depth * 2)]
        + [buffer(depth)] * 3
        + [
            pltpu.VMEM((depth * 2,) + rows.shape, low),
            pltpu.VMEM((2, quarter, width), low),
            pltpu.VMEM((2, quarter, width), low),
            pltpu.VMEM((quarter, width), low),
            pltpu.VMEM((quarter, width), low),
            pltpu.VMEM((quarter, width), low),
            pltpu.VMEM((turns + 1,) + small.shape, jnp.float32),
            pltpu.VMEM((turns,) + small.shape, jnp.float32),
        ]
        + [dma((depth * 4, 3))] * 3
        + [dma((depth * 2,))] * 2
        + [dma((depth,))] * 6
        + [dma(())]
        + [dma((depth,))] * 3
        + [dma((depth * 2,))]
        + [dma((2,))] * 2
        + [dma(())] * 2
        + [dma((3,)), dma((4,))]
        + [dma((turns,))] * 2,
        compiler_params=pltpu.CompilerParams(
            collective_id=1, has_side_effects=True, vmem_limit_bytes=62 * 2**20
        ),
        name="finish",
    )(*pieces, rows, places, small)


def moments(gradient, first, second):
    first_new = beta_one * first + (1.0 - beta_one) * gradient
    second_new = beta_two * second + (1.0 - beta_two) * gradient * gradient
    second_hat = second_new * (1.0 / (1.0 - beta_two**STEP))
    root = second_hat * lax.rsqrt(second_hat) + adam_eps
    direction = first_new * (1.0 / (1.0 - beta_one**STEP)) / root
    return direction, first_new, second_new


def update_kernel(steps, cuts, *refs):
    table_ref, table_m_ref, table_v_ref, table_g_ref = refs[0:4]
    small_ref, sums_ref, gains_ref, gains_m_ref, gains_v_ref = refs[4:9]
    grad_ref, block_ref, block_m_ref, block_v_ref, bases_ref = refs[9:14]
    table_new, table_m_new, table_v_new, table_low = refs[14:18]
    values_ref, gains_new, gains_m_new, gains_v_new = refs[18:22]
    block_new, block_m_new, block_v_new, block_low = refs[22:26]
    bases, turned, factor_ref, chosen, bases_sem = refs[26:31]
    now = pl.program_id(0)

    def base(index):
        return pltpu.make_async_copy(bases_ref.at[index], bases.at[index], bases_sem.at[index])

    @pl.when(now == 0)
    def begin():
        for index in range(4):
            base(index).start()
        lines = lax.broadcasted_iota(jnp.int32, small_ref.shape, 0)
        lanes = lax.broadcasted_iota(jnp.int32, small_ref.shape, 1)

        def value_at(place):
            there = (lines == place // 128) & (lanes == place % 128)
            return jnp.sum(jnp.where(there, small_ref[...], 0.0), axis=(0, 1), keepdims=True)

        count = value_at(3 * D + 1)
        gain_grads = sums_ref[...] / count
        squares = value_at((small_ref.shape[0] - 1) * 128) / (count * count)
        norm = jnp.sqrt(squares + jnp.sum(gain_grads * gain_grads, axis=(0, 1), keepdims=True))
        clip = jnp.minimum(1.0, clip_norm / norm)
        factor_ref[...] = jnp.broadcast_to(clip / count, factor_ref.shape)
        spots = lax.broadcasted_iota(jnp.int32, values_ref.shape, 1)
        values_ref[...] = jnp.where(spots == 0, value_at(3 * D) / count, norm)
        direction, gains_m_new[...], gains_v_new[...] = moments(
            gain_grads * clip, gains_m_ref[...], gains_v_ref[...]
        )
        gains_new[...] = gains_ref[...] - rate_gain * direction

    factor = factor_ref[0:1, 0:1]
    direction, table_m_new[...], table_v_new[...] = moments(
        table_g_ref[...].astype(jnp.float32) * factor, table_m_ref[...], table_v_ref[...]
    )
    table_tile = table_ref[...]
    table_tile = table_tile - rate_table * (direction + decay_rate * table_tile)
    table_new[...] = table_tile
    table_low[...] = table_tile.astype(low)

    spots = lax.broadcasted_iota(jnp.int32, turned.shape, 1)

    def columns(index, value):
        mine = (spots >= cuts[index]) & (spots < cuts[index + 1])
        return jnp.where(mine, value, 0.0).astype(low)

    third = turned.shape[0] // 3
    for turn in range(12):
        index, lines = turn // 3, pl.ds(turn % 3 * third, third)

        @pl.when(now == min(4 + turn, steps - 1))
        def rotate():
            if turn % 3 == 0:
                base(index).wait()
                chosen[...] = columns(index, grad_ref[...] * factor_ref[0:1, 0:1])
            term = contract_rows(bases[index, :, lines].astype(low), chosen[...])
            turned[lines] = term if index == 0 else turned[lines] + term

    @pl.when(now == min(16, steps - 1))
    def move():
        direction, block_m_new[...], block_v_new[...] = moments(
            turned[...], block_m_ref[...], block_v_ref[...]
        )
        turned[...] = direction

    for turn in range(12):
        index, lines = turn // 3, pl.ds(turn % 3 * third, third)

        @pl.when(now == min(17 + turn, steps - 1))
        def rotate_back():
            if turn % 3 == 0:
                chosen[...] = columns(index, turned[...])
            term = product(bases[index, lines].astype(low), chosen[...])
            block_new[lines] = term if index == 0 else block_new[lines] + term

    @pl.when(now == min(29, steps - 1))
    def store():
        block = block_ref[...]
        block = block - rate_block * (block_new[...] + decay_rate * block)
        block_new[...] = block
        block_low[...] = block.astype(low)


def update(cuts, tables, table_grads, small, gain_sums, gains, block_grads, blocks, bases):
    rows, width = tables[0].shape
    tile = max(
        size
        for size in range(8, 101, 8)
        if rows % size == 0 and (size % 16 == 0 or rows % 16)
    )
    steps = rows // tile
    f32 = jnp.float32

    def whole(array):
        return pl.BlockSpec(array.shape, lambda i: (0,) * array.ndim)

    tiles = pl.BlockSpec((tile, width), lambda i: (i, 0))
    table = jax.ShapeDtypeStruct(tables[0].shape, f32)
    gain = jax.ShapeDtypeStruct(gains[0].shape, f32)
    matrix = jax.ShapeDtypeStruct(blocks[0].shape, f32)
    values = jax.ShapeDtypeStruct((8, 128), f32)
    outs = [table] * 3 + [jax.ShapeDtypeStruct(table.shape, low)]
    outs += [values] + [gain] * 3
    outs += [matrix] * 3 + [jax.ShapeDtypeStruct(matrix.shape, low)]
    return pl.pallas_call(
        functools.partial(update_kernel, steps, cuts),
        grid=(steps,),
        out_shape=outs,
        in_specs=[tiles] * 4
        + [whole(small), whole(gain_sums)]
        + [whole(gain)] * 3
        + [whole(matrix)] * 4
        + [ANY],
        out_specs=[tiles] * 4 + [whole(values)] + [whole(gain)] * 3 + [whole(matrix)] * 4,
        scratch_shapes=[
            pltpu.VMEM(bases.shape, f32),
            pltpu.VMEM(matrix.shape, f32),
            pltpu.VMEM((8, 128), f32),
            pltpu.VMEM(matrix.shape, low),
            pltpu.SemaphoreType.DMA((4,)),
        ],
        compiler_params=pltpu.CompilerParams(vmem_limit_bytes=58 * 2**20),
        name="update",
    )(*tables, table_grads, small, gain_sums, *gains, block_grads, *blocks, bases)


def cost(flops):
    return pl.CostEstimate(flops=flops, bytes_accessed=10**6, transcendentals=0)


LARGE = 58 * 2**20
CHUNK = 512


def inverse_rms(value):
    return lax.rsqrt(jnp.mean(value * value, axis=-1, keepdims=True) + eps_norm)


def norm_back(value, r, gain, grad):
    scaled = grad * gain
    d_value = r * scaled - value * (r * r * r) * jnp.mean(value * scaled, axis=-1, keepdims=True)
    return d_value, jnp.sum(grad * value * r, axis=0, keepdims=True)


def local_call(kernel, name, flops, outs, args, scratch=(), remain=()):
    vmem = pl.BlockSpec(memory_space=pltpu.VMEM)
    return pl.pallas_call(
        kernel,
        out_shape=[jax.ShapeDtypeStruct(shape, kind) for shape, kind in outs],
        in_specs=[ANY if place in remain else vmem for place in range(len(args))],
        out_specs=[vmem] * len(outs),
        scratch_shapes=list(scratch),
        compiler_params=pltpu.CompilerParams(vmem_limit_bytes=LARGE),
        cost_estimate=cost(flops),
        name=name,
    )(*args)


def project_kernel(hidden_ref, gain_ref, weight_ref, cosine_ref, sine_ref, *refs):
    normed_ref, query_ref, own_ref = refs
    hidden = hidden_ref[...]
    normed = (hidden * inverse_rms(hidden) * gain_ref[...]).astype(low)
    normed_ref[...] = normed
    cosine, sine = cosine_ref[...], sine_ref[...]
    first = lax.broadcasted_iota(jnp.int32, cosine.shape, 1) % HD < HD // 2
    for index in range(3 * D // 128):
        columns = pl.ds(index * 128, 128)
        value = contract_cols(normed, weight_ref[columns])
        if index < 2 * D // 128:
            turned = jnp.where(
                first, -pltpu.roll(value, 128 - HD // 2, 1), pltpu.roll(value, HD // 2, 1)
            )
            value = value * cosine + turned * sine
        if index < D // 128:
            query_ref[:, columns] = value.astype(low)
        else:
            own_ref[:, pl.ds(index * 128 - D, 128)] = value.astype(low)


def project(hidden, gain, weight, cosine, sine):
    rows = hidden.shape[0]
    outs = [((rows, D), low), ((rows, D), low), ((rows, 2 * D), low)]
    return local_call(project_kernel, "project", 6 * 10**9, outs, [hidden, gain, weight, cosine, sine])


def allowed(rows_ref, columns_ref):
    return (rows_ref[:, 0:1] == columns_ref[0:1]) & (rows_ref[:, 1:2] >= columns_ref[1:2])


def pair_of_heads(index):
    return pl.ds(index * 128, 128)


def attention_weight(query, keys, allow):
    score = jnp.where(allow, contract_cols(query, keys) * scale, -1e30)
    power = jnp.exp(score - jnp.max(score, axis=-1, keepdims=True))
    return power * (1.0 / jnp.sum(power, axis=-1, keepdims=True))


def forward_kernel(hidden_ref, query_ref, own_ref, far_ref, rows_ref, columns_ref, *refs):
    out_weight, gain_ref, gate_hbm, down_hbm, output_ref, merged_ref, middle_ref = refs[:7]
    gates, downs, sems = refs[7:]
    copies = weight_copies(gate_hbm, down_hbm, gates, downs, sems)
    for group in copies:
        for copy in group:
            copy.start()
    allow = allowed(rows_ref, columns_ref)
    rows = hidden_ref.shape[0]
    first = lax.broadcasted_iota(jnp.int32, (rows, 128), 1) < HD

    @pl.loop(0, D // 128)
    def heads(index):
        columns = pl.ds(pl.multiple_of(index * 128, 128), 128)
        values_at = pl.ds(pl.multiple_of(index * 128 + D, 128), 128)
        query = query_ref[:, columns]
        keys = jnp.concatenate([own_ref[:, columns], far_ref[:, columns]], axis=0)
        values = jnp.concatenate([own_ref[:, values_at], far_ref[:, values_at]], axis=0)
        mixed = []
        for side in range(2):
            mine = jnp.where(first == (side == 0), query, jnp.zeros_like(query))
            weight = attention_weight(mine, keys, allow).astype(low)
            mixed.append(product(weight, values))
        merged_ref[:, columns] = jnp.where(first, mixed[0], mixed[1]).astype(low)

    middle = hidden_ref[...] + contract_cols(merged_ref[...], out_weight[...])
    middle_ref[...] = middle
    normed = (middle * inverse_rms(middle) * gain_ref[...]).astype(low)
    output_ref[...] = middle
    for index, group in enumerate(copies):
        for copy in group:
            copy.wait()
        gate = contract_cols(normed, gates[pl.ds(index * CHUNK, CHUNK)])
        up = contract_cols(normed, gates[pl.ds(FF + index * CHUNK, CHUNK)])
        action = (gate * jax.nn.sigmoid(gate) * up).astype(low)
        output_ref[...] += product(action, downs[pl.ds(index * CHUNK, CHUNK)])


def weight_copies(gate_hbm, down_hbm, gates, downs, sems):
    groups = []
    for index in range(FF // CHUNK):
        parts = [
            (gate_hbm, gates, index * CHUNK),
            (gate_hbm, gates, FF + index * CHUNK),
            (down_hbm, downs, index * CHUNK),
        ]
        groups.append(
            [
                pltpu.make_async_copy(
                    source.at[pl.ds(at, CHUNK)], goal.at[pl.ds(at, CHUNK)], sems.at[index, place]
                )
                for place, (source, goal, at) in enumerate(parts)
            ]
        )
    return groups


def weight_buffers():
    return [
        pltpu.VMEM((2 * FF, D), low),
        pltpu.VMEM((FF, D), low),
        pltpu.SemaphoreType.DMA((FF // CHUNK, 3)),
    ]


def forward(hidden, query, own, far, rows, columns, w_out, gain, w_gu, w_down):
    count = hidden.shape[0]
    outs = [((count, D), jnp.float32), ((count, D), low), ((count, D), jnp.float32)]
    args = [hidden, query, own, far, rows, columns, w_out, gain, w_gu, w_down]
    return local_call(forward_kernel, "forward", 17 * 10**9, outs, args, weight_buffers(), (8, 9))


def backward_kernel(gradient_ref, middle_ref, query_ref, own_ref, far_ref, *refs):
    rows_ref, columns_ref, out_weight, gain_ref, gate_hbm, down_hbm = refs[:6]
    d_query_ref, d_own_ref, d_far_ref, d_middle_ref, gain_out = refs[6:11]
    low_ref, normed_ref, action_ref, d_gate_ref, middle_low_ref = refs[11:16]
    gates, downs, sems, total = refs[16:]
    copies = weight_copies(gate_hbm, down_hbm, gates, downs, sems)
    for group in copies:
        for copy in group:
            copy.start()
    gradient = gradient_ref[...]
    grad_low = gradient.astype(low)
    low_ref[...] = grad_low
    middle = middle_ref[...]
    r = inverse_rms(middle)
    normed = (middle * r * gain_ref[...]).astype(low)
    normed_ref[...] = normed
    total[...] = jnp.zeros_like(total)
    for index, group in enumerate(copies):
        for copy in group:
            copy.wait()
        first = pl.ds(index * CHUNK, CHUNK)
        second = pl.ds(FF + index * CHUNK, CHUNK)
        gate = contract_cols(normed, gates[first])
        up = contract_cols(normed, gates[second])
        chance = jax.nn.sigmoid(gate)
        action_ref[:, first] = (gate * chance * up).astype(low)
        d_action = contract_cols(grad_low, downs[first])
        d_gate = (d_action * up * (chance + gate * chance * (1.0 - chance))).astype(low)
        d_up = (d_action * gate * chance).astype(low)
        d_gate_ref[:, first] = d_gate
        d_gate_ref[:, second] = d_up
        total[...] += product(d_gate, gates[first]) + product(d_up, gates[second])
    d_middle, gain_out[...] = norm_back(middle, r, gain_ref[...], total[...])
    d_middle = gradient + d_middle
    d_middle_ref[...] = d_middle
    middle_low = d_middle.astype(low)
    middle_low_ref[...] = middle_low
    total[...] = product(middle_low, out_weight[...])
    allow = allowed(rows_ref, columns_ref)
    rows = gradient.shape[0]
    first = lax.broadcasted_iota(jnp.int32, (rows, 128), 1) < HD
    first_all = lax.broadcasted_iota(jnp.int32, (2 * rows, 128), 1) < HD

    @pl.loop(0, D // 128)
    def heads(index):
        columns = pl.ds(pl.multiple_of(index * 128, 128), 128)
        values_at = pl.ds(pl.multiple_of(index * 128 + D, 128), 128)
        query = query_ref[:, columns]
        upstream = total[:, columns].astype(low)
        keys = jnp.concatenate([own_ref[:, columns], far_ref[:, columns]], axis=0)
        values = jnp.concatenate([own_ref[:, values_at], far_ref[:, values_at]], axis=0)
        d_queries, d_keys, d_values = [], [], []
        for side in range(2):
            mine = jnp.where(first == (side == 0), query, jnp.zeros_like(query))
            grad = jnp.where(first == (side == 0), upstream, jnp.zeros_like(upstream))
            weight = attention_weight(mine, keys, allow)
            d_values.append(contract_rows(weight.astype(low), upstream))
            d_weight = contract_cols(grad, values)
            d_score = weight * (d_weight - jnp.sum(d_weight * weight, axis=-1, keepdims=True))
            d_score = d_score.astype(low)
            d_queries.append(product(d_score, keys) * scale)
            d_keys.append(contract_rows(d_score, query) * scale)
        d_query_ref[:, columns] = jnp.where(first, *d_queries).astype(low)
        d_key = jnp.where(first_all, *d_keys)
        d_value = jnp.where(first_all, *d_values)
        d_own_ref[:, columns] = d_key[:rows]
        d_own_ref[:, values_at] = d_value[:rows]
        d_far_ref[:, columns] = d_key[rows:].astype(low)
        d_far_ref[:, values_at] = d_value[rows:].astype(low)


def backward(gradient, middle, query, own, far, rows, columns, w_out, gain, w_gu, w_down):
    count = gradient.shape[0]
    f32 = jnp.float32
    outs = [
        ((count, D), low),
        ((count, 2 * D), f32),
        ((count, 2 * D), low),
        ((count, D), f32),
        ((1, D), f32),
        ((count, D), low),
        ((count, D), low),
        ((count, FF), low),
        ((count, 2 * FF), low),
        ((count, D), low),
    ]
    args = [gradient, middle, query, own, far, rows, columns, w_out, gain, w_gu, w_down]
    scratch = weight_buffers() + [pltpu.VMEM((count, D), f32)]
    return local_call(backward_kernel, "backward", 30 * 10**9, outs, args, scratch, (9, 10))


def unproject_kernel(d_query_ref, d_own_ref, d_far_ref, d_middle_ref, hidden_ref, *refs):
    gain_ref, weight_ref, cosine_ref, sine_ref, gradient_ref, gain_out, d_qkv_ref = refs
    cosine, sine = cosine_ref[...], sine_ref[...]
    first = lax.broadcasted_iota(jnp.int32, cosine.shape, 1) % HD < HD // 2
    for index in range(3 * D // 128):
        columns = pl.ds(index * 128, 128)
        if index < D // 128:
            value = d_query_ref[:, columns].astype(jnp.float32)
        else:
            there = pl.ds(index * 128 - D, 128)
            value = d_own_ref[:, there] + d_far_ref[:, there].astype(jnp.float32)
            value = value.astype(low).astype(jnp.float32)
        if index < 2 * D // 128:
            part = value * sine
            turned = jnp.where(
                first, pltpu.roll(part, 128 - HD // 2, 1), -pltpu.roll(part, HD // 2, 1)
            )
            value = value * cosine + turned
        d_qkv_ref[:, columns] = value.astype(low)
    hidden = hidden_ref[...]
    d_hidden, gain_out[...] = norm_back(
        hidden, inverse_rms(hidden), gain_ref[...], product(d_qkv_ref[...], weight_ref[...])
    )
    gradient_ref[...] = d_middle_ref[...] + d_hidden


def unproject(d_query, d_own, d_far, d_middle, hidden, gain, weight, cosine, sine):
    rows = hidden.shape[0]
    outs = [((rows, D), jnp.float32), ((1, D), jnp.float32), ((rows, 3 * D), low)]
    args = [d_query, d_own, d_far, d_middle, hidden, gain, weight, cosine, sine]
    return local_call(unproject_kernel, "unproject", 10**6, outs, args)


def weigh_kernel(*refs):
    pairs = [refs[4 * index : 4 * index + 4] for index in range(4)]
    outs = refs[16:20]
    now = pl.program_id(0)

    def gradient(index):
        left_one, left_two, right_one, right_two = pairs[index]
        total = contract_rows(left_one[...], right_one[...])
        total = total + contract_rows(left_two[...], right_two[...])
        outs[index][...] = total.astype(low).reshape(outs[index].shape)

    gradient(0)
    gradient(1)

    @pl.when(now < 6)
    def qkv():
        gradient(2)

    @pl.when(now >= 6)
    def out():
        gradient(3)


def weigh(d_gates, normed_twos, actions, lows, d_qkvs, normeds, middles, merges, blocks):
    rows = lows[0].shape[0]

    def both(arrays, width, place):
        return [(array, pl.BlockSpec((rows, width), place)) for array in arrays]

    def whole(arrays):
        return [(array, pl.BlockSpec((rows, D), lambda i: (0, 0))) for array in arrays]

    def early(i):
        return (0, jnp.minimum(i, 5))

    def late(i):
        return (0, jnp.maximum(i - 6, 0))

    listed = both(d_gates, 768, lambda i: (0, i)) + whole(normed_twos)
    listed += both(actions, 384, lambda i: (0, i)) + whole(lows)
    listed += both(d_qkvs, 384, early) + whole(normeds)
    listed += both(middles, 384, late) + whole(merges)
    part = blocks // 8
    return pl.pallas_call(
        weigh_kernel,
        grid=(8,),
        out_shape=[
            jax.ShapeDtypeStruct((blocks, 2 * FF // blocks, D), low),
            jax.ShapeDtypeStruct((blocks, FF // blocks, D), low),
            jax.ShapeDtypeStruct((3 * D, D), low),
            jax.ShapeDtypeStruct((D, D), low),
        ],
        in_specs=[spec for unused, spec in listed],
        out_specs=[
            pl.BlockSpec((part, 2 * FF // blocks, D), lambda i: (i, 0, 0)),
            pl.BlockSpec((part, FF // blocks, D), lambda i: (i, 0, 0)),
            pl.BlockSpec((384, D), lambda i: (jnp.minimum(i, 5), 0)),
            pl.BlockSpec((384, D), lambda i: (jnp.maximum(i - 6, 0), 0)),
        ],
        compiler_params=pltpu.CompilerParams(vmem_limit_bytes=LARGE),
        cost_estimate=cost(10**6),
        name="weigh",
    )(*[array for array, unused in listed])


def loss_kernel(hidden_ref, gain_ref, near_ref, far_ref, own_ref, other_ref, weight_ref, *refs):
    gradient_ref, gain_out, loss_ref, near_out, far_out, logits, teach = refs
    head = lax.axis_index("head")
    rows = hidden_ref.shape[0]
    half = rows // 2
    size = near_ref.shape[1]
    hidden = hidden_ref[...]
    r = inverse_rms(hidden)
    normed = (hidden * r * gain_ref[...]).astype(low)
    parts = [(near_ref, near_out, 0, 0), (near_ref, near_out, 1, 2)]
    parts += [(far_ref, far_out, 0, 1), (far_ref, far_out, 1, 3)]
    for index, (source, unused, place, offset) in enumerate(parts):
        columns = pl.ds(pl.multiple_of((head ^ offset) * size, size), size)
        logits[index] = contract_cols(normed, source[place])
        teach[index, :half] = own_ref[:, columns].astype(jnp.float32)
        teach[index, half:] = other_ref[:, columns].astype(jnp.float32)

    def log_total(values):
        summit = jnp.max(jnp.max(values[...], axis=0), axis=-1, keepdims=True)
        return summit + jnp.log(
            jnp.sum(jnp.sum(jnp.exp(values[...] - summit[None]), axis=0), axis=-1, keepdims=True)
        )

    log_logits, log_teach = log_total(logits), log_total(teach)
    weighting = weight_ref[...]
    gradient = jnp.zeros((rows, hidden.shape[1]), jnp.float32)
    loss = jnp.zeros((rows, 1), jnp.float32)
    for index, (source, goal, place, offset) in enumerate(parts):
        log_prob = logits[index] - log_logits
        log_true = teach[index] - log_teach
        true = jnp.exp(log_true)
        loss = loss + jnp.sum(true * (log_true - log_prob), axis=-1, keepdims=True)
        d_logits = ((jnp.exp(log_prob) - true) * weighting).astype(low)
        goal[place] = contract_rows(d_logits, normed).astype(low)
        gradient = gradient + product(d_logits, source[place])
    loss_ref[...] = jnp.broadcast_to(
        jnp.sum(loss * weighting, axis=0, keepdims=True), loss_ref.shape
    )
    gradient_ref[...], gain_out[...] = norm_back(hidden, r, gain_ref[...], gradient)


def distill(hidden, gain, near, far, own, other, weighting):
    rows, width = hidden.shape
    size = near.shape[1]
    vmem = pl.BlockSpec(memory_space=pltpu.VMEM)
    f32 = jnp.float32
    return pl.pallas_call(
        loss_kernel,
        out_shape=[
            jax.ShapeDtypeStruct(hidden.shape, f32),
            jax.ShapeDtypeStruct(gain.shape, f32),
            jax.ShapeDtypeStruct((8, 128), f32),
            jax.ShapeDtypeStruct(near.shape, low),
            jax.ShapeDtypeStruct(far.shape, low),
        ],
        in_specs=[vmem] * 7,
        out_specs=[vmem] * 5,
        scratch_shapes=[pltpu.VMEM((4, rows, size), f32)] * 2,
        compiler_params=pltpu.CompilerParams(vmem_limit_bytes=58 * 2**20),
        name="distill",
    )(hidden, gain, near, far, own, other, weighting)


def on_device(
    token_ids,
    lengths,
    valid,
    vocab_ids,
    teacher,
    block,
    block_m,
    block_v,
    bases,
    table,
    table_m,
    table_v,
    gains,
    gains_m,
    gains_v,
):
    dp_count, head_count = lax.axis_size("dp"), lax.axis_size("head")
    device_total = dp_count * head_count
    head, dp = lax.axis_index("head"), lax.axis_index("dp")
    batch = head // 2
    tokens = token_ids.shape[1]
    shard_rows = table.shape[0]
    offset = dp * shard_rows
    part = TOPV // device_total

    widths = [3 * D // device_total, D // device_total, 2 * FF // device_total, FF // device_total]
    cuts = [sum(widths[:index]) for index in range(5)]
    block_low = block.T.astype(low)
    attention, gate_up, down, rows_in, codes, near, far = start(
        [block_low[: cuts[2]], block_low[cuts[2] : cuts[3]], block_low[cuts[3] :]],
        table,
        (token_ids * 2 + valid).reshape(-1, 1, tokens),
        vocab_ids,
        dp_count,
    )
    codes = codes.reshape(dp_count, 2 * tokens)
    weighting = (lax.dynamic_index_in_dim(codes, dp, 0, keepdims=False) & 1).astype(jnp.float32)
    vocab = lax.dynamic_index_in_dim(
        vocab_ids.reshape(head_count, dp_count, part), head, 0, keepdims=False
    )
    local = jnp.concatenate([vocab, codes >> 1], axis=1) - offset
    owned = (local >= 0) & (local < shard_rows)
    weights = [
        attention[:, : cuts[1]].reshape(-1, D),
        attention[:, cuts[1] :].reshape(-1, D),
        gate_up.reshape(-1, D),
        down.reshape(-1, D),
    ]
    near = near.reshape(2, -1, D)
    far = far.reshape(2, -1, D)
    hidden = rows_in[part:].astype(jnp.float32)

    teacher_own = lax.dynamic_index_in_dim(teacher, batch, 0, keepdims=False)
    teacher_far = swap(
        lax.dynamic_index_in_dim(teacher, 1 - batch, 0, keepdims=False), head_count, 2
    )

    run = jnp.arange(tokens, dtype=jnp.int32)
    places = jnp.concatenate([head * tokens + run, (head ^ 2) * tokens + run])
    places_far = jnp.concatenate([(head ^ 1) * tokens + run, (head ^ 3) * tokens + run])
    own_lengths = lax.dynamic_index_in_dim(lengths, batch, 0, keepdims=False)[0]
    segment, position = segments(own_lengths, places)
    segment_far, unused = segments(own_lengths, places_far)
    queries_at = jnp.stack([segment, places], axis=1)
    keys_at = jnp.stack(
        [jnp.concatenate([segment, segment_far]), jnp.concatenate([places, places_far])]
    )
    freqs = jnp.exp(jnp.arange(0, HD, 2, dtype=jnp.float32) * (-math.log(10000.0) / HD))
    angle = position.astype(jnp.float32)[:, None] * jnp.tile(freqs, 4)[None, :]
    cosine, sine = jnp.cos(angle), jnp.sin(angle)

    w_qkv, w_out, w_gu, w_down = weights
    saves = []
    for repeat in range(2):
        normed, query, own = project(hidden, gains[0:1], w_qkv, cosine, sine)
        other = swap(own, head_count, 1)
        output, merged, middle = forward(
            hidden, query, own, other, queries_at, keys_at, w_out, gains[1:2], w_gu, w_down
        )
        saves.append((hidden, normed, query, own, other, merged, middle))
        hidden = output

    gradient, d_gain_final, loss_sum, d_near, d_far = distill(
        hidden, gains[2:3], near, far, teacher_own, teacher_far, weighting[:, None]
    )
    d_gain_final, loss_sum = d_gain_final[0], loss_sum[0, 0]
    f32 = jnp.float32
    gradient, d_far = lax.optimization_barrier((gradient, swap(d_far, head_count, 1)))
    d_near = (d_near.astype(f32) + d_far.astype(f32)).astype(low)
    d_quarter = swap(d_near[1], head_count, 2)

    d_gains = [0.0, 0.0]
    parts = []
    for repeat in range(2):
        hidden, normed, query, own, other, merged, middle = saves[1 - repeat]
        back = backward(
            gradient, middle, query, own, other, queries_at, keys_at, w_out, gains[1:2], w_gu, w_down
        )
        d_query, d_own, d_other, d_middle, d_gain_two = back[:5]
        grad_low, normed_two, action, d_gate, middle_low = back[5:]
        gradient, d_gain_one, d_qkv = unproject(
            d_query,
            d_own,
            swap(d_other, head_count, 1),
            d_middle,
            hidden,
            gains[0:1],
            w_qkv,
            cosine,
            sine,
        )
        if repeat == 0:
            gradient, d_quarter = lax.optimization_barrier((gradient, d_quarter))
            d_quarter = (d_near[0].astype(f32) + d_quarter.astype(f32)).astype(low)
            chosen_grads = lax.psum_scatter(d_quarter, "dp", scatter_dimension=0, tiled=True)
        parts.append((d_gate, normed_two, action, grad_low, d_qkv, normed, middle_low, merged))
        d_gains = [d_gains[0] + d_gain_one[0], d_gains[1] + d_gain_two[0]]

    d_gu, d_down, d_qkv, d_out = weigh(*zip(*parts), device_total)
    d_qkv, d_out = [piece.reshape(device_total, -1, D) for piece in (d_qkv, d_out)]
    rows_back = jnp.concatenate([chosen_grads, gradient.astype(low)], axis=0)
    step = 80 if shard_rows % 80 == 0 else 40
    quarter = -(-shard_rows // (step * head_count)) * step
    tile = quarter // 5 if quarter % 80 == 0 and quarter // 5 % 16 == 0 else step
    small = [d_gains[0], d_gains[1], d_gain_final, loss_sum[None], jnp.sum(weighting)[None]]
    small = jnp.pad(jnp.concatenate(small), (0, 6 * 128 - 2)).reshape(-1, 128)
    block_grads, table_grads, small = finish(
        [jnp.concatenate([d_qkv, d_out], axis=1), d_gu, d_down],
        rows_back,
        jnp.where(owned, local, -1).reshape(1, -1),
        small,
        quarter,
        tile,
    )
    outs = update(
        cuts,
        [table, table_m, table_v],
        table_grads.reshape(-1, D),
        small,
        small[: 3 * D // 128].reshape(3, D),
        [gains, gains_m, gains_v],
        block_grads.T,
        [block, block_m, block_v],
        bases,
    )
    table_new, table_m_new, table_v_new, table_low = outs[0:4]
    values, gains_new, gains_m_new, gains_v_new = outs[4:8]
    block_new, block_m_new, block_v_new, block_low = outs[8:12]
    return (
        values[0, 0],
        values[0, 1],
        block_new,
        block_m_new,
        block_v_new,
        table_new,
        table_m_new,
        table_v_new,
        gains_new,
        gains_m_new,
        gains_v_new,
        block_low,
        table_low,
    )


def solution(mesh):
    tokens = P(None, ("dp", "head"))
    columns = P(None, ("dp", "head"))
    table = P("dp", None)
    return jax.shard_map(
        on_device,
        mesh=mesh,
        in_specs=(
            tokens,
            P(None, "dp", None),
            tokens,
            P(),
            P(None, ("dp", "head"), None),
            columns,
            columns,
            columns,
            P(),
            table,
            table,
            table,
            P(),
            P(),
            P(),
        ),
        out_specs=(
            P(),
            P(),
            columns,
            columns,
            columns,
            table,
            table,
            table,
            P(),
            P(),
            P(),
            columns,
            table,
        ),
        check_vma=False,
    )
```

```python
import functools
import math

import jax
import jax.numpy as jnp
from jax import lax
from jax.experimental import pallas as pl
from jax.experimental.pallas import tpu as pltpu
from jax.sharding import PartitionSpec as P

D = 768
H = 12
HD = 64
FF = 3072
TOPV = 4096
STEP = 5

low = jnp.bfloat16
scale = HD**-0.5
eps_norm = 1e-05
clip_norm = 0.002
beta_one = 0.9
beta_two = 0.99
adam_eps = 1e-08
decay_rate = 0.1
rate_block = 0.03
rate_table = 0.05
rate_gain = 0.4


def product(left, right):
    return jnp.dot(left, right, preferred_element_type=jnp.float32)


def contract_rows(left, right):
    return lax.dot_general(
        left, right, (((0,), (0,)), ((), ())), preferred_element_type=jnp.float32
    )


def contract_cols(left, right):
    return lax.dot_general(
        left, right, (((1,), (1,)), ((), ())), preferred_element_type=jnp.float32
    )


def segments(lengths, places):
    segment = jnp.zeros_like(places)
    begin = jnp.zeros_like(places)
    end = jnp.zeros((), jnp.int32)
    for index in range(lengths.shape[0] - 1):
        end = end + lengths[index]
        past = places >= end
        segment = segment + past.astype(jnp.int32)
        begin = jnp.where(past, end, begin)
    return segment, places - begin


def swap(value, head_count, offset):
    return lax.ppermute(value, "head", [(h, h ^ offset) for h in range(head_count)])


MESH = pl.DeviceIdType.MESH
ANY = pl.BlockSpec(memory_space=pl.ANY)


def coordinates(depth):
    dp, head = lax.axis_index("dp"), lax.axis_index("head")
    return dp // 2, dp % 2, head // 2, head % 2


def device(z, x, y, c):
    return (z * 2 + x, y * 2 + c)


def slot(z, x, y, c):
    return ((z * 2 + x) * 2 + y) * 2 + c


def greet(depth, z, x, y, c):
    barrier = pltpu.get_barrier_semaphore()
    for target in (device(z, 1 - x, y, c), device(z, x, 1 - y, c), device(z, x, y, 1 - c)):
        pl.semaphore_signal(barrier, 1, device_id=target, device_id_type=MESH)

    @pl.when(z > 0)
    def below():
        pl.semaphore_signal(barrier, 1, device_id=device(z - 1, x, y, c), device_id_type=MESH)

    @pl.when(z < depth - 1)
    def above():
        pl.semaphore_signal(barrier, 1, device_id=device(z + 1, x, y, c), device_id_type=MESH)

    pl.semaphore_wait(barrier, 3 + jnp.where(z > 0, 1, 0) + jnp.where(z < depth - 1, 1, 0))


def start_kernel(depth, *refs):
    pieces = refs[0:4]
    table_ref, codes_ref, vocab_ref = refs[4:7]
    wholes = refs[7:11]
    sum_ref, ids_ref, near_ref, far_ref = refs[11:15]
    far_x, from_low, from_high, total, rows_ref, shard, ids = refs[15:22]
    local_sem, up_sem, down_sem, x_sem, y_sem, c_sem, block_sem = refs[22:29]
    rx_send, rx_recv, ru_send, ru_recv, rd_send, rd_recv = refs[29:35]
    id_send, id_recv, table_sem, copy_sem = refs[35:39]
    su_send, sd_send, sx_send, sy_send, sc_send, s_recv, keep_sem = refs[39:46]
    z, x, y, c = coordinates(depth)
    mine = slot(z, x, y, c)
    dp, head = z * 2 + x, y * 2 + c
    groups, height = rows_ref.shape[:2]
    shard_rows, tokens = table_ref.shape[0], codes_ref.shape[2]
    part = height - 2 * tokens
    offset = dp * shard_rows
    barrier = pltpu.get_barrier_semaphore()
    pl.semaphore_signal(barrier, 1, device_id=device(z, x, y, 1 - c), device_id_type=MESH)
    for group in range(groups):
        for rank in range(2):

            @pl.when((group != dp) | (rank != y))
            def hello():
                pl.semaphore_signal(
                    barrier, 1, device_id=(group, rank * 2 + c), device_id_type=MESH
                )

    pl.semaphore_wait(barrier, groups * 2)

    def tell(group, rank):
        second = jnp.where(rank == y, 0, 1)
        return pltpu.make_async_remote_copy(
            codes_ref.at[rank],
            ids_ref.at[dp, second],
            id_send.at[group, rank],
            id_recv.at[dp, second],
            device_id=(group, rank * 2 + c),
            device_id_type=MESH,
        )

    def told(group, second):
        return pltpu.make_async_remote_copy(
            codes_ref.at[0],
            ids_ref.at[group, second],
            id_send.at[group, second],
            id_recv.at[group, second],
            device_id=device(z, x, y, 1 - c),
            device_id_type=MESH,
        )

    keep = pltpu.make_async_copy(codes_ref.at[y], ids_ref.at[dp, 0], copy_sem)
    fetch = pltpu.make_async_copy(table_ref, shard.at[pl.ds(0, shard_rows)], table_sem)
    fetch.start()
    keep.start()
    for group in range(groups):
        for rank in range(2):

            @pl.when((group != dp) | (rank != y))
            def telling():
                tell(group, rank).start()

    def gather(stage, group):
        def load(first, read):
            @pl.loop(0, (tokens if first else part) // 16)
            def some(index):
                base = index * 16
                lines = []
                for line in range(16):
                    place = read(base + line) - offset
                    held = (place >= 0) & (place < shard_rows)
                    lines.append(shard[pl.ds(jnp.where(held, place, shard_rows), 1)])
                rows_ref[group, pl.ds(pl.multiple_of(first + base, 16), 16)] = jnp.concatenate(
                    lines, axis=0
                ).astype(low)

        if stage == 0:
            load(0, lambda index: vocab_ref[(head * groups + group) * part + index])
        for second in range(2 if stage else 0):
            load(part + second * tokens, lambda index: ids[group, second, 0, index] >> 1)

    def own(block, piece, target, sem):
        return pltpu.make_async_remote_copy(
            pieces[piece],
            wholes[piece].at[block],
            sem.at[piece],
            block_sem.at[block, piece],
            device_id=target,
            device_id_type=MESH,
        )

    def onward(block, piece, target, sem):
        return pltpu.make_async_remote_copy(
            wholes[piece].at[block],
            wholes[piece].at[block],
            sem.at[piece],
            block_sem.at[block, piece],
            device_id=target,
            device_id_type=MESH,
        )

    def send(make, block, target, sem):
        for piece in range(4):
            make(block, piece, target, sem).start()

    def arrive(block):
        for piece in range(4):
            onward(block, piece, device(z, x, y, 1 - c), c_sem.at[0]).wait_recv()

    across_x, across_y, across_c = (
        device(z, 1 - x, y, c),
        device(z, x, 1 - y, c),
        device(z, x, y, 1 - c),
    )
    spans = (pl.ds(0, part), pl.ds(part, 2 * tokens))

    def rows_x(stage, goal):
        return pltpu.make_async_remote_copy(
            rows_ref.at[goal * 2 + 1 - x, spans[stage]],
            far_x.at[goal, spans[stage]],
            rx_send.at[stage, goal],
            rx_recv.at[stage, goal],
            device_id=across_x,
            device_id_type=MESH,
        )

    def rows_up(stage, goal):
        return pltpu.make_async_remote_copy(
            total.at[goal, spans[stage]],
            from_low.at[goal, spans[stage]],
            ru_send.at[stage, goal],
            ru_recv.at[stage, goal],
            device_id=device(z + 1, x, y, c),
            device_id_type=MESH,
        )

    def rows_down(stage, goal):
        return pltpu.make_async_remote_copy(
            total.at[goal, spans[stage]],
            from_high.at[goal, spans[stage]],
            rd_send.at[stage, goal],
            rd_recv.at[stage, goal],
            device_id=device(z - 1, x, y, c),
            device_id_type=MESH,
        )

    goals = [
        goal for pair in zip(range(depth // 2), range(depth - 1, 0, -1)) for goal in pair
    ]
    goals += [goal for goal in range(depth) if goal not in goals]

    def reduce(stage):
        span = spans[stage]
        for goal in goals:
            rows_x(stage, goal).wait_recv()
            both = rows_ref[goal * 2 + x, span] + far_x[goal, span]

            @pl.when(goal > z)
            def rising():
                @pl.when(z > 0)
                def more():
                    rows_up(stage, goal).wait_recv()
                    total[goal, span] = both + from_low[goal, span]

                @pl.when(z == 0)
                def alone():
                    total[goal, span] = both

                rows_up(stage, goal).start()

            @pl.when(goal < z)
            def falling():
                @pl.when(z < depth - 1)
                def more():
                    rows_down(stage, goal).wait_recv()
                    total[goal, span] = both + from_high[goal, span]

                @pl.when(z == depth - 1)
                def alone():
                    total[goal, span] = both

                rows_down(stage, goal).start()

            @pl.when(goal == z)
            def here():
                total[goal, span] = both

    def land(stage):
        span = spans[stage]
        for goal in range(depth):

            @pl.when(goal == z)
            def landed():
                @pl.when(z > 0)
                def low_part():
                    rows_up(stage, goal).wait_recv()
                    total[goal, span] = total[goal, span] + from_low[goal, span]

                @pl.when(z < depth - 1)
                def high_part():
                    rows_down(stage, goal).wait_recv()
                    total[goal, span] = total[goal, span] + from_high[goal, span]

                sum_ref[span] = total[goal, span]

    local = [
        pltpu.make_async_copy(pieces[piece], wholes[piece].at[mine], local_sem.at[piece])
        for piece in range(4)
    ]
    send(own, mine, across_y, y_sem.at[mine // 4])

    @pl.when(z < depth - 1)
    def first_up():
        send(own, mine, device(z + 1, x, y, c), up_sem.at[0])

    @pl.when(z > 0)
    def first_down():
        send(own, mine, device(z - 1, x, y, c), down_sem.at[0])

    send(own, mine, across_x, x_sem.at[z])
    send(own, mine, across_c, c_sem.at[mine // 2])
    for copy in local:
        copy.start()
    shard[pl.ds(shard_rows, 8)] = jnp.zeros((8, shard.shape[1]), jnp.float32)
    fetch.wait()
    for goal in goals:
        gather(0, goal * 2 + 1 - x)
        rows_x(0, goal).start()
    for goal in goals:
        gather(0, goal * 2 + x)
    keep.wait()
    for group in range(groups):
        for second in range(2):

            @pl.when((group != dp) | (second != 0))
            def heard():
                told(group, second).wait_recv()

    to_scalars = pltpu.make_async_copy(ids_ref, ids, copy_sem)
    to_scalars.start()

    def spread(block, over_x):
        send(onward, block, across_y, y_sem.at[block // 4])
        if over_x:
            send(onward, block, across_x, x_sem.at[block // 8])
        send(onward, block, across_c, c_sem.at[block // 2])

    def pass_on(step):
        @pl.when(z - step >= 0)
        def risen():
            block = slot(z - step, x, y, c)
            arrive(block)

            @pl.when(z < depth - 1)
            def further():
                send(onward, block, device(z + 1, x, y, c), up_sem.at[step])

            spread(block, True)

        @pl.when(z + step < depth)
        def fallen():
            block = slot(z + step, x, y, c)
            arrive(block)

            @pl.when(z > 0)
            def further():
                send(onward, block, device(z - 1, x, y, c), down_sem.at[step])

            spread(block, True)

    def crossed(step):
        for sign in (1, -1) if step else (1,):

            @pl.when((z + sign * step >= 0) & (z + sign * step < depth))
            def there():
                block = slot(z + sign * step, 1 - x, y, c)
                arrive(block)
                spread(block, False)

    pass_on(1)
    to_scalars.wait()
    for goal in goals:
        gather(1, goal * 2 + 1 - x)
        rows_x(1, goal).start()
    for step in range(2, min(depth, 3)):
        pass_on(step)
    reduce(0)
    for goal in goals:
        gather(1, goal * 2 + x)
    for step in range(3, depth):
        pass_on(step)
    land(0)

    def shared(source, ref, quarter, group, send_sem, target):
        where = ref.at[quarter, group]
        return pltpu.make_async_remote_copy(
            where if source is None else source,
            where,
            send_sem,
            s_recv.at[quarter if ref is near_ref else 2 + quarter, group],
            device_id=target,
            device_id_type=MESH,
        )

    own_shared = sum_ref.at[pl.ds(0, part)]
    keep_shared = pltpu.make_async_copy(own_shared, near_ref.at[0, dp], keep_sem)
    keep_shared.start()

    def plane(group):
        return near_ref.at[0, group]

    def shared_y(source, group):
        return pltpu.make_async_remote_copy(
            source,
            near_ref.at[1, group],
            sy_send.at[group],
            s_recv.at[1, group],
            device_id=across_y,
            device_id_type=MESH,
        )

    def shared_c(source, quarter, group):
        return pltpu.make_async_remote_copy(
            source,
            far_ref.at[quarter, group],
            sc_send.at[quarter, group],
            s_recv.at[2 + quarter, group],
            device_id=across_c,
            device_id_type=MESH,
        )

    @pl.when(z < depth - 1)
    def shared_up():
        shared(own_shared, near_ref, 0, dp, su_send.at[0], device(z + 1, x, y, c)).start()

    @pl.when(z > 0)
    def shared_down():
        shared(own_shared, near_ref, 0, dp, sd_send.at[0], device(z - 1, x, y, c)).start()

    shared(own_shared, near_ref, 0, dp, sx_send.at[z], across_x).start()
    shared_y(own_shared, dp).start()
    shared_c(own_shared, 0, dp).start()
    for step in range(1, depth):

        @pl.when(z - step >= 0)
        def shared_risen():
            group = (z - step) * 2 + x
            copy = shared(
                None, near_ref, 0, group, su_send.at[step], device(z + 1, x, y, c)
            )
            copy.wait_recv()

            @pl.when(z < depth - 1)
            def further():
                copy.start()

            shared(None, near_ref, 0, group, sx_send.at[z - step], across_x).start()
            shared_y(plane(group), group).start()
            shared_c(plane(group), 0, group).start()

        @pl.when(z + step < depth)
        def shared_fallen():
            group = (z + step) * 2 + x
            copy = shared(
                None, near_ref, 0, group, sd_send.at[step], device(z - 1, x, y, c)
            )
            copy.wait_recv()

            @pl.when(z > 0)
            def further():
                copy.start()

            shared(None, near_ref, 0, group, sx_send.at[z + step], across_x).start()
            shared_y(plane(group), group).start()
            shared_c(plane(group), 0, group).start()

    crossed(0)
    reduce(1)
    for step in range(1, depth):
        crossed(step)
    for place in range(depth):
        group = place * 2 + 1 - x
        shared(None, near_ref, 0, group, sx_send.at[place], across_x).wait_recv()
        shared_y(plane(group), group).start()
        shared_c(plane(group), 0, group).start()
    land(1)

    for step in range(depth):
        for sign in (1, -1) if step else (1,):

            @pl.when((z + sign * step >= 0) & (z + sign * step < depth))
            def level():
                for side in (x, 1 - x):
                    block = slot(z + sign * step, side, 1 - y, c)
                    arrive(block)
                    send(onward, block, across_c, c_sem.at[block // 2])

    for group in range(groups):
        shared_y(plane(group), group).wait_recv()
        shared_c(near_ref.at[1, group], 1, group).start()

    for block in range(depth * 8):

        @pl.when(block % 2 != c)
        def from_core():
            arrive(block)

    for group in range(groups):
        for quarter in range(2):
            shared_c(near_ref.at[quarter, group], quarter, group).wait_recv()

    keep_shared.wait()
    for group in range(groups):
        shared_y(plane(group), group).wait_send()
        for quarter in range(2):
            shared_c(near_ref.at[quarter, group], quarter, group).wait_send()
    for place in range(depth):
        shared(None, near_ref, 0, dp, sx_send.at[place], across_x).wait_send()

        @pl.when((z - place >= 0) & (z < depth - 1))
        def shared_rose():
            shared(None, near_ref, 0, dp, su_send.at[place], across_x).wait_send()

        @pl.when((z + place < depth) & (z > 0))
        def shared_fell():
            shared(None, near_ref, 0, dp, sd_send.at[place], across_x).wait_send()

    for copy in local:
        copy.wait()
    for group in range(groups):
        for rank in range(2):

            @pl.when((group != dp) | (rank != y))
            def spoken():
                tell(group, rank).wait_send()

    for goal in range(depth):
        for stage in range(2):
            rows_x(stage, goal).wait_send()

            @pl.when(goal > z)
            def rose():
                rows_up(stage, goal).wait_send()

            @pl.when(goal < z)
            def fell():
                rows_down(stage, goal).wait_send()

    def sent(block, target, sem):
        for piece in range(4):
            onward(block, piece, target, sem).wait_send()

    for step in range(depth):

        @pl.when((z - step >= 0) & (z < depth - 1))
        def rose():
            sent(mine, device(z + 1, x, y, c), up_sem.at[step])

        @pl.when((z + step < depth) & (z > 0))
        def fell():
            sent(mine, device(z - 1, x, y, c), down_sem.at[step])

        sent(mine, across_x, x_sem.at[step])
    for index in range(depth * 2):
        sent(mine, across_y, y_sem.at[index])
    for index in range(depth * 4):
        sent(mine, across_c, c_sem.at[index])


def start(pieces, table, codes, vocab_ids, groups):
    width = table.shape[1]
    height = vocab_ids.shape[0] // (groups * 4) + 2 * codes.shape[2]
    depth = groups // 2
    blocks = depth * 8
    told = (groups, 2, 1, codes.shape[2])
    dma = pltpu.SemaphoreType.DMA
    buffer = pltpu.VMEM((depth, height, width), low)
    return pl.pallas_call(
        functools.partial(start_kernel, depth),
        out_shape=[jax.ShapeDtypeStruct((blocks,) + piece.shape, low) for piece in pieces]
        + [jax.ShapeDtypeStruct((height, width), low), jax.ShapeDtypeStruct(told, jnp.int32)]
        + [jax.ShapeDtypeStruct((2, groups, vocab_ids.shape[0] // blocks, width), low)] * 2,
        in_specs=[ANY] * 5
        + [pl.BlockSpec(memory_space=pltpu.VMEM), pl.BlockSpec(memory_space=pltpu.SMEM)],
        out_specs=[ANY] * 4 + [pl.BlockSpec(memory_space=pltpu.VMEM)] * 2 + [ANY] * 2,
        scratch_shapes=[buffer] * 4
        + [
            pltpu.VMEM((groups, height, width), low),
            pltpu.VMEM((table.shape[0] + 8, width), jnp.float32),
            pltpu.SMEM(told, jnp.int32),
        ]
        + [dma((4,))]
        + [dma((depth, 4))] * 3
        + [dma((depth * 2, 4)), dma((depth * 4, 4)), dma((blocks, 4))]
        + [dma((2, depth))] * 6
        + [dma((groups, 2))] * 2
        + [dma(())] * 2
        + [dma((depth,))] * 3
        + [dma((groups,)), dma((2, groups)), dma((4, groups)), dma(())],
        compiler_params=pltpu.CompilerParams(
            collective_id=0, has_side_effects=True, vmem_limit_bytes=58 * 2**20
        ),
        name="start",
    )(*pieces, table, codes, vocab_ids)


def by_distance(depth, z, act):
    for step in range(depth - 1, -1, -1):
        for sign in (1, -1) if step else (1,):

            @pl.when((z + sign * step >= 0) & (z + sign * step < depth))
            def reached():
                act(z + sign * step)


def add_into(total, block, *terms):
    height = total.shape[1]
    chunk = 96 if height % 96 == 0 else height

    @pl.loop(0, height // chunk)
    def chunks(index):
        part = pl.ds(pl.multiple_of(index * chunk, chunk), chunk)
        value = total[block, part].astype(jnp.float32)
        for buffer, place in terms:
            value = value + buffer[place, part].astype(jnp.float32)
        total[block, part] = value.astype(low)


def finish_kernel(depth, heights, tile, *refs):
    pieces = refs[0:3]
    rows_ref, places_ref, small_ref = refs[3:6]
    grad_ref, table_out, small_out = refs[6:9]
    total, far_c, far_p, far_s, from_low, from_high = refs[9:15]
    rows, given, far_t, part, mine, far_part, small, far_small = refs[15:23]
    local_sem, c_send, c_recv, p_send, p_recv, s_send, s_recv = refs[23:30]
    u_send, u_recv, d_send, d_recv = refs[30:34]
    own_sem, ru_send, rd_send, rx_send, r_recv = refs[34:39]
    t_send, t_recv, ty_send, ty_recv, o_send, o_recv, e_send, e_recv = refs[39:47]
    z, x, y, c = coordinates(depth)
    dp = z * 2 + x
    firsts = [sum(heights[:index]) for index in range(3)]
    up, down = device(z + 1, x, y, c), device(z - 1, x, y, c)
    across_x, across_y, across_c = (
        device(z, 1 - x, y, c),
        device(z, x, 1 - y, c),
        device(z, x, y, 1 - c),
    )
    even = c == 0
    across_p = tuple(jnp.where(even, a, b) for a, b in zip(across_y, across_x))
    across_s = tuple(jnp.where(even, b, a) for a, b in zip(across_y, across_x))
    own_p, own_s = jnp.where(even, y, x), jnp.where(even, x, y)
    partners = [across_c, across_y, across_x]
    reach = 1
    while reach < depth:
        partners.append(device(z ^ reach, x, y, c))
        reach = reach * 2

    barrier = pltpu.get_barrier_semaphore()
    for target in partners[:3] + partners[4:]:
        pl.semaphore_signal(barrier, 1, device_id=target, device_id_type=MESH)

    @pl.when(z > 0)
    def below():
        pl.semaphore_signal(barrier, 1, device_id=down, device_id_type=MESH)

    @pl.when(z < depth - 1)
    def above():
        pl.semaphore_signal(barrier, 1, device_id=up, device_id_type=MESH)

    pl.semaphore_wait(
        barrier, len(partners) - 1 + jnp.where(z > 0, 1, 0) + jnp.where(z < depth - 1, 1, 0)
    )

    def remote(source, goal, send_sem, recv_sem, target):
        return pltpu.make_async_remote_copy(
            source, goal, send_sem, recv_sem, device_id=target, device_id_type=MESH
        )

    def block_of(place, s, p):
        return place * 4 + jnp.where(even, s * 2 + p, p * 2 + s)

    def local(block, piece):
        return pltpu.make_async_copy(
            pieces[piece].at[block * 2 + c],
            total.at[block, pl.ds(firsts[piece], heights[piece])],
            local_sem.at[block, piece],
        )

    def over_c(block, piece):
        return remote(
            pieces[piece].at[block * 2 + 1 - c],
            far_c.at[block, pl.ds(firsts[piece], heights[piece])],
            c_send.at[block, piece],
            c_recv.at[block, piece],
            across_c,
        )

    def over_p(place, s):
        pair = place * 2 + s
        return remote(
            total.at[block_of(place, s, 1 - own_p)],
            far_p.at[pair],
            p_send.at[pair],
            p_recv.at[pair],
            across_p,
        )

    def over_s(place):
        return remote(
            total.at[block_of(place, 1 - own_s, own_p)],
            far_s.at[place],
            s_send.at[place],
            s_recv.at[place],
            across_s,
        )

    def rise(place):
        block = block_of(place, own_s, own_p)
        return remote(
            total.at[block], from_low.at[place], u_send.at[place], u_recv.at[place], up
        )

    def fall(place):
        block = block_of(place, own_s, own_p)
        return remote(
            total.at[block], from_high.at[place], d_send.at[place], d_recv.at[place], down
        )

    def own_rows(send_sem, target):
        return remote(rows_ref, rows.at[dp], send_sem, r_recv.at[dp], target)

    def rows_on(place, send_sem, target):
        there = place * 2 + x
        return remote(rows.at[there], rows.at[there], send_sem, r_recv.at[there], target)

    own = pltpu.make_async_copy(rows_ref, rows.at[dp], own_sem)
    own.start()

    @pl.when(z < depth - 1)
    def first_up():
        own_rows(ru_send.at[0], up).start()

    @pl.when(z > 0)
    def first_down():
        own_rows(rd_send.at[0], down).start()

    own_rows(rx_send.at[z], across_x).start()

    for turn in range(2):
        for s, s_there in ((1 - own_s, 1 - own_p), (own_s, own_p)):
            p, p_there = (1 - own_p, 1 - own_s) if turn == 0 else (own_p, own_s)

            def launch(place):
                for piece in range(3):
                    over_c(
                        place * 4 + jnp.where(even, p_there * 2 + s_there, s_there * 2 + p_there),
                        piece,
                    ).start()
                    local(block_of(place, s, p), piece).start()

            by_distance(depth, z, launch)

    def ready(block):
        for piece in range(3):
            local(block, piece).wait()
            over_c(block, piece).wait_recv()

    def give_p():
        for s in (1 - own_s, own_s):

            def give(place):
                block = block_of(place, s, 1 - own_p)
                ready(block)
                add_into(total, block, (far_c, block))
                over_p(place, s).start()

            by_distance(depth, z, give)

    @pl.when(even)
    def early():
        give_p()

    for step in range(1, depth):

        @pl.when(z - step >= 0)
        def risen():
            rows_on(z - step, ru_send.at[step], up).wait_recv()

            @pl.when(z < depth - 1)
            def further():
                rows_on(z - step, ru_send.at[step], up).start()

            rows_on(z - step, rx_send.at[z - step], across_x).start()

        @pl.when(z + step < depth)
        def fallen():
            rows_on(z + step, rd_send.at[step], down).wait_recv()

            @pl.when(z > 0)
            def further():
                rows_on(z + step, rd_send.at[step], down).start()

            rows_on(z + step, rx_send.at[z + step], across_x).start()

    @pl.when(c == 1)
    def late():
        give_p()

    own.wait()
    for place in range(depth):
        there = place * 2 + 1 - x
        remote(
            rows.at[there], rows.at[there], rx_send.at[place], r_recv.at[there], across_x
        ).wait_recv()

    height = part.shape[0]
    count = places_ref.shape[1]

    def collect(rank, core, goal):
        @pl.loop(0, height // tile)
        def tiles(index):
            first = index * tile
            at = (
                (rank * 2 + core) * height
                + first
                + lax.broadcasted_iota(jnp.int32, (tile, count), 0)
            )
            picked = jnp.where(at == places_ref[...], 1.0, 0.0).astype(low)
            goal[pl.ds(pl.multiple_of(first, tile), tile)] = product(
                picked, rows[...].reshape(count, rows.shape[2])
            ).astype(low)

    def over_t(rank):
        index = jnp.where(rank == y, 1, 0)
        return remote(
            given.at[index], far_t.at[index], t_send.at[index], t_recv.at[index], across_c
        )

    chunk = 80 if height % 80 == 0 else height

    def pieces_of(act):
        @pl.loop(0, height // chunk)
        def step(index):
            act(pl.ds(pl.multiple_of(index * chunk, chunk), chunk))

    collect(1 - y, 1 - c, given.at[0])
    over_t(1 - y).start()
    collect(y, 1 - c, given.at[1])
    over_t(y).start()
    collect(1 - y, c, part)
    over_t(1 - y).wait_recv()

    def first_sum(lines):
        part[lines] = (part[lines].astype(jnp.float32) + far_t[0, lines].astype(jnp.float32)).astype(
            low
        )

    pieces_of(first_sum)
    over_part = remote(part, far_part, ty_send, ty_recv, across_y)
    over_part.start()
    collect(y, c, mine)

    def give_s(place):
        block = block_of(place, 1 - own_s, own_p)
        ready(block)
        over_p(place, 1 - own_s).wait_recv()
        add_into(total, block, (far_c, block), (far_p, place * 2 + 1 - own_s))
        over_s(place).start()

    by_distance(depth, z, give_s)

    over_t(y).wait_recv()
    over_part.wait_recv()

    def second_sum(index, squares):
        lines = pl.ds(pl.multiple_of(index * chunk, chunk), chunk)
        value = (
            mine[lines].astype(jnp.float32)
            + far_t[1, lines].astype(jnp.float32)
            + far_part[lines].astype(jnp.float32)
        ).astype(low)
        mine[lines] = value
        value = value.astype(jnp.float32)
        return squares + jnp.sum((value * value).reshape(-1, 8, value.shape[1]), axis=0)

    squares = lax.fori_loop(
        0, height // chunk, second_sum, jnp.zeros((8, part.shape[1]), jnp.float32)
    )

    def out_mine(index, target):
        where = table_out.at[y * 2 + c]
        return remote(mine, where, o_send.at[index], o_recv.at[y * 2 + c], target)

    def out(rank, core):
        where = table_out.at[rank * 2 + core]
        return remote(where, where, o_send.at[2], o_recv.at[rank * 2 + core], across_c)

    keep = pltpu.make_async_copy(mine, table_out.at[y * 2 + c], own_sem)
    out_mine(0, across_y).start()
    out_mine(1, across_c).start()
    keep.start()

    def give_z(place):
        block = block_of(place, own_s, own_p)
        ready(block)
        over_p(place, own_s).wait_recv()
        over_s(place).wait_recv()
        add_into(total, block, (far_c, block), (far_p, place * 2 + own_s), (far_s, place))

        @pl.when(place > z)
        def rising():
            @pl.when(z > 0)
            def more():
                rise(place).wait_recv()
                add_into(total, block, (from_low, place))

            rise(place).start()

        @pl.when(place < z)
        def falling():
            @pl.when(z < depth - 1)
            def more():
                fall(place).wait_recv()
                add_into(total, block, (from_high, place))

            fall(place).start()

    by_distance(depth, z, give_z)
    grad_ref[...] = total[block_of(z, own_s, own_p)].astype(jnp.float32)

    @pl.when(z > 0)
    def low_part():
        rise(z).wait_recv()
        grad_ref[...] = grad_ref[...] + from_low[z].astype(jnp.float32)

    @pl.when(z < depth - 1)
    def high_part():
        fall(z).wait_recv()
        grad_ref[...] = grad_ref[...] + from_high[z].astype(jnp.float32)

    lines = lax.broadcasted_iota(jnp.int32, small.shape[1:], 0)
    lanes = lax.broadcasted_iota(jnp.int32, small.shape[1:], 1)
    last = (lines == small.shape[1] - 1) & (lanes == 0)
    grad_squares = jnp.sum(grad_ref[...] * grad_ref[...])
    small[0] = small_ref[...] + jnp.where(last, jnp.sum(squares) + grad_squares, 0.0)

    def exchange(turn):
        return remote(
            small.at[turn], far_small.at[turn], e_send.at[turn], e_recv.at[turn], partners[turn]
        )

    for turn in range(len(partners)):
        exchange(turn).start()
        exchange(turn).wait_recv()
        small[turn + 1] = small[turn] + far_small[turn]
    small_out[...] = small[len(partners)]
    out(1 - y, c).wait_recv()
    out(1 - y, c).start()
    out(y, 1 - c).wait_recv()
    out(1 - y, 1 - c).wait_recv()

    keep.wait()
    out_mine(0, across_y).wait_send()
    out_mine(1, across_c).wait_send()
    out(1 - y, c).wait_send()
    over_part.wait_send()
    for turn in range(len(partners)):
        exchange(turn).wait_send()
    for rank in range(2):
        over_t(rank).wait_send()
    for place in range(depth):
        rows_on(place, rx_send.at[place], across_x).wait_send()
        over_s(place).wait_send()
        for side in range(2):
            over_p(place, side).wait_send()
            for rank in range(2):
                for piece in range(3):
                    over_c((place * 2 + side) * 2 + rank, piece).wait_send()

        @pl.when(place > z)
        def rose():
            rise(place).wait_send()

        @pl.when(place < z)
        def fell():
            fall(place).wait_send()

        @pl.when((z - place >= 0) & (z < depth - 1))
        def rows_rose():
            rows_on(z, ru_send.at[place], up).wait_send()

        @pl.when((z + place < depth) & (z > 0))
        def rows_fell():
            rows_on(z, rd_send.at[place], down).wait_send()


def finish(pieces, rows, places, small, quarter, tile):
    blocks = pieces[0].shape[0]
    heights = [piece.shape[1] for piece in pieces]
    height, width = sum(heights), pieces[0].shape[2]
    depth = blocks // 8
    turns = 3 + (depth - 1).bit_length()
    dma = pltpu.SemaphoreType.DMA
    vmem = pl.BlockSpec(memory_space=pltpu.VMEM)

    def buffer(count):
        return pltpu.VMEM((count, height, width), low)

    return pl.pallas_call(
        functools.partial(finish_kernel, depth, heights, tile),
        out_shape=[
            jax.ShapeDtypeStruct((height, width), jnp.float32),
            jax.ShapeDtypeStruct((4, quarter, width), low),
            jax.ShapeDtypeStruct(small.shape, jnp.float32),
        ],
        in_specs=[ANY] * 4 + [vmem] * 2,
        out_specs=[vmem, ANY, vmem],
        scratch_shapes=[buffer(depth * 4), buffer(depth * 4), buffer(depth * 2)]
        + [buffer(depth)] * 3
        + [
            pltpu.VMEM((depth * 2,) + rows.shape, low),
            pltpu.VMEM((2, quarter, width), low),
            pltpu.VMEM((2, quarter, width), low),
            pltpu.VMEM((quarter, width), low),
            pltpu.VMEM((quarter, width), low),
            pltpu.VMEM((quarter, width), low),
            pltpu.VMEM((turns + 1,) + small.shape, jnp.float32),
            pltpu.VMEM((turns,) + small.shape, jnp.float32),
        ]
        + [dma((depth * 4, 3))] * 3
        + [dma((depth * 2,))] * 2
        + [dma((depth,))] * 6
        + [dma(())]
        + [dma((depth,))] * 3
        + [dma((depth * 2,))]
        + [dma((2,))] * 2
        + [dma(())] * 2
        + [dma((3,)), dma((4,))]
        + [dma((turns,))] * 2,
        compiler_params=pltpu.CompilerParams(
            collective_id=1, has_side_effects=True, vmem_limit_bytes=62 * 2**20
        ),
        name="finish",
    )(*pieces, rows, places, small)


def moments(gradient, first, second):
    first_new = beta_one * first + (1.0 - beta_one) * gradient
    second_new = beta_two * second + (1.0 - beta_two) * gradient * gradient
    second_hat = second_new * (1.0 / (1.0 - beta_two**STEP))
    root = second_hat * lax.rsqrt(second_hat) + adam_eps
    direction = first_new * (1.0 / (1.0 - beta_one**STEP)) / root
    return direction, first_new, second_new


def update_kernel(steps, cuts, *refs):
    table_ref, table_m_ref, table_v_ref, table_g_ref = refs[0:4]
    small_ref, sums_ref, gains_ref, gains_m_ref, gains_v_ref = refs[4:9]
    grad_ref, block_ref, block_m_ref, block_v_ref, bases_ref = refs[9:14]
    table_new, table_m_new, table_v_new, table_low = refs[14:18]
    values_ref, gains_new, gains_m_new, gains_v_new = refs[18:22]
    block_new, block_m_new, block_v_new, block_low = refs[22:26]
    bases, turned, factor_ref, bases_sem = refs[26:30]
    now = pl.program_id(0)

    def base(index):
        return pltpu.make_async_copy(bases_ref.at[index], bases.at[index], bases_sem.at[index])

    @pl.when(now == 0)
    def begin():
        for index in range(4):
            base(index).start()
        lines = lax.broadcasted_iota(jnp.int32, small_ref.shape, 0)
        lanes = lax.broadcasted_iota(jnp.int32, small_ref.shape, 1)

        def value_at(place):
            there = (lines == place // 128) & (lanes == place % 128)
            return jnp.sum(jnp.where(there, small_ref[...], 0.0), axis=(0, 1), keepdims=True)

        count = value_at(3 * D + 1)
        gain_grads = sums_ref[...] / count
        squares = value_at((small_ref.shape[0] - 1) * 128) / (count * count)
        norm = jnp.sqrt(squares + jnp.sum(gain_grads * gain_grads, axis=(0, 1), keepdims=True))
        clip = jnp.minimum(1.0, clip_norm / norm)
        factor_ref[...] = jnp.broadcast_to(clip / count, factor_ref.shape)
        spots = lax.broadcasted_iota(jnp.int32, values_ref.shape, 1)
        values_ref[...] = jnp.where(spots == 0, value_at(3 * D) / count, norm)
        direction, gains_m_new[...], gains_v_new[...] = moments(
            gain_grads * clip, gains_m_ref[...], gains_v_ref[...]
        )
        gains_new[...] = gains_ref[...] - rate_gain * direction

    factor = factor_ref[0:1, 0:1]
    direction, table_m_new[...], table_v_new[...] = moments(
        table_g_ref[...].astype(jnp.float32) * factor, table_m_ref[...], table_v_ref[...]
    )
    table_tile = table_ref[...]
    table_tile = table_tile - rate_table * (direction + decay_rate * table_tile)
    table_new[...] = table_tile
    table_low[...] = table_tile.astype(low)

    spots = lax.broadcasted_iota(jnp.int32, turned.shape, 1)

    def columns(index, value):
        mine = (spots >= cuts[index]) & (spots < cuts[index + 1])
        return jnp.where(mine, value, 0.0).astype(low)

    for index in range(4):

        @pl.when(now == min(1 + index, steps - 1))
        def rotate():
            base(index).wait()
            term = contract_rows(
                bases[index].astype(low), columns(index, grad_ref[...] * factor_ref[0:1, 0:1])
            )
            turned[...] = term if index == 0 else turned[...] + term

    @pl.when(now == min(5, steps - 1))
    def move():
        direction, block_m_new[...], block_v_new[...] = moments(
            turned[...], block_m_ref[...], block_v_ref[...]
        )
        turned[...] = direction

    for index in range(4):

        @pl.when(now == min(5 + index, steps - 1))
        def rotate_back():
            term = product(bases[index].astype(low), columns(index, turned[...]))
            block_new[...] = term if index == 0 else block_new[...] + term

    @pl.when(now == min(8, steps - 1))
    def store():
        block = block_ref[...]
        block = block - rate_block * (block_new[...] + decay_rate * block)
        block_new[...] = block
        block_low[...] = block.astype(low)


def update(cuts, tables, table_grads, small, gain_sums, gains, block_grads, blocks, bases):
    rows, width = tables[0].shape
    tile = max(
        size
        for size in range(8, 401, 8)
        if rows % size == 0 and (size % 16 == 0 or rows % 16)
    )
    steps = rows // tile
    f32 = jnp.float32

    def whole(array):
        return pl.BlockSpec(array.shape, lambda i: (0,) * array.ndim)

    tiles = pl.BlockSpec((tile, width), lambda i: (i, 0))
    table = jax.ShapeDtypeStruct(tables[0].shape, f32)
    gain = jax.ShapeDtypeStruct(gains[0].shape, f32)
    matrix = jax.ShapeDtypeStruct(blocks[0].shape, f32)
    values = jax.ShapeDtypeStruct((8, 128), f32)
    outs = [table] * 3 + [jax.ShapeDtypeStruct(table.shape, low)]
    outs += [values] + [gain] * 3
    outs += [matrix] * 3 + [jax.ShapeDtypeStruct(matrix.shape, low)]
    return pl.pallas_call(
        functools.partial(update_kernel, steps, cuts),
        grid=(steps,),
        out_shape=outs,
        in_specs=[tiles] * 4
        + [whole(small), whole(gain_sums)]
        + [whole(gain)] * 3
        + [whole(matrix)] * 4
        + [ANY],
        out_specs=[tiles] * 4 + [whole(values)] + [whole(gain)] * 3 + [whole(matrix)] * 4,
        scratch_shapes=[
            pltpu.VMEM(bases.shape, f32),
            pltpu.VMEM(matrix.shape, f32),
            pltpu.VMEM((8, 128), f32),
            pltpu.SemaphoreType.DMA((4,)),
        ],
        compiler_params=pltpu.CompilerParams(vmem_limit_bytes=58 * 2**20),
        name="update",
    )(*tables, table_grads, small, gain_sums, *gains, block_grads, *blocks, bases)


def cost(flops):
    return pl.CostEstimate(flops=flops, bytes_accessed=10**6, transcendentals=0)


LARGE = 58 * 2**20
CHUNK = 512


def inverse_rms(value):
    return lax.rsqrt(jnp.mean(value * value, axis=-1, keepdims=True) + eps_norm)


def norm_back(value, r, gain, grad):
    scaled = grad * gain
    d_value = r * scaled - value * (r * r * r) * jnp.mean(value * scaled, axis=-1, keepdims=True)
    return d_value, jnp.sum(grad * value * r, axis=0, keepdims=True)


def local_call(kernel, name, flops, outs, args, scratch=(), remain=()):
    vmem = pl.BlockSpec(memory_space=pltpu.VMEM)
    return pl.pallas_call(
        kernel,
        out_shape=[jax.ShapeDtypeStruct(shape, kind) for shape, kind in outs],
        in_specs=[ANY if place in remain else vmem for place in range(len(args))],
        out_specs=[vmem] * len(outs),
        scratch_shapes=list(scratch),
        compiler_params=pltpu.CompilerParams(vmem_limit_bytes=LARGE),
        cost_estimate=cost(flops),
        name=name,
    )(*args)


def project_kernel(hidden_ref, gain_ref, weight_ref, cosine_ref, sine_ref, *refs):
    normed_ref, query_ref, own_ref = refs
    hidden = hidden_ref[...]
    normed = (hidden * inverse_rms(hidden) * gain_ref[...]).astype(low)
    normed_ref[...] = normed
    cosine, sine = cosine_ref[...], sine_ref[...]
    first = lax.broadcasted_iota(jnp.int32, cosine.shape, 1) % HD < HD // 2
    for index in range(3 * D // 128):
        columns = pl.ds(index * 128, 128)
        value = contract_cols(normed, weight_ref[columns])
        if index < 2 * D // 128:
            turned = jnp.where(
                first, -pltpu.roll(value, 128 - HD // 2, 1), pltpu.roll(value, HD // 2, 1)
            )
            value = value * cosine + turned * sine
        if index < D // 128:
            query_ref[:, columns] = value.astype(low)
        else:
            own_ref[:, pl.ds(index * 128 - D, 128)] = value.astype(low)


def project(hidden, gain, weight, cosine, sine):
    rows = hidden.shape[0]
    outs = [((rows, D), low), ((rows, D), low), ((rows, 2 * D), low)]
    return local_call(project_kernel, "project", 6 * 10**9, outs, [hidden, gain, weight, cosine, sine])


def allowed(rows_ref, columns_ref):
    return (rows_ref[:, 0:1] == columns_ref[0:1]) & (rows_ref[:, 1:2] >= columns_ref[1:2])


def pair_of_heads(index):
    return pl.ds(index * 128, 128)


def attention_weight(query, keys, allow):
    score = jnp.where(allow, contract_cols(query, keys) * scale, -1e30)
    power = jnp.exp(score - jnp.max(score, axis=-1, keepdims=True))
    return power * (1.0 / jnp.sum(power, axis=-1, keepdims=True))


def forward_kernel(hidden_ref, query_ref, own_ref, far_ref, rows_ref, columns_ref, *refs):
    out_weight, gain_ref, gate_hbm, down_hbm, output_ref, merged_ref, middle_ref = refs[:7]
    gates, downs, sems = refs[7:]
    copies = weight_copies(gate_hbm, down_hbm, gates, downs, sems)
    for group in copies:
        for copy in group:
            copy.start()
    allow = allowed(rows_ref, columns_ref)
    rows = hidden_ref.shape[0]
    first = lax.broadcasted_iota(jnp.int32, (rows, 128), 1) < HD

    @pl.loop(0, D // 128)
    def heads(index):
        columns = pl.ds(pl.multiple_of(index * 128, 128), 128)
        values_at = pl.ds(pl.multiple_of(index * 128 + D, 128), 128)
        query = query_ref[:, columns]
        keys = jnp.concatenate([own_ref[:, columns], far_ref[:, columns]], axis=0)
        values = jnp.concatenate([own_ref[:, values_at], far_ref[:, values_at]], axis=0)
        mixed = []
        for side in range(2):
            mine = jnp.where(first == (side == 0), query, jnp.zeros_like(query))
            weight = attention_weight(mine, keys, allow).astype(low)
            mixed.append(product(weight, values))
        merged_ref[:, columns] = jnp.where(first, mixed[0], mixed[1]).astype(low)

    middle = hidden_ref[...] + contract_cols(merged_ref[...], out_weight[...])
    middle_ref[...] = middle
    normed = (middle * inverse_rms(middle) * gain_ref[...]).astype(low)
    output_ref[...] = middle
    for index, group in enumerate(copies):
        for copy in group:
            copy.wait()
        gate = contract_cols(normed, gates[pl.ds(index * CHUNK, CHUNK)])
        up = contract_cols(normed, gates[pl.ds(FF + index * CHUNK, CHUNK)])
        action = (gate * jax.nn.sigmoid(gate) * up).astype(low)
        output_ref[...] += product(action, downs[pl.ds(index * CHUNK, CHUNK)])


def weight_copies(gate_hbm, down_hbm, gates, downs, sems):
    groups = []
    for index in range(FF // CHUNK):
        parts = [
            (gate_hbm, gates, index * CHUNK),
            (gate_hbm, gates, FF + index * CHUNK),
            (down_hbm, downs, index * CHUNK),
        ]
        groups.append(
            [
                pltpu.make_async_copy(
                    source.at[pl.ds(at, CHUNK)], goal.at[pl.ds(at, CHUNK)], sems.at[index, place]
                )
                for place, (source, goal, at) in enumerate(parts)
            ]
        )
    return groups


def weight_buffers():
    return [
        pltpu.VMEM((2 * FF, D), low),
        pltpu.VMEM((FF, D), low),
        pltpu.SemaphoreType.DMA((FF // CHUNK, 3)),
    ]


def forward(hidden, query, own, far, rows, columns, w_out, gain, w_gu, w_down):
    count = hidden.shape[0]
    outs = [((count, D), jnp.float32), ((count, D), low), ((count, D), jnp.float32)]
    args = [hidden, query, own, far, rows, columns, w_out, gain, w_gu, w_down]
    return local_call(forward_kernel, "forward", 5 * 10**9, outs, args, weight_buffers(), (8, 9))


def backward_kernel(gradient_ref, middle_ref, query_ref, own_ref, far_ref, *refs):
    rows_ref, columns_ref, out_weight, gain_ref, gate_hbm, down_hbm = refs[:6]
    d_query_ref, d_own_ref, d_far_ref, d_middle_ref, gain_out = refs[6:11]
    low_ref, normed_ref, action_ref, d_gate_ref, middle_low_ref = refs[11:16]
    gates, downs, sems, total = refs[16:]
    copies = weight_copies(gate_hbm, down_hbm, gates, downs, sems)
    for group in copies:
        for copy in group:
            copy.start()
    gradient = gradient_ref[...]
    grad_low = gradient.astype(low)
    low_ref[...] = grad_low
    middle = middle_ref[...]
    r = inverse_rms(middle)
    normed = (middle * r * gain_ref[...]).astype(low)
    normed_ref[...] = normed
    total[...] = jnp.zeros_like(total)
    for index, group in enumerate(copies):
        for copy in group:
            copy.wait()
        first = pl.ds(index * CHUNK, CHUNK)
        second = pl.ds(FF + index * CHUNK, CHUNK)
        gate = contract_cols(normed, gates[first])
        up = contract_cols(normed, gates[second])
        chance = jax.nn.sigmoid(gate)
        action_ref[:, first] = (gate * chance * up).astype(low)
        d_action = contract_cols(grad_low, downs[first])
        d_gate = (d_action * up * (chance + gate * chance * (1.0 - chance))).astype(low)
        d_up = (d_action * gate * chance).astype(low)
        d_gate_ref[:, first] = d_gate
        d_gate_ref[:, second] = d_up
        total[...] += product(d_gate, gates[first]) + product(d_up, gates[second])
    d_middle, gain_out[...] = norm_back(middle, r, gain_ref[...], total[...])
    d_middle = gradient + d_middle
    d_middle_ref[...] = d_middle
    middle_low = d_middle.astype(low)
    middle_low_ref[...] = middle_low
    total[...] = product(middle_low, out_weight[...])
    allow = allowed(rows_ref, columns_ref)
    rows = gradient.shape[0]
    first = lax.broadcasted_iota(jnp.int32, (rows, 128), 1) < HD
    first_all = lax.broadcasted_iota(jnp.int32, (2 * rows, 128), 1) < HD

    @pl.loop(0, D // 128)
    def heads(index):
        columns = pl.ds(pl.multiple_of(index * 128, 128), 128)
        values_at = pl.ds(pl.multiple_of(index * 128 + D, 128), 128)
        query = query_ref[:, columns]
        upstream = total[:, columns].astype(low)
        keys = jnp.concatenate([own_ref[:, columns], far_ref[:, columns]], axis=0)
        values = jnp.concatenate([own_ref[:, values_at], far_ref[:, values_at]], axis=0)
        d_queries, d_keys, d_values = [], [], []
        for side in range(2):
            mine = jnp.where(first == (side == 0), query, jnp.zeros_like(query))
            grad = jnp.where(first == (side == 0), upstream, jnp.zeros_like(upstream))
            weight = attention_weight(mine, keys, allow)
            d_values.append(contract_rows(weight.astype(low), upstream))
            d_weight = contract_cols(grad, values)
            d_score = weight * (d_weight - jnp.sum(d_weight * weight, axis=-1, keepdims=True))
            d_score = d_score.astype(low)
            d_queries.append(product(d_score, keys) * scale)
            d_keys.append(contract_rows(d_score, query) * scale)
        d_query_ref[:, columns] = jnp.where(first, *d_queries).astype(low)
        d_key = jnp.where(first_all, *d_keys)
        d_value = jnp.where(first_all, *d_values)
        d_own_ref[:, columns] = d_key[:rows]
        d_own_ref[:, values_at] = d_value[:rows]
        d_far_ref[:, columns] = d_key[rows:].astype(low)
        d_far_ref[:, values_at] = d_value[rows:].astype(low)


def backward(gradient, middle, query, own, far, rows, columns, w_out, gain, w_gu, w_down):
    count = gradient.shape[0]
    f32 = jnp.float32
    outs = [
        ((count, D), low),
        ((count, 2 * D), f32),
        ((count, 2 * D), low),
        ((count, D), f32),
        ((1, D), f32),
        ((count, D), low),
        ((count, D), low),
        ((count, FF), low),
        ((count, 2 * FF), low),
        ((count, D), low),
    ]
    args = [gradient, middle, query, own, far, rows, columns, w_out, gain, w_gu, w_down]
    scratch = weight_buffers() + [pltpu.VMEM((count, D), f32)]
    return local_call(backward_kernel, "backward", 30 * 10**9, outs, args, scratch, (9, 10))


def unproject_kernel(d_query_ref, d_own_ref, d_far_ref, d_middle_ref, hidden_ref, *refs):
    gain_ref, weight_ref, cosine_ref, sine_ref, gradient_ref, gain_out, d_qkv_ref = refs
    cosine, sine = cosine_ref[...], sine_ref[...]
    first = lax.broadcasted_iota(jnp.int32, cosine.shape, 1) % HD < HD // 2
    for index in range(3 * D // 128):
        columns = pl.ds(index * 128, 128)
        if index < D // 128:
            value = d_query_ref[:, columns].astype(jnp.float32)
        else:
            there = pl.ds(index * 128 - D, 128)
            value = d_own_ref[:, there] + d_far_ref[:, there].astype(jnp.float32)
            value = value.astype(low).astype(jnp.float32)
        if index < 2 * D // 128:
            part = value * sine
            turned = jnp.where(
                first, pltpu.roll(part, 128 - HD // 2, 1), -pltpu.roll(part, HD // 2, 1)
            )
            value = value * cosine + turned
        d_qkv_ref[:, columns] = value.astype(low)
    hidden = hidden_ref[...]
    d_hidden, gain_out[...] = norm_back(
        hidden, inverse_rms(hidden), gain_ref[...], product(d_qkv_ref[...], weight_ref[...])
    )
    gradient_ref[...] = d_middle_ref[...] + d_hidden


def unproject(d_query, d_own, d_far, d_middle, hidden, gain, weight, cosine, sine):
    rows = hidden.shape[0]
    outs = [((rows, D), jnp.float32), ((1, D), jnp.float32), ((rows, 3 * D), low)]
    args = [d_query, d_own, d_far, d_middle, hidden, gain, weight, cosine, sine]
    return local_call(unproject_kernel, "unproject", 10**6, outs, args)


def weigh_kernel(*refs):
    pairs = [refs[4 * index : 4 * index + 4] for index in range(4)]
    gate_out, down_out, joined, qkv, out = refs[16:21]
    now = pl.program_id(0)

    def gradient(index):
        left_one, left_two, right_one, right_two = pairs[index]
        total = contract_rows(left_one[...], right_one[...])
        return total + contract_rows(left_two[...], right_two[...])

    gate_out[...] = gradient(0).astype(low).reshape(gate_out.shape)
    down_out[...] = gradient(1).astype(low).reshape(down_out.shape)

    @pl.when(now < 6)
    def first():
        qkv[pl.ds(pl.multiple_of(now * 384, 384), 384)] = gradient(2)

    @pl.when(now >= 6)
    def second():
        out[pl.ds(pl.multiple_of((now - 6) * 384, 384), 384)] = gradient(3)

    @pl.when(now == 7)
    def join():
        blocks = joined.shape[0]
        tall, flat = 3 * D // blocks, D // blocks
        for block in range(blocks):
            parts = [qkv[block * tall : (block + 1) * tall], out[block * flat : (block + 1) * flat]]
            joined[block] = jnp.concatenate(parts, axis=0).astype(low)


def weigh(d_gates, normed_twos, actions, lows, d_qkvs, normeds, middles, merges, blocks):
    rows = lows[0].shape[0]

    def both(arrays, width, place):
        return [(array, pl.BlockSpec((rows, width), place)) for array in arrays]

    def whole(arrays):
        return [(array, pl.BlockSpec((rows, D), lambda i: (0, 0))) for array in arrays]

    def early(i):
        return (0, jnp.minimum(i, 5))

    def late(i):
        return (0, jnp.maximum(i - 6, 0))

    listed = both(d_gates, 768, lambda i: (0, i)) + whole(normed_twos)
    listed += both(actions, 384, lambda i: (0, i)) + whole(lows)
    listed += both(d_qkvs, 384, early) + whole(normeds)
    listed += both(middles, 384, late) + whole(merges)
    part = blocks // 8
    return pl.pallas_call(
        weigh_kernel,
        grid=(8,),
        out_shape=[
            jax.ShapeDtypeStruct((blocks, 2 * FF // blocks, D), low),
            jax.ShapeDtypeStruct((blocks, FF // blocks, D), low),
            jax.ShapeDtypeStruct((blocks, 4 * D // blocks, D), low),
        ],
        in_specs=[spec for unused, spec in listed],
        out_specs=[
            pl.BlockSpec((part, 2 * FF // blocks, D), lambda i: (i, 0, 0)),
            pl.BlockSpec((part, FF // blocks, D), lambda i: (i, 0, 0)),
            pl.BlockSpec((blocks, 4 * D // blocks, D), lambda i: (0, 0, 0)),
        ],
        scratch_shapes=[pltpu.VMEM((3 * D, D), jnp.float32), pltpu.VMEM((D, D), jnp.float32)],
        compiler_params=pltpu.CompilerParams(vmem_limit_bytes=LARGE),
        cost_estimate=cost(10**6),
        name="weigh",
    )(*[array for array, unused in listed])


def loss_kernel(hidden_ref, gain_ref, near_ref, far_ref, own_ref, other_ref, weight_ref, *refs):
    gradient_ref, gain_out, loss_ref, near_out, far_out, logits, teach = refs
    head = lax.axis_index("head")
    rows = hidden_ref.shape[0]
    half = rows // 2
    size = near_ref.shape[1]
    hidden = hidden_ref[...]
    r = inverse_rms(hidden)
    normed = (hidden * r * gain_ref[...]).astype(low)
    parts = [(near_ref, near_out, 0, 0), (near_ref, near_out, 1, 2)]
    parts += [(far_ref, far_out, 0, 1), (far_ref, far_out, 1, 3)]
    for index, (source, unused, place, offset) in enumerate(parts):
        columns = pl.ds(pl.multiple_of((head ^ offset) * size, size), size)
        logits[index] = contract_cols(normed, source[place])
        teach[index, :half] = own_ref[:, columns].astype(jnp.float32)
        teach[index, half:] = other_ref[:, columns].astype(jnp.float32)

    def log_total(values):
        summit = jnp.max(jnp.max(values[...], axis=0), axis=-1, keepdims=True)
        return summit + jnp.log(
            jnp.sum(jnp.sum(jnp.exp(values[...] - summit[None]), axis=0), axis=-1, keepdims=True)
        )

    log_logits, log_teach = log_total(logits), log_total(teach)
    weighting = weight_ref[...]
    gradient = jnp.zeros((rows, hidden.shape[1]), jnp.float32)
    loss = jnp.zeros((rows, 1), jnp.float32)
    for index, (source, goal, place, offset) in enumerate(parts):
        log_prob = logits[index] - log_logits
        log_true = teach[index] - log_teach
        true = jnp.exp(log_true)
        loss = loss + jnp.sum(true * (log_true - log_prob), axis=-1, keepdims=True)
        d_logits = ((jnp.exp(log_prob) - true) * weighting).astype(low)
        goal[place] = contract_rows(d_logits, normed).astype(low)
        gradient = gradient + product(d_logits, source[place])
    loss_ref[...] = jnp.broadcast_to(
        jnp.sum(loss * weighting, axis=0, keepdims=True), loss_ref.shape
    )
    gradient_ref[...], gain_out[...] = norm_back(hidden, r, gain_ref[...], gradient)


def distill(hidden, gain, near, far, own, other, weighting):
    rows, width = hidden.shape
    size = near.shape[1]
    vmem = pl.BlockSpec(memory_space=pltpu.VMEM)
    f32 = jnp.float32
    return pl.pallas_call(
        loss_kernel,
        out_shape=[
            jax.ShapeDtypeStruct(hidden.shape, f32),
            jax.ShapeDtypeStruct(gain.shape, f32),
            jax.ShapeDtypeStruct((8, 128), f32),
            jax.ShapeDtypeStruct(near.shape, low),
            jax.ShapeDtypeStruct(far.shape, low),
        ],
        in_specs=[vmem] * 7,
        out_specs=[vmem] * 5,
        scratch_shapes=[pltpu.VMEM((4, rows, size), f32)] * 2,
        compiler_params=pltpu.CompilerParams(vmem_limit_bytes=58 * 2**20),
        name="distill",
    )(hidden, gain, near, far, own, other, weighting)


def on_device(
    token_ids,
    lengths,
    valid,
    vocab_ids,
    teacher,
    block,
    block_m,
    block_v,
    bases,
    table,
    table_m,
    table_v,
    gains,
    gains_m,
    gains_v,
):
    dp_count, head_count = lax.axis_size("dp"), lax.axis_size("head")
    device_total = dp_count * head_count
    head, dp = lax.axis_index("head"), lax.axis_index("dp")
    batch = head // 2
    tokens = token_ids.shape[1]
    shard_rows = table.shape[0]
    offset = dp * shard_rows
    part = TOPV // device_total

    widths = [3 * D // device_total, D // device_total, 2 * FF // device_total, FF // device_total]
    cuts = [sum(widths[:index]) for index in range(5)]
    block_low = block.T.astype(low)
    pieces = [block_low[cuts[index] : cuts[index + 1]] for index in range(4)]
    *weights, rows_in, codes, near, far = start(
        pieces,
        table,
        (token_ids * 2 + valid).reshape(-1, 1, tokens),
        vocab_ids,
        dp_count,
    )
    codes = codes.reshape(dp_count, 2 * tokens)
    weighting = (lax.dynamic_index_in_dim(codes, dp, 0, keepdims=False) & 1).astype(jnp.float32)
    vocab = lax.dynamic_index_in_dim(
        vocab_ids.reshape(head_count, dp_count, part), head, 0, keepdims=False
    )
    local = jnp.concatenate([vocab, codes >> 1], axis=1) - offset
    owned = (local >= 0) & (local < shard_rows)
    weights = [weight.reshape(-1, D) for weight in weights]
    near = near.reshape(2, -1, D)
    far = far.reshape(2, -1, D)
    hidden = rows_in[part:].astype(jnp.float32)

    teacher_own = lax.dynamic_index_in_dim(teacher, batch, 0, keepdims=False)
    teacher_far = swap(
        lax.dynamic_index_in_dim(teacher, 1 - batch, 0, keepdims=False), head_count, 2
    )

    run = jnp.arange(tokens, dtype=jnp.int32)
    places = jnp.concatenate([head * tokens + run, (head ^ 2) * tokens + run])
    places_far = jnp.concatenate([(head ^ 1) * tokens + run, (head ^ 3) * tokens + run])
    own_lengths = lax.dynamic_index_in_dim(lengths, batch, 0, keepdims=False)[0]
    segment, position = segments(own_lengths, places)
    segment_far, unused = segments(own_lengths, places_far)
    queries_at = jnp.stack([segment, places], axis=1)
    keys_at = jnp.stack(
        [jnp.concatenate([segment, segment_far]), jnp.concatenate([places, places_far])]
    )
    freqs = jnp.exp(jnp.arange(0, HD, 2, dtype=jnp.float32) * (-math.log(10000.0) / HD))
    angle = position.astype(jnp.float32)[:, None] * jnp.tile(freqs, 4)[None, :]
    cosine, sine = jnp.cos(angle), jnp.sin(angle)

    w_qkv, w_out, w_gu, w_down = weights
    saves = []
    for repeat in range(2):
        normed, query, own = project(hidden, gains[0:1], w_qkv, cosine, sine)
        other = swap(own, head_count, 1)
        output, merged, middle = forward(
            hidden, query, own, other, queries_at, keys_at, w_out, gains[1:2], w_gu, w_down
        )
        saves.append((hidden, normed, query, own, other, merged, middle))
        hidden = output
        if repeat == 0:
            hidden, teacher_far = lax.optimization_barrier((hidden, teacher_far))

    gradient, d_gain_final, loss_sum, d_near, d_far = distill(
        hidden, gains[2:3], near, far, teacher_own, teacher_far, weighting[:, None]
    )
    d_gain_final, loss_sum = d_gain_final[0], loss_sum[0, 0]
    f32 = jnp.float32
    gradient, d_far = lax.optimization_barrier((gradient, swap(d_far, head_count, 1)))
    d_near = (d_near.astype(f32) + d_far.astype(f32)).astype(low)
    d_quarter = swap(d_near[1], head_count, 2)

    d_gains = [0.0, 0.0]
    parts = []
    for repeat in range(2):
        hidden, normed, query, own, other, merged, middle = saves[1 - repeat]
        back = backward(
            gradient, middle, query, own, other, queries_at, keys_at, w_out, gains[1:2], w_gu, w_down
        )
        d_query, d_own, d_other, d_middle, d_gain_two = back[:5]
        grad_low, normed_two, action, d_gate, middle_low = back[5:]
        gradient, d_gain_one, d_qkv = unproject(
            d_query,
            d_own,
            swap(d_other, head_count, 1),
            d_middle,
            hidden,
            gains[0:1],
            w_qkv,
            cosine,
            sine,
        )
        if repeat == 0:
            gradient, d_quarter = lax.optimization_barrier((gradient, d_quarter))
            d_quarter = (d_near[0].astype(f32) + d_quarter.astype(f32)).astype(low)
            chosen_grads = lax.psum_scatter(d_quarter, "dp", scatter_dimension=0, tiled=True)
        parts.append((d_gate, normed_two, action, grad_low, d_qkv, normed, middle_low, merged))
        d_gains = [d_gains[0] + d_gain_one[0], d_gains[1] + d_gain_two[0]]

    d_gu, d_down, d_attention = weigh(*zip(*parts), device_total)
    rows_back = jnp.concatenate([chosen_grads, gradient.astype(low)], axis=0)
    step = 80 if shard_rows % 80 == 0 else 40
    quarter = -(-shard_rows // (step * head_count)) * step
    tile = quarter // 5 if quarter % 80 == 0 and quarter // 5 % 16 == 0 else step
    small = [d_gains[0], d_gains[1], d_gain_final, loss_sum[None], jnp.sum(weighting)[None]]
    small = jnp.pad(jnp.concatenate(small), (0, 6 * 128 - 2)).reshape(-1, 128)
    block_grads, table_grads, small = finish(
        [d_attention, d_gu, d_down],
        rows_back,
        jnp.where(owned, local, -1).reshape(1, -1),
        small,
        quarter,
        tile,
    )
    outs = update(
        cuts,
        [table, table_m, table_v],
        table_grads.reshape(-1, D),
        small,
        small[: 3 * D // 128].reshape(3, D),
        [gains, gains_m, gains_v],
        block_grads.T,
        [block, block_m, block_v],
        bases,
    )
    table_new, table_m_new, table_v_new, table_low = outs[0:4]
    values, gains_new, gains_m_new, gains_v_new = outs[4:8]
    block_new, block_m_new, block_v_new, block_low = outs[8:12]
    return (
        values[0, 0],
        values[0, 1],
        block_new,
        block_m_new,
        block_v_new,
        table_new,
        table_m_new,
        table_v_new,
        gains_new,
        gains_m_new,
        gains_v_new,
        block_low,
        table_low,
    )


def solution(mesh):
    tokens = P(None, ("dp", "head"))
    columns = P(None, ("dp", "head"))
    table = P("dp", None)
    return jax.shard_map(
        on_device,
        mesh=mesh,
        in_specs=(
            tokens,
            P(None, "dp", None),
            tokens,
            P(),
            P(None, ("dp", "head"), None),
            columns,
            columns,
            columns,
            P(),
            table,
            table,
            table,
            P(),
            P(),
            P(),
        ),
        out_specs=(
            P(),
            P(),
            columns,
            columns,
            columns,
            table,
            table,
            table,
            P(),
            P(),
            P(),
            columns,
            table,
        ),
        check_vma=False,
    )
```

```python
import functools
import math

import jax
import jax.numpy as jnp
from jax import lax
from jax.experimental import pallas as pl
from jax.experimental.pallas import tpu as pltpu
from jax.sharding import PartitionSpec as P

D = 768
H = 12
HD = 64
FF = 3072
TOPV = 4096
STEP = 5

low = jnp.bfloat16
scale = HD**-0.5
eps_norm = 1e-05
clip_norm = 0.002
beta_one = 0.9
beta_two = 0.99
adam_eps = 1e-08
decay_rate = 0.1
rate_block = 0.03
rate_table = 0.05
rate_gain = 0.4


def product(left, right):
    return jnp.dot(left, right, preferred_element_type=jnp.float32)


def contract_rows(left, right):
    return lax.dot_general(
        left, right, (((0,), (0,)), ((), ())), preferred_element_type=jnp.float32
    )


def contract_cols(left, right):
    return lax.dot_general(
        left, right, (((1,), (1,)), ((), ())), preferred_element_type=jnp.float32
    )


def segments(lengths, places):
    segment = jnp.zeros_like(places)
    begin = jnp.zeros_like(places)
    end = jnp.zeros((), jnp.int32)
    for index in range(lengths.shape[0] - 1):
        end = end + lengths[index]
        past = places >= end
        segment = segment + past.astype(jnp.int32)
        begin = jnp.where(past, end, begin)
    return segment, places - begin


def swap(value, head_count, offset):
    return lax.ppermute(value, "head", [(h, h ^ offset) for h in range(head_count)])


MESH = pl.DeviceIdType.MESH
ANY = pl.BlockSpec(memory_space=pl.ANY)


def coordinates(depth):
    dp, head = lax.axis_index("dp"), lax.axis_index("head")
    return dp // 2, dp % 2, head // 2, head % 2


def device(z, x, y, c):
    return (z * 2 + x, y * 2 + c)


def slot(z, x, y, c):
    return ((z * 2 + x) * 2 + y) * 2 + c


def greet(depth, z, x, y, c):
    barrier = pltpu.get_barrier_semaphore()
    for target in (device(z, 1 - x, y, c), device(z, x, 1 - y, c), device(z, x, y, 1 - c)):
        pl.semaphore_signal(barrier, 1, device_id=target, device_id_type=MESH)

    @pl.when(z > 0)
    def below():
        pl.semaphore_signal(barrier, 1, device_id=device(z - 1, x, y, c), device_id_type=MESH)

    @pl.when(z < depth - 1)
    def above():
        pl.semaphore_signal(barrier, 1, device_id=device(z + 1, x, y, c), device_id_type=MESH)

    pl.semaphore_wait(barrier, 3 + jnp.where(z > 0, 1, 0) + jnp.where(z < depth - 1, 1, 0))


def start_kernel(depth, *refs):
    pieces = refs[0:4]
    table_ref, codes_ref, vocab_ref = refs[4:7]
    wholes = refs[7:11]
    sum_ref, ids_ref, near_ref, far_ref = refs[11:15]
    far_x, from_low, from_high, total, rows_ref, shard, ids = refs[15:22]
    local_sem, up_sem, down_sem, x_sem, y_sem, c_sem, block_sem = refs[22:29]
    rx_send, rx_recv, ru_send, ru_recv, rd_send, rd_recv = refs[29:35]
    id_send, id_recv, table_sem, copy_sem = refs[35:39]
    su_send, sd_send, sx_send, sy_send, sc_send, s_recv, keep_sem = refs[39:46]
    z, x, y, c = coordinates(depth)
    mine = slot(z, x, y, c)
    dp, head = z * 2 + x, y * 2 + c
    groups, height = rows_ref.shape[:2]
    shard_rows, tokens = table_ref.shape[0], codes_ref.shape[2]
    part = height - 2 * tokens
    offset = dp * shard_rows
    barrier = pltpu.get_barrier_semaphore()
    pl.semaphore_signal(barrier, 1, device_id=device(z, x, y, 1 - c), device_id_type=MESH)
    for group in range(groups):
        for rank in range(2):

            @pl.when((group != dp) | (rank != y))
            def hello():
                pl.semaphore_signal(
                    barrier, 1, device_id=(group, rank * 2 + c), device_id_type=MESH
                )

    pl.semaphore_wait(barrier, groups * 2)

    def tell(group, rank):
        second = jnp.where(rank == y, 0, 1)
        return pltpu.make_async_remote_copy(
            codes_ref.at[rank],
            ids_ref.at[dp, second],
            id_send.at[group, rank],
            id_recv.at[dp, second],
            device_id=(group, rank * 2 + c),
            device_id_type=MESH,
        )

    def told(group, second):
        return pltpu.make_async_remote_copy(
            codes_ref.at[0],
            ids_ref.at[group, second],
            id_send.at[group, second],
            id_recv.at[group, second],
            device_id=device(z, x, y, 1 - c),
            device_id_type=MESH,
        )

    keep = pltpu.make_async_copy(codes_ref.at[y], ids_ref.at[dp, 0], copy_sem)
    fetch = pltpu.make_async_copy(table_ref, shard.at[pl.ds(0, shard_rows)], table_sem)
    fetch.start()
    keep.start()
    for group in range(groups):
        for rank in range(2):

            @pl.when((group != dp) | (rank != y))
            def telling():
                tell(group, rank).start()

    def gather(stage, group):
        def load(first, read):
            @pl.loop(0, (tokens if first else part) // 16)
            def some(index):
                base = index * 16
                lines = []
                for line in range(16):
                    place = read(base + line) - offset
                    held = (place >= 0) & (place < shard_rows)
                    lines.append(shard[pl.ds(jnp.where(held, place, shard_rows), 1)])
                rows_ref[group, pl.ds(pl.multiple_of(first + base, 16), 16)] = jnp.concatenate(
                    lines, axis=0
                ).astype(low)

        if stage == 0:
            load(0, lambda index: vocab_ref[(head * groups + group) * part + index])
        for second in range(2 if stage else 0):
            load(part + second * tokens, lambda index: ids[group, second, 0, index] >> 1)

    def own(block, piece, target, sem):
        return pltpu.make_async_remote_copy(
            pieces[piece],
            wholes[piece].at[block],
            sem.at[piece],
            block_sem.at[block, piece],
            device_id=target,
            device_id_type=MESH,
        )

    def onward(block, piece, target, sem):
        return pltpu.make_async_remote_copy(
            wholes[piece].at[block],
            wholes[piece].at[block],
            sem.at[piece],
            block_sem.at[block, piece],
            device_id=target,
            device_id_type=MESH,
        )

    def send(make, block, target, sem):
        for piece in range(4):
            make(block, piece, target, sem).start()

    def arrive(block):
        for piece in range(4):
            onward(block, piece, device(z, x, y, 1 - c), c_sem.at[0]).wait_recv()

    across_x, across_y, across_c = (
        device(z, 1 - x, y, c),
        device(z, x, 1 - y, c),
        device(z, x, y, 1 - c),
    )
    spans = (pl.ds(0, part), pl.ds(part, 2 * tokens))

    def rows_x(stage, goal):
        return pltpu.make_async_remote_copy(
            rows_ref.at[goal * 2 + 1 - x, spans[stage]],
            far_x.at[goal, spans[stage]],
            rx_send.at[stage, goal],
            rx_recv.at[stage, goal],
            device_id=across_x,
            device_id_type=MESH,
        )

    def rows_up(stage, goal):
        return pltpu.make_async_remote_copy(
            total.at[goal, spans[stage]],
            from_low.at[goal, spans[stage]],
            ru_send.at[stage, goal],
            ru_recv.at[stage, goal],
            device_id=device(z + 1, x, y, c),
            device_id_type=MESH,
        )

    def rows_down(stage, goal):
        return pltpu.make_async_remote_copy(
            total.at[goal, spans[stage]],
            from_high.at[goal, spans[stage]],
            rd_send.at[stage, goal],
            rd_recv.at[stage, goal],
            device_id=device(z - 1, x, y, c),
            device_id_type=MESH,
        )

    goals = [
        goal for pair in zip(range(depth // 2), range(depth - 1, 0, -1)) for goal in pair
    ]
    goals += [goal for goal in range(depth) if goal not in goals]

    def reduce(stage):
        span = spans[stage]
        for goal in goals:
            rows_x(stage, goal).wait_recv()
            both = rows_ref[goal * 2 + x, span] + far_x[goal, span]

            @pl.when(goal > z)
            def rising():
                @pl.when(z > 0)
                def more():
                    rows_up(stage, goal).wait_recv()
                    total[goal, span] = both + from_low[goal, span]

                @pl.when(z == 0)
                def alone():
                    total[goal, span] = both

                rows_up(stage, goal).start()

            @pl.when(goal < z)
            def falling():
                @pl.when(z < depth - 1)
                def more():
                    rows_down(stage, goal).wait_recv()
                    total[goal, span] = both + from_high[goal, span]

                @pl.when(z == depth - 1)
                def alone():
                    total[goal, span] = both

                rows_down(stage, goal).start()

            @pl.when(goal == z)
            def here():
                total[goal, span] = both

    def land(stage):
        span = spans[stage]
        for goal in range(depth):

            @pl.when(goal == z)
            def landed():
                @pl.when(z > 0)
                def low_part():
                    rows_up(stage, goal).wait_recv()
                    total[goal, span] = total[goal, span] + from_low[goal, span]

                @pl.when(z < depth - 1)
                def high_part():
                    rows_down(stage, goal).wait_recv()
                    total[goal, span] = total[goal, span] + from_high[goal, span]

                sum_ref[span] = total[goal, span]

    local = [
        pltpu.make_async_copy(pieces[piece], wholes[piece].at[mine], local_sem.at[piece])
        for piece in range(4)
    ]
    send(own, mine, across_y, y_sem.at[mine // 4])

    @pl.when(z < depth - 1)
    def first_up():
        send(own, mine, device(z + 1, x, y, c), up_sem.at[0])

    @pl.when(z > 0)
    def first_down():
        send(own, mine, device(z - 1, x, y, c), down_sem.at[0])

    send(own, mine, across_x, x_sem.at[z])
    send(own, mine, across_c, c_sem.at[mine // 2])
    for copy in local:
        copy.start()
    shard[pl.ds(shard_rows, 8)] = jnp.zeros((8, shard.shape[1]), jnp.float32)
    fetch.wait()
    for goal in goals:
        gather(0, goal * 2 + 1 - x)
        rows_x(0, goal).start()
    for goal in goals:
        gather(0, goal * 2 + x)
    keep.wait()
    for group in range(groups):
        for second in range(2):

            @pl.when((group != dp) | (second != 0))
            def heard():
                told(group, second).wait_recv()

    to_scalars = pltpu.make_async_copy(ids_ref, ids, copy_sem)
    to_scalars.start()

    def spread(block, over_x):
        send(onward, block, across_y, y_sem.at[block // 4])
        if over_x:
            send(onward, block, across_x, x_sem.at[block // 8])
        send(onward, block, across_c, c_sem.at[block // 2])

    def pass_on(step):
        @pl.when(z - step >= 0)
        def risen():
            block = slot(z - step, x, y, c)
            arrive(block)

            @pl.when(z < depth - 1)
            def further():
                send(onward, block, device(z + 1, x, y, c), up_sem.at[step])

            spread(block, True)

        @pl.when(z + step < depth)
        def fallen():
            block = slot(z + step, x, y, c)
            arrive(block)

            @pl.when(z > 0)
            def further():
                send(onward, block, device(z - 1, x, y, c), down_sem.at[step])

            spread(block, True)

    def crossed(step):
        for sign in (1, -1) if step else (1,):

            @pl.when((z + sign * step >= 0) & (z + sign * step < depth))
            def there():
                block = slot(z + sign * step, 1 - x, y, c)
                arrive(block)
                spread(block, False)

    pass_on(1)
    to_scalars.wait()
    for goal in goals:
        gather(1, goal * 2 + 1 - x)
        rows_x(1, goal).start()
    for step in range(2, min(depth, 3)):
        pass_on(step)
    reduce(0)
    for goal in goals:
        gather(1, goal * 2 + x)
    for step in range(3, depth):
        pass_on(step)
    land(0)

    def shared(source, ref, quarter, group, send_sem, target):
        where = ref.at[quarter, group]
        return pltpu.make_async_remote_copy(
            where if source is None else source,
            where,
            send_sem,
            s_recv.at[quarter if ref is near_ref else 2 + quarter, group],
            device_id=target,
            device_id_type=MESH,
        )

    own_shared = sum_ref.at[pl.ds(0, part)]
    keep_shared = pltpu.make_async_copy(own_shared, near_ref.at[0, dp], keep_sem)
    keep_shared.start()

    def plane(group):
        return near_ref.at[0, group]

    def shared_y(source, group):
        return pltpu.make_async_remote_copy(
            source,
            near_ref.at[1, group],
            sy_send.at[group],
            s_recv.at[1, group],
            device_id=across_y,
            device_id_type=MESH,
        )

    def shared_c(source, quarter, group):
        return pltpu.make_async_remote_copy(
            source,
            far_ref.at[quarter, group],
            sc_send.at[quarter, group],
            s_recv.at[2 + quarter, group],
            device_id=across_c,
            device_id_type=MESH,
        )

    @pl.when(z < depth - 1)
    def shared_up():
        shared(own_shared, near_ref, 0, dp, su_send.at[0], device(z + 1, x, y, c)).start()

    @pl.when(z > 0)
    def shared_down():
        shared(own_shared, near_ref, 0, dp, sd_send.at[0], device(z - 1, x, y, c)).start()

    shared(own_shared, near_ref, 0, dp, sx_send.at[z], across_x).start()
    shared_y(own_shared, dp).start()
    shared_c(own_shared, 0, dp).start()
    for step in range(1, depth):

        @pl.when(z - step >= 0)
        def shared_risen():
            group = (z - step) * 2 + x
            copy = shared(
                None, near_ref, 0, group, su_send.at[step], device(z + 1, x, y, c)
            )
            copy.wait_recv()

            @pl.when(z < depth - 1)
            def further():
                copy.start()

            shared(None, near_ref, 0, group, sx_send.at[z - step], across_x).start()
            shared_y(plane(group), group).start()
            shared_c(plane(group), 0, group).start()

        @pl.when(z + step < depth)
        def shared_fallen():
            group = (z + step) * 2 + x
            copy = shared(
                None, near_ref, 0, group, sd_send.at[step], device(z - 1, x, y, c)
            )
            copy.wait_recv()

            @pl.when(z > 0)
            def further():
                copy.start()

            shared(None, near_ref, 0, group, sx_send.at[z + step], across_x).start()
            shared_y(plane(group), group).start()
            shared_c(plane(group), 0, group).start()

    crossed(0)
    reduce(1)
    for step in range(1, depth):
        crossed(step)
    for place in range(depth):
        group = place * 2 + 1 - x
        shared(None, near_ref, 0, group, sx_send.at[place], across_x).wait_recv()
        shared_y(plane(group), group).start()
        shared_c(plane(group), 0, group).start()
    land(1)

    for step in range(depth):
        for sign in (1, -1) if step else (1,):

            @pl.when((z + sign * step >= 0) & (z + sign * step < depth))
            def level():
                for side in (x, 1 - x):
                    block = slot(z + sign * step, side, 1 - y, c)
                    arrive(block)
                    send(onward, block, across_c, c_sem.at[block // 2])

    for group in range(groups):
        shared_y(plane(group), group).wait_recv()
        shared_c(near_ref.at[1, group], 1, group).start()

    for block in range(depth * 8):

        @pl.when(block % 2 != c)
        def from_core():
            arrive(block)

    for group in range(groups):
        for quarter in range(2):
            shared_c(near_ref.at[quarter, group], quarter, group).wait_recv()

    keep_shared.wait()
    for group in range(groups):
        shared_y(plane(group), group).wait_send()
        for quarter in range(2):
            shared_c(near_ref.at[quarter, group], quarter, group).wait_send()
    for place in range(depth):
        shared(None, near_ref, 0, dp, sx_send.at[place], across_x).wait_send()

        @pl.when((z - place >= 0) & (z < depth - 1))
        def shared_rose():
            shared(None, near_ref, 0, dp, su_send.at[place], across_x).wait_send()

        @pl.when((z + place < depth) & (z > 0))
        def shared_fell():
            shared(None, near_ref, 0, dp, sd_send.at[place], across_x).wait_send()

    for copy in local:
        copy.wait()
    for group in range(groups):
        for rank in range(2):

            @pl.when((group != dp) | (rank != y))
            def spoken():
                tell(group, rank).wait_send()

    for goal in range(depth):
        for stage in range(2):
            rows_x(stage, goal).wait_send()

            @pl.when(goal > z)
            def rose():
                rows_up(stage, goal).wait_send()

            @pl.when(goal < z)
            def fell():
                rows_down(stage, goal).wait_send()

    def sent(block, target, sem):
        for piece in range(4):
            onward(block, piece, target, sem).wait_send()

    for step in range(depth):

        @pl.when((z - step >= 0) & (z < depth - 1))
        def rose():
            sent(mine, device(z + 1, x, y, c), up_sem.at[step])

        @pl.when((z + step < depth) & (z > 0))
        def fell():
            sent(mine, device(z - 1, x, y, c), down_sem.at[step])

        sent(mine, across_x, x_sem.at[step])
    for index in range(depth * 2):
        sent(mine, across_y, y_sem.at[index])
    for index in range(depth * 4):
        sent(mine, across_c, c_sem.at[index])


def start(pieces, table, codes, vocab_ids, groups):
    width = table.shape[1]
    height = vocab_ids.shape[0] // (groups * 4) + 2 * codes.shape[2]
    depth = groups // 2
    blocks = depth * 8
    told = (groups, 2, 1, codes.shape[2])
    dma = pltpu.SemaphoreType.DMA
    buffer = pltpu.VMEM((depth, height, width), low)
    return pl.pallas_call(
        functools.partial(start_kernel, depth),
        out_shape=[jax.ShapeDtypeStruct((blocks,) + piece.shape, low) for piece in pieces]
        + [jax.ShapeDtypeStruct((height, width), low), jax.ShapeDtypeStruct(told, jnp.int32)]
        + [jax.ShapeDtypeStruct((2, groups, vocab_ids.shape[0] // blocks, width), low)] * 2,
        in_specs=[ANY] * 5
        + [pl.BlockSpec(memory_space=pltpu.VMEM), pl.BlockSpec(memory_space=pltpu.SMEM)],
        out_specs=[ANY] * 4 + [pl.BlockSpec(memory_space=pltpu.VMEM)] * 2 + [ANY] * 2,
        scratch_shapes=[buffer] * 4
        + [
            pltpu.VMEM((groups, height, width), low),
            pltpu.VMEM((table.shape[0] + 8, width), jnp.float32),
            pltpu.SMEM(told, jnp.int32),
        ]
        + [dma((4,))]
        + [dma((depth, 4))] * 3
        + [dma((depth * 2, 4)), dma((depth * 4, 4)), dma((blocks, 4))]
        + [dma((2, depth))] * 6
        + [dma((groups, 2))] * 2
        + [dma(())] * 2
        + [dma((depth,))] * 3
        + [dma((groups,)), dma((2, groups)), dma((4, groups)), dma(())],
        compiler_params=pltpu.CompilerParams(
            collective_id=0, has_side_effects=True, vmem_limit_bytes=58 * 2**20
        ),
        name="start",
    )(*pieces, table, codes, vocab_ids)


def by_distance(depth, z, act):
    for step in range(depth - 1, -1, -1):
        for sign in (1, -1) if step else (1,):

            @pl.when((z + sign * step >= 0) & (z + sign * step < depth))
            def reached():
                act(z + sign * step)


def add_into(total, block, *terms):
    height = total.shape[1]
    chunk = 96 if height % 96 == 0 else height

    @pl.loop(0, height // chunk)
    def chunks(index):
        part = pl.ds(pl.multiple_of(index * chunk, chunk), chunk)
        value = total[block, part].astype(jnp.float32)
        for buffer, place in terms:
            value = value + buffer[place, part].astype(jnp.float32)
        total[block, part] = value.astype(low)


def finish_kernel(depth, heights, tile, *refs):
    pieces = refs[0:3]
    rows_ref, places_ref, small_ref = refs[3:6]
    grad_ref, table_out, small_out = refs[6:9]
    total, far_c, far_p, far_s, from_low, from_high = refs[9:15]
    rows, given, far_t, part, mine, far_part, small, far_small = refs[15:23]
    local_sem, c_send, c_recv, p_send, p_recv, s_send, s_recv = refs[23:30]
    u_send, u_recv, d_send, d_recv = refs[30:34]
    own_sem, ru_send, rd_send, rx_send, r_recv = refs[34:39]
    t_send, t_recv, ty_send, ty_recv, o_send, o_recv = refs[39:45]
    e_send, e_recv, f_send, f_recv = refs[45:49]
    z, x, y, c = coordinates(depth)
    dp = z * 2 + x
    firsts = [sum(heights[:index]) for index in range(3)]
    up, down = device(z + 1, x, y, c), device(z - 1, x, y, c)
    across_x, across_y, across_c = (
        device(z, 1 - x, y, c),
        device(z, x, 1 - y, c),
        device(z, x, y, 1 - c),
    )

    def y_first(place, core):
        return (core == 0) & (place >= 0)

    def across_p(place):
        first = y_first(place, c)
        return tuple(jnp.where(first, one, two) for one, two in zip(across_y, across_x))

    def across_s(place):
        first = y_first(place, c)
        return tuple(jnp.where(first, two, one) for one, two in zip(across_y, across_x))

    def own_p(place, core=c):
        return jnp.where(y_first(place, core), y, x)

    def own_s(place, core=c):
        return jnp.where(y_first(place, core), x, y)

    def own_block(place):
        return (place * 2 + x) * 2 + y

    def mate(offset):
        return device(z, (x + offset // 4) % 2, (y + offset // 2) % 2, (c + offset) % 2)

    barrier = pltpu.get_barrier_semaphore()
    for offset in range(1, 8):
        pl.semaphore_signal(barrier, 1, device_id=mate(offset), device_id_type=MESH)
    for other in range(depth):

        @pl.when(other != z)
        def hello():
            pl.semaphore_signal(
                barrier, 1, device_id=device(other, x, y, c), device_id_type=MESH
            )

    pl.semaphore_wait(barrier, 7 + depth - 1)

    def remote(source, goal, send_sem, recv_sem, target):
        return pltpu.make_async_remote_copy(
            source, goal, send_sem, recv_sem, device_id=target, device_id_type=MESH
        )

    def block_of(place, s, p, core=c):
        return place * 4 + jnp.where(y_first(place, core), s * 2 + p, p * 2 + s)

    def local(block, piece):
        return pltpu.make_async_copy(
            pieces[piece].at[block * 2 + c],
            total.at[block, pl.ds(firsts[piece], heights[piece])],
            local_sem.at[block, piece],
        )

    def over_c(block, piece):
        return remote(
            pieces[piece].at[block * 2 + 1 - c],
            far_c.at[block, pl.ds(firsts[piece], heights[piece])],
            c_send.at[block, piece],
            c_recv.at[block, piece],
            across_c,
        )

    def over_p(place, s):
        pair = place * 2 + s
        return remote(
            total.at[block_of(place, s, 1 - own_p(place))],
            far_p.at[pair],
            p_send.at[pair],
            p_recv.at[pair],
            across_p(place),
        )

    def over_s(place):
        return remote(
            total.at[block_of(place, 1 - own_s(place), own_p(place))],
            far_s.at[place],
            s_send.at[place],
            s_recv.at[place],
            across_s(place),
        )

    half = total.shape[1] // 2

    def rise(place, side):
        lines = pl.ds(side * half, half)
        return remote(
            total.at[own_block(place), lines],
            from_low.at[place, lines],
            u_send.at[place, side],
            u_recv.at[place, side],
            up,
        )

    def fall(place, side):
        lines = pl.ds(side * half, half)
        return remote(
            total.at[own_block(place), lines],
            from_high.at[place, lines],
            d_send.at[place, side],
            d_recv.at[place, side],
            down,
        )

    def add_half(block, side, buffer, place):
        lines = pl.ds(side * half, half)
        value = total[block, lines].astype(jnp.float32) + buffer[place, lines].astype(jnp.float32)
        total[block, lines] = value.astype(low)

    def own_rows(send_sem, target, side):
        return remote(rows_ref, rows.at[side, z], send_sem, r_recv.at[side, z], target)

    def rows_on(place, send_sem, target, side):
        return remote(
            rows.at[0, place], rows.at[side, place], send_sem, r_recv.at[side, place], target
        )

    own = pltpu.make_async_copy(rows_ref, rows.at[0, z], own_sem)
    own.start()

    @pl.when(z < depth - 1)
    def first_up():
        own_rows(ru_send.at[0], up, 0).start()

    @pl.when(z > 0)
    def first_down():
        own_rows(rd_send.at[0], down, 0).start()

    own_rows(rx_send.at[z], across_x, 1).start()

    for turn in range(2):
        for side in range(2):

            def launch(place):
                s, p = own_s(place, 1 - c), own_p(place, 1 - c)
                s, p = (s if side else 1 - s), (p if turn else 1 - p)
                there = block_of(place, s, p, 1 - c)
                s, p = own_s(place), own_p(place)
                s, p = (s if side else 1 - s), (p if turn else 1 - p)
                here = block_of(place, s, p)
                for piece in range(3):
                    over_c(there, piece).start()
                    local(here, piece).start()

            by_distance(depth, z, launch)

    def ready(block):
        for piece in range(3):
            local(block, piece).wait()
            over_c(block, piece).wait_recv()

    def give_p(along_y):
        for side in range(2):

            def give(place):
                @pl.when(y_first(place, c) == along_y)
                def now():
                    s = own_s(place)
                    s = s if side else 1 - s
                    block = block_of(place, s, 1 - own_p(place))
                    ready(block)
                    add_into(total, block, (far_c, block))
                    over_p(place, s).start()

            by_distance(depth, z, give)

    give_p(True)

    for step in range(1, depth):

        @pl.when(z - step >= 0)
        def risen():
            rows_on(z - step, ru_send.at[step], up, 0).wait_recv()

            @pl.when(z < depth - 1)
            def further():
                rows_on(z - step, ru_send.at[step], up, 0).start()

            rows_on(z - step, rx_send.at[z - step], across_x, 1).start()

        @pl.when(z + step < depth)
        def fallen():
            rows_on(z + step, rd_send.at[step], down, 0).wait_recv()

            @pl.when(z > 0)
            def further():
                rows_on(z + step, rd_send.at[step], down, 0).start()

            rows_on(z + step, rx_send.at[z + step], across_x, 1).start()

    give_p(False)
    own.wait()

    height = part.shape[0]
    count = places_ref.shape[2]

    def collect(rank, core, goal, side):
        @pl.loop(0, height // tile)
        def tiles(index):
            first = index * tile
            lines = pl.ds(pl.multiple_of(first, tile), tile)
            at = (
                (rank * 2 + core) * height
                + first
                + lax.broadcasted_iota(jnp.int32, (tile, count), 0)
            )
            picked = jnp.where(at == places_ref[side], 1.0, 0.0).astype(low)
            value = product(picked, rows[side].reshape(count, rows.shape[3]))
            if side:
                value = value + goal[lines].astype(jnp.float32)
            goal[lines] = value.astype(low)

    def over_t(rank):
        index = jnp.where(rank == y, 1, 0)
        return remote(
            given.at[index], far_t.at[index], t_send.at[index], t_recv.at[index], across_c
        )

    chunk = 80 if height % 80 == 0 else height

    def pieces_of(act):
        @pl.loop(0, height // chunk)
        def step(index):
            act(pl.ds(pl.multiple_of(index * chunk, chunk), chunk))

    collect(1 - y, 1 - c, given.at[0], 0)
    collect(1 - y, c, part, 0)
    collect(y, 1 - c, given.at[1], 0)
    collect(y, c, mine, 0)
    for place in range(depth):
        rows_on(place, rx_send.at[place], across_x, 1).wait_recv()
    collect(1 - y, 1 - c, given.at[0], 1)
    over_t(1 - y).start()
    collect(1 - y, c, part, 1)
    over_t(1 - y).wait_recv()

    def first_sum(lines):
        part[lines] = (part[lines].astype(jnp.float32) + far_t[0, lines].astype(jnp.float32)).astype(
            low
        )

    pieces_of(first_sum)
    over_part = remote(part, far_part, ty_send, ty_recv, across_y)
    over_part.start()
    collect(y, 1 - c, given.at[1], 1)
    over_t(y).start()
    collect(y, c, mine, 1)

    def give_s(place):
        s = 1 - own_s(place)
        block = block_of(place, s, own_p(place))
        ready(block)
        over_p(place, s).wait_recv()
        add_into(total, block, (far_c, block), (far_p, place * 2 + s))
        over_s(place).start()

    by_distance(depth, z, give_s)

    over_t(y).wait_recv()
    over_part.wait_recv()

    def second_sum(index, squares):
        lines = pl.ds(pl.multiple_of(index * chunk, chunk), chunk)
        value = (
            mine[lines].astype(jnp.float32)
            + far_t[1, lines].astype(jnp.float32)
            + far_part[lines].astype(jnp.float32)
        ).astype(low)
        mine[lines] = value
        value = value.astype(jnp.float32)
        return squares + jnp.sum((value * value).reshape(-1, 8, value.shape[1]), axis=0)

    squares = lax.fori_loop(
        0, height // chunk, second_sum, jnp.zeros((8, part.shape[1]), jnp.float32)
    )

    def out_mine(index, target):
        where = table_out.at[y * 2 + c]
        return remote(mine, where, o_send.at[index], o_recv.at[y * 2 + c], target)

    def out(rank, core):
        where = table_out.at[rank * 2 + core]
        return remote(where, where, o_send.at[2], o_recv.at[rank * 2 + core], across_c)

    keep = pltpu.make_async_copy(mine, table_out.at[y * 2 + c], own_sem)
    out_mine(0, across_y).start()
    out_mine(1, across_c).start()
    keep.start()

    def give_z(place):
        block = own_block(place)
        s = own_s(place)
        ready(block)
        over_p(place, s).wait_recv()
        over_s(place).wait_recv()
        add_into(total, block, (far_c, block), (far_p, place * 2 + s), (far_s, place))
        for side in range(2):

            @pl.when(place > z)
            def rising():
                @pl.when(z > 0)
                def more():
                    rise(place, side).wait_recv()
                    add_half(block, side, from_low, place)

                rise(place, side).start()

            @pl.when(place < z)
            def falling():
                @pl.when(z < depth - 1)
                def more():
                    fall(place, side).wait_recv()
                    add_half(block, side, from_high, place)

                fall(place, side).start()

    by_distance(depth, z, give_z)
    grad_ref[...] = total[own_block(z)].astype(jnp.float32)
    for side in range(2):
        there = pl.ds(side * half, half)

        @pl.when(z > 0)
        def low_part():
            rise(z, side).wait_recv()
            grad_ref[there] = grad_ref[there] + from_low[z, there].astype(jnp.float32)

        @pl.when(z < depth - 1)
        def high_part():
            fall(z, side).wait_recv()
            grad_ref[there] = grad_ref[there] + from_high[z, there].astype(jnp.float32)

    lines = lax.broadcasted_iota(jnp.int32, small.shape[1:], 0)
    lanes = lax.broadcasted_iota(jnp.int32, small.shape[1:], 1)
    last = (lines == small.shape[1] - 1) & (lanes == 0)
    grad_squares = jnp.sum(grad_ref[...] * grad_ref[...])
    small[0] = small_ref[...] + jnp.where(last, jnp.sum(squares) + grad_squares, 0.0)

    def exchange(offset):
        return remote(
            small.at[0], small.at[offset], e_send.at[offset], e_recv.at[offset], mate(offset)
        )

    def announce(other, source):
        where = far_small.at[source]
        return remote(where, where, f_send.at[other], f_recv.at[source], device(other, x, y, c))

    for offset in range(1, 8):
        exchange(offset).start()
    for offset in range(1, 8):
        exchange(offset).wait_recv()
    gathered = jnp.zeros(small.shape[1:], jnp.float32)
    for rank in range(8):
        gathered = gathered + small[
            (x + rank // 4) % 2 * 4 + (y + rank // 2) % 2 * 2 + (c + rank) % 2
        ]
    far_small[z] = gathered
    for other in range(depth):

        @pl.when(other != z)
        def telling():
            announce(other, z).start()

    for other in range(depth):

        @pl.when(other != z)
        def hearing():
            announce(other, other).wait_recv()

    gathered = far_small[0]
    for other in range(1, depth):
        gathered = gathered + far_small[other]
    small_out[...] = gathered
    out(1 - y, c).wait_recv()
    out(1 - y, c).start()
    out(y, 1 - c).wait_recv()
    out(1 - y, 1 - c).wait_recv()

    keep.wait()
    out_mine(0, across_y).wait_send()
    out_mine(1, across_c).wait_send()
    out(1 - y, c).wait_send()
    over_part.wait_send()
    for offset in range(1, 8):
        exchange(offset).wait_send()
    for other in range(depth):

        @pl.when(other != z)
        def told():
            announce(other, z).wait_send()

    for rank in range(2):
        over_t(rank).wait_send()
    for place in range(depth):
        rows_on(place, rx_send.at[place], across_x, 1).wait_send()
        over_s(place).wait_send()
        for side in range(2):
            over_p(place, side).wait_send()
            for rank in range(2):
                for piece in range(3):
                    over_c((place * 2 + side) * 2 + rank, piece).wait_send()

        for side in range(2):

            @pl.when(place > z)
            def rose():
                rise(place, side).wait_send()

            @pl.when(place < z)
            def fell():
                fall(place, side).wait_send()

        @pl.when((z - place >= 0) & (z < depth - 1))
        def rows_rose():
            rows_on(z, ru_send.at[place], up, 0).wait_send()

        @pl.when((z + place < depth) & (z > 0))
        def rows_fell():
            rows_on(z, rd_send.at[place], down, 0).wait_send()


def finish(pieces, rows, places, small, quarter, tile):
    blocks = pieces[0].shape[0]
    heights = [piece.shape[1] for piece in pieces]
    height, width = sum(heights), pieces[0].shape[2]
    depth = blocks // 8
    dma = pltpu.SemaphoreType.DMA
    vmem = pl.BlockSpec(memory_space=pltpu.VMEM)

    def buffer(count):
        return pltpu.VMEM((count, height, width), low)

    return pl.pallas_call(
        functools.partial(finish_kernel, depth, heights, tile),
        out_shape=[
            jax.ShapeDtypeStruct((height, width), jnp.float32),
            jax.ShapeDtypeStruct((4, quarter, width), low),
            jax.ShapeDtypeStruct(small.shape, jnp.float32),
        ],
        in_specs=[ANY] * 4 + [vmem] * 2,
        out_specs=[vmem, ANY, vmem],
        scratch_shapes=[buffer(depth * 4), buffer(depth * 4), buffer(depth * 2)]
        + [buffer(depth)] * 3
        + [
            pltpu.VMEM((2, depth) + rows.shape, low),
            pltpu.VMEM((2, quarter, width), low),
            pltpu.VMEM((2, quarter, width), low),
            pltpu.VMEM((quarter, width), low),
            pltpu.VMEM((quarter, width), low),
            pltpu.VMEM((quarter, width), low),
            pltpu.VMEM((8,) + small.shape, jnp.float32),
            pltpu.VMEM((depth,) + small.shape, jnp.float32),
        ]
        + [dma((depth * 4, 3))] * 3
        + [dma((depth * 2,))] * 2
        + [dma((depth,))] * 2
        + [dma((depth, 2))] * 4
        + [dma(())]
        + [dma((depth,))] * 3
        + [dma((2, depth))]
        + [dma((2,))] * 2
        + [dma(())] * 2
        + [dma((3,)), dma((4,))]
        + [dma((8,))] * 2
        + [dma((depth,))] * 2,
        compiler_params=pltpu.CompilerParams(
            collective_id=1, has_side_effects=True, vmem_limit_bytes=62 * 2**20
        ),
        name="finish",
    )(*pieces, rows, places, small)


def by_side(places, depth):
    places = places.reshape(depth, 2, -1)
    x = lax.axis_index("dp") % 2
    sides = [lax.dynamic_index_in_dim(places, side, 1, keepdims=False) for side in (x, 1 - x)]
    return jnp.stack(sides).reshape(2, 1, -1)


def moments(gradient, first, second):
    first_new = beta_one * first + (1.0 - beta_one) * gradient
    second_new = beta_two * second + (1.0 - beta_two) * gradient * gradient
    second_hat = second_new * (1.0 / (1.0 - beta_two**STEP))
    root = second_hat * lax.rsqrt(second_hat) + adam_eps
    direction = first_new * (1.0 / (1.0 - beta_one**STEP)) / root
    return direction, first_new, second_new


def update_kernel(steps, cuts, *refs):
    table_ref, table_m_ref, table_v_ref, table_g_ref = refs[0:4]
    small_ref, sums_ref, gains_ref, gains_m_ref, gains_v_ref = refs[4:9]
    grad_ref, block_ref, block_m_ref, block_v_ref, bases_ref = refs[9:14]
    table_new, table_m_new, table_v_new, table_low = refs[14:18]
    values_ref, gains_new, gains_m_new, gains_v_new = refs[18:22]
    block_new, block_m_new, block_v_new, block_low = refs[22:26]
    bases, turned, factor_ref, bases_sem = refs[26:30]
    now = pl.program_id(0)

    def base(index):
        return pltpu.make_async_copy(bases_ref.at[index], bases.at[index], bases_sem.at[index])

    @pl.when(now == 0)
    def begin():
        for index in range(4):
            base(index).start()
        lines = lax.broadcasted_iota(jnp.int32, small_ref.shape, 0)
        lanes = lax.broadcasted_iota(jnp.int32, small_ref.shape, 1)

        def value_at(place):
            there = (lines == place // 128) & (lanes == place % 128)
            return jnp.sum(jnp.where(there, small_ref[...], 0.0), axis=(0, 1), keepdims=True)

        count = value_at(3 * D + 1)
        gain_grads = sums_ref[...] / count
        squares = value_at((small_ref.shape[0] - 1) * 128) / (count * count)
        norm = jnp.sqrt(squares + jnp.sum(gain_grads * gain_grads, axis=(0, 1), keepdims=True))
        clip = jnp.minimum(1.0, clip_norm / norm)
        factor_ref[...] = jnp.broadcast_to(clip / count, factor_ref.shape)
        spots = lax.broadcasted_iota(jnp.int32, values_ref.shape, 1)
        values_ref[...] = jnp.where(spots == 0, value_at(3 * D) / count, norm)
        direction, gains_m_new[...], gains_v_new[...] = moments(
            gain_grads * clip, gains_m_ref[...], gains_v_ref[...]
        )
        gains_new[...] = gains_ref[...] - rate_gain * direction

    factor = factor_ref[0:1, 0:1]
    direction, table_m_new[...], table_v_new[...] = moments(
        table_g_ref[...].astype(jnp.float32) * factor, table_m_ref[...], table_v_ref[...]
    )
    table_tile = table_ref[...]
    table_tile = table_tile - rate_table * (direction + decay_rate * table_tile)
    table_new[...] = table_tile
    table_low[...] = table_tile.astype(low)

    spots = lax.broadcasted_iota(jnp.int32, turned.shape, 1)

    def columns(index, value):
        mine = (spots >= cuts[index]) & (spots < cuts[index + 1])
        return jnp.where(mine, value, 0.0).astype(low)

    for index in range(4):

        @pl.when(now == min(1 + index, steps - 1))
        def rotate():
            base(index).wait()
            term = contract_rows(
                bases[index].astype(low), columns(index, grad_ref[...] * factor_ref[0:1, 0:1])
            )
            turned[...] = term if index == 0 else turned[...] + term

    @pl.when(now == min(5, steps - 1))
    def move():
        direction, block_m_new[...], block_v_new[...] = moments(
            turned[...], block_m_ref[...], block_v_ref[...]
        )
        turned[...] = direction

    for index in range(4):

        @pl.when(now == min(5 + index, steps - 1))
        def rotate_back():
            term = product(bases[index].astype(low), columns(index, turned[...]))
            block_new[...] = term if index == 0 else block_new[...] + term

    @pl.when(now == min(8, steps - 1))
    def store():
        block = block_ref[...]
        block = block - rate_block * (block_new[...] + decay_rate * block)
        block_new[...] = block
        block_low[...] = block.astype(low)


def update(cuts, tables, table_grads, small, gain_sums, gains, block_grads, blocks, bases):
    rows, width = tables[0].shape
    tile = max(
        size
        for size in range(8, 401, 8)
        if rows % size == 0 and (size % 16 == 0 or rows % 16)
    )
    steps = rows // tile
    f32 = jnp.float32

    def whole(array):
        return pl.BlockSpec(array.shape, lambda i: (0,) * array.ndim)

    tiles = pl.BlockSpec((tile, width), lambda i: (i, 0))
    table = jax.ShapeDtypeStruct(tables[0].shape, f32)
    gain = jax.ShapeDtypeStruct(gains[0].shape, f32)
    matrix = jax.ShapeDtypeStruct(blocks[0].shape, f32)
    values = jax.ShapeDtypeStruct((8, 128), f32)
    outs = [table] * 3 + [jax.ShapeDtypeStruct(table.shape, low)]
    outs += [values] + [gain] * 3
    outs += [matrix] * 3 + [jax.ShapeDtypeStruct(matrix.shape, low)]
    return pl.pallas_call(
        functools.partial(update_kernel, steps, cuts),
        grid=(steps,),
        out_shape=outs,
        in_specs=[tiles] * 4
        + [whole(small), whole(gain_sums)]
        + [whole(gain)] * 3
        + [whole(matrix)] * 4
        + [ANY],
        out_specs=[tiles] * 4 + [whole(values)] + [whole(gain)] * 3 + [whole(matrix)] * 4,
        scratch_shapes=[
            pltpu.VMEM(bases.shape, f32),
            pltpu.VMEM(matrix.shape, f32),
            pltpu.VMEM((8, 128), f32),
            pltpu.SemaphoreType.DMA((4,)),
        ],
        compiler_params=pltpu.CompilerParams(vmem_limit_bytes=58 * 2**20),
        name="update",
    )(*tables, table_grads, small, gain_sums, *gains, block_grads, *blocks, bases)


def cost(flops):
    return pl.CostEstimate(flops=flops, bytes_accessed=10**6, transcendentals=0)


LARGE = 58 * 2**20
CHUNK = 512


def inverse_rms(value):
    return lax.rsqrt(jnp.mean(value * value, axis=-1, keepdims=True) + eps_norm)


def norm_back(value, r, gain, grad):
    scaled = grad * gain
    d_value = r * scaled - value * (r * r * r) * jnp.mean(value * scaled, axis=-1, keepdims=True)
    return d_value, jnp.sum(grad * value * r, axis=0, keepdims=True)


def local_call(kernel, name, flops, outs, args, scratch=(), remain=()):
    vmem = pl.BlockSpec(memory_space=pltpu.VMEM)
    return pl.pallas_call(
        kernel,
        out_shape=[jax.ShapeDtypeStruct(shape, kind) for shape, kind in outs],
        in_specs=[ANY if place in remain else vmem for place in range(len(args))],
        out_specs=[vmem] * len(outs),
        scratch_shapes=list(scratch),
        compiler_params=pltpu.CompilerParams(vmem_limit_bytes=LARGE),
        cost_estimate=cost(flops),
        name=name,
    )(*args)


def project_kernel(hidden_ref, gain_ref, weight_ref, cosine_ref, sine_ref, *refs):
    normed_ref, query_ref, own_ref = refs
    hidden = hidden_ref[...]
    normed = (hidden * inverse_rms(hidden) * gain_ref[...]).astype(low)
    normed_ref[...] = normed
    cosine, sine = cosine_ref[...], sine_ref[...]
    first = lax.broadcasted_iota(jnp.int32, cosine.shape, 1) % HD < HD // 2
    for index in range(3 * D // 128):
        columns = pl.ds(index * 128, 128)
        value = contract_cols(normed, weight_ref[columns])
        if index < 2 * D // 128:
            turned = jnp.where(
                first, -pltpu.roll(value, 128 - HD // 2, 1), pltpu.roll(value, HD // 2, 1)
            )
            value = value * cosine + turned * sine
        if index < D // 128:
            query_ref[:, columns] = value.astype(low)
        else:
            own_ref[:, pl.ds(index * 128 - D, 128)] = value.astype(low)


def project(hidden, gain, weight, cosine, sine):
    rows = hidden.shape[0]
    outs = [((rows, D), low), ((rows, D), low), ((rows, 2 * D), low)]
    return local_call(project_kernel, "project", 6 * 10**9, outs, [hidden, gain, weight, cosine, sine])


def allowed(rows_ref, columns_ref):
    return (rows_ref[:, 0:1] == columns_ref[0:1]) & (rows_ref[:, 1:2] >= columns_ref[1:2])


def pair_of_heads(index):
    return pl.ds(index * 128, 128)


def attention_weight(query, keys, allow):
    score = jnp.where(allow, contract_cols(query, keys) * scale, -1e30)
    power = jnp.exp(score - jnp.max(score, axis=-1, keepdims=True))
    return power * (1.0 / jnp.sum(power, axis=-1, keepdims=True))


def forward_kernel(hidden_ref, query_ref, own_ref, far_ref, rows_ref, columns_ref, *refs):
    out_weight, gain_ref, gate_hbm, down_hbm, output_ref, merged_ref, middle_ref = refs[:7]
    gates, downs, sems = refs[7:]
    copies = weight_copies(gate_hbm, down_hbm, gates, downs, sems)
    for group in copies:
        for copy in group:
            copy.start()
    allow = allowed(rows_ref, columns_ref)
    rows = hidden_ref.shape[0]
    first = lax.broadcasted_iota(jnp.int32, (rows, 128), 1) < HD

    @pl.loop(0, D // 128)
    def heads(index):
        columns = pl.ds(pl.multiple_of(index * 128, 128), 128)
        values_at = pl.ds(pl.multiple_of(index * 128 + D, 128), 128)
        query = query_ref[:, columns]
        keys = jnp.concatenate([own_ref[:, columns], far_ref[:, columns]], axis=0)
        values = jnp.concatenate([own_ref[:, values_at], far_ref[:, values_at]], axis=0)
        mixed = []
        for side in range(2):
            mine = jnp.where(first == (side == 0), query, jnp.zeros_like(query))
            weight = attention_weight(mine, keys, allow).astype(low)
            mixed.append(product(weight, values))
        merged_ref[:, columns] = jnp.where(first, mixed[0], mixed[1]).astype(low)

    middle = hidden_ref[...] + contract_cols(merged_ref[...], out_weight[...])
    middle_ref[...] = middle
    normed = (middle * inverse_rms(middle) * gain_ref[...]).astype(low)
    output_ref[...] = middle
    for index, group in enumerate(copies):
        for copy in group:
            copy.wait()
        gate = contract_cols(normed, gates[pl.ds(index * CHUNK, CHUNK)])
        up = contract_cols(normed, gates[pl.ds(FF + index * CHUNK, CHUNK)])
        action = (gate * jax.nn.sigmoid(gate) * up).astype(low)
        output_ref[...] += product(action, downs[pl.ds(index * CHUNK, CHUNK)])


def weight_copies(gate_hbm, down_hbm, gates, downs, sems):
    groups = []
    for index in range(FF // CHUNK):
        parts = [
            (gate_hbm, gates, index * CHUNK),
            (gate_hbm, gates, FF + index * CHUNK),
            (down_hbm, downs, index * CHUNK),
        ]
        groups.append(
            [
                pltpu.make_async_copy(
                    source.at[pl.ds(at, CHUNK)], goal.at[pl.ds(at, CHUNK)], sems.at[index, place]
                )
                for place, (source, goal, at) in enumerate(parts)
            ]
        )
    return groups


def weight_buffers():
    return [
        pltpu.VMEM((2 * FF, D), low),
        pltpu.VMEM((FF, D), low),
        pltpu.SemaphoreType.DMA((FF // CHUNK, 3)),
    ]


def forward(hidden, query, own, far, rows, columns, w_out, gain, w_gu, w_down):
    count = hidden.shape[0]
    outs = [((count, D), jnp.float32), ((count, D), low), ((count, D), jnp.float32)]
    args = [hidden, query, own, far, rows, columns, w_out, gain, w_gu, w_down]
    return local_call(forward_kernel, "forward", 5 * 10**9, outs, args, weight_buffers(), (8, 9))


def backward_kernel(gradient_ref, middle_ref, query_ref, own_ref, far_ref, *refs):
    rows_ref, columns_ref, out_weight, gain_ref, gate_hbm, down_hbm = refs[:6]
    d_query_ref, d_own_ref, d_far_ref, d_middle_ref, gain_out = refs[6:11]
    low_ref, normed_ref, action_ref, d_gate_ref, middle_low_ref = refs[11:16]
    gates, downs, sems, total = refs[16:]
    copies = weight_copies(gate_hbm, down_hbm, gates, downs, sems)
    for group in copies:
        for copy in group:
            copy.start()
    gradient = gradient_ref[...]
    grad_low = gradient.astype(low)
    low_ref[...] = grad_low
    middle = middle_ref[...]
    r = inverse_rms(middle)
    normed = (middle * r * gain_ref[...]).astype(low)
    normed_ref[...] = normed
    total[...] = jnp.zeros_like(total)
    for index, group in enumerate(copies):
        for copy in group:
            copy.wait()
        first = pl.ds(index * CHUNK, CHUNK)
        second = pl.ds(FF + index * CHUNK, CHUNK)
        gate = contract_cols(normed, gates[first])
        up = contract_cols(normed, gates[second])
        chance = jax.nn.sigmoid(gate)
        action_ref[:, first] = (gate * chance * up).astype(low)
        d_action = contract_cols(grad_low, downs[first])
        d_gate = (d_action * up * (chance + gate * chance * (1.0 - chance))).astype(low)
        d_up = (d_action * gate * chance).astype(low)
        d_gate_ref[:, first] = d_gate
        d_gate_ref[:, second] = d_up
        total[...] += product(d_gate, gates[first]) + product(d_up, gates[second])
    d_middle, gain_out[...] = norm_back(middle, r, gain_ref[...], total[...])
    d_middle = gradient + d_middle
    d_middle_ref[...] = d_middle
    middle_low = d_middle.astype(low)
    middle_low_ref[...] = middle_low
    total[...] = product(middle_low, out_weight[...])
    allow = allowed(rows_ref, columns_ref)
    rows = gradient.shape[0]
    first = lax.broadcasted_iota(jnp.int32, (rows, 128), 1) < HD
    first_all = lax.broadcasted_iota(jnp.int32, (2 * rows, 128), 1) < HD

    @pl.loop(0, D // 128)
    def heads(index):
        columns = pl.ds(pl.multiple_of(index * 128, 128), 128)
        values_at = pl.ds(pl.multiple_of(index * 128 + D, 128), 128)
        query = query_ref[:, columns]
        upstream = total[:, columns].astype(low)
        keys = jnp.concatenate([own_ref[:, columns], far_ref[:, columns]], axis=0)
        values = jnp.concatenate([own_ref[:, values_at], far_ref[:, values_at]], axis=0)
        d_queries, d_keys, d_values = [], [], []
        for side in range(2):
            mine = jnp.where(first == (side == 0), query, jnp.zeros_like(query))
            grad = jnp.where(first == (side == 0), upstream, jnp.zeros_like(upstream))
            weight = attention_weight(mine, keys, allow)
            d_values.append(contract_rows(weight.astype(low), upstream))
            d_weight = contract_cols(grad, values)
            d_score = weight * (d_weight - jnp.sum(d_weight * weight, axis=-1, keepdims=True))
            d_score = d_score.astype(low)
            d_queries.append(product(d_score, keys) * scale)
            d_keys.append(contract_rows(d_score, query) * scale)
        d_query_ref[:, columns] = jnp.where(first, *d_queries).astype(low)
        d_key = jnp.where(first_all, *d_keys)
        d_value = jnp.where(first_all, *d_values)
        d_own_ref[:, columns] = d_key[:rows]
        d_own_ref[:, values_at] = d_value[:rows]
        d_far_ref[:, columns] = d_key[rows:].astype(low)
        d_far_ref[:, values_at] = d_value[rows:].astype(low)


def backward(gradient, middle, query, own, far, rows, columns, w_out, gain, w_gu, w_down):
    count = gradient.shape[0]
    f32 = jnp.float32
    outs = [
        ((count, D), low),
        ((count, 2 * D), f32),
        ((count, 2 * D), low),
        ((count, D), f32),
        ((1, D), f32),
        ((count, D), low),
        ((count, D), low),
        ((count, FF), low),
        ((count, 2 * FF), low),
        ((count, D), low),
    ]
    args = [gradient, middle, query, own, far, rows, columns, w_out, gain, w_gu, w_down]
    scratch = weight_buffers() + [pltpu.VMEM((count, D), f32)]
    return local_call(backward_kernel, "backward", 30 * 10**9, outs, args, scratch, (9, 10))


def unproject_kernel(d_query_ref, d_own_ref, d_far_ref, d_middle_ref, hidden_ref, *refs):
    gain_ref, weight_ref, cosine_ref, sine_ref, gradient_ref, gain_out, d_qkv_ref = refs
    cosine, sine = cosine_ref[...], sine_ref[...]
    first = lax.broadcasted_iota(jnp.int32, cosine.shape, 1) % HD < HD // 2
    for index in range(3 * D // 128):
        columns = pl.ds(index * 128, 128)
        if index < D // 128:
            value = d_query_ref[:, columns].astype(jnp.float32)
        else:
            there = pl.ds(index * 128 - D, 128)
            value = d_own_ref[:, there] + d_far_ref[:, there].astype(jnp.float32)
            value = value.astype(low).astype(jnp.float32)
        if index < 2 * D // 128:
            part = value * sine
            turned = jnp.where(
                first, pltpu.roll(part, 128 - HD // 2, 1), -pltpu.roll(part, HD // 2, 1)
            )
            value = value * cosine + turned
        d_qkv_ref[:, columns] = value.astype(low)
    hidden = hidden_ref[...]
    d_hidden, gain_out[...] = norm_back(
        hidden, inverse_rms(hidden), gain_ref[...], product(d_qkv_ref[...], weight_ref[...])
    )
    gradient_ref[...] = d_middle_ref[...] + d_hidden


def unproject(d_query, d_own, d_far, d_middle, hidden, gain, weight, cosine, sine):
    rows = hidden.shape[0]
    outs = [((rows, D), jnp.float32), ((1, D), jnp.float32), ((rows, 3 * D), low)]
    args = [d_query, d_own, d_far, d_middle, hidden, gain, weight, cosine, sine]
    return local_call(unproject_kernel, "unproject", 10**6, outs, args)


def weigh_kernel(*refs):
    pairs = [refs[4 * index : 4 * index + 4] for index in range(4)]
    gate_out, down_out, joined, qkv, out = refs[16:21]
    now = pl.program_id(0)

    def gradient(index):
        left_one, left_two, right_one, right_two = pairs[index]
        total = contract_rows(left_one[...], right_one[...])
        return total + contract_rows(left_two[...], right_two[...])

    gate_out[...] = gradient(0).astype(low).reshape(gate_out.shape)
    down_out[...] = gradient(1).astype(low).reshape(down_out.shape)

    @pl.when(now < 6)
    def first():
        qkv[pl.ds(pl.multiple_of(now * 384, 384), 384)] = gradient(2)

    @pl.when(now >= 6)
    def second():
        out[pl.ds(pl.multiple_of((now - 6) * 384, 384), 384)] = gradient(3)

    @pl.when(now == 7)
    def join():
        blocks = joined.shape[0]
        tall, flat = 3 * D // blocks, D // blocks
        for block in range(blocks):
            parts = [qkv[block * tall : (block + 1) * tall], out[block * flat : (block + 1) * flat]]
            joined[block] = jnp.concatenate(parts, axis=0).astype(low)


def weigh(d_gates, normed_twos, actions, lows, d_qkvs, normeds, middles, merges, blocks):
    rows = lows[0].shape[0]

    def both(arrays, width, place):
        return [(array, pl.BlockSpec((rows, width), place)) for array in arrays]

    def whole(arrays):
        return [(array, pl.BlockSpec((rows, D), lambda i: (0, 0))) for array in arrays]

    def early(i):
        return (0, jnp.minimum(i, 5))

    def late(i):
        return (0, jnp.maximum(i - 6, 0))

    listed = both(d_gates, 768, lambda i: (0, i)) + whole(normed_twos)
    listed += both(actions, 384, lambda i: (0, i)) + whole(lows)
    listed += both(d_qkvs, 384, early) + whole(normeds)
    listed += both(middles, 384, late) + whole(merges)
    part = blocks // 8
    return pl.pallas_call(
        weigh_kernel,
        grid=(8,),
        out_shape=[
            jax.ShapeDtypeStruct((blocks, 2 * FF // blocks, D), low),
            jax.ShapeDtypeStruct((blocks, FF // blocks, D), low),
            jax.ShapeDtypeStruct((blocks, 4 * D // blocks, D), low),
        ],
        in_specs=[spec for unused, spec in listed],
        out_specs=[
            pl.BlockSpec((part, 2 * FF // blocks, D), lambda i: (i, 0, 0)),
            pl.BlockSpec((part, FF // blocks, D), lambda i: (i, 0, 0)),
            pl.BlockSpec((blocks, 4 * D // blocks, D), lambda i: (0, 0, 0)),
        ],
        scratch_shapes=[pltpu.VMEM((3 * D, D), jnp.float32), pltpu.VMEM((D, D), jnp.float32)],
        compiler_params=pltpu.CompilerParams(vmem_limit_bytes=LARGE),
        cost_estimate=cost(10**6),
        name="weigh",
    )(*[array for array, unused in listed])


def loss_kernel(hidden_ref, gain_ref, near_ref, far_ref, own_ref, other_ref, weight_ref, *refs):
    gradient_ref, gain_out, loss_ref, near_out, far_out, logits, teach = refs
    head = lax.axis_index("head")
    rows = hidden_ref.shape[0]
    half = rows // 2
    size = near_ref.shape[1]
    hidden = hidden_ref[...]
    r = inverse_rms(hidden)
    normed = (hidden * r * gain_ref[...]).astype(low)
    parts = [(near_ref, near_out, 0, 0), (near_ref, near_out, 1, 2)]
    parts += [(far_ref, far_out, 0, 1), (far_ref, far_out, 1, 3)]
    for index, (source, unused, place, offset) in enumerate(parts):
        columns = pl.ds(pl.multiple_of((head ^ offset) * size, size), size)
        logits[index] = contract_cols(normed, source[place])
        teach[index, :half] = own_ref[:, columns].astype(jnp.float32)
        teach[index, half:] = other_ref[:, columns].astype(jnp.float32)

    def log_total(values):
        summit = jnp.max(jnp.max(values[...], axis=0), axis=-1, keepdims=True)
        return summit + jnp.log(
            jnp.sum(jnp.sum(jnp.exp(values[...] - summit[None]), axis=0), axis=-1, keepdims=True)
        )

    log_logits, log_teach = log_total(logits), log_total(teach)
    weighting = weight_ref[...]
    gradient = jnp.zeros((rows, hidden.shape[1]), jnp.float32)
    loss = jnp.zeros((rows, 1), jnp.float32)
    for index, (source, goal, place, offset) in enumerate(parts):
        log_prob = logits[index] - log_logits
        log_true = teach[index] - log_teach
        true = jnp.exp(log_true)
        loss = loss + jnp.sum(true * (log_true - log_prob), axis=-1, keepdims=True)
        d_logits = ((jnp.exp(log_prob) - true) * weighting).astype(low)
        goal[place] = contract_rows(d_logits, normed).astype(low)
        gradient = gradient + product(d_logits, source[place])
    loss_ref[...] = jnp.broadcast_to(
        jnp.sum(loss * weighting, axis=0, keepdims=True), loss_ref.shape
    )
    gradient_ref[...], gain_out[...] = norm_back(hidden, r, gain_ref[...], gradient)


def distill(hidden, gain, near, far, own, other, weighting):
    rows, width = hidden.shape
    size = near.shape[1]
    vmem = pl.BlockSpec(memory_space=pltpu.VMEM)
    f32 = jnp.float32
    return pl.pallas_call(
        loss_kernel,
        out_shape=[
            jax.ShapeDtypeStruct(hidden.shape, f32),
            jax.ShapeDtypeStruct(gain.shape, f32),
            jax.ShapeDtypeStruct((8, 128), f32),
            jax.ShapeDtypeStruct(near.shape, low),
            jax.ShapeDtypeStruct(far.shape, low),
        ],
        in_specs=[vmem] * 7,
        out_specs=[vmem] * 5,
        scratch_shapes=[pltpu.VMEM((4, rows, size), f32)] * 2,
        compiler_params=pltpu.CompilerParams(vmem_limit_bytes=58 * 2**20),
        name="distill",
    )(hidden, gain, near, far, own, other, weighting)


def on_device(
    token_ids,
    lengths,
    valid,
    vocab_ids,
    teacher,
    block,
    block_m,
    block_v,
    bases,
    table,
    table_m,
    table_v,
    gains,
    gains_m,
    gains_v,
):
    dp_count, head_count = lax.axis_size("dp"), lax.axis_size("head")
    device_total = dp_count * head_count
    head, dp = lax.axis_index("head"), lax.axis_index("dp")
    batch = head // 2
    tokens = token_ids.shape[1]
    shard_rows = table.shape[0]
    offset = dp * shard_rows
    part = TOPV // device_total

    widths = [3 * D // device_total, D // device_total, 2 * FF // device_total, FF // device_total]
    cuts = [sum(widths[:index]) for index in range(5)]
    block_low = block.T.astype(low)
    pieces = [block_low[cuts[index] : cuts[index + 1]] for index in range(4)]
    *weights, rows_in, codes, near, far = start(
        pieces,
        table,
        (token_ids * 2 + valid).reshape(-1, 1, tokens),
        vocab_ids,
        dp_count,
    )
    codes = codes.reshape(dp_count, 2 * tokens)
    weighting = (lax.dynamic_index_in_dim(codes, dp, 0, keepdims=False) & 1).astype(jnp.float32)
    vocab = lax.dynamic_index_in_dim(
        vocab_ids.reshape(head_count, dp_count, part), head, 0, keepdims=False
    )
    local = jnp.concatenate([vocab, codes >> 1], axis=1) - offset
    owned = (local >= 0) & (local < shard_rows)
    weights = [weight.reshape(-1, D) for weight in weights]
    near = near.reshape(2, -1, D)
    far = far.reshape(2, -1, D)
    hidden = rows_in[part:].astype(jnp.float32)

    teacher_own = lax.dynamic_index_in_dim(teacher, batch, 0, keepdims=False)
    teacher_far = swap(
        lax.dynamic_index_in_dim(teacher, 1 - batch, 0, keepdims=False), head_count, 2
    )

    run = jnp.arange(tokens, dtype=jnp.int32)
    places = jnp.concatenate([head * tokens + run, (head ^ 2) * tokens + run])
    places_far = jnp.concatenate([(head ^ 1) * tokens + run, (head ^ 3) * tokens + run])
    own_lengths = lax.dynamic_index_in_dim(lengths, batch, 0, keepdims=False)[0]
    segment, position = segments(own_lengths, places)
    segment_far, unused = segments(own_lengths, places_far)
    queries_at = jnp.stack([segment, places], axis=1)
    keys_at = jnp.stack(
        [jnp.concatenate([segment, segment_far]), jnp.concatenate([places, places_far])]
    )
    freqs = jnp.exp(jnp.arange(0, HD, 2, dtype=jnp.float32) * (-math.log(10000.0) / HD))
    angle = position.astype(jnp.float32)[:, None] * jnp.tile(freqs, 4)[None, :]
    cosine, sine = jnp.cos(angle), jnp.sin(angle)

    w_qkv, w_out, w_gu, w_down = weights
    saves = []
    for repeat in range(2):
        normed, query, own = project(hidden, gains[0:1], w_qkv, cosine, sine)
        if repeat == 1:
            own, teacher_far = lax.optimization_barrier((own, teacher_far))
        other = swap(own, head_count, 1)
        output, merged, middle = forward(
            hidden, query, own, other, queries_at, keys_at, w_out, gains[1:2], w_gu, w_down
        )
        saves.append((hidden, normed, query, own, other, merged, middle))
        hidden = output
    gradient, d_gain_final, loss_sum, d_near, d_far = distill(
        hidden, gains[2:3], near, far, teacher_own, teacher_far, weighting[:, None]
    )
    d_gain_final, loss_sum = d_gain_final[0], loss_sum[0, 0]
    f32 = jnp.float32
    gradient, d_far = lax.optimization_barrier((gradient, swap(d_far, head_count, 1)))
    d_near = (d_near.astype(f32) + d_far.astype(f32)).astype(low)
    d_quarter = swap(d_near[1], head_count, 2)

    d_gains = [0.0, 0.0]
    parts = []
    for repeat in range(2):
        hidden, normed, query, own, other, merged, middle = saves[1 - repeat]
        back = backward(
            gradient, middle, query, own, other, queries_at, keys_at, w_out, gains[1:2], w_gu, w_down
        )
        d_query, d_own, d_other, d_middle, d_gain_two = back[:5]
        grad_low, normed_two, action, d_gate, middle_low = back[5:]
        gradient, d_gain_one, d_qkv = unproject(
            d_query,
            d_own,
            swap(d_other, head_count, 1),
            d_middle,
            hidden,
            gains[0:1],
            w_qkv,
            cosine,
            sine,
        )
        if repeat == 0:
            gradient, d_quarter = lax.optimization_barrier((gradient, d_quarter))
            d_quarter = (d_near[0].astype(f32) + d_quarter.astype(f32)).astype(low)
            chosen_grads = lax.psum_scatter(d_quarter, "dp", scatter_dimension=0, tiled=True)
        parts.append((d_gate, normed_two, action, grad_low, d_qkv, normed, middle_low, merged))
        d_gains = [d_gains[0] + d_gain_one[0], d_gains[1] + d_gain_two[0]]

    d_gu, d_down, d_attention = weigh(*zip(*parts), device_total)
    rows_back = jnp.concatenate([chosen_grads, gradient.astype(low)], axis=0)
    step = 80 if shard_rows % 80 == 0 else 40
    quarter = -(-shard_rows // (step * head_count)) * step
    tile = quarter // 5 if quarter % 80 == 0 and quarter // 5 % 16 == 0 else step
    small = [d_gains[0], d_gains[1], d_gain_final, loss_sum[None], jnp.sum(weighting)[None]]
    small = jnp.pad(jnp.concatenate(small), (0, 6 * 128 - 2)).reshape(-1, 128)
    block_grads, table_grads, small = finish(
        [d_attention, d_gu, d_down],
        rows_back,
        by_side(jnp.where(owned, local, -1), dp_count // 2),
        small,
        quarter,
        tile,
    )
    outs = update(
        cuts,
        [table, table_m, table_v],
        table_grads.reshape(-1, D),
        small,
        small[: 3 * D // 128].reshape(3, D),
        [gains, gains_m, gains_v],
        block_grads.T,
        [block, block_m, block_v],
        bases,
    )
    table_new, table_m_new, table_v_new, table_low = outs[0:4]
    values, gains_new, gains_m_new, gains_v_new = outs[4:8]
    block_new, block_m_new, block_v_new, block_low = outs[8:12]
    return (
        values[0, 0],
        values[0, 1],
        block_new,
        block_m_new,
        block_v_new,
        table_new,
        table_m_new,
        table_v_new,
        gains_new,
        gains_m_new,
        gains_v_new,
        block_low,
        table_low,
    )


def solution(mesh):
    tokens = P(None, ("dp", "head"))
    columns = P(None, ("dp", "head"))
    table = P("dp", None)
    return jax.shard_map(
        on_device,
        mesh=mesh,
        in_specs=(
            tokens,
            P(None, "dp", None),
            tokens,
            P(),
            P(None, ("dp", "head"), None),
            columns,
            columns,
            columns,
            P(),
            table,
            table,
            table,
            P(),
            P(),
            P(),
        ),
        out_specs=(
            P(),
            P(),
            columns,
            columns,
            columns,
            table,
            table,
            table,
            P(),
            P(),
            P(),
            columns,
            table,
        ),
        check_vma=False,
    )
```

```python
import functools
import math

import jax
import jax.numpy as jnp
from jax import lax
from jax.experimental import pallas as pl
from jax.experimental.pallas import tpu as pltpu
from jax.sharding import PartitionSpec as P

D = 768
H = 12
HD = 64
FF = 3072
TOPV = 4096
STEP = 5

low = jnp.bfloat16
scale = HD**-0.5
eps_norm = 1e-05
clip_norm = 0.002
beta_one = 0.9
beta_two = 0.99
adam_eps = 1e-08
decay_rate = 0.1
rate_block = 0.03
rate_table = 0.05
rate_gain = 0.4


def product(left, right):
    return jnp.dot(left, right, preferred_element_type=jnp.float32)


def contract_rows(left, right):
    return lax.dot_general(
        left, right, (((0,), (0,)), ((), ())), preferred_element_type=jnp.float32
    )


def contract_cols(left, right):
    return lax.dot_general(
        left, right, (((1,), (1,)), ((), ())), preferred_element_type=jnp.float32
    )


def segments(lengths, places):
    segment = jnp.zeros_like(places)
    begin = jnp.zeros_like(places)
    end = jnp.zeros((), jnp.int32)
    for index in range(lengths.shape[0] - 1):
        end = end + lengths[index]
        past = places >= end
        segment = segment + past.astype(jnp.int32)
        begin = jnp.where(past, end, begin)
    return segment, places - begin


def swap(value, head_count, offset):
    return lax.ppermute(value, "head", [(h, h ^ offset) for h in range(head_count)])


MESH = pl.DeviceIdType.MESH
ANY = pl.BlockSpec(memory_space=pl.ANY)


def coordinates(depth):
    dp, head = lax.axis_index("dp"), lax.axis_index("head")
    return dp // 2, dp % 2, head // 2, head % 2


def device(z, x, y, c):
    return (z * 2 + x, y * 2 + c)


def slot(z, x, y, c):
    return ((z * 2 + x) * 2 + y) * 2 + c


def greet(depth, z, x, y, c):
    barrier = pltpu.get_barrier_semaphore()
    for target in (device(z, 1 - x, y, c), device(z, x, 1 - y, c), device(z, x, y, 1 - c)):
        pl.semaphore_signal(barrier, 1, device_id=target, device_id_type=MESH)

    @pl.when(z > 0)
    def below():
        pl.semaphore_signal(barrier, 1, device_id=device(z - 1, x, y, c), device_id_type=MESH)

    @pl.when(z < depth - 1)
    def above():
        pl.semaphore_signal(barrier, 1, device_id=device(z + 1, x, y, c), device_id_type=MESH)

    pl.semaphore_wait(barrier, 3 + jnp.where(z > 0, 1, 0) + jnp.where(z < depth - 1, 1, 0))


def start_kernel(depth, *refs):
    pieces = refs[0:4]
    table_ref, codes_ref, vocab_ref = refs[4:7]
    wholes = refs[7:11]
    sum_ref, ids_ref, near_ref, far_ref = refs[11:15]
    far_x, from_low, from_high, total, rows_ref, shard, ids = refs[15:22]
    local_sem, up_sem, down_sem, x_sem, y_sem, c_sem, block_sem = refs[22:29]
    rx_send, rx_recv, ru_send, ru_recv, rd_send, rd_recv = refs[29:35]
    id_send, id_recv, table_sem, copy_sem = refs[35:39]
    su_send, sd_send, sx_send, sy_send, sc_send, s_recv, keep_sem = refs[39:46]
    z, x, y, c = coordinates(depth)
    mine = slot(z, x, y, c)
    dp, head = z * 2 + x, y * 2 + c
    groups, height = rows_ref.shape[:2]
    shard_rows, tokens = table_ref.shape[0], codes_ref.shape[2]
    part = height - 2 * tokens
    offset = dp * shard_rows
    barrier = pltpu.get_barrier_semaphore()
    pl.semaphore_signal(barrier, 1, device_id=device(z, x, y, 1 - c), device_id_type=MESH)
    for group in range(groups):
        for rank in range(2):

            @pl.when((group != dp) | (rank != y))
            def hello():
                pl.semaphore_signal(
                    barrier, 1, device_id=(group, rank * 2 + c), device_id_type=MESH
                )

    pl.semaphore_wait(barrier, groups * 2)

    def tell(group, rank):
        second = jnp.where(rank == y, 0, 1)
        return pltpu.make_async_remote_copy(
            codes_ref.at[rank],
            ids_ref.at[dp, second],
            id_send.at[group, rank],
            id_recv.at[dp, second],
            device_id=(group, rank * 2 + c),
            device_id_type=MESH,
        )

    def told(group, second):
        return pltpu.make_async_remote_copy(
            codes_ref.at[0],
            ids_ref.at[group, second],
            id_send.at[group, second],
            id_recv.at[group, second],
            device_id=device(z, x, y, 1 - c),
            device_id_type=MESH,
        )

    keep = pltpu.make_async_copy(codes_ref.at[y], ids_ref.at[dp, 0], copy_sem)
    fetch = pltpu.make_async_copy(table_ref, shard.at[pl.ds(0, shard_rows)], table_sem)
    fetch.start()
    keep.start()
    for group in range(groups):
        for rank in range(2):

            @pl.when((group != dp) | (rank != y))
            def telling():
                tell(group, rank).start()

    def gather(stage, group):
        def load(first, read):
            @pl.loop(0, (tokens if first else part) // 16)
            def some(index):
                base = index * 16
                lines = []
                for line in range(16):
                    place = read(base + line) - offset
                    held = (place >= 0) & (place < shard_rows)
                    lines.append(shard[pl.ds(jnp.where(held, place, shard_rows), 1)])
                rows_ref[group, pl.ds(pl.multiple_of(first + base, 16), 16)] = jnp.concatenate(
                    lines, axis=0
                ).astype(low)

        if stage == 0:
            load(0, lambda index: vocab_ref[(head * groups + group) * part + index])
        for second in range(2 if stage else 0):
            load(part + second * tokens, lambda index: ids[group, second, 0, index] >> 1)

    def own(block, piece, target, sem):
        return pltpu.make_async_remote_copy(
            pieces[piece],
            wholes[piece].at[block],
            sem.at[piece],
            block_sem.at[block, piece],
            device_id=target,
            device_id_type=MESH,
        )

    def onward(block, piece, target, sem):
        return pltpu.make_async_remote_copy(
            wholes[piece].at[block],
            wholes[piece].at[block],
            sem.at[piece],
            block_sem.at[block, piece],
            device_id=target,
            device_id_type=MESH,
        )

    def send(make, block, target, sem):
        for piece in range(4):
            make(block, piece, target, sem).start()

    def arrive(block):
        for piece in range(4):
            onward(block, piece, device(z, x, y, 1 - c), c_sem.at[0]).wait_recv()

    across_x, across_y, across_c = (
        device(z, 1 - x, y, c),
        device(z, x, 1 - y, c),
        device(z, x, y, 1 - c),
    )
    spans = (pl.ds(0, part), pl.ds(part, 2 * tokens))

    def rows_x(stage, goal):
        return pltpu.make_async_remote_copy(
            rows_ref.at[goal * 2 + 1 - x, spans[stage]],
            far_x.at[goal, spans[stage]],
            rx_send.at[stage, goal],
            rx_recv.at[stage, goal],
            device_id=across_x,
            device_id_type=MESH,
        )

    def rows_up(stage, goal):
        return pltpu.make_async_remote_copy(
            total.at[goal, spans[stage]],
            from_low.at[goal, spans[stage]],
            ru_send.at[stage, goal],
            ru_recv.at[stage, goal],
            device_id=device(z + 1, x, y, c),
            device_id_type=MESH,
        )

    def rows_down(stage, goal):
        return pltpu.make_async_remote_copy(
            total.at[goal, spans[stage]],
            from_high.at[goal, spans[stage]],
            rd_send.at[stage, goal],
            rd_recv.at[stage, goal],
            device_id=device(z - 1, x, y, c),
            device_id_type=MESH,
        )

    goals = [
        goal for pair in zip(range(depth // 2), range(depth - 1, 0, -1)) for goal in pair
    ]
    goals += [goal for goal in range(depth) if goal not in goals]

    def reduce(stage):
        span = spans[stage]
        for goal in goals:
            rows_x(stage, goal).wait_recv()
            both = rows_ref[goal * 2 + x, span] + far_x[goal, span]

            @pl.when(goal > z)
            def rising():
                @pl.when(z > 0)
                def more():
                    rows_up(stage, goal).wait_recv()
                    total[goal, span] = both + from_low[goal, span]

                @pl.when(z == 0)
                def alone():
                    total[goal, span] = both

                rows_up(stage, goal).start()

            @pl.when(goal < z)
            def falling():
                @pl.when(z < depth - 1)
                def more():
                    rows_down(stage, goal).wait_recv()
                    total[goal, span] = both + from_high[goal, span]

                @pl.when(z == depth - 1)
                def alone():
                    total[goal, span] = both

                rows_down(stage, goal).start()

            @pl.when(goal == z)
            def here():
                total[goal, span] = both

    def land(stage):
        span = spans[stage]
        for goal in range(depth):

            @pl.when(goal == z)
            def landed():
                @pl.when(z > 0)
                def low_part():
                    rows_up(stage, goal).wait_recv()
                    total[goal, span] = total[goal, span] + from_low[goal, span]

                @pl.when(z < depth - 1)
                def high_part():
                    rows_down(stage, goal).wait_recv()
                    total[goal, span] = total[goal, span] + from_high[goal, span]

                sum_ref[span] = total[goal, span]

    local = [
        pltpu.make_async_copy(pieces[piece], wholes[piece].at[mine], local_sem.at[piece])
        for piece in range(4)
    ]
    send(own, mine, across_y, y_sem.at[mine // 4])

    @pl.when(z < depth - 1)
    def first_up():
        send(own, mine, device(z + 1, x, y, c), up_sem.at[0])

    @pl.when(z > 0)
    def first_down():
        send(own, mine, device(z - 1, x, y, c), down_sem.at[0])

    send(own, mine, across_x, x_sem.at[z])
    send(own, mine, across_c, c_sem.at[mine // 2])
    for copy in local:
        copy.start()
    shard[pl.ds(shard_rows, 8)] = jnp.zeros((8, shard.shape[1]), jnp.float32)
    fetch.wait()
    for goal in goals:
        gather(0, goal * 2 + 1 - x)
        rows_x(0, goal).start()
    for goal in goals:
        gather(0, goal * 2 + x)
    keep.wait()
    for group in range(groups):
        for second in range(2):

            @pl.when((group != dp) | (second != 0))
            def heard():
                told(group, second).wait_recv()

    to_scalars = pltpu.make_async_copy(ids_ref, ids, copy_sem)
    to_scalars.start()

    def spread(block, over_x):
        send(onward, block, across_y, y_sem.at[block // 4])
        if over_x:
            send(onward, block, across_x, x_sem.at[block // 8])
        send(onward, block, across_c, c_sem.at[block // 2])

    def pass_on(step):
        @pl.when(z - step >= 0)
        def risen():
            block = slot(z - step, x, y, c)
            arrive(block)

            @pl.when(z < depth - 1)
            def further():
                send(onward, block, device(z + 1, x, y, c), up_sem.at[step])

            spread(block, True)

        @pl.when(z + step < depth)
        def fallen():
            block = slot(z + step, x, y, c)
            arrive(block)

            @pl.when(z > 0)
            def further():
                send(onward, block, device(z - 1, x, y, c), down_sem.at[step])

            spread(block, True)

    def crossed(step):
        for sign in (1, -1) if step else (1,):

            @pl.when((z + sign * step >= 0) & (z + sign * step < depth))
            def there():
                block = slot(z + sign * step, 1 - x, y, c)
                arrive(block)
                spread(block, False)

    pass_on(1)
    to_scalars.wait()
    for goal in goals:
        gather(1, goal * 2 + 1 - x)
        rows_x(1, goal).start()
    for step in range(2, min(depth, 3)):
        pass_on(step)
    reduce(0)
    for goal in goals:
        gather(1, goal * 2 + x)
    for step in range(3, depth):
        pass_on(step)
    land(0)

    def shared(source, ref, quarter, group, send_sem, target):
        where = ref.at[quarter, group]
        return pltpu.make_async_remote_copy(
            where if source is None else source,
            where,
            send_sem,
            s_recv.at[quarter if ref is near_ref else 2 + quarter, group],
            device_id=target,
            device_id_type=MESH,
        )

    own_shared = sum_ref.at[pl.ds(0, part)]
    keep_shared = pltpu.make_async_copy(own_shared, near_ref.at[0, dp], keep_sem)
    keep_shared.start()

    def plane(group):
        return near_ref.at[0, group]

    def shared_y(source, group):
        return pltpu.make_async_remote_copy(
            source,
            near_ref.at[1, group],
            sy_send.at[group],
            s_recv.at[1, group],
            device_id=across_y,
            device_id_type=MESH,
        )

    def shared_c(source, quarter, group):
        return pltpu.make_async_remote_copy(
            source,
            far_ref.at[quarter, group],
            sc_send.at[quarter, group],
            s_recv.at[2 + quarter, group],
            device_id=across_c,
            device_id_type=MESH,
        )

    @pl.when(z < depth - 1)
    def shared_up():
        shared(own_shared, near_ref, 0, dp, su_send.at[0], device(z + 1, x, y, c)).start()

    @pl.when(z > 0)
    def shared_down():
        shared(own_shared, near_ref, 0, dp, sd_send.at[0], device(z - 1, x, y, c)).start()

    shared(own_shared, near_ref, 0, dp, sx_send.at[z], across_x).start()
    shared_y(own_shared, dp).start()
    shared_c(own_shared, 0, dp).start()
    for step in range(1, depth):

        @pl.when(z - step >= 0)
        def shared_risen():
            group = (z - step) * 2 + x
            copy = shared(
                None, near_ref, 0, group, su_send.at[step], device(z + 1, x, y, c)
            )
            copy.wait_recv()

            @pl.when(z < depth - 1)
            def further():
                copy.start()

            shared(None, near_ref, 0, group, sx_send.at[z - step], across_x).start()
            shared_y(plane(group), group).start()
            shared_c(plane(group), 0, group).start()

        @pl.when(z + step < depth)
        def shared_fallen():
            group = (z + step) * 2 + x
            copy = shared(
                None, near_ref, 0, group, sd_send.at[step], device(z - 1, x, y, c)
            )
            copy.wait_recv()

            @pl.when(z > 0)
            def further():
                copy.start()

            shared(None, near_ref, 0, group, sx_send.at[z + step], across_x).start()
            shared_y(plane(group), group).start()
            shared_c(plane(group), 0, group).start()

    crossed(0)
    reduce(1)
    for step in range(1, depth):
        crossed(step)
    for place in range(depth):
        group = place * 2 + 1 - x
        shared(None, near_ref, 0, group, sx_send.at[place], across_x).wait_recv()
        shared_y(plane(group), group).start()
        shared_c(plane(group), 0, group).start()
    land(1)

    for step in range(depth):
        for sign in (1, -1) if step else (1,):

            @pl.when((z + sign * step >= 0) & (z + sign * step < depth))
            def level():
                for side in (x, 1 - x):
                    block = slot(z + sign * step, side, 1 - y, c)
                    arrive(block)
                    send(onward, block, across_c, c_sem.at[block // 2])

    for group in range(groups):
        shared_y(plane(group), group).wait_recv()
        shared_c(near_ref.at[1, group], 1, group).start()

    for block in range(depth * 8):

        @pl.when(block % 2 != c)
        def from_core():
            arrive(block)

    for group in range(groups):
        for quarter in range(2):
            shared_c(near_ref.at[quarter, group], quarter, group).wait_recv()

    keep_shared.wait()
    for group in range(groups):
        shared_y(plane(group), group).wait_send()
        for quarter in range(2):
            shared_c(near_ref.at[quarter, group], quarter, group).wait_send()
    for place in range(depth):
        shared(None, near_ref, 0, dp, sx_send.at[place], across_x).wait_send()

        @pl.when((z - place >= 0) & (z < depth - 1))
        def shared_rose():
            shared(None, near_ref, 0, dp, su_send.at[place], across_x).wait_send()

        @pl.when((z + place < depth) & (z > 0))
        def shared_fell():
            shared(None, near_ref, 0, dp, sd_send.at[place], across_x).wait_send()

    for copy in local:
        copy.wait()
    for group in range(groups):
        for rank in range(2):

            @pl.when((group != dp) | (rank != y))
            def spoken():
                tell(group, rank).wait_send()

    for goal in range(depth):
        for stage in range(2):
            rows_x(stage, goal).wait_send()

            @pl.when(goal > z)
            def rose():
                rows_up(stage, goal).wait_send()

            @pl.when(goal < z)
            def fell():
                rows_down(stage, goal).wait_send()

    def sent(block, target, sem):
        for piece in range(4):
            onward(block, piece, target, sem).wait_send()

    for step in range(depth):

        @pl.when((z - step >= 0) & (z < depth - 1))
        def rose():
            sent(mine, device(z + 1, x, y, c), up_sem.at[step])

        @pl.when((z + step < depth) & (z > 0))
        def fell():
            sent(mine, device(z - 1, x, y, c), down_sem.at[step])

        sent(mine, across_x, x_sem.at[step])
    for index in range(depth * 2):
        sent(mine, across_y, y_sem.at[index])
    for index in range(depth * 4):
        sent(mine, across_c, c_sem.at[index])


def start(pieces, table, codes, vocab_ids, groups):
    width = table.shape[1]
    height = vocab_ids.shape[0] // (groups * 4) + 2 * codes.shape[2]
    depth = groups // 2
    blocks = depth * 8
    told = (groups, 2, 1, codes.shape[2])
    dma = pltpu.SemaphoreType.DMA
    buffer = pltpu.VMEM((depth, height, width), low)
    return pl.pallas_call(
        functools.partial(start_kernel, depth),
        out_shape=[jax.ShapeDtypeStruct((blocks,) + piece.shape, low) for piece in pieces]
        + [jax.ShapeDtypeStruct((height, width), low), jax.ShapeDtypeStruct(told, jnp.int32)]
        + [jax.ShapeDtypeStruct((2, groups, vocab_ids.shape[0] // blocks, width), low)] * 2,
        in_specs=[ANY] * 5
        + [pl.BlockSpec(memory_space=pltpu.VMEM), pl.BlockSpec(memory_space=pltpu.SMEM)],
        out_specs=[ANY] * 4 + [pl.BlockSpec(memory_space=pltpu.VMEM)] * 2 + [ANY] * 2,
        scratch_shapes=[buffer] * 4
        + [
            pltpu.VMEM((groups, height, width), low),
            pltpu.VMEM((table.shape[0] + 8, width), jnp.float32),
            pltpu.SMEM(told, jnp.int32),
        ]
        + [dma((4,))]
        + [dma((depth, 4))] * 3
        + [dma((depth * 2, 4)), dma((depth * 4, 4)), dma((blocks, 4))]
        + [dma((2, depth))] * 6
        + [dma((groups, 2))] * 2
        + [dma(())] * 2
        + [dma((depth,))] * 3
        + [dma((groups,)), dma((2, groups)), dma((4, groups)), dma(())],
        compiler_params=pltpu.CompilerParams(
            collective_id=0, has_side_effects=True, vmem_limit_bytes=58 * 2**20
        ),
        name="start",
    )(*pieces, table, codes, vocab_ids)


def by_distance(depth, z, act):
    for step in range(depth - 1, -1, -1):
        for sign in (1, -1) if step else (1,):

            @pl.when((z + sign * step >= 0) & (z + sign * step < depth))
            def reached():
                act(z + sign * step)


def add_into(total, block, *terms):
    height = total.shape[1]
    chunk = 96 if height % 96 == 0 else height

    @pl.loop(0, height // chunk)
    def chunks(index):
        part = pl.ds(pl.multiple_of(index * chunk, chunk), chunk)
        value = total[block, part].astype(jnp.float32)
        for buffer, place in terms:
            value = value + buffer[place, part].astype(jnp.float32)
        total[block, part] = value.astype(low)


def finish_kernel(depth, heights, tile, *refs):
    pieces = refs[0:3]
    rows_ref, places_ref, small_ref = refs[3:6]
    grad_ref, table_out, small_out = refs[6:9]
    total, far_c, far_p, far_s, from_low, from_high = refs[9:15]
    rows, given, far_t, part, mine, far_part, small, far_small = refs[15:23]
    local_sem, c_send, c_recv, p_send, p_recv, s_send, s_recv = refs[23:30]
    u_send, u_recv, d_send, d_recv = refs[30:34]
    own_sem, ru_send, rd_send, rx_send, r_recv = refs[34:39]
    t_send, t_recv, ty_send, ty_recv, o_send, o_recv = refs[39:45]
    e_send, e_recv, f_send, f_recv = refs[45:49]
    z, x, y, c = coordinates(depth)
    dp = z * 2 + x
    firsts = [sum(heights[:index]) for index in range(3)]
    up, down = device(z + 1, x, y, c), device(z - 1, x, y, c)
    across_x, across_y, across_c = (
        device(z, 1 - x, y, c),
        device(z, x, 1 - y, c),
        device(z, x, y, 1 - c),
    )

    def y_first(place, core):
        return (core == 0) & (place >= 0)

    def across_p(place):
        first = y_first(place, c)
        return tuple(jnp.where(first, one, two) for one, two in zip(across_y, across_x))

    def across_s(place):
        first = y_first(place, c)
        return tuple(jnp.where(first, two, one) for one, two in zip(across_y, across_x))

    def own_p(place, core=c):
        return jnp.where(y_first(place, core), y, x)

    def own_s(place, core=c):
        return jnp.where(y_first(place, core), x, y)

    def own_block(place):
        return (place * 2 + x) * 2 + y

    def mate(offset):
        return device(z, (x + offset // 4) % 2, (y + offset // 2) % 2, (c + offset) % 2)

    barrier = pltpu.get_barrier_semaphore()
    for offset in range(1, 8):
        pl.semaphore_signal(barrier, 1, device_id=mate(offset), device_id_type=MESH)
    for other in range(depth):

        @pl.when(other != z)
        def hello():
            pl.semaphore_signal(
                barrier, 1, device_id=device(other, x, y, c), device_id_type=MESH
            )

    pl.semaphore_wait(barrier, 7 + depth - 1)

    def remote(source, goal, send_sem, recv_sem, target):
        return pltpu.make_async_remote_copy(
            source, goal, send_sem, recv_sem, device_id=target, device_id_type=MESH
        )

    def block_of(place, s, p, core=c):
        return place * 4 + jnp.where(y_first(place, core), s * 2 + p, p * 2 + s)

    def local(block, piece):
        return pltpu.make_async_copy(
            pieces[piece].at[block * 2 + c],
            total.at[block, pl.ds(firsts[piece], heights[piece])],
            local_sem.at[block, piece],
        )

    def over_c(block, piece):
        return remote(
            pieces[piece].at[block * 2 + 1 - c],
            far_c.at[block, pl.ds(firsts[piece], heights[piece])],
            c_send.at[block, piece],
            c_recv.at[block, piece],
            across_c,
        )

    def over_p(place, s):
        pair = place * 2 + s
        return remote(
            total.at[block_of(place, s, 1 - own_p(place))],
            far_p.at[pair],
            p_send.at[pair],
            p_recv.at[pair],
            across_p(place),
        )

    def over_s(place):
        return remote(
            total.at[block_of(place, 1 - own_s(place), own_p(place))],
            far_s.at[place],
            s_send.at[place],
            s_recv.at[place],
            across_s(place),
        )

    half = total.shape[1] // 2

    def rise(place, side):
        lines = pl.ds(side * half, half)
        return remote(
            total.at[own_block(place), lines],
            from_low.at[place, lines],
            u_send.at[place, side],
            u_recv.at[place, side],
            up,
        )

    def fall(place, side):
        lines = pl.ds(side * half, half)
        return remote(
            total.at[own_block(place), lines],
            from_high.at[place, lines],
            d_send.at[place, side],
            d_recv.at[place, side],
            down,
        )

    def add_half(block, side, buffer, place):
        lines = pl.ds(side * half, half)
        value = total[block, lines].astype(jnp.float32) + buffer[place, lines].astype(jnp.float32)
        total[block, lines] = value.astype(low)

    def own_rows(send_sem, target, side):
        return remote(rows_ref, rows.at[side, z], send_sem, r_recv.at[side, z], target)

    def rows_on(place, send_sem, target, side):
        return remote(
            rows.at[0, place], rows.at[side, place], send_sem, r_recv.at[side, place], target
        )

    own = pltpu.make_async_copy(rows_ref, rows.at[0, z], own_sem)
    own.start()

    @pl.when(z < depth - 1)
    def first_up():
        own_rows(ru_send.at[0], up, 0).start()

    @pl.when(z > 0)
    def first_down():
        own_rows(rd_send.at[0], down, 0).start()

    own_rows(rx_send.at[z], across_x, 1).start()

    for turn in range(2):
        for side in range(2):

            def launch(place):
                s, p = own_s(place, 1 - c), own_p(place, 1 - c)
                s, p = (s if side else 1 - s), (p if turn else 1 - p)
                there = block_of(place, s, p, 1 - c)
                s, p = own_s(place), own_p(place)
                s, p = (s if side else 1 - s), (p if turn else 1 - p)
                here = block_of(place, s, p)
                for piece in range(3):
                    over_c(there, piece).start()
                    local(here, piece).start()

            by_distance(depth, z, launch)

    def ready(block):
        for piece in range(3):
            local(block, piece).wait()
            over_c(block, piece).wait_recv()

    def give_p(along_y):
        for side in range(2):

            def give(place):
                @pl.when(y_first(place, c) == along_y)
                def now():
                    s = own_s(place)
                    s = s if side else 1 - s
                    block = block_of(place, s, 1 - own_p(place))
                    ready(block)
                    add_into(total, block, (far_c, block))
                    over_p(place, s).start()

            by_distance(depth, z, give)

    give_p(True)

    for step in range(1, depth):

        @pl.when(z - step >= 0)
        def risen():
            rows_on(z - step, ru_send.at[step], up, 0).wait_recv()

            @pl.when(z < depth - 1)
            def further():
                rows_on(z - step, ru_send.at[step], up, 0).start()

            rows_on(z - step, rx_send.at[z - step], across_x, 1).start()

        @pl.when(z + step < depth)
        def fallen():
            rows_on(z + step, rd_send.at[step], down, 0).wait_recv()

            @pl.when(z > 0)
            def further():
                rows_on(z + step, rd_send.at[step], down, 0).start()

            rows_on(z + step, rx_send.at[z + step], across_x, 1).start()

    give_p(False)
    own.wait()

    height = part.shape[0]
    count = places_ref.shape[2]

    def collect(rank, core, goal, side):
        @pl.loop(0, height // tile)
        def tiles(index):
            first = index * tile
            lines = pl.ds(pl.multiple_of(first, tile), tile)
            at = (
                (rank * 2 + core) * height
                + first
                + lax.broadcasted_iota(jnp.int32, (tile, count), 0)
            )
            picked = jnp.where(at == places_ref[side], 1.0, 0.0).astype(low)
            value = product(picked, rows[side].reshape(count, rows.shape[3]))
            if side:
                value = value + goal[lines].astype(jnp.float32)
            goal[lines] = value.astype(low)

    def over_t(rank):
        index = jnp.where(rank == y, 1, 0)
        return remote(
            given.at[index], far_t.at[index], t_send.at[index], t_recv.at[index], across_c
        )

    chunk = 80 if height % 80 == 0 else height

    def pieces_of(act):
        @pl.loop(0, height // chunk)
        def step(index):
            act(pl.ds(pl.multiple_of(index * chunk, chunk), chunk))

    collect(1 - y, 1 - c, given.at[0], 0)
    collect(1 - y, c, part, 0)
    collect(y, 1 - c, given.at[1], 0)
    collect(y, c, mine, 0)
    for place in range(depth):
        rows_on(place, rx_send.at[place], across_x, 1).wait_recv()
    collect(1 - y, 1 - c, given.at[0], 1)
    over_t(1 - y).start()
    collect(1 - y, c, part, 1)
    over_t(1 - y).wait_recv()

    def first_sum(lines):
        part[lines] = (part[lines].astype(jnp.float32) + far_t[0, lines].astype(jnp.float32)).astype(
            low
        )

    pieces_of(first_sum)
    over_part = remote(part, far_part, ty_send, ty_recv, across_y)
    over_part.start()
    collect(y, 1 - c, given.at[1], 1)
    over_t(y).start()
    collect(y, c, mine, 1)

    def give_s(place):
        s = 1 - own_s(place)
        block = block_of(place, s, own_p(place))
        ready(block)
        over_p(place, s).wait_recv()
        add_into(total, block, (far_c, block), (far_p, place * 2 + s))
        over_s(place).start()

    by_distance(depth, z, give_s)

    over_t(y).wait_recv()
    over_part.wait_recv()

    def second_sum(index, squares):
        lines = pl.ds(pl.multiple_of(index * chunk, chunk), chunk)
        value = (
            mine[lines].astype(jnp.float32)
            + far_t[1, lines].astype(jnp.float32)
            + far_part[lines].astype(jnp.float32)
        ).astype(low)
        mine[lines] = value
        value = value.astype(jnp.float32)
        return squares + jnp.sum((value * value).reshape(-1, 8, value.shape[1]), axis=0)

    squares = lax.fori_loop(
        0, height // chunk, second_sum, jnp.zeros((8, part.shape[1]), jnp.float32)
    )

    def out_mine(index, target):
        where = table_out.at[y * 2 + c]
        return remote(mine, where, o_send.at[index], o_recv.at[y * 2 + c], target)

    def out(rank, core):
        where = table_out.at[rank * 2 + core]
        return remote(where, where, o_send.at[2], o_recv.at[rank * 2 + core], across_c)

    keep = pltpu.make_async_copy(mine, table_out.at[y * 2 + c], own_sem)
    out_mine(0, across_y).start()
    out_mine(1, across_c).start()
    keep.start()

    def give_z(place):
        block = own_block(place)
        s = own_s(place)
        ready(block)
        over_p(place, s).wait_recv()
        over_s(place).wait_recv()
        add_into(total, block, (far_c, block), (far_p, place * 2 + s), (far_s, place))
        for side in range(2):

            @pl.when(place > z)
            def rising():
                @pl.when(z > 0)
                def more():
                    rise(place, side).wait_recv()
                    add_half(block, side, from_low, place)

                rise(place, side).start()

            @pl.when(place < z)
            def falling():
                @pl.when(z < depth - 1)
                def more():
                    fall(place, side).wait_recv()
                    add_half(block, side, from_high, place)

                fall(place, side).start()

    by_distance(depth, z, give_z)
    grad_ref[...] = total[own_block(z)].astype(jnp.float32)
    for side in range(2):
        there = pl.ds(side * half, half)

        @pl.when(z > 0)
        def low_part():
            rise(z, side).wait_recv()
            grad_ref[there] = grad_ref[there] + from_low[z, there].astype(jnp.float32)

        @pl.when(z < depth - 1)
        def high_part():
            fall(z, side).wait_recv()
            grad_ref[there] = grad_ref[there] + from_high[z, there].astype(jnp.float32)

    lines = lax.broadcasted_iota(jnp.int32, small.shape[1:], 0)
    lanes = lax.broadcasted_iota(jnp.int32, small.shape[1:], 1)
    last = (lines == small.shape[1] - 1) & (lanes == 0)
    grad_squares = jnp.sum(grad_ref[...] * grad_ref[...])
    small[0] = small_ref[...] + jnp.where(last, jnp.sum(squares) + grad_squares, 0.0)

    def exchange(offset):
        return remote(
            small.at[0], small.at[offset], e_send.at[offset], e_recv.at[offset], mate(offset)
        )

    def announce(other, source):
        where = far_small.at[source]
        return remote(where, where, f_send.at[other], f_recv.at[source], device(other, x, y, c))

    for offset in range(1, 8):
        exchange(offset).start()
    for offset in range(1, 8):
        exchange(offset).wait_recv()
    gathered = jnp.zeros(small.shape[1:], jnp.float32)
    for rank in range(8):
        gathered = gathered + small[
            (x + rank // 4) % 2 * 4 + (y + rank // 2) % 2 * 2 + (c + rank) % 2
        ]
    far_small[z] = gathered
    for other in range(depth):

        @pl.when(other != z)
        def telling():
            announce(other, z).start()

    for other in range(depth):

        @pl.when(other != z)
        def hearing():
            announce(other, other).wait_recv()

    gathered = far_small[0]
    for other in range(1, depth):
        gathered = gathered + far_small[other]
    small_out[...] = gathered
    out(1 - y, c).wait_recv()
    out(1 - y, c).start()
    out(y, 1 - c).wait_recv()
    out(1 - y, 1 - c).wait_recv()

    keep.wait()
    out_mine(0, across_y).wait_send()
    out_mine(1, across_c).wait_send()
    out(1 - y, c).wait_send()
    over_part.wait_send()
    for offset in range(1, 8):
        exchange(offset).wait_send()
    for other in range(depth):

        @pl.when(other != z)
        def told():
            announce(other, z).wait_send()

    for rank in range(2):
        over_t(rank).wait_send()
    for place in range(depth):
        rows_on(place, rx_send.at[place], across_x, 1).wait_send()
        over_s(place).wait_send()
        for side in range(2):
            over_p(place, side).wait_send()
            for rank in range(2):
                for piece in range(3):
                    over_c((place * 2 + side) * 2 + rank, piece).wait_send()

        for side in range(2):

            @pl.when(place > z)
            def rose():
                rise(place, side).wait_send()

            @pl.when(place < z)
            def fell():
                fall(place, side).wait_send()

        @pl.when((z - place >= 0) & (z < depth - 1))
        def rows_rose():
            rows_on(z, ru_send.at[place], up, 0).wait_send()

        @pl.when((z + place < depth) & (z > 0))
        def rows_fell():
            rows_on(z, rd_send.at[place], down, 0).wait_send()


def finish(pieces, rows, places, small, quarter, tile):
    blocks = pieces[0].shape[0]
    heights = [piece.shape[1] for piece in pieces]
    height, width = sum(heights), pieces[0].shape[2]
    depth = blocks // 8
    dma = pltpu.SemaphoreType.DMA
    vmem = pl.BlockSpec(memory_space=pltpu.VMEM)

    def buffer(count):
        return pltpu.VMEM((count, height, width), low)

    return pl.pallas_call(
        functools.partial(finish_kernel, depth, heights, tile),
        out_shape=[
            jax.ShapeDtypeStruct((height, width), jnp.float32),
            jax.ShapeDtypeStruct((4, quarter, width), low),
            jax.ShapeDtypeStruct(small.shape, jnp.float32),
        ],
        in_specs=[ANY] * 4 + [vmem] * 2,
        out_specs=[vmem, ANY, vmem],
        scratch_shapes=[buffer(depth * 4), buffer(depth * 4), buffer(depth * 2)]
        + [buffer(depth)] * 3
        + [
            pltpu.VMEM((2, depth) + rows.shape, low),
            pltpu.VMEM((2, quarter, width), low),
            pltpu.VMEM((2, quarter, width), low),
            pltpu.VMEM((quarter, width), low),
            pltpu.VMEM((quarter, width), low),
            pltpu.VMEM((quarter, width), low),
            pltpu.VMEM((8,) + small.shape, jnp.float32),
            pltpu.VMEM((depth,) + small.shape, jnp.float32),
        ]
        + [dma((depth * 4, 3))] * 3
        + [dma((depth * 2,))] * 2
        + [dma((depth,))] * 2
        + [dma((depth, 2))] * 4
        + [dma(())]
        + [dma((depth,))] * 3
        + [dma((2, depth))]
        + [dma((2,))] * 2
        + [dma(())] * 2
        + [dma((3,)), dma((4,))]
        + [dma((8,))] * 2
        + [dma((depth,))] * 2,
        compiler_params=pltpu.CompilerParams(
            collective_id=1, has_side_effects=True, vmem_limit_bytes=62 * 2**20
        ),
        name="finish",
    )(*pieces, rows, places, small)


def by_side(places, depth):
    places = places.reshape(depth, 2, -1)
    x = lax.axis_index("dp") % 2
    sides = [lax.dynamic_index_in_dim(places, side, 1, keepdims=False) for side in (x, 1 - x)]
    return jnp.stack(sides).reshape(2, 1, -1)


def moments(gradient, first, second):
    first_new = beta_one * first + (1.0 - beta_one) * gradient
    second_new = beta_two * second + (1.0 - beta_two) * gradient * gradient
    second_hat = second_new * (1.0 / (1.0 - beta_two**STEP))
    root = second_hat * lax.rsqrt(second_hat) + adam_eps
    direction = first_new * (1.0 / (1.0 - beta_one**STEP)) / root
    return direction, first_new, second_new


def update_kernel(steps, cuts, *refs):
    table_ref, table_m_ref, table_v_ref, table_g_ref = refs[0:4]
    small_ref, sums_ref, gains_ref, gains_m_ref, gains_v_ref = refs[4:9]
    grad_ref, block_ref, block_m_ref, block_v_ref, bases_ref = refs[9:14]
    table_new, table_m_new, table_v_new, table_low = refs[14:18]
    values_ref, gains_new, gains_m_new, gains_v_new = refs[18:22]
    block_new, block_m_new, block_v_new, block_low = refs[22:26]
    bases, turned, factor_ref, bases_sem = refs[26:30]
    now = pl.program_id(0)

    def base(index):
        return pltpu.make_async_copy(bases_ref.at[index], bases.at[index], bases_sem.at[index])

    @pl.when(now == 0)
    def begin():
        for index in range(4):
            base(index).start()
        lines = lax.broadcasted_iota(jnp.int32, small_ref.shape, 0)
        lanes = lax.broadcasted_iota(jnp.int32, small_ref.shape, 1)

        def value_at(place):
            there = (lines == place // 128) & (lanes == place % 128)
            return jnp.sum(jnp.where(there, small_ref[...], 0.0), axis=(0, 1), keepdims=True)

        count = value_at(3 * D + 1)
        gain_grads = sums_ref[...] / count
        squares = value_at((small_ref.shape[0] - 1) * 128) / (count * count)
        norm = jnp.sqrt(squares + jnp.sum(gain_grads * gain_grads, axis=(0, 1), keepdims=True))
        clip = jnp.minimum(1.0, clip_norm / norm)
        factor_ref[...] = jnp.broadcast_to(clip / count, factor_ref.shape)
        spots = lax.broadcasted_iota(jnp.int32, values_ref.shape, 1)
        values_ref[...] = jnp.where(spots == 0, value_at(3 * D) / count, norm)
        direction, gains_m_new[...], gains_v_new[...] = moments(
            gain_grads * clip, gains_m_ref[...], gains_v_ref[...]
        )
        gains_new[...] = gains_ref[...] - rate_gain * direction

    factor = factor_ref[0:1, 0:1]
    direction, table_m_new[...], table_v_new[...] = moments(
        table_g_ref[...].astype(jnp.float32) * factor, table_m_ref[...], table_v_ref[...]
    )
    table_tile = table_ref[...]
    table_tile = table_tile - rate_table * (direction + decay_rate * table_tile)
    table_new[...] = table_tile
    table_low[...] = table_tile.astype(low)

    spots = lax.broadcasted_iota(jnp.int32, turned.shape, 1)

    def columns(index, value):
        mine = (spots >= cuts[index]) & (spots < cuts[index + 1])
        return jnp.where(mine, value, 0.0).astype(low)

    for index in range(4):

        @pl.when(now == min(1 + index, steps - 1))
        def rotate():
            base(index).wait()
            term = contract_rows(
                bases[index].astype(low), columns(index, grad_ref[...] * factor_ref[0:1, 0:1])
            )
            turned[...] = term if index == 0 else turned[...] + term

    @pl.when(now == min(5, steps - 1))
    def move():
        direction, block_m_new[...], block_v_new[...] = moments(
            turned[...], block_m_ref[...], block_v_ref[...]
        )
        turned[...] = direction

    for index in range(4):

        @pl.when(now == min(5 + index, steps - 1))
        def rotate_back():
            term = product(bases[index].astype(low), columns(index, turned[...]))
            block_new[...] = term if index == 0 else block_new[...] + term

    @pl.when(now == min(8, steps - 1))
    def store():
        block = block_ref[...]
        block = block - rate_block * (block_new[...] + decay_rate * block)
        block_new[...] = block
        block_low[...] = block.astype(low)


def update(cuts, tables, table_grads, small, gain_sums, gains, block_grads, blocks, bases):
    rows, width = tables[0].shape
    tile = max(
        size
        for size in range(8, 401, 8)
        if rows % size == 0 and (size % 16 == 0 or rows % 16)
    )
    steps = rows // tile
    f32 = jnp.float32

    def whole(array):
        return pl.BlockSpec(array.shape, lambda i: (0,) * array.ndim)

    tiles = pl.BlockSpec((tile, width), lambda i: (i, 0))
    table = jax.ShapeDtypeStruct(tables[0].shape, f32)
    gain = jax.ShapeDtypeStruct(gains[0].shape, f32)
    matrix = jax.ShapeDtypeStruct(blocks[0].shape, f32)
    values = jax.ShapeDtypeStruct((8, 128), f32)
    outs = [table] * 3 + [jax.ShapeDtypeStruct(table.shape, low)]
    outs += [values] + [gain] * 3
    outs += [matrix] * 3 + [jax.ShapeDtypeStruct(matrix.shape, low)]
    return pl.pallas_call(
        functools.partial(update_kernel, steps, cuts),
        grid=(steps,),
        out_shape=outs,
        in_specs=[tiles] * 4
        + [whole(small), whole(gain_sums)]
        + [whole(gain)] * 3
        + [whole(matrix)] * 4
        + [ANY],
        out_specs=[tiles] * 4 + [whole(values)] + [whole(gain)] * 3 + [whole(matrix)] * 4,
        scratch_shapes=[
            pltpu.VMEM(bases.shape, f32),
            pltpu.VMEM(matrix.shape, f32),
            pltpu.VMEM((8, 128), f32),
            pltpu.SemaphoreType.DMA((4,)),
        ],
        compiler_params=pltpu.CompilerParams(vmem_limit_bytes=58 * 2**20),
        name="update",
    )(*tables, table_grads, small, gain_sums, *gains, block_grads, *blocks, bases)


def cost(flops):
    return pl.CostEstimate(flops=flops, bytes_accessed=10**6, transcendentals=0)


LARGE = 58 * 2**20
CHUNK = 512


def inverse_rms(value):
    return lax.rsqrt(jnp.mean(value * value, axis=-1, keepdims=True) + eps_norm)


def norm_back(value, r, gain, grad):
    scaled = grad * gain
    d_value = r * scaled - value * (r * r * r) * jnp.mean(value * scaled, axis=-1, keepdims=True)
    return d_value, jnp.sum(grad * value * r, axis=0, keepdims=True)


def local_call(kernel, name, flops, outs, args, scratch=(), remain=()):
    vmem = pl.BlockSpec(memory_space=pltpu.VMEM)
    return pl.pallas_call(
        kernel,
        out_shape=[jax.ShapeDtypeStruct(shape, kind) for shape, kind in outs],
        in_specs=[ANY if place in remain else vmem for place in range(len(args))],
        out_specs=[vmem] * len(outs),
        scratch_shapes=list(scratch),
        compiler_params=pltpu.CompilerParams(vmem_limit_bytes=LARGE),
        cost_estimate=cost(flops),
        name=name,
    )(*args)


def project_kernel(hidden_ref, gain_ref, weight_ref, cosine_ref, sine_ref, *refs):
    normed_ref, query_ref, own_ref = refs
    hidden = hidden_ref[...]
    normed = (hidden * inverse_rms(hidden) * gain_ref[...]).astype(low)
    normed_ref[...] = normed
    cosine, sine = cosine_ref[...], sine_ref[...]
    first = lax.broadcasted_iota(jnp.int32, cosine.shape, 1) % HD < HD // 2
    for index in range(3 * D // 128):
        columns = pl.ds(index * 128, 128)
        value = contract_cols(normed, weight_ref[columns])
        if index < 2 * D // 128:
            turned = jnp.where(
                first, -pltpu.roll(value, 128 - HD // 2, 1), pltpu.roll(value, HD // 2, 1)
            )
            value = value * cosine + turned * sine
        if index < D // 128:
            query_ref[:, columns] = value.astype(low)
        else:
            own_ref[:, pl.ds(index * 128 - D, 128)] = value.astype(low)


def project(hidden, gain, weight, cosine, sine):
    rows = hidden.shape[0]
    outs = [((rows, D), low), ((rows, D), low), ((rows, 2 * D), low)]
    return local_call(project_kernel, "project", 6 * 10**9, outs, [hidden, gain, weight, cosine, sine])


def allowed(rows_ref, columns_ref):
    return (rows_ref[:, 0:1] == columns_ref[0:1]) & (rows_ref[:, 1:2] >= columns_ref[1:2])


def pair_of_heads(index):
    return pl.ds(index * 128, 128)


def attention_weight(query, keys, allow):
    score = jnp.where(allow, contract_cols(query, keys) * scale, -1e30)
    power = jnp.exp(score - jnp.max(score, axis=-1, keepdims=True))
    return power * (1.0 / jnp.sum(power, axis=-1, keepdims=True))


def forward_kernel(hidden_ref, query_ref, own_ref, far_ref, rows_ref, columns_ref, *refs):
    out_weight, gain_ref, gate_hbm, down_hbm, output_ref, merged_ref, middle_ref = refs[:7]
    gates, downs, sems = refs[7:]
    copies = weight_copies(gate_hbm, down_hbm, gates, downs, sems)
    for group in copies:
        for copy in group:
            copy.start()
    allow = allowed(rows_ref, columns_ref)
    rows = hidden_ref.shape[0]
    first = lax.broadcasted_iota(jnp.int32, (rows, 128), 1) < HD

    @pl.loop(0, D // 128, unroll=2)
    def heads(index):
        columns = pl.ds(pl.multiple_of(index * 128, 128), 128)
        values_at = pl.ds(pl.multiple_of(index * 128 + D, 128), 128)
        query = query_ref[:, columns]
        keys = jnp.concatenate([own_ref[:, columns], far_ref[:, columns]], axis=0)
        values = jnp.concatenate([own_ref[:, values_at], far_ref[:, values_at]], axis=0)
        mixed = []
        for side in range(2):
            mine = jnp.where(first == (side == 0), query, jnp.zeros_like(query))
            weight = attention_weight(mine, keys, allow).astype(low)
            mixed.append(product(weight, values))
        merged_ref[:, columns] = jnp.where(first, mixed[0], mixed[1]).astype(low)

    middle = hidden_ref[...] + contract_cols(merged_ref[...], out_weight[...])
    middle_ref[...] = middle
    normed = (middle * inverse_rms(middle) * gain_ref[...]).astype(low)
    output_ref[...] = middle
    for index, group in enumerate(copies):
        for copy in group:
            copy.wait()
        gate = contract_cols(normed, gates[pl.ds(index * CHUNK, CHUNK)])
        up = contract_cols(normed, gates[pl.ds(FF + index * CHUNK, CHUNK)])
        action = (gate * jax.nn.sigmoid(gate) * up).astype(low)
        output_ref[...] += product(action, downs[pl.ds(index * CHUNK, CHUNK)])


def weight_copies(gate_hbm, down_hbm, gates, downs, sems):
    groups = []
    for index in range(FF // CHUNK):
        parts = [
            (gate_hbm, gates, index * CHUNK),
            (gate_hbm, gates, FF + index * CHUNK),
            (down_hbm, downs, index * CHUNK),
        ]
        groups.append(
            [
                pltpu.make_async_copy(
                    source.at[pl.ds(at, CHUNK)], goal.at[pl.ds(at, CHUNK)], sems.at[index, place]
                )
                for place, (source, goal, at) in enumerate(parts)
            ]
        )
    return groups


def weight_buffers():
    return [
        pltpu.VMEM((2 * FF, D), low),
        pltpu.VMEM((FF, D), low),
        pltpu.SemaphoreType.DMA((FF // CHUNK, 3)),
    ]


def forward(hidden, query, own, far, rows, columns, w_out, gain, w_gu, w_down):
    count = hidden.shape[0]
    outs = [((count, D), jnp.float32), ((count, D), low), ((count, D), jnp.float32)]
    args = [hidden, query, own, far, rows, columns, w_out, gain, w_gu, w_down]
    return local_call(forward_kernel, "forward", 5 * 10**9, outs, args, weight_buffers(), (8, 9))


def backward_kernel(gradient_ref, middle_ref, query_ref, own_ref, far_ref, *refs):
    rows_ref, columns_ref, out_weight, gain_ref, gate_hbm, down_hbm = refs[:6]
    d_query_ref, d_own_ref, d_far_ref, d_middle_ref, gain_out = refs[6:11]
    low_ref, normed_ref, action_ref, d_gate_ref, middle_low_ref = refs[11:16]
    gates, downs, sems, total = refs[16:]
    copies = weight_copies(gate_hbm, down_hbm, gates, downs, sems)
    for group in copies:
        for copy in group:
            copy.start()
    gradient = gradient_ref[...]
    grad_low = gradient.astype(low)
    low_ref[...] = grad_low
    middle = middle_ref[...]
    r = inverse_rms(middle)
    normed = (middle * r * gain_ref[...]).astype(low)
    normed_ref[...] = normed
    total[...] = jnp.zeros_like(total)
    for index, group in enumerate(copies):
        for copy in group:
            copy.wait()
        first = pl.ds(index * CHUNK, CHUNK)
        second = pl.ds(FF + index * CHUNK, CHUNK)
        gate = contract_cols(normed, gates[first])
        up = contract_cols(normed, gates[second])
        chance = jax.nn.sigmoid(gate)
        action_ref[:, first] = (gate * chance * up).astype(low)
        d_action = contract_cols(grad_low, downs[first])
        d_gate = (d_action * up * (chance + gate * chance * (1.0 - chance))).astype(low)
        d_up = (d_action * gate * chance).astype(low)
        d_gate_ref[:, first] = d_gate
        d_gate_ref[:, second] = d_up
        total[...] += product(d_gate, gates[first]) + product(d_up, gates[second])
    d_middle, gain_out[...] = norm_back(middle, r, gain_ref[...], total[...])
    d_middle = gradient + d_middle
    d_middle_ref[...] = d_middle
    middle_low = d_middle.astype(low)
    middle_low_ref[...] = middle_low
    total[...] = product(middle_low, out_weight[...])
    allow = allowed(rows_ref, columns_ref)
    rows = gradient.shape[0]
    first = lax.broadcasted_iota(jnp.int32, (rows, 128), 1) < HD
    first_all = lax.broadcasted_iota(jnp.int32, (2 * rows, 128), 1) < HD

    @pl.loop(0, D // 128, unroll=2)
    def heads(index):
        columns = pl.ds(pl.multiple_of(index * 128, 128), 128)
        values_at = pl.ds(pl.multiple_of(index * 128 + D, 128), 128)
        query = query_ref[:, columns]
        upstream = total[:, columns].astype(low)
        keys = jnp.concatenate([own_ref[:, columns], far_ref[:, columns]], axis=0)
        values = jnp.concatenate([own_ref[:, values_at], far_ref[:, values_at]], axis=0)
        d_queries, d_keys, d_values = [], [], []
        for side in range(2):
            mine = jnp.where(first == (side == 0), query, jnp.zeros_like(query))
            grad = jnp.where(first == (side == 0), upstream, jnp.zeros_like(upstream))
            weight = attention_weight(mine, keys, allow)
            d_values.append(contract_rows(weight.astype(low), upstream))
            d_weight = contract_cols(grad, values)
            d_score = weight * (d_weight - jnp.sum(d_weight * weight, axis=-1, keepdims=True))
            d_score = d_score.astype(low)
            d_queries.append(product(d_score, keys) * scale)
            d_keys.append(contract_rows(d_score, query) * scale)
        d_query_ref[:, columns] = jnp.where(first, *d_queries).astype(low)
        d_key = jnp.where(first_all, *d_keys)
        d_value = jnp.where(first_all, *d_values)
        d_own_ref[:, columns] = d_key[:rows]
        d_own_ref[:, values_at] = d_value[:rows]
        d_far_ref[:, columns] = d_key[rows:].astype(low)
        d_far_ref[:, values_at] = d_value[rows:].astype(low)


def backward(gradient, middle, query, own, far, rows, columns, w_out, gain, w_gu, w_down):
    count = gradient.shape[0]
    f32 = jnp.float32
    outs = [
        ((count, D), low),
        ((count, 2 * D), f32),
        ((count, 2 * D), low),
        ((count, D), f32),
        ((1, D), f32),
        ((count, D), low),
        ((count, D), low),
        ((count, FF), low),
        ((count, 2 * FF), low),
        ((count, D), low),
    ]
    args = [gradient, middle, query, own, far, rows, columns, w_out, gain, w_gu, w_down]
    scratch = weight_buffers() + [pltpu.VMEM((count, D), f32)]
    return local_call(backward_kernel, "backward", 30 * 10**9, outs, args, scratch, (9, 10))


def unproject_kernel(d_query_ref, d_own_ref, d_far_ref, d_middle_ref, hidden_ref, *refs):
    gain_ref, weight_ref, cosine_ref, sine_ref, gradient_ref, gain_out, d_qkv_ref = refs
    cosine, sine = cosine_ref[...], sine_ref[...]
    first = lax.broadcasted_iota(jnp.int32, cosine.shape, 1) % HD < HD // 2
    for index in range(3 * D // 128):
        columns = pl.ds(index * 128, 128)
        if index < D // 128:
            value = d_query_ref[:, columns].astype(jnp.float32)
        else:
            there = pl.ds(index * 128 - D, 128)
            value = d_own_ref[:, there] + d_far_ref[:, there].astype(jnp.float32)
            value = value.astype(low).astype(jnp.float32)
        if index < 2 * D // 128:
            part = value * sine
            turned = jnp.where(
                first, pltpu.roll(part, 128 - HD // 2, 1), -pltpu.roll(part, HD // 2, 1)
            )
            value = value * cosine + turned
        d_qkv_ref[:, columns] = value.astype(low)
    hidden = hidden_ref[...]
    d_hidden, gain_out[...] = norm_back(
        hidden, inverse_rms(hidden), gain_ref[...], product(d_qkv_ref[...], weight_ref[...])
    )
    gradient_ref[...] = d_middle_ref[...] + d_hidden


def unproject(d_query, d_own, d_far, d_middle, hidden, gain, weight, cosine, sine):
    rows = hidden.shape[0]
    outs = [((rows, D), jnp.float32), ((1, D), jnp.float32), ((rows, 3 * D), low)]
    args = [d_query, d_own, d_far, d_middle, hidden, gain, weight, cosine, sine]
    return local_call(unproject_kernel, "unproject", 10**6, outs, args)


def weigh_kernel(*refs):
    pairs = [refs[4 * index : 4 * index + 4] for index in range(4)]
    gate_out, down_out, joined, qkv, out = refs[16:21]
    now = pl.program_id(0)

    def gradient(index):
        left_one, left_two, right_one, right_two = pairs[index]
        total = contract_rows(left_one[...], right_one[...])
        return total + contract_rows(left_two[...], right_two[...])

    gate_out[...] = gradient(0).astype(low).reshape(gate_out.shape)
    down_out[...] = gradient(1).astype(low).reshape(down_out.shape)

    @pl.when(now < 6)
    def first():
        qkv[pl.ds(pl.multiple_of(now * 384, 384), 384)] = gradient(2)

    @pl.when(now >= 6)
    def second():
        out[pl.ds(pl.multiple_of((now - 6) * 384, 384), 384)] = gradient(3)

    @pl.when(now == 7)
    def join():
        blocks = joined.shape[0]
        tall, flat = 3 * D // blocks, D // blocks
        for block in range(blocks):
            parts = [qkv[block * tall : (block + 1) * tall], out[block * flat : (block + 1) * flat]]
            joined[block] = jnp.concatenate(parts, axis=0).astype(low)


def weigh(d_gates, normed_twos, actions, lows, d_qkvs, normeds, middles, merges, blocks):
    rows = lows[0].shape[0]

    def both(arrays, width, place):
        return [(array, pl.BlockSpec((rows, width), place)) for array in arrays]

    def whole(arrays):
        return [(array, pl.BlockSpec((rows, D), lambda i: (0, 0))) for array in arrays]

    def early(i):
        return (0, jnp.minimum(i, 5))

    def late(i):
        return (0, jnp.maximum(i - 6, 0))

    listed = both(d_gates, 768, lambda i: (0, i)) + whole(normed_twos)
    listed += both(actions, 384, lambda i: (0, i)) + whole(lows)
    listed += both(d_qkvs, 384, early) + whole(normeds)
    listed += both(middles, 384, late) + whole(merges)
    part = blocks // 8
    return pl.pallas_call(
        weigh_kernel,
        grid=(8,),
        out_shape=[
            jax.ShapeDtypeStruct((blocks, 2 * FF // blocks, D), low),
            jax.ShapeDtypeStruct((blocks, FF // blocks, D), low),
            jax.ShapeDtypeStruct((blocks, 4 * D // blocks, D), low),
        ],
        in_specs=[spec for unused, spec in listed],
        out_specs=[
            pl.BlockSpec((part, 2 * FF // blocks, D), lambda i: (i, 0, 0)),
            pl.BlockSpec((part, FF // blocks, D), lambda i: (i, 0, 0)),
            pl.BlockSpec((blocks, 4 * D // blocks, D), lambda i: (0, 0, 0)),
        ],
        scratch_shapes=[pltpu.VMEM((3 * D, D), jnp.float32), pltpu.VMEM((D, D), jnp.float32)],
        compiler_params=pltpu.CompilerParams(vmem_limit_bytes=LARGE),
        cost_estimate=cost(10**6),
        name="weigh",
    )(*[array for array, unused in listed])


def loss_kernel(hidden_ref, gain_ref, near_ref, far_ref, own_ref, other_ref, weight_ref, *refs):
    gradient_ref, gain_out, loss_ref, near_out, far_out, logits, teach = refs
    head = lax.axis_index("head")
    rows = hidden_ref.shape[0]
    half = rows // 2
    size = near_ref.shape[1]
    hidden = hidden_ref[...]
    r = inverse_rms(hidden)
    normed = (hidden * r * gain_ref[...]).astype(low)
    parts = [(near_ref, near_out, 0, 0), (near_ref, near_out, 1, 2)]
    parts += [(far_ref, far_out, 0, 1), (far_ref, far_out, 1, 3)]
    for index, (source, unused, place, offset) in enumerate(parts):
        columns = pl.ds(pl.multiple_of((head ^ offset) * size, size), size)
        logits[index] = contract_cols(normed, source[place])
        teach[index, :half] = own_ref[:, columns].astype(jnp.float32)
        teach[index, half:] = other_ref[:, columns].astype(jnp.float32)

    def log_total(values):
        summit = jnp.max(jnp.max(values[...], axis=0), axis=-1, keepdims=True)
        return summit + jnp.log(
            jnp.sum(jnp.sum(jnp.exp(values[...] - summit[None]), axis=0), axis=-1, keepdims=True)
        )

    log_logits, log_teach = log_total(logits), log_total(teach)
    weighting = weight_ref[...]
    gradient = jnp.zeros((rows, hidden.shape[1]), jnp.float32)
    loss = jnp.zeros((rows, 1), jnp.float32)
    for index, (source, goal, place, offset) in enumerate(parts):
        log_prob = logits[index] - log_logits
        log_true = teach[index] - log_teach
        true = jnp.exp(log_true)
        loss = loss + jnp.sum(true * (log_true - log_prob), axis=-1, keepdims=True)
        d_logits = ((jnp.exp(log_prob) - true) * weighting).astype(low)
        goal[place] = contract_rows(d_logits, normed).astype(low)
        gradient = gradient + product(d_logits, source[place])
    loss_ref[...] = jnp.broadcast_to(
        jnp.sum(loss * weighting, axis=0, keepdims=True), loss_ref.shape
    )
    gradient_ref[...], gain_out[...] = norm_back(hidden, r, gain_ref[...], gradient)


def distill(hidden, gain, near, far, own, other, weighting):
    rows, width = hidden.shape
    size = near.shape[1]
    vmem = pl.BlockSpec(memory_space=pltpu.VMEM)
    f32 = jnp.float32
    return pl.pallas_call(
        loss_kernel,
        out_shape=[
            jax.ShapeDtypeStruct(hidden.shape, f32),
            jax.ShapeDtypeStruct(gain.shape, f32),
            jax.ShapeDtypeStruct((8, 128), f32),
            jax.ShapeDtypeStruct(near.shape, low),
            jax.ShapeDtypeStruct(far.shape, low),
        ],
        in_specs=[vmem] * 7,
        out_specs=[vmem] * 5,
        scratch_shapes=[pltpu.VMEM((4, rows, size), f32)] * 2,
        compiler_params=pltpu.CompilerParams(vmem_limit_bytes=58 * 2**20),
        name="distill",
    )(hidden, gain, near, far, own, other, weighting)


def on_device(
    token_ids,
    lengths,
    valid,
    vocab_ids,
    teacher,
    block,
    block_m,
    block_v,
    bases,
    table,
    table_m,
    table_v,
    gains,
    gains_m,
    gains_v,
):
    dp_count, head_count = lax.axis_size("dp"), lax.axis_size("head")
    device_total = dp_count * head_count
    head, dp = lax.axis_index("head"), lax.axis_index("dp")
    batch = head // 2
    tokens = token_ids.shape[1]
    shard_rows = table.shape[0]
    offset = dp * shard_rows
    part = TOPV // device_total

    widths = [3 * D // device_total, D // device_total, 2 * FF // device_total, FF // device_total]
    cuts = [sum(widths[:index]) for index in range(5)]
    block_low = block.T.astype(low)
    pieces = [block_low[cuts[index] : cuts[index + 1]] for index in range(4)]
    *weights, rows_in, codes, near, far = start(
        pieces,
        table,
        (token_ids * 2 + valid).reshape(-1, 1, tokens),
        vocab_ids,
        dp_count,
    )
    codes = codes.reshape(dp_count, 2 * tokens)
    weighting = (lax.dynamic_index_in_dim(codes, dp, 0, keepdims=False) & 1).astype(jnp.float32)
    vocab = lax.dynamic_index_in_dim(
        vocab_ids.reshape(head_count, dp_count, part), head, 0, keepdims=False
    )
    local = jnp.concatenate([vocab, codes >> 1], axis=1) - offset
    owned = (local >= 0) & (local < shard_rows)
    weights = [weight.reshape(-1, D) for weight in weights]
    near = near.reshape(2, -1, D)
    far = far.reshape(2, -1, D)
    hidden = rows_in[part:].astype(jnp.float32)

    teacher_own = lax.dynamic_index_in_dim(teacher, batch, 0, keepdims=False)
    teacher_far = swap(
        lax.dynamic_index_in_dim(teacher, 1 - batch, 0, keepdims=False), head_count, 2
    )

    run = jnp.arange(tokens, dtype=jnp.int32)
    places = jnp.concatenate([head * tokens + run, (head ^ 2) * tokens + run])
    places_far = jnp.concatenate([(head ^ 1) * tokens + run, (head ^ 3) * tokens + run])
    own_lengths = lax.dynamic_index_in_dim(lengths, batch, 0, keepdims=False)[0]
    segment, position = segments(own_lengths, places)
    segment_far, unused = segments(own_lengths, places_far)
    queries_at = jnp.stack([segment, places], axis=1)
    keys_at = jnp.stack(
        [jnp.concatenate([segment, segment_far]), jnp.concatenate([places, places_far])]
    )
    freqs = jnp.exp(jnp.arange(0, HD, 2, dtype=jnp.float32) * (-math.log(10000.0) / HD))
    angle = position.astype(jnp.float32)[:, None] * jnp.tile(freqs, 4)[None, :]
    cosine, sine = jnp.cos(angle), jnp.sin(angle)

    w_qkv, w_out, w_gu, w_down = weights
    saves = []
    for repeat in range(2):
        normed, query, own = project(hidden, gains[0:1], w_qkv, cosine, sine)
        if repeat == 1:
            own, teacher_far = lax.optimization_barrier((own, teacher_far))
        other = swap(own, head_count, 1)
        output, merged, middle = forward(
            hidden, query, own, other, queries_at, keys_at, w_out, gains[1:2], w_gu, w_down
        )
        saves.append((hidden, normed, query, own, other, merged, middle))
        hidden = output
    gradient, d_gain_final, loss_sum, d_near, d_far = distill(
        hidden, gains[2:3], near, far, teacher_own, teacher_far, weighting[:, None]
    )
    d_gain_final, loss_sum = d_gain_final[0], loss_sum[0, 0]
    f32 = jnp.float32
    gradient, d_far = lax.optimization_barrier((gradient, swap(d_far, head_count, 1)))
    d_near = (d_near.astype(f32) + d_far.astype(f32)).astype(low)
    d_quarter = swap(d_near[1], head_count, 2)

    d_gains = [0.0, 0.0]
    parts = []
    for repeat in range(2):
        hidden, normed, query, own, other, merged, middle = saves[1 - repeat]
        back = backward(
            gradient, middle, query, own, other, queries_at, keys_at, w_out, gains[1:2], w_gu, w_down
        )
        d_query, d_own, d_other, d_middle, d_gain_two = back[:5]
        grad_low, normed_two, action, d_gate, middle_low = back[5:]
        gradient, d_gain_one, d_qkv = unproject(
            d_query,
            d_own,
            swap(d_other, head_count, 1),
            d_middle,
            hidden,
            gains[0:1],
            w_qkv,
            cosine,
            sine,
        )
        if repeat == 0:
            gradient, d_quarter = lax.optimization_barrier((gradient, d_quarter))
            d_quarter = (d_near[0].astype(f32) + d_quarter.astype(f32)).astype(low)
            chosen_grads = lax.psum_scatter(d_quarter, "dp", scatter_dimension=0, tiled=True)
        parts.append((d_gate, normed_two, action, grad_low, d_qkv, normed, middle_low, merged))
        d_gains = [d_gains[0] + d_gain_one[0], d_gains[1] + d_gain_two[0]]

    d_gu, d_down, d_attention = weigh(*zip(*parts), device_total)
    rows_back = jnp.concatenate([chosen_grads, gradient.astype(low)], axis=0)
    step = 80 if shard_rows % 80 == 0 else 40
    quarter = -(-shard_rows // (step * head_count)) * step
    tile = quarter // 5 if quarter % 80 == 0 and quarter // 5 % 16 == 0 else step
    small = [d_gains[0], d_gains[1], d_gain_final, loss_sum[None], jnp.sum(weighting)[None]]
    small = jnp.pad(jnp.concatenate(small), (0, 6 * 128 - 2)).reshape(-1, 128)
    block_grads, table_grads, small = finish(
        [d_attention, d_gu, d_down],
        rows_back,
        by_side(jnp.where(owned, local, -1), dp_count // 2),
        small,
        quarter,
        tile,
    )
    outs = update(
        cuts,
        [table, table_m, table_v],
        table_grads.reshape(-1, D),
        small,
        small[: 3 * D // 128].reshape(3, D),
        [gains, gains_m, gains_v],
        block_grads.T,
        [block, block_m, block_v],
        bases,
    )
    table_new, table_m_new, table_v_new, table_low = outs[0:4]
    values, gains_new, gains_m_new, gains_v_new = outs[4:8]
    block_new, block_m_new, block_v_new, block_low = outs[8:12]
    return (
        values[0, 0],
        values[0, 1],
        block_new,
        block_m_new,
        block_v_new,
        table_new,
        table_m_new,
        table_v_new,
        gains_new,
        gains_m_new,
        gains_v_new,
        block_low,
        table_low,
    )


def solution(mesh):
    tokens = P(None, ("dp", "head"))
    columns = P(None, ("dp", "head"))
    table = P("dp", None)
    return jax.shard_map(
        on_device,
        mesh=mesh,
        in_specs=(
            tokens,
            P(None, "dp", None),
            tokens,
            P(),
            P(None, ("dp", "head"), None),
            columns,
            columns,
            columns,
            P(),
            table,
            table,
            table,
            P(),
            P(),
            P(),
        ),
        out_specs=(
            P(),
            P(),
            columns,
            columns,
            columns,
            table,
            table,
            table,
            P(),
            P(),
            P(),
            columns,
            table,
        ),
        check_vma=False,
    )
```
